32 devices in a mesh: grp: 4 (over x, core), dp: 8 (over z, y).
Axes of the slice: x: 2, y: 2, z: 4, core: 2. Of those that a mesh axis runs over, the one named last changes fastest.
Arguments:
- tokens: bfloat16 [2, 8192, 512], P(None, ('grp', 'dp')), may hold values from -6 to 6
- memory: bfloat16 [2, 8192, 512], P(None, ('grp', 'dp')), may hold values from -6 to 6
- expert_slot: int32 [2, 8192, 1], P(None, ('grp', 'dp')), may hold values from 0 to 1; in each aligned block of 256 rows (0 to 255, 256 to 511, ..., all dimensions but the last counted through in order) at most 160 rows name the same one
- doc_lengths: int32 [2, 4, 4], P(None, 'grp'), may hold values from 1 to 2045, as said below
- source_lengths: int32 [2, 4, 4], P(None, 'grp'), may hold values from 1 to 2045, as said below
- cotangent: bfloat16 [2, 8192, 512], P(None, ('grp', 'dp')), may hold values from -6 to 6
- norm1_gain: float32 [512], replicated, may hold values from 0.1 to 1.9
- norm1_shift: float32 [512], replicated, may hold values from -1.25 to 1.25
- self_query: bfloat16 [512, 512], replicated, may hold values from -0.25 to 0.25
- self_key: bfloat16 [512, 512], replicated, may hold values from -0.25 to 0.25
- self_value: bfloat16 [512, 512], replicated, may hold values from -0.25 to 0.25
- self_out: bfloat16 [512, 512], replicated, may hold values from -2 to 2
- norm2_gain: float32 [512], replicated, may hold values from 0.1 to 1.9
- norm2_shift: float32 [512], replicated, may hold values from -1.25 to 1.25
- cross_query: bfloat16 [512, 512], replicated, may hold values from -0.25 to 0.25
- cross_key: bfloat16 [512, 512], replicated, may hold values from -0.25 to 0.25
- cross_value: bfloat16 [512, 512], replicated, may hold values from -0.25 to 0.25
- cross_out: bfloat16 [512, 512], replicated, may hold values from -3 to 3
- norm3_gain: float32 [512], replicated, may hold values from 0.1 to 1.9
- norm3_shift: float32 [512], replicated, may hold values from -1.25 to 1.25
- up_weight: bfloat16 [8, 512, 2048], P('grp'), may hold values from -0.25 to 0.25
- up_bias: float32 [8, 2048], P('grp'), may hold values from -1.75 to 1.75
- down_weight: bfloat16 [8, 2048, 512], P('grp'), may hold values from -0.125 to 0.125
- down_bias: float32 [8, 512], P('grp'), may hold values from -1.75 to 1.75
Outputs:
- block_out: bfloat16 [2, 8192, 512], P(None, ('grp', 'dp'))
- token_grad: float32 [2, 8192, 512], P(None, ('grp', 'dp'))
- norm1_gain_grad: float32 [512], replicated
- norm1_shift_grad: float32 [512], replicated
- self_query_grad: float32 [512, 512], replicated
- self_key_grad: float32 [512, 512], replicated
- self_value_grad: float32 [512, 512], replicated
- self_out_grad: float32 [512, 512], replicated
- norm2_gain_grad: float32 [512], replicated
- norm2_shift_grad: float32 [512], replicated
- cross_query_grad: float32 [512, 512], replicated
- cross_key_grad: float32 [512, 512], replicated
- cross_value_grad: float32 [512, 512], replicated
- cross_out_grad: float32 [512, 512], replicated
- norm3_gain_grad: float32 [512], replicated
- norm3_shift_grad: float32 [512], replicated
- up_weight_grad: float32 [8, 512, 2048], P('grp')
- up_bias_grad: float32 [8, 2048], P('grp')
- down_weight_grad: float32 [8, 2048, 512], P('grp')
- down_bias_grad: float32 [8, 512], P('grp')
The draws below stay inside these ranges and needn't reach their ends.
Inputs may be any that keep to these rules, and one draw needn't show every extreme that they name: `expert_slot`: the rows of one device in one micro-batch name each of their group's 2 experts at most 160 times. `doc_lengths`: A row holds the lengths of the 4 documents of one target stream, in order; they sum to 2048. `source_lengths`: A row holds the lengths of the 4 documents of one source stream, in order; they sum to 2048.
All inputs are finite; a program needn't handle non-finite values.
Results may differ from the reference program's by a relative error of at most 0.022.
Values may be sent and summed in bfloat16 or wider, within the bound.
A program may use at most 448 MiB of HBM per device.

```python
import math
import jax
import jax.numpy as jnp
import numpy as np
from jax import lax

D = 512
HEADS = 8
FF = 2048
EXP_GRP = 2
MB = 2
DOCS = 4
TOK_MB = 256
MEM_DEV = 256
CAP = 160
GROUPS = 4
EXPERTS = 8
GROUP_LEN = 2048
SRC_LEN = 2048
TOKENS = 8192
SOURCES = 8192


def long_place(key):
    return jax.random.randint(jax.random.fold_in(key, 7), (MB, GROUPS, 1), 0, DOCS)


def document_lengths(key, chosen, whole, short_most):
    shorts = jax.random.randint(key, (MB, GROUPS, DOCS), 1, short_most + 1)
    picked = jax.random.randint(jax.random.fold_in(key, 5), (), 0, MB * GROUPS)
    stream_ids = jnp.arange(MB * GROUPS, dtype=jnp.int32).reshape(MB, GROUPS, 1)
    shorts = jnp.where(stream_ids == picked, 1, shorts)
    places = jnp.arange(DOCS, dtype=jnp.int32)[None, None, :]
    is_long = places == chosen
    shorts = jnp.where(is_long, 0, shorts)
    remainder = whole - jnp.sum(shorts, axis=2, keepdims=True)
    return jnp.where(is_long, remainder, shorts).astype(jnp.int32)


def draw_doc_lengths(key, part):
    chosen = long_place(key)
    key = jax.random.fold_in(key, 11)
    return document_lengths(key, chosen, GROUP_LEN, TOK_MB // DOCS)


def draw_source_lengths(key, part):
    chosen = long_place(key)
    key = jax.random.fold_in(key, 12)
    return document_lengths(key, chosen, SRC_LEN, MEM_DEV // DOCS)


def levels(rng, dims, shards, least, largest):
    def one(position, blocks):
        heights = jax.random.uniform(jax.random.fold_in(jax.random.fold_in(rng, 6), position), (blocks,), jnp.float32, least / len(shards), largest / len(shards))
        return jnp.repeat(jnp.exp(heights), dims[position] // blocks).reshape((-1,) + (1,) * (len(dims) - position - 1))

    factor_of = one(*shards[0])
    for cut in shards[1:]:
        factor_of = factor_of * one(*cut)
    return factor_of


def shared_out(rng, own, number, rows, number_of, top, reach, lean):
    sequence = jax.random.permutation(rng, number_of)
    packed, common = load_shares(number_of, rows * top, reach, lean, True), load_shares(number_of, rows * top, reach, lean, False)
    places = jnp.arange(number_of)

    def named(tallies, turn):
        used = int((tallies > 0).sum())
        fixed = max(1, used // 4)
        passed = fixed + (places - fixed + turn * (used - fixed)) % max(1, number_of - fixed)
        return jnp.zeros((number_of,), jnp.int32).at[sequence[jnp.where(places < fixed, places, passed)]].set(jnp.asarray(tallies, jnp.int32))

    tallies = jnp.where(number % 4 == 0, named(packed, number // 4), named(common, number - number // 4 - 1))
    mixed = jax.random.permutation(jax.random.fold_in(own, 3), number_of)
    giver, sink = mixed[0:number_of // 2 * 2:2], mixed[1:number_of // 2 * 2:2]
    slack = jnp.minimum(tallies[giver] - 1, reach - tallies[sink]) // 2
    slack = jnp.where((giver == sequence[0]) | (sink == sequence[0]) | (tallies[sink] == 0), 0, jnp.maximum(slack, 0))
    passed = jax.random.randint(jax.random.fold_in(own, 4), (number_of // 2,), 0, 1 << 20) % (slack + 1)
    tallies = tallies.at[giver].add(-passed).at[sink].add(passed)
    members = jnp.searchsorted(jnp.cumsum(tallies), jnp.arange(rows * top), side="right").astype(jnp.int32)
    listing = members.reshape(top, rows).T
    listing = listing[jax.random.permutation(jax.random.fold_in(own, 1), rows)]
    turn = jax.random.randint(jax.random.fold_in(own, 2), (rows, 1), 0, top)
    return jnp.take_along_axis(listing, (jnp.arange(top)[None, :] + turn) % top, axis=1)


def load_shares(count, total, bound, slope, full):
    portions = [(1 << 20) // math.isqrt(standing ** slope) + 1 for standing in range(1, count + 1)]
    largest = bound if full else min(bound, max(-(-total // count), total * portions[0] // sum(portions)))
    least = 1 if total - largest >= count - 1 else 0
    counts, surplus = [largest] + [least] * (count - 1), total - largest - least * (count - 1)
    while surplus > 0:
        movable = [i for i in range(1, count) if counts[i] < largest] or [i for i in range(1, count) if counts[i] < bound]
        whole, left = sum([portions[i] for i in movable]), surplus
        for i in movable:
            extra = min(bound - counts[i], max(1, left * portions[i] // whole), surplus)
            counts[i] = counts[i] + extra
            surplus = surplus - extra
    return np.array(counts)


def bell_draw(rng, extent, scale, reach, cuts=(), kind=jnp.bfloat16):
    level = levels(rng, extent, cuts, -0.22, 0.18) if cuts else 1.0
    drawn = jax.random.normal(rng, extent, jnp.float32) * scale * level
    return jnp.minimum(jnp.maximum(drawn, -reach), reach).astype(kind)


def setup_inputs(seed: int = 0) -> dict:
    key_of = jax.random.split(jax.random.key(seed), 25)
    tokens = bell_draw(key_of[0], (MB, TOKENS, D), 1.0, 6.0, ((1, 32),))
    memory = bell_draw(key_of[1], (MB, SOURCES, D), 1.0, 6.0, ((1, 32),))
    expert_slot_keys = jax.random.split(jax.random.fold_in(key_of[2], 1), MB * TOKENS // TOK_MB)
    expert_slot_turns = jax.random.permutation(jax.random.fold_in(key_of[2], 3), MB * TOKENS // TOK_MB)
    expert_slot = jax.vmap(lambda own, number: shared_out(jax.random.fold_in(key_of[2], 2), own, number, TOK_MB, EXP_GRP, 1, CAP, 1))(expert_slot_keys, expert_slot_turns).reshape((MB, TOKENS, 1))
    doc_lengths = draw_doc_lengths(jax.random.fold_in(key_of[24], 71), 0)
    source_lengths = draw_source_lengths(jax.random.fold_in(key_of[24], 71), 0)
    cotangent = bell_draw(key_of[5], (MB, TOKENS, D), 1.0, 6.0, ((1, 32),))
    norm1_gain = jnp.clip(1.0 + 0.18 * jax.random.normal(key_of[6], (D,), jnp.float32), 0.1, 1.9)
    norm1_shift = bell_draw(key_of[7], (D,), 0.2, 1.25, (), jnp.float32)
    self_query = bell_draw(key_of[8], (D, D), D ** -0.5, 0.25)
    self_key = bell_draw(key_of[9], (D, D), D ** -0.5, 0.25)
    self_value = bell_draw(key_of[10], (D, D), D ** -0.5, 0.25)
    self_out = bell_draw(key_of[11], (D, D), (max(D // 64, 2)) ** -0.5, 2.0)
    norm2_gain = jnp.clip(1.0 + 0.18 * jax.random.normal(key_of[12], (D,), jnp.float32), 0.1, 1.9)
    norm2_shift = bell_draw(key_of[13], (D,), 0.2, 1.25, (), jnp.float32)
    cross_query = bell_draw(key_of[14], (D, D), D ** -0.5, 0.25)
    cross_key = bell_draw(key_of[15], (D, D), D ** -0.5, 0.25)
    cross_value = bell_draw(key_of[16], (D, D), D ** -0.5, 0.25)
    cross_out = bell_draw(key_of[17], (D, D), (max(D // 128, 2)) ** -0.5, 3.0)
    norm3_gain = jnp.clip(1.0 + 0.18 * jax.random.normal(key_of[18], (D,), jnp.float32), 0.1, 1.9)
    norm3_shift = bell_draw(key_of[19], (D,), 0.2, 1.25, (), jnp.float32)
    up_weight = bell_draw(key_of[20], (EXPERTS, D, FF), D ** -0.5, 0.25, ((0, 4),))
    up_bias = bell_draw(key_of[21], (EXPERTS, FF), 0.3, 1.75, ((0, 4),), jnp.float32)
    down_weight = bell_draw(key_of[22], (EXPERTS, FF, D), FF ** -0.5, 0.125, ((0, 4),))
    down_bias = bell_draw(key_of[23], (EXPERTS, D), 0.3, 1.75, ((0, 4),), jnp.float32)
    return dict(tokens=tokens, memory=memory, expert_slot=expert_slot, doc_lengths=doc_lengths, source_lengths=source_lengths, cotangent=cotangent, norm1_gain=norm1_gain, norm1_shift=norm1_shift, self_query=self_query, self_key=self_key, self_value=self_value, self_out=self_out, norm2_gain=norm2_gain, norm2_shift=norm2_shift, cross_query=cross_query, cross_key=cross_key, cross_value=cross_value, cross_out=cross_out, norm3_gain=norm3_gain, norm3_shift=norm3_shift, up_weight=up_weight, up_bias=up_bias, down_weight=down_weight, down_bias=down_bias)


@jax.custom_vjp
def low(v):
    return lax.optimization_barrier(v.astype(jnp.bfloat16)).astype(jnp.float32)

@jax.custom_vjp
def low_back(v):
    return v

def low_keep(v):
    return (low(v), None)

def low_pass(kept, grad):
    return (grad,)

def back_keep(v):
    return (v, None)

def back_low(kept, grad):
    return (low(grad),)
low.defvjp(low_keep, low_pass)
low_back.defvjp(back_keep, back_low)
masked_score = -1e+30

def matmul(left, right):
    return jnp.dot(left, right, precision=lax.Precision.HIGHEST)

def layer_norm(inputs, norm_gain, norm_shift):
    mean_row = lax.optimization_barrier(jnp.mean(inputs, axis=-1, keepdims=True))
    centred = inputs - mean_row
    spread = lax.optimization_barrier(jnp.mean(centred * centred, axis=-1, keepdims=True))
    return centred * lax.rsqrt(spread + 1e-05) * norm_gain + norm_shift

def doc_index(lengths, places):
    doc_ends = jnp.cumsum(lengths).astype(jnp.int32)
    return lax.optimization_barrier(jnp.sum((places[:, None] >= doc_ends[None, :]).astype(jnp.int32), axis=1)).astype(jnp.int32)

def attend(queries, keys_all, values_all, query_docs, key_docs, query_places, key_places, causal):
    count = queries.shape[0]
    block = min(512, count)
    head_size = D // HEADS
    scaling = 1.0 / math.sqrt(head_size)
    key_heads = keys_all.reshape(keys_all.shape[0], HEADS, head_size)
    value_heads = values_all.reshape(values_all.shape[0], HEADS, head_size)

    @jax.checkpoint
    def one_block(pieces):
        query_part, docs_part, places_part = pieces
        scores = low_back(jnp.einsum('qhd,khd->hqk', query_part, key_heads, precision=lax.Precision.HIGHEST) * scaling)
        allowed = docs_part[:, None] == key_docs[None, :]
        if causal:
            allowed = allowed & (key_places[None, :] <= places_part[:, None])
        scores = jnp.where(allowed[None], scores, masked_score)
        maximum = lax.optimization_barrier(jnp.max(scores, axis=-1, keepdims=True))
        exponent = jnp.exp(scores - maximum)
        probability = low(exponent / lax.optimization_barrier(jnp.sum(exponent, axis=-1, keepdims=True)))
        mixed = jnp.einsum('hqk,khd->qhd', probability, value_heads, precision=lax.Precision.HIGHEST)
        return mixed.reshape(block, D)
    blocks = count // block
    result = lax.map(one_block, (queries.reshape(blocks, block, HEADS, head_size), query_docs.reshape(blocks, block), query_places.reshape(blocks, block)))
    return result.reshape(count, D)

def stream_forward(params, pieces):
    gain_one, shift_one, weight_sq, weight_sk, weight_sv, weight_so, gain_two, shift_two, weight_cq, weight_ck, weight_cv, weight_co, gain_three, shift_three, up_all, up_bias_all, down_all, down_bias_all = params
    stream_in, source_in, slots, lengths, source_lens, index = pieces
    first = (index % GROUPS * EXP_GRP).astype(jnp.int32)
    places = jnp.arange(GROUP_LEN, dtype=jnp.int32)
    source_places = jnp.arange(SRC_LEN, dtype=jnp.int32)
    query_docs = doc_index(lengths, places)
    source_docs = doc_index(source_lens, source_places)
    attn_in = low(layer_norm(stream_in, gain_one, shift_one))
    queries = low(low_back(matmul(attn_in, weight_sq)))
    keys_self = low(low_back(matmul(attn_in, weight_sk)))
    values_self = low(low_back(matmul(attn_in, weight_sv)))
    self_mixed = low(low_back(attend(queries, keys_self, values_self, query_docs, query_docs, places, places, True)))
    after_self = stream_in + low_back(matmul(self_mixed, weight_so))
    cross_in = low(layer_norm(after_self, gain_two, shift_two))
    cross_queries = low(low_back(matmul(cross_in, weight_cq)))
    cross_keys = low(matmul(source_in, weight_ck))
    cross_values = low(matmul(source_in, weight_cv))
    cross_mixed = low(low_back(attend(cross_queries, cross_keys, cross_values, query_docs, source_docs, places, source_places, False)))
    after_cross = after_self + low_back(matmul(cross_mixed, weight_co))
    expert_in = low(layer_norm(after_cross, gain_three, shift_three))
    up_here = lax.dynamic_slice_in_dim(up_all, first, EXP_GRP, 0)
    up_bias_here = lax.dynamic_slice_in_dim(up_bias_all, first, EXP_GRP, 0)
    down_here = lax.dynamic_slice_in_dim(down_all, first, EXP_GRP, 0)
    down_bias_here = lax.dynamic_slice_in_dim(down_bias_all, first, EXP_GRP, 0)
    result = after_cross
    for slot_number in range(EXP_GRP):
        pre_act = low_back(matmul(expert_in, up_here[slot_number]) + up_bias_here[slot_number])
        hidden = low(jax.nn.gelu(pre_act))
        branch = low_back(matmul(hidden, down_here[slot_number]) + down_bias_here[slot_number])
        result = result + jnp.where((slots == slot_number)[:, None], branch, 0.0)
    return result

def reference(tokens, memory, expert_slot, doc_lengths, source_lengths, cotangent, norm1_gain, norm1_shift, self_query, self_key, self_value, self_out, norm2_gain, norm2_shift, cross_query, cross_key, cross_value, cross_out, norm3_gain, norm3_shift, up_weight, up_bias, down_weight, down_bias):
    params = tuple((weight.astype(jnp.float32) for weight in (norm1_gain, norm1_shift, self_query, self_key, self_value, self_out, norm2_gain, norm2_shift, cross_query, cross_key, cross_value, cross_out, norm3_gain, norm3_shift, up_weight, up_bias, down_weight, down_bias)))
    streams = MB * GROUPS
    stream_inputs = tokens.astype(jnp.float32).reshape(streams, GROUP_LEN, D)
    sources = memory.astype(jnp.float32).reshape(streams, SRC_LEN, D)
    slots = expert_slot.reshape(streams, GROUP_LEN)
    lengths = doc_lengths.reshape(streams, DOCS)
    source_lens = source_lengths.reshape(streams, DOCS)
    order = jnp.arange(streams, dtype=jnp.int32)

    def forward(weights, inputs):

        def one_stream(pieces):
            return stream_forward(weights, pieces)
        return lax.map(jax.checkpoint(one_stream), (inputs, sources, slots, lengths, source_lens, order))
    outputs, backward = jax.vjp(forward, params, stream_inputs)
    grads, input_grad = backward(cotangent.astype(jnp.float32).reshape(streams, GROUP_LEN, D))
    block_out = outputs.reshape(MB, TOKENS, D).astype(jnp.bfloat16)
    token_grad = input_grad.reshape(MB, TOKENS, D)
    return (block_out, token_grad, grads[0], grads[1], grads[2], grads[3], grads[4], grads[5], grads[6], grads[7], grads[8], grads[9], grads[10], grads[11], grads[12], grads[13], grads[14], grads[15], grads[16], grads[17])
```

```python
import functools
import math

import jax
import jax.numpy as jnp
from jax import lax
from jax.experimental import pallas as pl
from jax.experimental.pallas import tpu as pltpu
from jax.sharding import PartitionSpec as P

HEADS = 8
CAP = 160


masked_score = -1e30


def layer_norm(inputs, norm_gain, norm_shift):
    mean_row = jnp.mean(inputs, axis=-1, keepdims=True)
    centred = inputs - mean_row
    spread = jnp.mean(centred * centred, axis=-1, keepdims=True)
    return centred * lax.rsqrt(spread + 1e-05) * norm_gain + norm_shift


def doc_index(lengths, places):
    doc_ends = jnp.cumsum(lengths)
    return jnp.sum((places[:, None] >= doc_ends[None, :]).astype(jnp.int32), axis=1)


def product(left, right):
    return jnp.dot(left, right, preferred_element_type=jnp.float32)


def left_product(left, right):
    return jnp.einsum("nd,ne->de", left, right, preferred_element_type=jnp.float32)


def right_product(left, right):
    return jnp.einsum("nd,ed->ne", left, right, preferred_element_type=jnp.float32)


def exact_left(left, right):
    return jnp.einsum("nd,ne->de", left, right, precision=lax.Precision.HIGHEST)


def split_heads(matrix, head_count):
    return matrix.reshape(matrix.shape[0], head_count, matrix.shape[1] // head_count)


def attend_forward(queries, keys_all, values_all, allowed, head_count):
    scaling = 1.0 / math.sqrt(queries.shape[1] // head_count)
    scores = (
        jnp.einsum(
            "qhd,khd->hqk",
            split_heads(queries, head_count),
            split_heads(keys_all, head_count),
            preferred_element_type=jnp.float32,
        )
        * scaling
    )
    scores = jnp.where(allowed[None], scores, masked_score)
    maximum = jnp.max(scores, axis=-1, keepdims=True)
    exponent = jnp.exp(scores - maximum)
    totals = jnp.sum(exponent, axis=-1, keepdims=True)
    probability = (exponent / totals).astype(jnp.bfloat16)
    mixed = jnp.einsum(
        "hqk,khd->qhd",
        probability,
        split_heads(values_all, head_count),
        preferred_element_type=jnp.float32,
    )
    return (mixed.reshape(queries.shape[0], queries.shape[1]), maximum + jnp.log(totals))


def score_parts(
    query_heads, key_heads, value_heads, grad_heads, allowed, scaling, log_total, centre
):
    scores = (
        jnp.einsum("qhd,khd->hqk", query_heads, key_heads, preferred_element_type=jnp.float32)
        * scaling
    )
    scores = jnp.where(allowed[None], scores, masked_score)
    probability = jnp.exp(scores - log_total)
    prob_grad = jnp.einsum(
        "qhd,khd->hqk", grad_heads, value_heads, preferred_element_type=jnp.float32
    )
    centre = jnp.sum(probability * prob_grad, axis=-1, keepdims=True)
    score_grad = (probability * (prob_grad - centre)).astype(jnp.bfloat16)
    return (probability, score_grad, centre)


def attend_backward(queries, keys_all, values_all, allowed, head_count, log_total, out_grad):
    scaling = 1.0 / math.sqrt(queries.shape[1] // head_count)
    query_heads = split_heads(queries, head_count)
    key_heads = split_heads(keys_all, head_count)
    grad_heads = split_heads(out_grad, head_count)
    probability, score_grad, centre = score_parts(
        query_heads,
        key_heads,
        split_heads(values_all, head_count),
        grad_heads,
        allowed,
        scaling,
        log_total,
        None,
    )
    query_back = (
        jnp.einsum("hqk,khd->qhd", score_grad, key_heads, preferred_element_type=jnp.float32)
        * scaling
    )
    key_back = (
        jnp.einsum("hqk,qhd->khd", score_grad, query_heads, preferred_element_type=jnp.float32)
        * scaling
    )
    value_back = jnp.einsum(
        "hqk,qhd->khd",
        probability.astype(jnp.bfloat16),
        grad_heads,
        preferred_element_type=jnp.float32,
    )
    width = queries.shape[1]
    return (
        query_back.reshape(queries.shape[0], width),
        key_back.reshape(keys_all.shape[0], width),
        value_back.reshape(keys_all.shape[0], width),
    )


def per_device(
    tokens,
    memory,
    expert_slot,
    doc_lengths,
    source_lengths,
    cotangent,
    norm1_gain,
    norm1_shift,
    self_query,
    self_key,
    self_value,
    self_out,
    norm2_gain,
    norm2_shift,
    cross_query,
    cross_key,
    cross_value,
    cross_out,
    norm3_gain,
    norm3_shift,
    up_weight,
    up_bias,
    down_weight,
    down_bias,
):
    micro = tokens.shape[0]
    rows = tokens.shape[1]
    width = tokens.shape[2]
    source_rows = memory.shape[1]
    parts = lax.axis_size("dp")
    place = lax.axis_index("dp")
    experts_here = up_weight.shape[0]
    capacity = CAP
    head_count = HEADS
    local_places = place * rows + jnp.arange(rows, dtype=jnp.int32)
    stream_places = jnp.arange(rows * parts, dtype=jnp.int32)
    source_places = jnp.arange(source_rows * parts, dtype=jnp.int32)
    slot_ids = jnp.arange(experts_here * capacity, dtype=jnp.int32)
    expert_ids = jnp.arange(experts_here, dtype=jnp.int32)
    inputs = tokens.astype(jnp.float32)
    normed_first, first_back = jax.vjp(layer_norm, inputs, norm1_gain, norm1_shift)
    attn_in = normed_first.astype(jnp.bfloat16)
    queries = product(attn_in, self_query).astype(jnp.bfloat16)
    keys_mine = product(attn_in, self_key).astype(jnp.bfloat16)
    values_mine = product(attn_in, self_value).astype(jnp.bfloat16)
    keys_all, values_all = (
        lax.all_gather(keys_mine, "dp", axis=1, tiled=True),
        lax.all_gather(values_mine, "dp", axis=1, tiled=True),
    )
    cross_keys_all, cross_values_all = (
        lax.all_gather(product(memory, cross_key).astype(jnp.bfloat16), "dp", axis=1, tiled=True),
        lax.all_gather(product(memory, cross_value).astype(jnp.bfloat16), "dp", axis=1, tiled=True),
    )
    square_zero = jnp.zeros((width, width), jnp.float32)
    vector_zero = jnp.zeros((width,), jnp.float32)
    grad_self_query, grad_self_key, grad_self_value, grad_self_out = (
        square_zero,
        square_zero,
        square_zero,
        square_zero,
    )
    grad_cross_query, grad_cross_key, grad_cross_value, grad_cross_out = (
        square_zero,
        square_zero,
        square_zero,
        square_zero,
    )
    second_gain_sum, second_shift_sum, third_gain_sum, third_shift_sum = (
        vector_zero,
        vector_zero,
        vector_zero,
        vector_zero,
    )
    grad_up = jnp.zeros(up_weight.shape, jnp.float32)
    grad_up_bias = jnp.zeros(up_bias.shape, jnp.float32)
    grad_down = jnp.zeros(down_weight.shape, jnp.float32)
    grad_down_bias = jnp.zeros(down_bias.shape, jnp.float32)
    outputs = []
    attn_in_grads = []
    resid_grads = []
    for batch_index in range(micro):
        lengths_now = doc_lengths[batch_index, 0]
        query_docs = doc_index(lengths_now, local_places)
        stream_docs = doc_index(lengths_now, stream_places)
        source_docs = doc_index(source_lengths[batch_index, 0], source_places)
        self_allowed = (query_docs[:, None] == stream_docs[None, :]) & (
            stream_places[None, :] <= local_places[:, None]
        )
        cross_allowed = query_docs[:, None] == source_docs[None, :]
        self_result, self_log = attend_forward(
            queries[batch_index],
            keys_all[batch_index],
            values_all[batch_index],
            self_allowed,
            head_count,
        )
        self_mixed = self_result.astype(jnp.bfloat16)
        after_self = inputs[batch_index] + product(self_mixed, self_out)
        normed_second, second_back = jax.vjp(layer_norm, after_self, norm2_gain, norm2_shift)
        cross_in = normed_second.astype(jnp.bfloat16)
        cross_queries = product(cross_in, cross_query).astype(jnp.bfloat16)
        cross_result, cross_log = attend_forward(
            cross_queries,
            cross_keys_all[batch_index],
            cross_values_all[batch_index],
            cross_allowed,
            head_count,
        )
        cross_mixed = cross_result.astype(jnp.bfloat16)
        after_cross = after_self + product(cross_mixed, cross_out)
        normed_third, third_back = jax.vjp(layer_norm, after_cross, norm3_gain, norm3_shift)
        expert_in = normed_third.astype(jnp.bfloat16)
        chosen = expert_slot[batch_index, :, 0]
        one_hot = (chosen[:, None] == expert_ids[None, :]).astype(jnp.int32)
        ranks = jnp.sum((jnp.cumsum(one_hot, axis=0) - 1) * one_hot, axis=1)
        target = chosen * capacity + ranks
        dispatch = (slot_ids[:, None] == target[None, :]).astype(jnp.bfloat16)
        buffer_in = (
            product(dispatch, expert_in).astype(jnp.bfloat16).reshape(experts_here, capacity, width)
        )
        pre_act = (
            jnp.einsum("ecd,edf->ecf", buffer_in, up_weight, preferred_element_type=jnp.float32)
            + up_bias[:, None, :]
        )
        activated, gelu_back = jax.vjp(jax.nn.gelu, pre_act)
        hidden = activated.astype(jnp.bfloat16)
        buffer_out = (
            jnp.einsum("ecf,efd->ecd", hidden, down_weight, preferred_element_type=jnp.float32)
            + down_bias[:, None, :]
        )
        expert_out = jnp.take(buffer_out.reshape(experts_here * capacity, width), target, axis=0)
        outputs.append((after_cross + expert_out).astype(jnp.bfloat16))
        out_grad = cotangent[batch_index].astype(jnp.float32)
        grad_rows = out_grad.astype(jnp.bfloat16)
        buffer_grad = (
            product(dispatch, grad_rows).astype(jnp.bfloat16).reshape(experts_here, capacity, width)
        )
        grad_down = grad_down + jnp.einsum(
            "ecf,ecd->efd", hidden, buffer_grad, preferred_element_type=jnp.float32
        )
        grad_down_bias = grad_down_bias + jnp.sum(buffer_grad.astype(jnp.float32), axis=1)
        hidden_grad = jnp.einsum(
            "ecd,efd->ecf", buffer_grad, down_weight, preferred_element_type=jnp.float32
        )
        pre_grad = gelu_back(hidden_grad)[0].astype(jnp.bfloat16)
        grad_up = grad_up + jnp.einsum(
            "ecd,ecf->edf", buffer_in, pre_grad, preferred_element_type=jnp.float32
        )
        grad_up_bias = grad_up_bias + jnp.sum(pre_grad.astype(jnp.float32), axis=1)
        buffer_back = jnp.einsum(
            "ecf,edf->ecd", pre_grad, up_weight, preferred_element_type=jnp.float32
        )
        expert_in_grad = jnp.take(
            buffer_back.reshape(experts_here * capacity, width), target, axis=0
        )
        third_resid, third_gain, third_shift = third_back(expert_in_grad)
        third_gain_sum = third_gain_sum + third_gain
        third_shift_sum = third_shift_sum + third_shift
        cross_grad = out_grad + third_resid
        cross_rows_grad = cross_grad.astype(jnp.bfloat16)
        grad_cross_out = grad_cross_out + left_product(cross_mixed, cross_rows_grad)
        cross_mixed_grad = right_product(cross_rows_grad, cross_out).astype(jnp.bfloat16)
        cross_query_back, cross_key_back, cross_value_back = attend_backward(
            cross_queries,
            cross_keys_all[batch_index],
            cross_values_all[batch_index],
            cross_allowed,
            head_count,
            cross_log,
            cross_mixed_grad,
        )
        cross_query_low = cross_query_back.astype(jnp.bfloat16)
        grad_cross_query = grad_cross_query + left_product(cross_in, cross_query_low)
        cross_key_mine, cross_value_mine = (
            lax.psum_scatter(
                cross_key_back.astype(jnp.bfloat16), "dp", scatter_dimension=0, tiled=True
            ).astype(jnp.float32),
            lax.psum_scatter(
                cross_value_back.astype(jnp.bfloat16), "dp", scatter_dimension=0, tiled=True
            ).astype(jnp.float32),
        )
        source_exact = memory[batch_index].astype(jnp.float32)
        grad_cross_key = grad_cross_key + exact_left(source_exact, cross_key_mine)
        grad_cross_value = grad_cross_value + exact_left(source_exact, cross_value_mine)
        second_resid, second_gain, second_shift = second_back(
            right_product(cross_query_low, cross_query)
        )
        second_gain_sum = second_gain_sum + second_gain
        second_shift_sum = second_shift_sum + second_shift
        self_grad = cross_grad + second_resid
        self_rows_grad = self_grad.astype(jnp.bfloat16)
        grad_self_out = grad_self_out + left_product(self_mixed, self_rows_grad)
        self_mixed_grad = right_product(self_rows_grad, self_out).astype(jnp.bfloat16)
        self_query_back, self_key_back, self_value_back = attend_backward(
            queries[batch_index],
            keys_all[batch_index],
            values_all[batch_index],
            self_allowed,
            head_count,
            self_log,
            self_mixed_grad,
        )
        self_key_mine, self_value_mine = (
            lax.psum_scatter(
                self_key_back.astype(jnp.bfloat16), "dp", scatter_dimension=0, tiled=True
            ).astype(jnp.float32),
            lax.psum_scatter(
                self_value_back.astype(jnp.bfloat16), "dp", scatter_dimension=0, tiled=True
            ).astype(jnp.float32),
        )
        query_low = self_query_back.astype(jnp.bfloat16)
        key_low = self_key_mine.astype(jnp.bfloat16)
        value_low = self_value_mine.astype(jnp.bfloat16)
        grad_self_query = grad_self_query + left_product(attn_in[batch_index], query_low)
        grad_self_key = grad_self_key + left_product(attn_in[batch_index], key_low)
        grad_self_value = grad_self_value + left_product(attn_in[batch_index], value_low)
        attn_in_grads.append(
            right_product(query_low, self_query)
            + right_product(key_low, self_key)
            + right_product(value_low, self_value)
        )
        resid_grads.append(self_grad)
    first_resid, first_gain, first_shift = first_back(jnp.stack(attn_in_grads))
    token_grad = jnp.stack(resid_grads) + first_resid
    block_out = jnp.stack(outputs)
    up_share, up_bias_share, down_share, down_bias_share = (
        lax.psum_scatter(
            grad_up.astype(jnp.bfloat16), "dp", scatter_dimension=2, tiled=True
        ).astype(jnp.float32),
        lax.psum_scatter(
            grad_up_bias.astype(jnp.bfloat16), "dp", scatter_dimension=1, tiled=True
        ).astype(jnp.float32),
        lax.psum_scatter(
            grad_down.astype(jnp.bfloat16), "dp", scatter_dimension=1, tiled=True
        ).astype(jnp.float32),
        lax.psum_scatter(
            grad_down_bias.astype(jnp.bfloat16), "dp", scatter_dimension=1, tiled=True
        ).astype(jnp.float32),
    )
    up_total, up_bias_total, down_total, down_bias_total = (
        lax.all_gather(up_share.astype(jnp.bfloat16), "dp", axis=2, tiled=True).astype(
            up_share.dtype
        ),
        lax.all_gather(up_bias_share.astype(jnp.bfloat16), "dp", axis=1, tiled=True).astype(
            up_bias_share.dtype
        ),
        lax.all_gather(down_share.astype(jnp.bfloat16), "dp", axis=1, tiled=True).astype(
            down_share.dtype
        ),
        lax.all_gather(down_bias_share.astype(jnp.bfloat16), "dp", axis=1, tiled=True).astype(
            down_bias_share.dtype
        ),
    )
    shared = lax.psum(
        (
            first_gain,
            first_shift,
            grad_self_query,
            grad_self_key,
            grad_self_value,
            grad_self_out,
            second_gain_sum,
            second_shift_sum,
            grad_cross_query,
            grad_cross_key,
            grad_cross_value,
            grad_cross_out,
            third_gain_sum,
            third_shift_sum,
        ),
        ("grp", "dp"),
    )
    return (
        block_out,
        token_grad,
        shared[0],
        shared[1],
        shared[2],
        shared[3],
        shared[4],
        shared[5],
        shared[6],
        shared[7],
        shared[8],
        shared[9],
        shared[10],
        shared[11],
        shared[12],
        shared[13],
        up_total,
        up_bias_total,
        down_total,
        down_bias_total,
    )


MESH = pl.DeviceIdType.MESH
BF = jnp.bfloat16
F32 = jnp.float32
VMEM_BYTES = 56 * 1024 * 1024
HIDE = -1e30


def mm(left, right):
    return lax.dot_general(left, right, (((1,), (0,)), ((), ())), preferred_element_type=F32)


def mm_right(left, right):
    return lax.dot_general(left, right, (((1,), (1,)), ((), ())), preferred_element_type=F32)


def mm_left(left, right):
    return lax.dot_general(left, right, (((0,), (0,)), ((), ())), preferred_element_type=F32)


def norm_parts(inputs):
    mean_row = jnp.mean(inputs, axis=-1, keepdims=True)
    centred = inputs - mean_row
    spread = jnp.mean(centred * centred, axis=-1, keepdims=True)
    inverse = lax.rsqrt(spread + 1e-05)
    return centred * inverse, inverse


def norm_back(unit, inverse, gain, grad):
    scaled = grad * gain
    first = jnp.mean(scaled, axis=-1, keepdims=True)
    second = jnp.mean(scaled * unit, axis=-1, keepdims=True)
    return inverse * (scaled - first - unit * second)


def col_sum(values):
    return jnp.sum(values, axis=0, keepdims=True)


def three_parts(values):
    high = values.astype(BF).astype(F32)
    rest = values - high
    middle = rest.astype(BF).astype(F32)
    return high, middle, rest - middle


def doc_of(lengths_ref, batch, positions):
    total = jnp.int32(0)
    docs = jnp.zeros(positions.shape, jnp.int32)
    for j in range(lengths_ref.shape[2]):
        total = total + lengths_ref[batch, 0, j]
        docs = docs + (positions >= total).astype(jnp.int32)
    return docs


def lanes_of(shape, head):
    lane = lax.broadcasted_iota(jnp.int32, shape, 1)
    half = shape[1] // 2
    own = (lane < half) if head == 0 else (lane >= half)
    return own, (lane - half if head == 0 else lane)


def greet(grp, me, parts):
    barrier = pltpu.get_barrier_semaphore()
    for k in range(1, parts):
        pl.semaphore_signal(
            barrier, inc=1, device_id=(grp, lax.rem(me + k, parts)), device_id_type=MESH
        )
    pl.semaphore_wait(barrier, parts - 1)


def sender(grp, src, dst, ssem, rsem, target):
    return pltpu.make_async_remote_copy(
        src_ref=src,
        dst_ref=dst,
        send_sem=ssem,
        recv_sem=rsem,
        device_id=(grp, target),
        device_id_type=MESH,
    )


def key_features(values, docs, head):
    own, place = lanes_of(values.shape, head)
    other = jnp.where(place == docs, 0.0, HIDE)
    other = jnp.where((place >= 4) & (place < 7), 1.0, other)
    return jnp.where(own, values.astype(F32), other).astype(BF)


def query_features(values, docs, head, scaling):
    own, place = lanes_of(values.shape, head)
    return jnp.where(
        own, values.astype(F32) * scaling, jnp.where(place == docs, 1.0, 0.0)
    ).astype(BF)


def value_features(values, head):
    own, _ = lanes_of(values.shape, head)
    return jnp.where(own, values.astype(F32), 1.0).astype(BF)


def forward_kernel(
    parts, pairs, rows, scaling,
    doc_len, src_len, tokens, memory, gain1, shift1, gain2, shift2,
    wq, wk, wv, wo, cq, ck, cv, co,
    a_out, x1_out, c_out, x2_out, o1_own, o2_own,
    qa1, ka1, va1, o1, qa2, ka2, va2, o2,
    st_qkv, rv_qkv, st_kv, rv_kv, st_q2, rv_q2, tmp_o,
    local_sem, s_qkv, r_qkv, s_kv, r_kv, s_o1, r_o1, s_q2, r_q2, s_o2, r_o2,
):
    grp = lax.axis_index("grp")
    me = lax.axis_index("dp")
    batch = lax.div(me, pairs)
    pair = lax.rem(me, pairs)
    micro = tokens.shape[0]
    lanes = 128
    length = parts * rows

    def a2a(src, dst, ssem, rsem, target):
        return sender(grp, src.at[target], dst.at[me], ssem.at[target], rsem.at[me], target)

    def arrived(dst, ssem, rsem, source):
        sender(grp, dst.at[source], dst.at[source], ssem.at[source], rsem.at[source], source).wait_recv()

    greet(grp, me, parts)

    def first_norm(mb, _):
        unit, _inv = norm_parts(tokens[mb].astype(F32))
        a = (unit * gain1[...] + shift1[...]).astype(BF)
        a_out[mb] = a
        for n, weight in enumerate((wq, wk, wv)):
            got = mm(a, weight[...]).astype(BF)
            for p in range(pairs):
                st_qkv[mb * pairs + p, n * rows : (n + 1) * rows, :] = got[:, p * lanes : (p + 1) * lanes]

        def send(p, _):
            target = mb * pairs + p

            @pl.when(target != me)
            def _():
                a2a(st_qkv, rv_qkv, s_qkv, r_qkv, target).start()

            return 0

        lax.fori_loop(0, pairs, send, 0)
        return 0

    lax.fori_loop(0, micro, first_norm, 0)
    mine = pltpu.make_async_copy(st_qkv.at[me], rv_qkv.at[me], local_sem)
    mine.start()
    mine.wait()

    def source_heads(mb, _):
        source = memory[mb]
        for n, weight in enumerate((ck, cv)):
            got = mm(source, weight[...]).astype(BF)
            for p in range(pairs):
                st_kv[mb * pairs + p, n * rows : (n + 1) * rows, :] = got[:, p * lanes : (p + 1) * lanes]
        return 0

    lax.fori_loop(0, micro, source_heads, 0)

    for k in range(1, parts):
        arrived(rv_qkv, s_qkv, r_qkv, lax.rem(me + k, parts))
    for k in range(1, parts):
        a2a(st_kv, rv_kv, s_kv, r_kv, lax.rem(me + k, parts)).start()
    mine = pltpu.make_async_copy(st_kv.at[me], rv_kv.at[me], local_sem)
    mine.start()
    mine.wait()

    def build_self(s, _):
        r0 = pl.multiple_of(s * rows, rows)
        places = r0 + lax.broadcasted_iota(jnp.int32, (rows, lanes), 0)
        docs = doc_of(doc_len, batch, places)
        for h in range(2):
            qa1[h, pl.ds(r0, rows), :] = query_features(rv_qkv[s, 0:rows, :], docs, h, scaling)
            ka1[h, pl.ds(r0, rows), :] = key_features(rv_qkv[s, rows : 2 * rows, :], docs, h)
            va1[h, pl.ds(r0, rows), :] = value_features(rv_qkv[s, 2 * rows : 3 * rows, :], h)
        return 0

    lax.fori_loop(0, parts, build_self, 0)

    def finish(qa, r0, h, query, top, acc):
        own, place = lanes_of((rows, lanes), h)
        total = pltpu.roll(acc, lanes // 2, 1)
        high, middle, low = three_parts(top + jnp.log(acc))
        query = query.astype(F32)
        query = jnp.where(~own & (place == 4), -high, query)
        query = jnp.where(~own & (place == 5), -middle, query)
        query = jnp.where(~own & (place == 6), -low, query)
        qa[h, pl.ds(r0, rows), :] = query.astype(BF)
        return acc / total

    def emit(t, heads, out, own_ref, ssem, rsem):
        own, _ = lanes_of((rows, lanes), 0)
        out[t] = jnp.where(own, heads[0], heads[1]).astype(BF)

        @pl.when(t != me)
        def _():
            sender(grp, out.at[t], own_ref.at[me], ssem.at[t], rsem.at[me], t).start()

        @pl.when(t == me)
        def _():
            own_ref[me] = out[t]

    for e in range(parts // 2):
        reach = 2 * rows * (e + 1)
        cut = reach - 2 * rows

        def self_block(i, _, reach=reach, cut=cut, e=e):
            t = 2 * e + i
            r0 = pl.multiple_of(t * rows, rows)
            row = r0 + lax.broadcasted_iota(jnp.int32, (rows, 2 * rows), 0)
            col = cut + lax.broadcasted_iota(jnp.int32, (rows, 2 * rows), 1)
            heads = []
            for h in range(2):
                query = qa1[h, pl.ds(r0, rows), :]
                near = mm_right(query, ka1[h, cut:reach, :])
                near = jnp.where(col <= row, near, HIDE)
                top = jnp.max(near, axis=1, keepdims=True)
                if cut:
                    far = mm_right(query, ka1[h, 0:cut, :])
                    top = jnp.maximum(top, jnp.max(far, axis=1, keepdims=True))
                acc = mm(jnp.exp(near - top).astype(BF), va1[h, cut:reach, :])
                if cut:
                    acc = acc + mm(jnp.exp(far - top).astype(BF), va1[h, 0:cut, :])
                heads.append(finish(qa1, r0, h, query, top, acc))
            emit(t, heads, o1, o1_own, s_o1, r_o1)
            return 0

        lax.fori_loop(0, 2, self_block, 0)

    def own_wait(own_ref, ssem, rsem):
        for k in range(1, parts):
            arrived(own_ref, ssem, rsem, lax.rem(me + k, parts))

    own_wait(o1_own, s_o1, r_o1)

    def second_norm(mb, _):
        mixed = jnp.concatenate([o1_own[mb * pairs + p] for p in range(pairs)], axis=1)
        x1 = tokens[mb].astype(F32) + mm(mixed, wo[...])
        x1_out[mb] = x1
        unit, _inv = norm_parts(x1)
        c = (unit * gain2[...] + shift2[...]).astype(BF)
        c_out[mb] = c
        got = mm(c, cq[...]).astype(BF)
        for p in range(pairs):
            st_q2[mb * pairs + p] = got[:, p * lanes : (p + 1) * lanes]

        def send(p, _):
            target = mb * pairs + p

            @pl.when(target != me)
            def _():
                a2a(st_q2, rv_q2, s_q2, r_q2, target).start()

            @pl.when(target == me)
            def _():
                rv_q2[me] = st_q2[me]

            return 0

        lax.fori_loop(0, pairs, send, 0)
        return 0

    lax.fori_loop(0, micro, second_norm, 0)

    for k in range(1, parts):
        arrived(rv_kv, s_kv, r_kv, lax.rem(me + k, parts))

    def build_cross(s, _):
        r0 = pl.multiple_of(s * rows, rows)
        places = r0 + lax.broadcasted_iota(jnp.int32, (rows, lanes), 0)
        docs = doc_of(src_len, batch, places)
        for h in range(2):
            ka2[h, pl.ds(r0, rows), :] = key_features(rv_kv[s, 0:rows, :], docs, h)
            va2[h, pl.ds(r0, rows), :] = value_features(rv_kv[s, rows : 2 * rows, :], h)
        return 0

    lax.fori_loop(0, parts, build_cross, 0)

    def cross_block(k, _):
        t = lax.rem(me + k, parts)

        @pl.when(k > 0)
        def _():
            arrived(rv_q2, s_q2, r_q2, t)

        r0 = pl.multiple_of(t * rows, rows)
        places = r0 + lax.broadcasted_iota(jnp.int32, (rows, lanes), 0)
        docs = doc_of(doc_len, batch, places)
        heads = []
        for h in range(2):
            query = query_features(rv_q2[t], docs, h, scaling)
            scores = mm_right(query, ka2[h])
            top = jnp.max(scores, axis=1, keepdims=True)
            acc = mm(jnp.exp(scores - top).astype(BF), va2[h])
            heads.append(finish(qa2, r0, h, query, top, acc))
        emit(t, heads, o2, o2_own, s_o2, r_o2)
        return 0

    lax.fori_loop(0, parts, cross_block, 0)
    own_wait(o2_own, s_o2, r_o2)

    def third(mb, _):
        mixed = jnp.concatenate([o2_own[mb * pairs + p] for p in range(pairs)], axis=1)
        x2_out[mb] = x1_out[mb] + mm(mixed, co[...])
        return 0

    lax.fori_loop(0, micro, third, 0)

    for k in range(1, parts):
        target = lax.rem(me + k, parts)
        a2a(st_qkv, rv_qkv, s_qkv, r_qkv, target).wait_send()
        a2a(st_kv, rv_kv, s_kv, r_kv, target).wait_send()
        a2a(st_q2, rv_q2, s_q2, r_q2, target).wait_send()
        a2a(o1, o1_own, s_o1, r_o1, target).wait_send()
        a2a(o2, o2_own, s_o2, r_o2, target).wait_send()


def gelu_both(z):
    root = math.sqrt(2.0 / math.pi)
    square = z * z
    bent = jnp.tanh(root * z * (1.0 + 0.044715 * square))
    half = 0.5 * (1.0 + bent)
    slope = half + 0.5 * z * (1.0 - bent * bent) * (root * (1.0 + 3 * 0.044715 * square))
    return z * half, slope


def expert_kernel(
    tiles, pairs,
    x2, slots, cot, gain3, shift3, up, up_b, down, down_b, co, o2_own,
    block_out, gx2_out, do2, g_co, g_gain3, g_shift3, g_up, g_upb, g_down, g_downb,
    e_ref, y_ref, de_ref,
):
    step = pl.program_id(0)
    micro, rows, width = x2.shape
    lanes = 128
    count = micro * rows
    is_one = slots[...] == 1

    @pl.when(step == 0)
    def _():
        for mb in range(micro):
            unit, _inv = norm_parts(x2[mb])
            e_ref[mb * rows : (mb + 1) * rows, :] = (unit * gain3[...] + shift3[...]).astype(BF)
        y_ref[...] = jnp.where(is_one, down_b[1:2, :], down_b[0:1, :])
        de_ref[...] = jnp.zeros_like(de_ref)

    e = e_ref[...]
    gf = cot[...].reshape(count, width)
    u = jnp.where(
        is_one, mm(e, up[1]) + up_b[1:2, :], mm(e, up[0]) + up_b[0:1, :]
    )
    act, slope = gelu_both(u)
    du = jnp.where(is_one, mm_right(gf, down[1]), mm_right(gf, down[0])) * slope
    zero = jnp.zeros_like(act)
    y = y_ref[...]
    de = de_ref[...]
    for n in range(2):
        mask = is_one if n else ~is_one
        h_n = jnp.where(mask, act, zero).astype(BF)
        du_n = jnp.where(mask, du, zero).astype(BF)
        y = y + mm(h_n, down[n])
        de = de + mm_right(du_n, up[n])
        g_up[n] = mm_left(e, du_n).astype(BF)
        g_down[n] = mm_left(h_n, gf).astype(BF)
        g_upb[n : n + 1, :] = col_sum(du_n.astype(F32))
    y_ref[...] = y
    de_ref[...] = de

    @pl.when(step == tiles - 1)
    def _():
        gain_sum = jnp.zeros((1, width), F32)
        shift_sum = jnp.zeros((1, width), F32)
        cross = jnp.zeros((width, width), F32)
        for mb in range(micro):
            part = slice(mb * rows, (mb + 1) * rows)
            block_out[mb] = (x2[mb] + y_ref[part, :]).astype(BF)
            unit, inverse = norm_parts(x2[mb])
            grad = de_ref[part, :]
            gain_sum = gain_sum + col_sum(grad * unit)
            shift_sum = shift_sum + col_sum(grad)
            gx2 = cot[mb].astype(F32) + norm_back(unit, inverse, gain3[...], grad)
            gx2_out[mb] = gx2
            gy2 = gx2.astype(BF)
            back = mm_right(gy2, co[...]).astype(BF)
            for p in range(pairs):
                do2[mb * pairs + p] = back[:, p * lanes : (p + 1) * lanes]
            mixed = jnp.concatenate([o2_own[mb * pairs + p] for p in range(pairs)], axis=1)
            cross = cross + mm_left(mixed, gy2)
        g_co[...] = cross
        g_gain3[...] = gain_sum
        g_shift3[...] = shift_sum
        all_grad = gf.astype(F32)
        g_downb[1:2, :] = col_sum(jnp.where(is_one, all_grad, 0.0))
        g_downb[0:1, :] = col_sum(jnp.where(is_one, 0.0, all_grad))


def backward_kernel(
    parts, pairs, rows, scaling,
    gx2, do2_st, qa1, ka1, va1, o1, qa2, ka2, va2, o2,
    tokens, memory, x1, c_in, a_in, o1_own, gain1, gain2,
    wq, wk, wv, wo, cq,
    token_grad, g_gain1, g_shift1, g_sq, g_sk, g_sv, g_so, g_gain2, g_shift2, g_cq, g_ck, g_cv,
    rv_do2, st_dq2, rv_dq2, st_dkv2, rv_dkv2, st_do1, rv_do1, st_d, rv_d, doa,
    dq_acc, dk_acc, dv_acc, gx1_ref,
    s_do2, r_do2, s_dq2, r_dq2, s_dkv2, r_dkv2, s_do1, r_do1, s_d, r_d,
):
    grp = lax.axis_index("grp")
    me = lax.axis_index("dp")
    micro = tokens.shape[0]
    lanes = 128
    length = parts * rows

    def a2a(src, dst, ssem, rsem, target):
        return sender(grp, src.at[target], dst.at[me], ssem.at[target], rsem.at[me], target)

    def arrived(dst, ssem, rsem, source):
        sender(grp, dst.at[source], dst.at[source], ssem.at[source], rsem.at[source], source).wait_recv()

    greet(grp, me, parts)
    for k in range(1, parts):
        a2a(do2_st, rv_do2, s_do2, r_do2, lax.rem(me + k, parts)).start()
    rv_do2[me] = do2_st[me]

    def clear(s, _):
        part = pl.ds(pl.multiple_of(s * rows, rows), rows)
        for h in range(2):
            dk_acc[h, part, :] = jnp.zeros((rows, lanes), F32)
            dv_acc[h, part, :] = jnp.zeros((rows, lanes), F32)
            dq_acc[h, part, :] = jnp.zeros((rows, lanes), F32)
        return 0

    def grad_features(grads, mixed, head):
        own, place = lanes_of(grads.shape, head)
        grads = grads.astype(F32)
        delta = jnp.sum(jnp.where(own, grads * mixed.astype(F32), 0.0), axis=1, keepdims=True)
        high, middle, low = three_parts(delta)
        other = jnp.where(place == 0, -high, 0.0)
        other = jnp.where(place == 1, -middle, other)
        other = jnp.where(place == 2, -low, other)
        return jnp.where(own, grads, other).astype(BF)

    def tile(query, grads, keys, values, mask):
        scores = mm_right(keys, query)
        if mask is not None:
            scores = jnp.where(mask, scores, HIDE)
        prob = jnp.exp(scores)
        back = mm_right(values, grads)
        score_grad = (prob * back).astype(BF)
        return (
            mm_left(score_grad, keys),
            mm(score_grad, query),
            mm(prob.astype(BF), grads),
        )

    def join(zero_head, one_head):
        own, _ = lanes_of(zero_head.shape, 0)
        return jnp.where(own, zero_head, one_head)

    lax.fori_loop(0, parts, clear, 0)

    chunk = 2 * rows

    def cross_block(k, _):
        t = lax.rem(me + k, parts)

        @pl.when(k > 0)
        def _():
            arrived(rv_do2, s_do2, r_do2, t)

        part = pl.ds(pl.multiple_of(t * rows, rows), rows)
        grads = [grad_features(rv_do2[t], o2[t], h) for h in range(2)]
        queries = [qa2[h, part, :] for h in range(2)]
        sums = [jnp.zeros((rows, lanes), F32)] * 2
        for n in range(length // chunk):
            keys = slice(n * chunk, (n + 1) * chunk)
            for h in range(2):
                dq, dk, dv = tile(queries[h], grads[h], ka2[h, keys, :], va2[h, keys, :], None)
                sums[h] = sums[h] + dq
                dk_acc[h, keys, :] += dk
                dv_acc[h, keys, :] += dv
        st_dq2[t] = (join(sums[0], sums[1]) * scaling).astype(BF)

        @pl.when(k > 0)
        def _():
            a2a(st_dq2, rv_dq2, s_dq2, r_dq2, t).start()

        @pl.when(k == 0)
        def _():
            rv_dq2[me] = st_dq2[me]

        return 0

    lax.fori_loop(0, parts, cross_block, 0)

    def give_cross(k, _):
        s = lax.rem(me + k, parts)
        part = pl.ds(pl.multiple_of(s * rows, rows), rows)
        st_dkv2[s, 0:rows, :] = join(dk_acc[0, part, :], dk_acc[1, part, :]).astype(BF)
        st_dkv2[s, rows : 2 * rows, :] = join(dv_acc[0, part, :], dv_acc[1, part, :]).astype(BF)

        @pl.when(k > 0)
        def _():
            a2a(st_dkv2, rv_dkv2, s_dkv2, r_dkv2, s).start()

        @pl.when(k == 0)
        def _():
            rv_dkv2[me] = st_dkv2[me]

        return 0

    for k in range(1, parts):
        arrived(rv_dq2, s_dq2, r_dq2, lax.rem(me + k, parts))

    def gathered(ref, mb, first):
        return jnp.concatenate(
            [ref[mb * pairs + p, first * rows : (first + 1) * rows, :] for p in range(pairs)], axis=1
        )

    g_gain2[...] = jnp.zeros_like(g_gain2)
    g_shift2[...] = jnp.zeros_like(g_shift2)

    def second_back(mb, _):
        dq2 = gathered(rv_dq2, mb, 0)
        dc = mm_right(dq2, cq[...])
        unit, inverse = norm_parts(x1[mb])
        g_gain2[...] += col_sum(dc * unit)
        g_shift2[...] += col_sum(dc)
        gx1 = gx2[mb] + norm_back(unit, inverse, gain2[...], dc)
        gx1_ref[mb] = gx1
        back = mm_right(gx1.astype(BF), wo[...]).astype(BF)
        for p in range(pairs):
            st_do1[mb * pairs + p] = back[:, p * lanes : (p + 1) * lanes]

        def send(p, _):
            target = mb * pairs + p

            @pl.when(target != me)
            def _():
                a2a(st_do1, rv_do1, s_do1, r_do1, target).start()

            @pl.when(target == me)
            def _():
                rv_do1[me] = st_do1[me]

            return 0

        lax.fori_loop(0, pairs, send, 0)
        return 0

    lax.fori_loop(0, micro, second_back, 0)
    lax.fori_loop(0, parts, give_cross, 0)

    g_cq[...] = jnp.zeros_like(g_cq)
    g_so[...] = jnp.zeros_like(g_so)

    def cross_weights(mb, _):
        g_cq[...] += mm_left(c_in[mb], gathered(rv_dq2, mb, 0))
        mixed = jnp.concatenate([o1_own[mb * pairs + p] for p in range(pairs)], axis=1)
        g_so[...] += mm_left(mixed, gx1_ref[mb].astype(BF))
        return 0

    lax.fori_loop(0, micro, cross_weights, 0)

    for k in range(1, parts):
        arrived(rv_do1, s_do1, r_do1, lax.rem(me + k, parts))

    lax.fori_loop(0, parts, clear, 0)

    def build(s, _):
        part = pl.ds(pl.multiple_of(s * rows, rows), rows)
        for h in range(2):
            doa[h, part, :] = grad_features(rv_do1[s], o1[s], h)
        return 0

    lax.fori_loop(0, parts, build, 0)

    def self_tile(i, j, mask):
        q_part = pl.ds(pl.multiple_of(i * chunk, chunk), chunk)
        k_part = pl.ds(pl.multiple_of(j * chunk, chunk), chunk)
        for h in range(2):
            dq, dk, dv = tile(
                qa1[h, q_part, :], doa[h, q_part, :], ka1[h, k_part, :], va1[h, k_part, :], mask
            )
            dq_acc[h, q_part, :] += dq
            dk_acc[h, k_part, :] += dk
            dv_acc[h, k_part, :] += dv

    def self_column(j, _):
        key_place = lax.broadcasted_iota(jnp.int32, (chunk, chunk), 0)
        query_place = lax.broadcasted_iota(jnp.int32, (chunk, chunk), 1)
        self_tile(j, j, key_place <= query_place)

        def below(i, _):
            self_tile(i, j, None)
            return 0

        lax.fori_loop(j + 1, length // chunk, below, 0)

        def give(n, _):
            s = j * (chunk // rows) + n
            part = pl.ds(pl.multiple_of(s * rows, rows), rows)
            for m, (acc, factor) in enumerate(((dq_acc, scaling), (dk_acc, 1.0), (dv_acc, 1.0))):
                st_d[s, m * rows : (m + 1) * rows, :] = (
                    join(acc[0, part, :], acc[1, part, :]) * factor
                ).astype(BF)

            @pl.when(s != me)
            def _():
                a2a(st_d, rv_d, s_d, r_d, s).start()

            @pl.when(s == me)
            def _():
                rv_d[me] = st_d[me]

            return 0

        lax.fori_loop(0, chunk // rows, give, 0)
        return 0

    lax.fori_loop(0, length // chunk, self_column, 0)

    for k in range(1, parts):
        arrived(rv_dkv2, s_dkv2, r_dkv2, lax.rem(me + k, parts))
    g_ck[...] = jnp.zeros_like(g_ck)
    g_cv[...] = jnp.zeros_like(g_cv)

    def source_weights(mb, _):
        g_ck[...] += mm_left(memory[mb], gathered(rv_dkv2, mb, 0))
        g_cv[...] += mm_left(memory[mb], gathered(rv_dkv2, mb, 1))
        return 0

    lax.fori_loop(0, micro, source_weights, 0)

    for k in range(1, parts):
        arrived(rv_d, s_d, r_d, lax.rem(me + k, parts))
    g_gain1[...] = jnp.zeros_like(g_gain1)
    g_shift1[...] = jnp.zeros_like(g_shift1)
    for ref in (g_sq, g_sk, g_sv):
        ref[...] = jnp.zeros_like(ref)

    def first_back(mb, _):
        da = jnp.zeros((rows, pairs * lanes), F32)
        for m, (weight, ref) in enumerate(((wq, g_sq), (wk, g_sk), (wv, g_sv))):
            grads = gathered(rv_d, mb, m)
            da = da + mm_right(grads, weight[...])
            ref[...] += mm_left(a_in[mb], grads)
        unit, inverse = norm_parts(tokens[mb].astype(F32))
        g_gain1[...] += col_sum(da * unit)
        g_shift1[...] += col_sum(da)
        token_grad[mb] = gx1_ref[mb] + norm_back(unit, inverse, gain1[...], da)
        return 0

    lax.fori_loop(0, micro, first_back, 0)

    for k in range(1, parts):
        target = lax.rem(me + k, parts)
        a2a(do2_st, rv_do2, s_do2, r_do2, target).wait_send()
        a2a(st_dq2, rv_dq2, s_dq2, r_dq2, target).wait_send()
        a2a(st_dkv2, rv_dkv2, s_dkv2, r_dkv2, target).wait_send()
        a2a(st_do1, rv_do1, s_do1, r_do1, target).wait_send()
        a2a(st_d, rv_d, s_d, r_d, target).wait_send()


def vmem_spec():
    return pl.BlockSpec(memory_space=pltpu.VMEM)


def fast_device(
    tokens, memory, expert_slot, doc_lengths, source_lengths, cotangent,
    norm1_gain, norm1_shift, self_query, self_key, self_value, self_out,
    norm2_gain, norm2_shift, cross_query, cross_key, cross_value, cross_out,
    norm3_gain, norm3_shift, up_weight, up_bias, down_weight, down_bias,
):
    micro, rows, width = tokens.shape
    parts = lax.axis_size("dp")
    pairs = HEADS // 2
    lanes = width // pairs
    length = parts * rows
    scaling = 1.0 / math.sqrt(width // HEADS)
    experts, _, hidden = up_weight.shape
    shape = jax.ShapeDtypeStruct
    dma = pltpu.SemaphoreType.DMA((parts,))
    line = lambda v: v.reshape(1, width)

    aug = shape((2, length, lanes), BF)
    blocks = shape((parts, rows, lanes), BF)
    full = shape((micro, rows, width), F32)
    low = shape((micro, rows, width), BF)
    vec = shape((1, width), F32)
    square = shape((width, width), F32)
    buf = lambda n: pltpu.VMEM((parts, n * rows, lanes), BF)

    outs1 = [low, full, low, full, blocks, blocks, aug, aug, aug, blocks, aug, aug, aug, blocks]
    (a, x1, c, x2, o1_own, o2_own, qa1, ka1, va1, o1, qa2, ka2, va2, o2) = pl.pallas_call(
        functools.partial(forward_kernel, parts, pairs, rows, scaling),
        out_shape=outs1,
        in_specs=[pl.BlockSpec(memory_space=pltpu.SMEM)] * 2 + [vmem_spec()] * 14,
        out_specs=[vmem_spec()] * len(outs1),
        scratch_shapes=[buf(3), buf(3), buf(2), buf(2), buf(1), buf(1),
                        pltpu.VMEM((2, rows, lanes), F32), pltpu.SemaphoreType.DMA]
        + [dma] * 10,
        compiler_params=pltpu.CompilerParams(
            collective_id=1, has_side_effects=True, vmem_limit_bytes=VMEM_BYTES
        ),
        name="attend_forward",
    )(
        doc_lengths, source_lengths, tokens, memory, line(norm1_gain), line(norm1_shift),
        line(norm2_gain), line(norm2_shift), self_query, self_key, self_value, self_out,
        cross_query, cross_key, cross_value, cross_out,
    )

    tiles = 8
    depth = hidden // tiles
    whole = lambda *dims: pl.BlockSpec(dims, lambda f: (0,) * len(dims))
    count = micro * rows
    outs2 = [low, full, blocks, square, vec, vec,
             shape((experts, width, hidden), BF), shape((experts, hidden), F32),
             shape((experts, hidden, width), BF), shape((experts, width), F32)]
    up_spec = pl.BlockSpec((experts, width, depth), lambda f: (0, 0, f))
    down_spec = pl.BlockSpec((experts, depth, width), lambda f: (0, f, 0))
    bias_spec = pl.BlockSpec((experts, depth), lambda f: (0, f))
    (block_out, gx2, do2, g_co, g_gain3, g_shift3, g_up, g_upb, g_down, g_downb) = pl.pallas_call(
        functools.partial(expert_kernel, tiles, pairs),
        grid=(tiles,),
        out_shape=outs2,
        in_specs=[whole(micro, rows, width), whole(count, 1), whole(micro, rows, width),
                  whole(1, width), whole(1, width), up_spec, bias_spec, down_spec,
                  whole(experts, width), whole(width, width), whole(parts, rows, lanes)],
        out_specs=[whole(micro, rows, width), whole(micro, rows, width), whole(parts, rows, lanes),
                   whole(width, width), whole(1, width), whole(1, width),
                   up_spec, bias_spec, down_spec, whole(experts, width)],
        scratch_shapes=[pltpu.VMEM((count, width), BF), pltpu.VMEM((count, width), F32),
                        pltpu.VMEM((count, width), F32)],
        compiler_params=pltpu.CompilerParams(vmem_limit_bytes=VMEM_BYTES),
        name="experts",
    )(
        x2, expert_slot.reshape(count, 1), cotangent, line(norm3_gain), line(norm3_shift),
        up_weight, up_bias, down_weight, down_bias, cross_out, o2_own,
    )

    up_share = lax.psum_scatter(g_up, "dp", scatter_dimension=2, tiled=True)
    down_share = lax.psum_scatter(g_down, "dp", scatter_dimension=1, tiled=True)
    up_total = lax.all_gather(up_share, "dp", axis=2, tiled=True).astype(F32)
    down_total = lax.all_gather(down_share, "dp", axis=1, tiled=True).astype(F32)

    outs3 = [full, vec, vec, square, square, square, square, vec, vec, square, square, square]
    acc = pltpu.VMEM((2, length, lanes), F32)
    (token_grad, g_gain1, g_shift1, g_sq, g_sk, g_sv, g_so, g_gain2, g_shift2, g_cq, g_ck, g_cv) = pl.pallas_call(
        functools.partial(backward_kernel, parts, pairs, rows, scaling),
        out_shape=outs3,
        in_specs=[vmem_spec()] * 23,
        out_specs=[vmem_spec()] * len(outs3),
        scratch_shapes=[buf(1), buf(1), buf(1), buf(2), buf(2), buf(1), buf(1), buf(3), buf(3),
                        pltpu.VMEM((2, length, lanes), BF), acc, acc, acc,
                        pltpu.VMEM((micro, rows, width), F32)]
        + [dma] * 10,
        compiler_params=pltpu.CompilerParams(
            collective_id=3, has_side_effects=True, vmem_limit_bytes=VMEM_BYTES
        ),
        name="attend_backward",
    )(
        gx2, do2, qa1, ka1, va1, o1, qa2, ka2, va2, o2, tokens, memory, x1, c, a, o1_own,
        line(norm1_gain), line(norm2_gain), self_query, self_key, self_value, self_out, cross_query,
    )

    shared = lax.psum(
        (g_gain1, g_shift1, g_sq, g_sk, g_sv, g_so, g_gain2, g_shift2, g_cq, g_ck, g_cv, g_co,
         g_gain3, g_shift3),
        ("grp", "dp"),
    )
    biases = lax.psum((g_upb, g_downb), "dp")
    flat = lambda v: v.reshape(width)
    return (
        block_out, token_grad, flat(shared[0]), flat(shared[1]), shared[2], shared[3], shared[4],
        shared[5], flat(shared[6]), flat(shared[7]), shared[8], shared[9], shared[10], shared[11],
        flat(shared[12]), flat(shared[13]), up_total, biases[0], down_total, biases[1],
    )


def solution(mesh):
    fits = mesh.shape["dp"] * 2 == HEADS * 2
    return jax.shard_map(
        fast_device if fits else per_device,
        mesh=mesh,
        in_specs=(
            P(None, ("grp", "dp"), None),
            P(None, ("grp", "dp"), None),
            P(None, ("grp", "dp"), None),
            P(None, "grp", None),
            P(None, "grp", None),
            P(None, ("grp", "dp"), None),
            P(),
            P(),
            P(),
            P(),
            P(),
            P(),
            P(),
            P(),
            P(),
            P(),
            P(),
            P(),
            P(),
            P(),
            P("grp", None, None),
            P("grp", None),
            P("grp", None, None),
            P("grp", None),
        ),
        out_specs=(
            P(None, ("grp", "dp"), None),
            P(None, ("grp", "dp"), None),
            P(),
            P(),
            P(),
            P(),
            P(),
            P(),
            P(),
            P(),
            P(),
            P(),
            P(),
            P(),
            P(),
            P(),
            P("grp", None, None),
            P("grp", None),
            P("grp", None, None),
            P("grp", None),
        ),
        check_vma=False,
    )
```

```python
import functools
import math

import jax
import jax.numpy as jnp
from jax import lax
from jax.experimental import pallas as pl
from jax.experimental.pallas import tpu as pltpu
from jax.sharding import PartitionSpec as P

HEADS = 8
CAP = 160


masked_score = -1e30


def layer_norm(inputs, norm_gain, norm_shift):
    mean_row = jnp.mean(inputs, axis=-1, keepdims=True)
    centred = inputs - mean_row
    spread = jnp.mean(centred * centred, axis=-1, keepdims=True)
    return centred * lax.rsqrt(spread + 1e-05) * norm_gain + norm_shift


def doc_index(lengths, places):
    doc_ends = jnp.cumsum(lengths)
    return jnp.sum((places[:, None] >= doc_ends[None, :]).astype(jnp.int32), axis=1)


def product(left, right):
    return jnp.dot(left, right, preferred_element_type=jnp.float32)


def left_product(left, right):
    return jnp.einsum("nd,ne->de", left, right, preferred_element_type=jnp.float32)


def right_product(left, right):
    return jnp.einsum("nd,ed->ne", left, right, preferred_element_type=jnp.float32)


def exact_left(left, right):
    return jnp.einsum("nd,ne->de", left, right, precision=lax.Precision.HIGHEST)


def split_heads(matrix, head_count):
    return matrix.reshape(matrix.shape[0], head_count, matrix.shape[1] // head_count)


def attend_forward(queries, keys_all, values_all, allowed, head_count):
    scaling = 1.0 / math.sqrt(queries.shape[1] // head_count)
    scores = (
        jnp.einsum(
            "qhd,khd->hqk",
            split_heads(queries, head_count),
            split_heads(keys_all, head_count),
            preferred_element_type=jnp.float32,
        )
        * scaling
    )
    scores = jnp.where(allowed[None], scores, masked_score)
    maximum = jnp.max(scores, axis=-1, keepdims=True)
    exponent = jnp.exp(scores - maximum)
    totals = jnp.sum(exponent, axis=-1, keepdims=True)
    probability = (exponent / totals).astype(jnp.bfloat16)
    mixed = jnp.einsum(
        "hqk,khd->qhd",
        probability,
        split_heads(values_all, head_count),
        preferred_element_type=jnp.float32,
    )
    return (mixed.reshape(queries.shape[0], queries.shape[1]), maximum + jnp.log(totals))


def score_parts(
    query_heads, key_heads, value_heads, grad_heads, allowed, scaling, log_total, centre
):
    scores = (
        jnp.einsum("qhd,khd->hqk", query_heads, key_heads, preferred_element_type=jnp.float32)
        * scaling
    )
    scores = jnp.where(allowed[None], scores, masked_score)
    probability = jnp.exp(scores - log_total)
    prob_grad = jnp.einsum(
        "qhd,khd->hqk", grad_heads, value_heads, preferred_element_type=jnp.float32
    )
    centre = jnp.sum(probability * prob_grad, axis=-1, keepdims=True)
    score_grad = (probability * (prob_grad - centre)).astype(jnp.bfloat16)
    return (probability, score_grad, centre)


def attend_backward(queries, keys_all, values_all, allowed, head_count, log_total, out_grad):
    scaling = 1.0 / math.sqrt(queries.shape[1] // head_count)
    query_heads = split_heads(queries, head_count)
    key_heads = split_heads(keys_all, head_count)
    grad_heads = split_heads(out_grad, head_count)
    probability, score_grad, centre = score_parts(
        query_heads,
        key_heads,
        split_heads(values_all, head_count),
        grad_heads,
        allowed,
        scaling,
        log_total,
        None,
    )
    query_back = (
        jnp.einsum("hqk,khd->qhd", score_grad, key_heads, preferred_element_type=jnp.float32)
        * scaling
    )
    key_back = (
        jnp.einsum("hqk,qhd->khd", score_grad, query_heads, preferred_element_type=jnp.float32)
        * scaling
    )
    value_back = jnp.einsum(
        "hqk,qhd->khd",
        probability.astype(jnp.bfloat16),
        grad_heads,
        preferred_element_type=jnp.float32,
    )
    width = queries.shape[1]
    return (
        query_back.reshape(queries.shape[0], width),
        key_back.reshape(keys_all.shape[0], width),
        value_back.reshape(keys_all.shape[0], width),
    )


def per_device(
    tokens,
    memory,
    expert_slot,
    doc_lengths,
    source_lengths,
    cotangent,
    norm1_gain,
    norm1_shift,
    self_query,
    self_key,
    self_value,
    self_out,
    norm2_gain,
    norm2_shift,
    cross_query,
    cross_key,
    cross_value,
    cross_out,
    norm3_gain,
    norm3_shift,
    up_weight,
    up_bias,
    down_weight,
    down_bias,
):
    micro = tokens.shape[0]
    rows = tokens.shape[1]
    width = tokens.shape[2]
    source_rows = memory.shape[1]
    parts = lax.axis_size("dp")
    place = lax.axis_index("dp")
    experts_here = up_weight.shape[0]
    capacity = CAP
    head_count = HEADS
    local_places = place * rows + jnp.arange(rows, dtype=jnp.int32)
    stream_places = jnp.arange(rows * parts, dtype=jnp.int32)
    source_places = jnp.arange(source_rows * parts, dtype=jnp.int32)
    slot_ids = jnp.arange(experts_here * capacity, dtype=jnp.int32)
    expert_ids = jnp.arange(experts_here, dtype=jnp.int32)
    inputs = tokens.astype(jnp.float32)
    normed_first, first_back = jax.vjp(layer_norm, inputs, norm1_gain, norm1_shift)
    attn_in = normed_first.astype(jnp.bfloat16)
    queries = product(attn_in, self_query).astype(jnp.bfloat16)
    keys_mine = product(attn_in, self_key).astype(jnp.bfloat16)
    values_mine = product(attn_in, self_value).astype(jnp.bfloat16)
    keys_all, values_all = (
        lax.all_gather(keys_mine, "dp", axis=1, tiled=True),
        lax.all_gather(values_mine, "dp", axis=1, tiled=True),
    )
    cross_keys_all, cross_values_all = (
        lax.all_gather(product(memory, cross_key).astype(jnp.bfloat16), "dp", axis=1, tiled=True),
        lax.all_gather(product(memory, cross_value).astype(jnp.bfloat16), "dp", axis=1, tiled=True),
    )
    square_zero = jnp.zeros((width, width), jnp.float32)
    vector_zero = jnp.zeros((width,), jnp.float32)
    grad_self_query, grad_self_key, grad_self_value, grad_self_out = (
        square_zero,
        square_zero,
        square_zero,
        square_zero,
    )
    grad_cross_query, grad_cross_key, grad_cross_value, grad_cross_out = (
        square_zero,
        square_zero,
        square_zero,
        square_zero,
    )
    second_gain_sum, second_shift_sum, third_gain_sum, third_shift_sum = (
        vector_zero,
        vector_zero,
        vector_zero,
        vector_zero,
    )
    grad_up = jnp.zeros(up_weight.shape, jnp.float32)
    grad_up_bias = jnp.zeros(up_bias.shape, jnp.float32)
    grad_down = jnp.zeros(down_weight.shape, jnp.float32)
    grad_down_bias = jnp.zeros(down_bias.shape, jnp.float32)
    outputs = []
    attn_in_grads = []
    resid_grads = []
    for batch_index in range(micro):
        lengths_now = doc_lengths[batch_index, 0]
        query_docs = doc_index(lengths_now, local_places)
        stream_docs = doc_index(lengths_now, stream_places)
        source_docs = doc_index(source_lengths[batch_index, 0], source_places)
        self_allowed = (query_docs[:, None] == stream_docs[None, :]) & (
            stream_places[None, :] <= local_places[:, None]
        )
        cross_allowed = query_docs[:, None] == source_docs[None, :]
        self_result, self_log = attend_forward(
            queries[batch_index],
            keys_all[batch_index],
            values_all[batch_index],
            self_allowed,
            head_count,
        )
        self_mixed = self_result.astype(jnp.bfloat16)
        after_self = inputs[batch_index] + product(self_mixed, self_out)
        normed_second, second_back = jax.vjp(layer_norm, after_self, norm2_gain, norm2_shift)
        cross_in = normed_second.astype(jnp.bfloat16)
        cross_queries = product(cross_in, cross_query).astype(jnp.bfloat16)
        cross_result, cross_log = attend_forward(
            cross_queries,
            cross_keys_all[batch_index],
            cross_values_all[batch_index],
            cross_allowed,
            head_count,
        )
        cross_mixed = cross_result.astype(jnp.bfloat16)
        after_cross = after_self + product(cross_mixed, cross_out)
        normed_third, third_back = jax.vjp(layer_norm, after_cross, norm3_gain, norm3_shift)
        expert_in = normed_third.astype(jnp.bfloat16)
        chosen = expert_slot[batch_index, :, 0]
        one_hot = (chosen[:, None] == expert_ids[None, :]).astype(jnp.int32)
        ranks = jnp.sum((jnp.cumsum(one_hot, axis=0) - 1) * one_hot, axis=1)
        target = chosen * capacity + ranks
        dispatch = (slot_ids[:, None] == target[None, :]).astype(jnp.bfloat16)
        buffer_in = (
            product(dispatch, expert_in).astype(jnp.bfloat16).reshape(experts_here, capacity, width)
        )
        pre_act = (
            jnp.einsum("ecd,edf->ecf", buffer_in, up_weight, preferred_element_type=jnp.float32)
            + up_bias[:, None, :]
        )
        activated, gelu_back = jax.vjp(jax.nn.gelu, pre_act)
        hidden = activated.astype(jnp.bfloat16)
        buffer_out = (
            jnp.einsum("ecf,efd->ecd", hidden, down_weight, preferred_element_type=jnp.float32)
            + down_bias[:, None, :]
        )
        expert_out = jnp.take(buffer_out.reshape(experts_here * capacity, width), target, axis=0)
        outputs.append((after_cross + expert_out).astype(jnp.bfloat16))
        out_grad = cotangent[batch_index].astype(jnp.float32)
        grad_rows = out_grad.astype(jnp.bfloat16)
        buffer_grad = (
            product(dispatch, grad_rows).astype(jnp.bfloat16).reshape(experts_here, capacity, width)
        )
        grad_down = grad_down + jnp.einsum(
            "ecf,ecd->efd", hidden, buffer_grad, preferred_element_type=jnp.float32
        )
        grad_down_bias = grad_down_bias + jnp.sum(buffer_grad.astype(jnp.float32), axis=1)
        hidden_grad = jnp.einsum(
            "ecd,efd->ecf", buffer_grad, down_weight, preferred_element_type=jnp.float32
        )
        pre_grad = gelu_back(hidden_grad)[0].astype(jnp.bfloat16)
        grad_up = grad_up + jnp.einsum(
            "ecd,ecf->edf", buffer_in, pre_grad, preferred_element_type=jnp.float32
        )
        grad_up_bias = grad_up_bias + jnp.sum(pre_grad.astype(jnp.float32), axis=1)
        buffer_back = jnp.einsum(
            "ecf,edf->ecd", pre_grad, up_weight, preferred_element_type=jnp.float32
        )
        expert_in_grad = jnp.take(
            buffer_back.reshape(experts_here * capacity, width), target, axis=0
        )
        third_resid, third_gain, third_shift = third_back(expert_in_grad)
        third_gain_sum = third_gain_sum + third_gain
        third_shift_sum = third_shift_sum + third_shift
        cross_grad = out_grad + third_resid
        cross_rows_grad = cross_grad.astype(jnp.bfloat16)
        grad_cross_out = grad_cross_out + left_product(cross_mixed, cross_rows_grad)
        cross_mixed_grad = right_product(cross_rows_grad, cross_out).astype(jnp.bfloat16)
        cross_query_back, cross_key_back, cross_value_back = attend_backward(
            cross_queries,
            cross_keys_all[batch_index],
            cross_values_all[batch_index],
            cross_allowed,
            head_count,
            cross_log,
            cross_mixed_grad,
        )
        cross_query_low = cross_query_back.astype(jnp.bfloat16)
        grad_cross_query = grad_cross_query + left_product(cross_in, cross_query_low)
        cross_key_mine, cross_value_mine = (
            lax.psum_scatter(
                cross_key_back.astype(jnp.bfloat16), "dp", scatter_dimension=0, tiled=True
            ).astype(jnp.float32),
            lax.psum_scatter(
                cross_value_back.astype(jnp.bfloat16), "dp", scatter_dimension=0, tiled=True
            ).astype(jnp.float32),
        )
        source_exact = memory[batch_index].astype(jnp.float32)
        grad_cross_key = grad_cross_key + exact_left(source_exact, cross_key_mine)
        grad_cross_value = grad_cross_value + exact_left(source_exact, cross_value_mine)
        second_resid, second_gain, second_shift = second_back(
            right_product(cross_query_low, cross_query)
        )
        second_gain_sum = second_gain_sum + second_gain
        second_shift_sum = second_shift_sum + second_shift
        self_grad = cross_grad + second_resid
        self_rows_grad = self_grad.astype(jnp.bfloat16)
        grad_self_out = grad_self_out + left_product(self_mixed, self_rows_grad)
        self_mixed_grad = right_product(self_rows_grad, self_out).astype(jnp.bfloat16)
        self_query_back, self_key_back, self_value_back = attend_backward(
            queries[batch_index],
            keys_all[batch_index],
            values_all[batch_index],
            self_allowed,
            head_count,
            self_log,
            self_mixed_grad,
        )
        self_key_mine, self_value_mine = (
            lax.psum_scatter(
                self_key_back.astype(jnp.bfloat16), "dp", scatter_dimension=0, tiled=True
            ).astype(jnp.float32),
            lax.psum_scatter(
                self_value_back.astype(jnp.bfloat16), "dp", scatter_dimension=0, tiled=True
            ).astype(jnp.float32),
        )
        query_low = self_query_back.astype(jnp.bfloat16)
        key_low = self_key_mine.astype(jnp.bfloat16)
        value_low = self_value_mine.astype(jnp.bfloat16)
        grad_self_query = grad_self_query + left_product(attn_in[batch_index], query_low)
        grad_self_key = grad_self_key + left_product(attn_in[batch_index], key_low)
        grad_self_value = grad_self_value + left_product(attn_in[batch_index], value_low)
        attn_in_grads.append(
            right_product(query_low, self_query)
            + right_product(key_low, self_key)
            + right_product(value_low, self_value)
        )
        resid_grads.append(self_grad)
    first_resid, first_gain, first_shift = first_back(jnp.stack(attn_in_grads))
    token_grad = jnp.stack(resid_grads) + first_resid
    block_out = jnp.stack(outputs)
    up_share, up_bias_share, down_share, down_bias_share = (
        lax.psum_scatter(
            grad_up.astype(jnp.bfloat16), "dp", scatter_dimension=2, tiled=True
        ).astype(jnp.float32),
        lax.psum_scatter(
            grad_up_bias.astype(jnp.bfloat16), "dp", scatter_dimension=1, tiled=True
        ).astype(jnp.float32),
        lax.psum_scatter(
            grad_down.astype(jnp.bfloat16), "dp", scatter_dimension=1, tiled=True
        ).astype(jnp.float32),
        lax.psum_scatter(
            grad_down_bias.astype(jnp.bfloat16), "dp", scatter_dimension=1, tiled=True
        ).astype(jnp.float32),
    )
    up_total, up_bias_total, down_total, down_bias_total = (
        lax.all_gather(up_share.astype(jnp.bfloat16), "dp", axis=2, tiled=True).astype(
            up_share.dtype
        ),
        lax.all_gather(up_bias_share.astype(jnp.bfloat16), "dp", axis=1, tiled=True).astype(
            up_bias_share.dtype
        ),
        lax.all_gather(down_share.astype(jnp.bfloat16), "dp", axis=1, tiled=True).astype(
            down_share.dtype
        ),
        lax.all_gather(down_bias_share.astype(jnp.bfloat16), "dp", axis=1, tiled=True).astype(
            down_bias_share.dtype
        ),
    )
    shared = lax.psum(
        (
            first_gain,
            first_shift,
            grad_self_query,
            grad_self_key,
            grad_self_value,
            grad_self_out,
            second_gain_sum,
            second_shift_sum,
            grad_cross_query,
            grad_cross_key,
            grad_cross_value,
            grad_cross_out,
            third_gain_sum,
            third_shift_sum,
        ),
        ("grp", "dp"),
    )
    return (
        block_out,
        token_grad,
        shared[0],
        shared[1],
        shared[2],
        shared[3],
        shared[4],
        shared[5],
        shared[6],
        shared[7],
        shared[8],
        shared[9],
        shared[10],
        shared[11],
        shared[12],
        shared[13],
        up_total,
        up_bias_total,
        down_total,
        down_bias_total,
    )


MESH = pl.DeviceIdType.MESH
BF = jnp.bfloat16
F32 = jnp.float32
VMEM_BYTES = 56 * 1024 * 1024
HIDE = -1e30


def mm(left, right):
    return lax.dot_general(left, right, (((1,), (0,)), ((), ())), preferred_element_type=F32)


def mm_right(left, right):
    return lax.dot_general(left, right, (((1,), (1,)), ((), ())), preferred_element_type=F32)


def mm_left(left, right):
    return lax.dot_general(left, right, (((0,), (0,)), ((), ())), preferred_element_type=F32)


def norm_parts(inputs):
    mean_row = jnp.mean(inputs, axis=-1, keepdims=True)
    centred = inputs - mean_row
    spread = jnp.mean(centred * centred, axis=-1, keepdims=True)
    inverse = lax.rsqrt(spread + 1e-05)
    return centred * inverse, inverse


def norm_back(unit, inverse, gain, grad):
    scaled = grad * gain
    first = jnp.mean(scaled, axis=-1, keepdims=True)
    second = jnp.mean(scaled * unit, axis=-1, keepdims=True)
    return inverse * (scaled - first - unit * second)


def col_sum(values):
    return jnp.sum(values, axis=0, keepdims=True)


def three_parts(values):
    high = values.astype(BF).astype(F32)
    rest = values - high
    middle = rest.astype(BF).astype(F32)
    return high, middle, rest - middle


def doc_of(lengths_ref, batch, positions):
    total = jnp.int32(0)
    docs = jnp.zeros(positions.shape, jnp.int32)
    for j in range(lengths_ref.shape[2]):
        total = total + lengths_ref[batch, 0, j]
        docs = docs + (positions >= total).astype(jnp.int32)
    return docs


def lanes_of(shape, head):
    lane = lax.broadcasted_iota(jnp.int32, shape, 1)
    half = shape[1] // 2
    own = (lane < half) if head == 0 else (lane >= half)
    return own, (lane - half if head == 0 else lane)


def greet(grp, me, parts):
    barrier = pltpu.get_barrier_semaphore()
    for k in range(1, parts):
        pl.semaphore_signal(
            barrier, inc=1, device_id=(grp, lax.rem(me + k, parts)), device_id_type=MESH
        )
    pl.semaphore_wait(barrier, parts - 1)


def sender(grp, src, dst, ssem, rsem, target):
    return pltpu.make_async_remote_copy(
        src_ref=src,
        dst_ref=dst,
        send_sem=ssem,
        recv_sem=rsem,
        device_id=(grp, target),
        device_id_type=MESH,
    )


def partner_of(grp, me, axis):
    place = lax.div(me, 2)
    if axis == "core":
        return grp + 1 - 2 * lax.rem(grp, 2), me
    if axis == "x":
        return lax.rem(grp + 2, 4), me
    if axis == "y":
        return grp, me + 1 - 2 * lax.rem(me, 2)
    if axis == "near":
        return grp, me + 2 - 4 * lax.rem(place, 2)
    return grp, lax.rem(me + 4, 8)


def push(src, dst, ssem, rsem, device):
    return pltpu.make_async_remote_copy(
        src_ref=src, dst_ref=dst, send_sem=ssem, recv_sem=rsem, device_id=device, device_id_type=MESH
    )


def key_features(values, docs, head):
    own, place = lanes_of(values.shape, head)
    other = jnp.where(place == docs, 0.0, HIDE)
    other = jnp.where((place >= 4) & (place < 7), 1.0, other)
    return jnp.where(own, values.astype(F32), other).astype(BF)


def query_features(values, docs, head, scaling):
    own, place = lanes_of(values.shape, head)
    return jnp.where(
        own, values.astype(F32) * scaling, jnp.where(place == docs, 1.0, 0.0)
    ).astype(BF)


def value_features(values, head):
    own, _ = lanes_of(values.shape, head)
    return jnp.where(own, values.astype(F32), 1.0).astype(BF)


def forward_kernel(
    parts, pairs, rows, scaling,
    doc_len, src_len, tokens, memory, gain1, shift1, gain2, shift2,
    wq, wk, wv, wo, cq, ck, cv, co, cot, marks,
    a_out, x1_out, c_out, x2_out, o1_own, o2_own,
    qa1, ka1, va1, o1, qa2, ka2, va2, o2, gf_got, marks_got,
    st_qkv, rv_qkv, st_kv, rv_kv, st_q2, rv_q2, tmp_o,
    local_sem, s_qkv, r_qkv, s_kv, r_kv, s_o1, r_o1, s_q2, r_q2, s_o2, r_o2, s_y, r_y,
):
    grp = lax.axis_index("grp")
    me = lax.axis_index("dp")
    batch = lax.div(me, pairs)
    pair = lax.rem(me, pairs)
    micro = tokens.shape[0]
    lanes = 128
    length = parts * rows

    def a2a(src, dst, ssem, rsem, target):
        return sender(grp, src.at[target], dst.at[me], ssem.at[target], rsem.at[me], target)

    def arrived(dst, ssem, rsem, source):
        sender(grp, dst.at[source], dst.at[source], ssem.at[source], rsem.at[source], source).wait_recv()

    greet(grp, me, parts)

    def first_norm(mb, _):
        unit, _inv = norm_parts(tokens[mb].astype(F32))
        a = (unit * gain1[...] + shift1[...]).astype(BF)
        a_out[mb] = a
        for n, weight in enumerate((wq, wk, wv)):
            got = mm(a, weight[...]).astype(BF)
            for p in range(pairs):
                st_qkv[mb * pairs + p, n * rows : (n + 1) * rows, :] = got[:, p * lanes : (p + 1) * lanes]

        def send(p, _):
            target = mb * pairs + p

            @pl.when(target != me)
            def _():
                a2a(st_qkv, rv_qkv, s_qkv, r_qkv, target).start()

            return 0

        lax.fori_loop(0, pairs, send, 0)
        return 0

    lax.fori_loop(0, micro, first_norm, 0)
    mine = pltpu.make_async_copy(st_qkv.at[me], rv_qkv.at[me], local_sem)
    mine.start()
    mine.wait()

    def source_heads(mb, _):
        source = memory[mb]
        for n, weight in enumerate((ck, cv)):
            got = mm(source, weight[...]).astype(BF)
            for p in range(pairs):
                st_kv[mb * pairs + p, n * rows : (n + 1) * rows, :] = got[:, p * lanes : (p + 1) * lanes]
        return 0

    lax.fori_loop(0, micro, source_heads, 0)

    for k in range(1, parts):
        arrived(rv_qkv, s_qkv, r_qkv, lax.rem(me + k, parts))
    for k in range(1, parts):
        a2a(st_kv, rv_kv, s_kv, r_kv, lax.rem(me + k, parts)).start()
    mine = pltpu.make_async_copy(st_kv.at[me], rv_kv.at[me], local_sem)
    mine.start()
    mine.wait()

    def build_self(s, _):
        r0 = pl.multiple_of(s * rows, rows)
        places = r0 + lax.broadcasted_iota(jnp.int32, (rows, lanes), 0)
        docs = doc_of(doc_len, batch, places)
        for h in range(2):
            qa1[h, pl.ds(r0, rows), :] = query_features(rv_qkv[s, 0:rows, :], docs, h, scaling)
            ka1[h, pl.ds(r0, rows), :] = key_features(rv_qkv[s, rows : 2 * rows, :], docs, h)
            va1[h, pl.ds(r0, rows), :] = value_features(rv_qkv[s, 2 * rows : 3 * rows, :], h)
        return 0

    lax.fori_loop(0, parts, build_self, 0)

    def finish(qa, r0, h, query, top, acc):
        own, place = lanes_of((rows, lanes), h)
        total = pltpu.roll(acc, lanes // 2, 1)
        high, middle, low = three_parts(top + jnp.log(acc))
        query = query.astype(F32)
        query = jnp.where(~own & (place == 4), -high, query)
        query = jnp.where(~own & (place == 5), -middle, query)
        query = jnp.where(~own & (place == 6), -low, query)
        qa[h, pl.ds(r0, rows), :] = query.astype(BF)
        return acc / total

    def emit(t, heads, out, own_ref, ssem, rsem):
        own, _ = lanes_of((rows, lanes), 0)
        out[t] = jnp.where(own, heads[0], heads[1]).astype(BF)

        @pl.when(t != me)
        def _():
            sender(grp, out.at[t], own_ref.at[me], ssem.at[t], rsem.at[me], t).start()

        @pl.when(t == me)
        def _():
            own_ref[me] = out[t]

    for e in range(parts // 2):
        reach = 2 * rows * (e + 1)
        cut = reach - 2 * rows

        def self_block(i, _, reach=reach, cut=cut, e=e):
            t = 2 * e + i
            r0 = pl.multiple_of(t * rows, rows)
            row = r0 + lax.broadcasted_iota(jnp.int32, (rows, 2 * rows), 0)
            col = cut + lax.broadcasted_iota(jnp.int32, (rows, 2 * rows), 1)
            heads = []
            for h in range(2):
                query = qa1[h, pl.ds(r0, rows), :]
                near = mm_right(query, ka1[h, cut:reach, :])
                near = jnp.where(col <= row, near, HIDE)
                top = jnp.max(near, axis=1, keepdims=True)
                if cut:
                    far = mm_right(query, ka1[h, 0:cut, :])
                    top = jnp.maximum(top, jnp.max(far, axis=1, keepdims=True))
                acc = mm(jnp.exp(near - top).astype(BF), va1[h, cut:reach, :])
                if cut:
                    acc = acc + mm(jnp.exp(far - top).astype(BF), va1[h, 0:cut, :])
                heads.append(finish(qa1, r0, h, query, top, acc))
            emit(t, heads, o1, o1_own, s_o1, r_o1)
            return 0

        lax.fori_loop(0, 2, self_block, 0)

    def own_wait(own_ref, ssem, rsem):
        for k in range(1, parts):
            arrived(own_ref, ssem, rsem, lax.rem(me + k, parts))

    own_wait(o1_own, s_o1, r_o1)

    def second_norm(mb, _):
        mixed = jnp.concatenate([o1_own[mb * pairs + p] for p in range(pairs)], axis=1)
        x1 = tokens[mb].astype(F32) + mm(mixed, wo[...])
        x1_out[mb] = x1
        unit, _inv = norm_parts(x1)
        c = (unit * gain2[...] + shift2[...]).astype(BF)
        c_out[mb] = c
        got = mm(c, cq[...]).astype(BF)
        for p in range(pairs):
            st_q2[mb * pairs + p] = got[:, p * lanes : (p + 1) * lanes]

        def send(p, _):
            target = mb * pairs + p

            @pl.when(target != me)
            def _():
                a2a(st_q2, rv_q2, s_q2, r_q2, target).start()

            @pl.when(target == me)
            def _():
                rv_q2[me] = st_q2[me]

            return 0

        lax.fori_loop(0, pairs, send, 0)
        return 0

    lax.fori_loop(0, micro, second_norm, 0)

    for k in range(1, parts):
        arrived(rv_kv, s_kv, r_kv, lax.rem(me + k, parts))

    def build_cross(s, _):
        r0 = pl.multiple_of(s * rows, rows)
        places = r0 + lax.broadcasted_iota(jnp.int32, (rows, lanes), 0)
        docs = doc_of(src_len, batch, places)
        for h in range(2):
            ka2[h, pl.ds(r0, rows), :] = key_features(rv_kv[s, 0:rows, :], docs, h)
            va2[h, pl.ds(r0, rows), :] = value_features(rv_kv[s, rows : 2 * rows, :], h)
        return 0

    lax.fori_loop(0, parts, build_cross, 0)

    to_y = partner_of(grp, me, "y")
    swaps = [
        push(cot, gf_got, s_y.at[0], r_y.at[0], to_y),
        push(marks, marks_got, s_y.at[1], r_y.at[1], to_y),
    ]
    for swap in swaps:
        swap.start()

    def cross_block(k, _):
        t = lax.rem(me + k, parts)

        @pl.when(k > 0)
        def _():
            arrived(rv_q2, s_q2, r_q2, t)

        r0 = pl.multiple_of(t * rows, rows)
        places = r0 + lax.broadcasted_iota(jnp.int32, (rows, lanes), 0)
        docs = doc_of(doc_len, batch, places)
        heads = []
        for h in range(2):
            query = query_features(rv_q2[t], docs, h, scaling)
            scores = mm_right(query, ka2[h])
            top = jnp.max(scores, axis=1, keepdims=True)
            acc = mm(jnp.exp(scores - top).astype(BF), va2[h])
            heads.append(finish(qa2, r0, h, query, top, acc))
        emit(t, heads, o2, o2_own, s_o2, r_o2)
        return 0

    lax.fori_loop(0, parts, cross_block, 0)
    own_wait(o2_own, s_o2, r_o2)

    def third(mb, _):
        mixed = jnp.concatenate([o2_own[mb * pairs + p] for p in range(pairs)], axis=1)
        x2_out[mb] = x1_out[mb] + mm(mixed, co[...])
        return 0

    lax.fori_loop(0, micro, third, 0)

    for k in range(1, parts):
        target = lax.rem(me + k, parts)
        a2a(st_qkv, rv_qkv, s_qkv, r_qkv, target).wait_send()
        a2a(st_kv, rv_kv, s_kv, r_kv, target).wait_send()
        a2a(st_q2, rv_q2, s_q2, r_q2, target).wait_send()
        a2a(o1, o1_own, s_o1, r_o1, target).wait_send()
        a2a(o2, o2_own, s_o2, r_o2, target).wait_send()
    for swap in swaps:
        swap.wait()


def gelu_both(z):
    root = math.sqrt(2.0 / math.pi)
    square = z * z
    bent = jnp.tanh(root * z * (1.0 + 0.044715 * square))
    half = 0.5 * (1.0 + bent)
    slope = half + 0.5 * z * (1.0 - bent * bent) * (root * (1.0 + 3 * 0.044715 * square))
    return z * half, slope


def expert_kernel(
    pairs, tiles,
    x2, o2_own, marks, marks_got, cot, gf_got, gain3, shift3, up_hbm, up_b, down_hbm, down_b, co,
    block_out, gx2_out, do2, g_co, vec, shares,
    up, down, e_all, act, du_all, de_acc, de_low, de_got, y_low, y_got,
    load_sem, ssem, rsem,
):
    grp = lax.axis_index("grp")
    me = lax.axis_index("dp")
    half = lax.rem(me, 2)
    other = partner_of(grp, me, "y")
    micro, rows, width = x2.shape
    lanes = 128
    count = micro * rows
    depth = up.shape[2] // tiles
    span = up.shape[2]

    barrier = pltpu.get_barrier_semaphore()
    pl.semaphore_signal(barrier, inc=1, device_id=other, device_id_type=MESH)
    first_col = pl.multiple_of(half * span, span)
    loads = [
        pltpu.make_async_copy(up_hbm.at[:, :, pl.ds(first_col, span)], up, load_sem.at[0]),
        pltpu.make_async_copy(down_hbm.at[:, pl.ds(first_col, span), :], down, load_sem.at[1]),
    ]
    for load in loads:
        load.start()
    mark_all = (marks, marks_got)
    gf_all = tuple(
        jnp.concatenate([ref[mb] for mb in range(micro)], axis=0) for ref in (cot, gf_got)
    )
    for mb in range(micro):
        part = slice(mb * rows, (mb + 1) * rows)
        unit, _inv = norm_parts(x2[mb])
        e_all[0, part, :] = (unit * gain3[...] + shift3[...]).astype(BF)
    pl.semaphore_wait(barrier, 1)
    swaps = [
        push(src, dst, ssem.at[n], rsem.at[n], other)
        for n, (src, dst) in enumerate(
            (
                (e_all.at[0], e_all.at[1]),
                (de_low, de_got),
                (y_low, y_got),
            )
        )
    ]
    swaps[0].start()
    for load in loads:
        load.wait()

    def ones_of(rowset, wide):
        return jnp.concatenate([mark_all[rowset][...]] * (wide // lanes), axis=1) > 0.5

    def split(values, is_one):
        zero = jnp.zeros_like(values)
        return jnp.where(is_one, zero, values), jnp.where(is_one, values, zero)

    def through(rowset):
        de_acc[...] = jnp.zeros_like(de_acc)

        def tile(f, _):
            cols = pl.ds(pl.multiple_of(f * depth, depth), depth)
            bias_cols = pl.ds(pl.multiple_of(first_col + f * depth, depth), depth)
            is_one = ones_of(rowset, depth)
            e = e_all[rowset]
            gf = gf_all[rowset]
            u = jnp.where(
                is_one,
                mm(e, up[1, :, cols]) + up_b[1:2, bias_cols],
                mm(e, up[0, :, cols]) + up_b[0:1, bias_cols],
            )
            hidden, slope = gelu_both(u)
            act[rowset, f] = hidden.astype(BF)
            back = jnp.where(is_one, mm_right(gf, down[1, cols, :]), mm_right(gf, down[0, cols, :]))
            du = (back * slope).astype(BF)
            du_all[rowset, f] = du
            none, one = split(du, is_one)
            de_acc[...] += mm_right(none, up[0, :, cols]) + mm_right(one, up[1, :, cols])
            return 0

        lax.fori_loop(0, tiles, tile, 0)

    def branch(rowset):
        is_one = ones_of(rowset, depth)

        def tile(f, total):
            cols = pl.ds(pl.multiple_of(f * depth, depth), depth)
            none, one = split(act[rowset, f], is_one)
            return total + mm(none, down[0, cols, :]) + mm(one, down[1, cols, :])

        return lax.fori_loop(0, tiles, tile, jnp.zeros((count, width), F32))

    vec[...] = jnp.zeros_like(vec)
    through(0)
    de_mine = de_acc[...]
    swaps[0].wait()
    through(1)
    de_low[...] = de_acc[...].astype(BF)
    swaps[1].start()
    de_acc[...] = de_mine
    y_low[...] = branch(1).astype(BF)
    swaps[2].start()

    for n in range(2):
        def weights(f, _, n=n):
            slot = lax.rem(f, 2) * 2 + lax.div(f, 2)
            up_sum = jnp.zeros((width, depth), F32)
            down_sum = jnp.zeros((depth, width), F32)
            bias = jnp.zeros((1, depth), F32)
            for rowset in range(2):
                is_one = ones_of(rowset, depth)
                du_n = split(du_all[rowset, f], is_one)[n]
                act_n = split(act[rowset, f], is_one)[n]
                up_sum = up_sum + mm_left(e_all[rowset], du_n)
                down_sum = down_sum + mm_left(act_n, gf_all[rowset])
                bias = bias + col_sum(du_n.astype(F32))
            for m in range(2):
                part = slice(m * depth, (m + 1) * depth)
                shares[2 * n + m, slot] = up_sum[part, :].astype(BF)
                shares[4 + 2 * n + m, slot] = down_sum[:, part].astype(BF)
            row = 8 + n * 4 + half * 2 + lax.div(f, 2)
            col = pl.ds(pl.multiple_of(lax.rem(f, 2) * depth, depth), depth)
            vec[pl.ds(row, 1), col] = bias
            return 0

        lax.fori_loop(0, tiles, weights, 0)

    all_grad = gf_all[0].astype(F32)
    none, one = split(all_grad, ones_of(0, width))
    vec[6:7, :] = col_sum(none)
    vec[7:8, :] = col_sum(one)

    swaps[1].wait()
    cross = jnp.zeros((width, width), F32)
    for mb in range(micro):
        part = slice(mb * rows, (mb + 1) * rows)
        unit, inverse = norm_parts(x2[mb])
        grad = de_acc[part, :] + de_got[part, :].astype(F32)
        vec[4:5, :] += col_sum(grad * unit)
        vec[5:6, :] += col_sum(grad)
        gx2 = cot[mb].astype(F32) + norm_back(unit, inverse, gain3[...], grad)
        gx2_out[mb] = gx2
        gy2 = gx2.astype(BF)
        back = mm_right(gy2, co[...]).astype(BF)
        for p in range(pairs):
            do2[mb * pairs + p] = back[:, p * lanes : (p + 1) * lanes]
        mixed = jnp.concatenate([o2_own[mb * pairs + p] for p in range(pairs)], axis=1)
        cross = cross + mm_left(mixed, gy2)
    g_co[...] = cross.astype(BF)

    own_branch = branch(0) + jnp.where(ones_of(0, width), down_b[1:2, :], down_b[0:1, :])
    swaps[2].wait()
    for mb in range(micro):
        part = slice(mb * rows, (mb + 1) * rows)
        block_out[mb] = (x2[mb] + own_branch[part, :] + y_got[part, :].astype(F32)).astype(BF)


def backward_kernel(
    parts, pairs, rows, scaling,
    gx2, do2_st, qa1_in, ka1_in, va1_in, o1, qa2_in, ka2_in, va2_in, o2,
    tokens, memory, x1, c_in, a_in, o1_own, gain1, gain2,
    wq, wk, wv, wo, cq, g_co, vec_in, shares_in,
    token_grad, vec_out, all_shares, all_early, all_late,
    rv_do2, st_dq2, rv_dq2, st_dkv2, rv_dkv2, st_do1, rv_do1, st_d, rv_d, doa,
    dq_acc, dk_acc, dv_acc, gx1_ref, low_grad,
    qa, ka, va, shares, got_near, got_far, early, late, *rest
):
    got_early, got_late, rest = rest[:5], rest[5:10], rest[10:]
    vec, got_vec, sums, rest = rest[0], rest[1], rest[2:6], rest[6:]
    bulk_s, bulk_r, local_sem, load_sem, early_s, early_r, late_s, late_r, vec_s, vec_r, rest = *rest[:10], rest[10:]
    s_do2, r_do2, s_dq2, r_dq2, s_dkv2, r_dkv2, s_do1, r_do1, s_d, r_d = rest
    g_cq, g_so, g_sum0, g_sum1 = sums
    grp = lax.axis_index("grp")
    me = lax.axis_index("dp")
    micro = tokens.shape[0]
    width = tokens.shape[2]
    lanes = 128
    length = parts * rows

    def a2a(src, dst, ssem, rsem, target):
        return sender(grp, src.at[target], dst.at[me], ssem.at[target], rsem.at[me], target)

    def arrived(dst, ssem, rsem, source):
        sender(grp, dst.at[source], dst.at[source], ssem.at[source], rsem.at[source], source).wait_recv()

    half = lax.rem(me, 2)
    near_bit = lax.rem(lax.div(me, 2), 2)
    far_bit = lax.div(me, 4)
    axes = ("core", "x", "y", "near", "far")
    bits = (lax.rem(grp, 2), lax.div(grp, 2), half, near_bit, far_bit)
    partners = [partner_of(grp, me, axis) for axis in axes]
    barrier = pltpu.get_barrier_semaphore()
    for k in range(1, parts):
        pl.semaphore_signal(
            barrier, inc=1, device_id=(grp, lax.rem(me + k, parts)), device_id_type=MESH
        )
    for d in range(2):
        pl.semaphore_signal(barrier, inc=1, device_id=partners[d], device_id_type=MESH)
    pl.semaphore_wait(barrier, parts + 1)

    pieces = shares_in.shape[0]
    mine = near_bit * 2 + far_bit
    kept, given = pl.ds(near_bit * 2, 2), pl.ds((1 - near_bit) * 2, 2)
    to_y, to_near, to_far = partners[2:]

    def share_copy(s, stage):
        sems = (bulk_s.at[s, stage], bulk_r.at[s, stage])
        if stage == 0:
            return push(shares_in.at[s, given], got_near.at[s], *sems, to_near)
        if stage == 1:
            return push(shares.at[s, 1 - far_bit], got_far.at[s], *sems, to_far)
        if stage == 2:
            return push(shares.at[s, far_bit], all_shares.at[half, s, mine], *sems, to_far)
        if stage == 3:
            return push(all_shares.at[half, s, kept], all_shares.at[half, s, kept], *sems, to_near)
        return push(all_shares.at[half, s], all_shares.at[half, s], *sems, to_y)

    def share_local(s):
        return pltpu.make_async_copy(
            shares.at[s, far_bit], all_shares.at[half, s, mine], local_sem.at[s]
        )

    def share_load(s):
        return pltpu.make_async_copy(shares_in.at[s, kept], shares.at[s], load_sem.at[s])

    def load_three(refs, n):
        return [
            pltpu.make_async_copy(src, dst, load_sem.at[pieces + 3 * n + m])
            for m, (src, dst) in enumerate(zip(refs, (qa, ka, va)))
        ]

    def share_step(s, stage):
        if stage == 1:
            share_copy(s, 0).wait_recv()
            share_load(s).wait()
            for n in range(2):
                shares[s, n] = (shares[s, n].astype(F32) + got_near[s, n].astype(F32)).astype(BF)
        if stage == 2:
            share_copy(s, 1).wait_recv()
            shares[s, far_bit] = (
                shares[s, far_bit].astype(F32) + got_far[s].astype(F32)
            ).astype(BF)
            share_local(s).start()
        if stage == 3:
            share_copy(s, 2).wait_recv()
            share_local(s).wait()
        if stage == 4:
            share_copy(s, 3).wait_recv()
        share_copy(s, stage).start()

    def tick(i):
        for stage in (0, 4, 1, 2, 3):
            s = i - stage
            if isinstance(s, int):
                if 0 <= s < pieces:
                    share_step(s, stage)
            else:

                @pl.when((s >= 0) & (s < pieces))
                def _(s=s, stage=stage):
                    share_step(s, stage)

    def offset_of(total, upto):
        place = jnp.int32(0)
        for d in range(upto):
            place = place + bits[d] * (total >> (d + 1))
        return place

    def rows_at(total, start, size):
        unit = total >> 5
        return pl.ds(pl.multiple_of(start, unit), size)

    def sum_copy(own, out, got, ssem, rsem, stage):
        total = own.shape[0]
        if stage < 5:
            size = total >> (stage + 1)
            start = offset_of(total, stage) + (1 - bits[stage]) * size
            return push(
                own.at[rows_at(total, start, size)], got[stage], ssem.at[stage], rsem.at[stage],
                partners[stage],
            )
        d = 9 - stage
        size = total >> (d + 1)
        part = rows_at(total, offset_of(total, d + 1), size)
        src = own if stage == 5 else out
        return push(src.at[part], out.at[part], ssem.at[stage], rsem.at[stage], partners[d])

    def sum_local(own, out, sem):
        total = own.shape[0]
        part = rows_at(total, offset_of(total, 5), total >> 5)
        return pltpu.make_async_copy(own.at[part], out.at[part], sem)

    def sum_step(own, out, got, ssem, rsem, sem, stage):
        total = own.shape[0]
        if 1 <= stage <= 5:
            sum_copy(own, out, got, ssem, rsem, stage - 1).wait_recv()
            size = total >> stage
            part = rows_at(total, offset_of(total, stage), size)
            own[part, :] = (own[part, :].astype(F32) + got[stage - 1][...].astype(F32)).astype(BF)
        if stage == 5:
            sum_local(own, out, sem).start()
        if stage == 6:
            sum_local(own, out, sem).wait()
        if stage >= 6:
            sum_copy(own, out, got, ssem, rsem, stage - 1).wait_recv()
        if stage < 10:
            sum_copy(own, out, got, ssem, rsem, stage).start()

    def early_step(stage):
        sum_step(early, all_early, got_early, early_s, early_r, local_sem.at[pieces], stage)

    def vec_copy(d):
        return push(vec.at[d], got_vec.at[d], vec_s.at[d], vec_r.at[d], partners[d])

    def late_step(stage):
        sum_step(late, all_late, got_late, late_s, late_r, local_sem.at[pieces + 1], stage)
        if 1 <= stage <= 5:
            d = stage - 1
            vec_copy(d).wait_recv()
            row = lax.broadcasted_iota(jnp.int32, vec.shape[1:], 0)
            added = got_vec[d] if d >= 2 else jnp.where(row < 6, got_vec[d], 0.0)
            vec[d + 1] = vec[d] + added
        if stage < 5:
            vec_copy(stage).start()

    for k in range(1, parts):
        a2a(do2_st, rv_do2, s_do2, r_do2, lax.rem(me + k, parts)).start()
    rv_do2[me] = do2_st[me]
    loads = load_three((qa2_in, ka2_in, va2_in), 0)
    for load in loads:
        load.start()
    for s in range(pieces):
        share_load(s).start()
    tick(0)

    def clear(s, _):
        part = pl.ds(pl.multiple_of(s * rows, rows), rows)
        for h in range(2):
            dk_acc[h, part, :] = jnp.zeros((rows, lanes), F32)
            dv_acc[h, part, :] = jnp.zeros((rows, lanes), F32)
            dq_acc[h, part, :] = jnp.zeros((rows, lanes), F32)
        return 0

    def grad_features(grads, mixed, head):
        own, place = lanes_of(grads.shape, head)
        grads = grads.astype(F32)
        delta = jnp.sum(jnp.where(own, grads * mixed.astype(F32), 0.0), axis=1, keepdims=True)
        high, middle, low = three_parts(delta)
        other = jnp.where(place == 0, -high, 0.0)
        other = jnp.where(place == 1, -middle, other)
        other = jnp.where(place == 2, -low, other)
        return jnp.where(own, grads, other).astype(BF)

    def tile(query, grads, keys, values, mask):
        scores = mm_right(keys, query)
        if mask is not None:
            scores = jnp.where(mask, scores, HIDE)
        prob = jnp.exp(scores)
        back = mm_right(values, grads)
        score_grad = (prob * back).astype(BF)
        return (
            mm_left(score_grad, keys),
            mm(score_grad, query),
            mm(prob.astype(BF), grads),
        )

    def join(zero_head, one_head):
        own, _ = lanes_of(zero_head.shape, 0)
        return jnp.where(own, zero_head, one_head)

    lax.fori_loop(0, parts, clear, 0)

    chunk = 2 * rows
    for load in loads:
        load.wait()

    def cross_block(k, _):
        t = lax.rem(me + k, parts)

        @pl.when(k > 0)
        def _():
            arrived(rv_do2, s_do2, r_do2, t)

        part = pl.ds(pl.multiple_of(t * rows, rows), rows)
        grads = [grad_features(rv_do2[t], o2[t], h) for h in range(2)]
        queries = [qa[h, part, :] for h in range(2)]
        sums = [jnp.zeros((rows, lanes), F32)] * 2
        for n in range(length // chunk):
            keys = slice(n * chunk, (n + 1) * chunk)
            for h in range(2):
                dq, dk, dv = tile(queries[h], grads[h], ka[h, keys, :], va[h, keys, :], None)
                sums[h] = sums[h] + dq
                dk_acc[h, keys, :] += dk
                dv_acc[h, keys, :] += dv
        st_dq2[t] = (join(sums[0], sums[1]) * scaling).astype(BF)

        @pl.when(k > 0)
        def _():
            a2a(st_dq2, rv_dq2, s_dq2, r_dq2, t).start()

        @pl.when(k == 0)
        def _():
            rv_dq2[me] = st_dq2[me]

        @pl.when(lax.rem(k, 2) == 1)
        def _():
            tick(lax.div(k + 1, 2))

        return 0

    lax.fori_loop(0, parts, cross_block, 0)

    loads = load_three((qa1_in, ka1_in, va1_in), 1)
    for load in loads:
        load.start()

    def give_cross(k, _):
        s = lax.rem(me + k, parts)
        part = pl.ds(pl.multiple_of(s * rows, rows), rows)
        st_dkv2[s, 0:rows, :] = join(dk_acc[0, part, :], dk_acc[1, part, :]).astype(BF)
        st_dkv2[s, rows : 2 * rows, :] = join(dv_acc[0, part, :], dv_acc[1, part, :]).astype(BF)

        @pl.when(k > 0)
        def _():
            a2a(st_dkv2, rv_dkv2, s_dkv2, r_dkv2, s).start()

        @pl.when(k == 0)
        def _():
            rv_dkv2[me] = st_dkv2[me]

        return 0

    for k in range(1, parts):
        arrived(rv_dq2, s_dq2, r_dq2, lax.rem(me + k, parts))

    def gathered(ref, mb, first):
        return jnp.concatenate(
            [ref[mb * pairs + p, first * rows : (first + 1) * rows, :] for p in range(pairs)], axis=1
        )

    vec[0] = vec_in[...]

    def second_back(mb, _):
        dq2 = gathered(rv_dq2, mb, 0)
        dc = mm_right(dq2, cq[...])
        unit, inverse = norm_parts(x1[mb])
        vec[0, 2:3, :] += col_sum(dc * unit)
        vec[0, 3:4, :] += col_sum(dc)
        gx1 = gx2[mb] + norm_back(unit, inverse, gain2[...], dc)
        gx1_ref[mb] = gx1
        low_grad[mb] = gx1.astype(BF)
        back = mm_right(low_grad[mb], wo[...]).astype(BF)
        for p in range(pairs):
            st_do1[mb * pairs + p] = back[:, p * lanes : (p + 1) * lanes]

        def send(p, _):
            target = mb * pairs + p

            @pl.when(target != me)
            def _():
                a2a(st_do1, rv_do1, s_do1, r_do1, target).start()

            @pl.when(target == me)
            def _():
                rv_do1[me] = st_do1[me]

            return 0

        lax.fori_loop(0, pairs, send, 0)
        return 0

    lax.fori_loop(0, micro, second_back, 0)
    tick(5)
    lax.fori_loop(0, parts, give_cross, 0)

    g_cq[...] = jnp.zeros_like(g_cq)
    g_so[...] = jnp.zeros_like(g_so)

    def cross_weights(mb, _):
        g_cq[...] += mm_left(c_in[mb], gathered(rv_dq2, mb, 0))
        mixed = jnp.concatenate([o1_own[mb * pairs + p] for p in range(pairs)], axis=1)
        g_so[...] += mm_left(mixed, low_grad[mb])
        return 0

    lax.fori_loop(0, micro, cross_weights, 0)
    early[0:width, :] = g_co[...]
    early[width : 2 * width, :] = g_cq[...].astype(BF)
    early[2 * width : 3 * width, :] = g_so[...].astype(BF)
    tick(6)
    for load in loads:
        load.wait()

    for k in range(1, parts):
        arrived(rv_do1, s_do1, r_do1, lax.rem(me + k, parts))

    lax.fori_loop(0, parts, clear, 0)

    def build(s, _):
        part = pl.ds(pl.multiple_of(s * rows, rows), rows)
        for h in range(2):
            doa[h, part, :] = grad_features(rv_do1[s], o1[s], h)
        return 0

    lax.fori_loop(0, parts, build, 0)

    def self_tile(i, j, mask):
        q_part = pl.ds(pl.multiple_of(i * chunk, chunk), chunk)
        k_part = pl.ds(pl.multiple_of(j * chunk, chunk), chunk)
        for h in range(2):
            dq, dk, dv = tile(
                qa[h, q_part, :], doa[h, q_part, :], ka[h, k_part, :], va[h, k_part, :], mask
            )
            dq_acc[h, q_part, :] += dq
            dk_acc[h, k_part, :] += dk
            dv_acc[h, k_part, :] += dv

    def source_part():
        for k in range(1, parts):
            arrived(rv_dkv2, s_dkv2, r_dkv2, lax.rem(me + k, parts))
        g_sum0[...] = jnp.zeros_like(g_sum0)
        g_sum1[...] = jnp.zeros_like(g_sum1)

        def source_weights(mb, _):
            g_sum0[...] += mm_left(memory[mb], gathered(rv_dkv2, mb, 0))
            g_sum1[...] += mm_left(memory[mb], gathered(rv_dkv2, mb, 1))
            return 0

        lax.fori_loop(0, micro, source_weights, 0)
        early[3 * width : 4 * width, :] = g_sum0[...].astype(BF)
        early[4 * width : 5 * width, :] = g_sum1[...].astype(BF)
        early_step(0)

    def self_column(j, _):
        key_place = lax.broadcasted_iota(jnp.int32, (chunk, chunk), 0)
        query_place = lax.broadcasted_iota(jnp.int32, (chunk, chunk), 1)
        self_tile(j, j, key_place <= query_place)

        def below(i, _):
            self_tile(i, j, None)
            return 0

        lax.fori_loop(j + 1, length // chunk, below, 0)

        def give(n, _):
            s = j * (chunk // rows) + n
            part = pl.ds(pl.multiple_of(s * rows, rows), rows)
            for m, (acc, factor) in enumerate(((dq_acc, scaling), (dk_acc, 1.0), (dv_acc, 1.0))):
                st_d[s, m * rows : (m + 1) * rows, :] = (
                    join(acc[0, part, :], acc[1, part, :]) * factor
                ).astype(BF)

            @pl.when(s != me)
            def _():
                a2a(st_d, rv_d, s_d, r_d, s).start()

            @pl.when(s == me)
            def _():
                rv_d[me] = st_d[me]

            return 0

        lax.fori_loop(0, chunk // rows, give, 0)

        @pl.when(j == 0)
        def _():
            source_part()

        @pl.when(j == 1)
        def _():
            early_step(1)

        @pl.when(j == 2)
        def _():
            early_step(2)

        @pl.when(j < 3)
        def _():
            tick(7 + j)

        return 0

    lax.fori_loop(0, length // chunk, self_column, 0)
    early_step(3)
    tick(10)
    early_step(4)

    for k in range(1, parts):
        arrived(rv_d, s_d, r_d, lax.rem(me + k, parts))
    for ref in (g_sum0, g_sum1, g_so):
        ref[...] = jnp.zeros_like(ref)

    def first_back(mb, _):
        da = jnp.zeros((rows, pairs * lanes), F32)
        for m, (weight, ref) in enumerate(((wq, g_sum0), (wk, g_sum1), (wv, g_so))):
            grads = gathered(rv_d, mb, m)
            da = da + mm_right(grads, weight[...])
            ref[...] += mm_left(a_in[mb], grads)
        unit, inverse = norm_parts(tokens[mb].astype(F32))
        vec[0, 0:1, :] += col_sum(da * unit)
        vec[0, 1:2, :] += col_sum(da)
        token_grad[mb] = gx1_ref[mb] + norm_back(unit, inverse, gain1[...], da)
        return 0

    lax.fori_loop(0, micro, first_back, 0)
    late[0:width, :] = g_sum0[...].astype(BF)
    late[width : 2 * width, :] = g_sum1[...].astype(BF)
    late[2 * width : 3 * width, :] = g_so[...].astype(BF)
    late_step(0)
    early_step(5)
    late_step(1)
    early_step(6)
    tick(11)
    late_step(2)
    early_step(7)
    late_step(3)
    early_step(8)
    late_step(4)
    early_step(9)
    late_step(5)
    early_step(10)
    for n in range(6, 11):
        late_step(n)
    for s in range(pieces):
        share_copy(s, 4).wait_recv()
    vec_out[...] = vec[5]
    for s in range(pieces):
        for stage in range(5):
            share_copy(s, stage).wait_send()
    for stage in range(10):
        sum_copy(early, all_early, got_early, early_s, early_r, stage).wait_send()
        sum_copy(late, all_late, got_late, late_s, late_r, stage).wait_send()
    for d in range(5):
        vec_copy(d).wait_send()

    for k in range(1, parts):
        target = lax.rem(me + k, parts)
        a2a(do2_st, rv_do2, s_do2, r_do2, target).wait_send()
        a2a(st_dq2, rv_dq2, s_dq2, r_dq2, target).wait_send()
        a2a(st_dkv2, rv_dkv2, s_dkv2, r_dkv2, target).wait_send()
        a2a(st_do1, rv_do1, s_do1, r_do1, target).wait_send()
        a2a(st_d, rv_d, s_d, r_d, target).wait_send()


def finish_kernel(shares, early, late, up, down, *grads):
    depth = shares.shape[3]
    for n in range(2):
        for m in range(2):
            part = slice(m * depth, (m + 1) * depth)
            up[n, part, :] = shares[0, 2 * n + m, 0].astype(F32)
            down[n, :, part] = shares[0, 4 + 2 * n + m, 0].astype(F32)
    for n, ref in enumerate(grads):
        ref[...] = (early[n] if n < early.shape[0] else late[n - early.shape[0]]).astype(F32)


def vmem_spec():
    return pl.BlockSpec(memory_space=pltpu.VMEM)


def fast_device(
    tokens, memory, expert_slot, doc_lengths, source_lengths, cotangent,
    norm1_gain, norm1_shift, self_query, self_key, self_value, self_out,
    norm2_gain, norm2_shift, cross_query, cross_key, cross_value, cross_out,
    norm3_gain, norm3_shift, up_weight, up_bias, down_weight, down_bias,
):
    micro, rows, width = tokens.shape
    parts = lax.axis_size("dp")
    pairs = HEADS // 2
    lanes = width // pairs
    length = parts * rows
    scaling = 1.0 / math.sqrt(width // HEADS)
    experts, _, hidden = up_weight.shape
    shape = jax.ShapeDtypeStruct
    dma = pltpu.SemaphoreType.DMA((parts,))
    line = lambda v: v.reshape(1, width)

    aug = shape((2, length, lanes), BF)
    blocks = shape((parts, rows, lanes), BF)
    full = shape((micro, rows, width), F32)
    low = shape((micro, rows, width), BF)
    vec = shape((1, width), F32)
    square = shape((width, width), F32)
    buf = lambda n: pltpu.VMEM((parts, n * rows, lanes), BF)

    count = micro * rows
    marks = jnp.broadcast_to(expert_slot.reshape(count, 1).astype(BF), (count, lanes))
    outs1 = [low, full, low, full, blocks, blocks, aug, aug, aug, blocks, aug, aug, aug, blocks,
             low, shape((count, lanes), BF)]
    (a, x1, c, x2, o1_own, o2_own, qa1, ka1, va1, o1, qa2, ka2, va2, o2, gf_got, marks_got) = pl.pallas_call(
        functools.partial(forward_kernel, parts, pairs, rows, scaling),
        out_shape=outs1,
        in_specs=[pl.BlockSpec(memory_space=pltpu.SMEM)] * 2 + [vmem_spec()] * 16,
        out_specs=[vmem_spec()] * len(outs1),
        scratch_shapes=[buf(3), buf(3), buf(2), buf(2), buf(1), buf(1),
                        pltpu.VMEM((2, rows, lanes), F32), pltpu.SemaphoreType.DMA]
        + [dma] * 10 + [pltpu.SemaphoreType.DMA((2,))] * 2,
        compiler_params=pltpu.CompilerParams(
            collective_id=1, has_side_effects=True, vmem_limit_bytes=VMEM_BYTES
        ),
        name="attend_forward",
    )(
        doc_lengths, source_lengths, tokens, memory, line(norm1_gain), line(norm1_shift),
        line(norm2_gain), line(norm2_shift), self_query, self_key, self_value, self_out,
        cross_query, cross_key, cross_value, cross_out, cotangent, marks,
    )

    tiles = 4
    span = hidden // 2
    depth = span // tiles
    any_spec = pl.BlockSpec(memory_space=pl.ANY)
    shares_shape = shape((8, tiles, depth, depth), BF)
    vec_pack = shape((16, width), F32)
    outs2 = [low, full, blocks, shape((width, width), BF), vec_pack, shares_shape]
    wide = lambda dtype, *dims: pltpu.VMEM(dims, dtype)
    block_out, gx2, do2, g_co, vec, shares = pl.pallas_call(
        functools.partial(expert_kernel, pairs, tiles),
        out_shape=outs2,
        in_specs=[vmem_spec()] * 8 + [any_spec, vmem_spec(), any_spec, vmem_spec(), vmem_spec()],
        out_specs=[vmem_spec()] * len(outs2),
        scratch_shapes=[
            wide(BF, experts, width, span), wide(BF, experts, span, width),
            wide(BF, 2, count, width),
            wide(BF, 2, tiles, count, depth), wide(BF, 2, tiles, count, depth),
            wide(F32, count, width), wide(BF, count, width), wide(BF, count, width),
            wide(BF, count, width), wide(BF, count, width),
            pltpu.SemaphoreType.DMA((2,)), pltpu.SemaphoreType.DMA((3,)), pltpu.SemaphoreType.DMA((3,)),
        ],
        compiler_params=pltpu.CompilerParams(
            collective_id=2, has_side_effects=True, vmem_limit_bytes=VMEM_BYTES
        ),
        name="experts",
    )(
        x2, o2_own, marks, marks_got, cotangent, gf_got, line(norm3_gain), line(norm3_shift),
        up_weight, up_bias, down_weight, down_bias, cross_out,
    )

    early_shape, late_shape = shape((5 * width, width), BF), shape((3 * width, width), BF)
    all_shape = shape((2, 8, tiles, depth, depth), BF)
    outs3 = [full, vec_pack, all_shape, early_shape, late_shape]
    acc = pltpu.VMEM((2, length, lanes), F32)
    total = wide(F32, width, width)
    dmas = lambda *dims: pltpu.SemaphoreType.DMA(dims)
    token_grad, vec, all_shares, all_early, all_late = pl.pallas_call(
        functools.partial(backward_kernel, parts, pairs, rows, scaling),
        out_shape=outs3,
        in_specs=[vmem_spec()] * 2 + [any_spec] * 3 + [vmem_spec()] + [any_spec] * 3
        + [vmem_spec()] * 16 + [any_spec],
        out_specs=[vmem_spec()] * 2 + [any_spec] * 3,
        scratch_shapes=[buf(1), buf(1), buf(1), buf(2), buf(2), buf(1), buf(1), buf(3), buf(3),
                        pltpu.VMEM((2, length, lanes), BF), acc, acc, acc,
                        wide(F32, micro, rows, width), wide(BF, micro, rows, width),
                        pltpu.VMEM((2, length, lanes), BF), pltpu.VMEM((2, length, lanes), BF),
                        pltpu.VMEM((2, length, lanes), BF),
                        wide(BF, 8, 2, depth, depth), wide(BF, 8, 2, depth, depth),
                        wide(BF, 8, depth, depth), wide(BF, 5 * width, width), wide(BF, 3 * width, width)]
        + [wide(BF, (5 * width) >> (d + 1), width) for d in range(5)]
        + [wide(BF, (3 * width) >> (d + 1), width) for d in range(5)]
        + [wide(F32, 6, 16, width), wide(F32, 5, 16, width), total, total, total, total]
        + [dmas(8, 5), dmas(8, 5), dmas(10), dmas(14), dmas(10), dmas(10), dmas(10), dmas(10), dmas(5), dmas(5)]
        + [dma] * 10,
        compiler_params=pltpu.CompilerParams(
            collective_id=3, has_side_effects=True, vmem_limit_bytes=VMEM_BYTES
        ),
        name="attend_backward",
    )(
        gx2, do2, qa1, ka1, va1, o1, qa2, ka2, va2, o2, tokens, memory, x1, c, a, o1_own,
        line(norm1_gain), line(norm2_gain), self_query, self_key, self_value, self_out, cross_query,
        g_co, vec, shares,
    )

    steps = 2 * tiles
    strip = width // steps
    place = lambda i: lax.div(i, tiles) * tiles + lax.rem(i, 2) * 2 + lax.div(lax.rem(i, tiles), 2)
    outs4 = [shape(up_weight.shape, F32), shape(down_weight.shape, F32)] + [square] * 8
    up_total, down_total, g_co, g_cq, g_so, g_ck, g_cv, g_sq, g_sk, g_sv = pl.pallas_call(
        finish_kernel,
        grid=(steps,),
        out_shape=outs4,
        in_specs=[
            pl.BlockSpec((1, 8, 1, depth, depth),
                         lambda i: (lax.div(i, tiles), 0, lax.rem(place(i), tiles), 0, 0)),
            pl.BlockSpec((5, strip, width), lambda i: (0, i, 0)),
            pl.BlockSpec((3, strip, width), lambda i: (0, i, 0)),
        ],
        out_specs=[
            pl.BlockSpec((experts, width, depth), lambda i: (0, 0, i)),
            pl.BlockSpec((experts, depth, width), lambda i: (0, i, 0)),
        ] + [pl.BlockSpec((strip, width), lambda i: (i, 0))] * 8,
        compiler_params=pltpu.CompilerParams(vmem_limit_bytes=VMEM_BYTES),
        name="finish",
    )(all_shares, all_early.reshape(5, width, width), all_late.reshape(3, width, width))

    return (
        block_out, token_grad, vec[0], vec[1], g_sq, g_sk, g_sv, g_so, vec[2], vec[3],
        g_cq, g_ck, g_cv, g_co, vec[4], vec[5],
        up_total, vec[8:16].reshape(experts, hidden), down_total, vec[6:8],
    )


def solution(mesh):
    fits = dict(mesh.shape) == {"grp": 4, "dp": 8}
    return jax.shard_map(
        fast_device if fits else per_device,
        mesh=mesh,
        in_specs=(
            P(None, ("grp", "dp"), None),
            P(None, ("grp", "dp"), None),
            P(None, ("grp", "dp"), None),
            P(None, "grp", None),
            P(None, "grp", None),
            P(None, ("grp", "dp"), None),
            P(),
            P(),
            P(),
            P(),
            P(),
            P(),
            P(),
            P(),
            P(),
            P(),
            P(),
            P(),
            P(),
            P(),
            P("grp", None, None),
            P("grp", None),
            P("grp", None, None),
            P("grp", None),
        ),
        out_specs=(
            P(None, ("grp", "dp"), None),
            P(None, ("grp", "dp"), None),
            P(),
            P(),
            P(),
            P(),
            P(),
            P(),
            P(),
            P(),
            P(),
            P(),
            P(),
            P(),
            P(),
            P(),
            P("grp", None, None),
            P("grp", None),
            P("grp", None, None),
            P("grp", None),
        ),
        check_vma=False,
    )
```

```python
import functools
import math

import jax
import jax.numpy as jnp
from jax import lax
from jax.experimental import pallas as pl
from jax.experimental.pallas import tpu as pltpu
from jax.sharding import PartitionSpec as P

HEADS = 8
CAP = 160


masked_score = -1e30


def layer_norm(inputs, norm_gain, norm_shift):
    mean_row = jnp.mean(inputs, axis=-1, keepdims=True)
    centred = inputs - mean_row
    spread = jnp.mean(centred * centred, axis=-1, keepdims=True)
    return centred * lax.rsqrt(spread + 1e-05) * norm_gain + norm_shift


def doc_index(lengths, places):
    doc_ends = jnp.cumsum(lengths)
    return jnp.sum((places[:, None] >= doc_ends[None, :]).astype(jnp.int32), axis=1)


def product(left, right):
    return jnp.dot(left, right, preferred_element_type=jnp.float32)


def left_product(left, right):
    return jnp.einsum("nd,ne->de", left, right, preferred_element_type=jnp.float32)


def right_product(left, right):
    return jnp.einsum("nd,ed->ne", left, right, preferred_element_type=jnp.float32)


def exact_left(left, right):
    return jnp.einsum("nd,ne->de", left, right, precision=lax.Precision.HIGHEST)


def split_heads(matrix, head_count):
    return matrix.reshape(matrix.shape[0], head_count, matrix.shape[1] // head_count)


def attend_forward(queries, keys_all, values_all, allowed, head_count):
    scaling = 1.0 / math.sqrt(queries.shape[1] // head_count)
    scores = (
        jnp.einsum(
            "qhd,khd->hqk",
            split_heads(queries, head_count),
            split_heads(keys_all, head_count),
            preferred_element_type=jnp.float32,
        )
        * scaling
    )
    scores = jnp.where(allowed[None], scores, masked_score)
    maximum = jnp.max(scores, axis=-1, keepdims=True)
    exponent = jnp.exp(scores - maximum)
    totals = jnp.sum(exponent, axis=-1, keepdims=True)
    probability = (exponent / totals).astype(jnp.bfloat16)
    mixed = jnp.einsum(
        "hqk,khd->qhd",
        probability,
        split_heads(values_all, head_count),
        preferred_element_type=jnp.float32,
    )
    return (mixed.reshape(queries.shape[0], queries.shape[1]), maximum + jnp.log(totals))


def score_parts(
    query_heads, key_heads, value_heads, grad_heads, allowed, scaling, log_total, centre
):
    scores = (
        jnp.einsum("qhd,khd->hqk", query_heads, key_heads, preferred_element_type=jnp.float32)
        * scaling
    )
    scores = jnp.where(allowed[None], scores, masked_score)
    probability = jnp.exp(scores - log_total)
    prob_grad = jnp.einsum(
        "qhd,khd->hqk", grad_heads, value_heads, preferred_element_type=jnp.float32
    )
    centre = jnp.sum(probability * prob_grad, axis=-1, keepdims=True)
    score_grad = (probability * (prob_grad - centre)).astype(jnp.bfloat16)
    return (probability, score_grad, centre)


def attend_backward(queries, keys_all, values_all, allowed, head_count, log_total, out_grad):
    scaling = 1.0 / math.sqrt(queries.shape[1] // head_count)
    query_heads = split_heads(queries, head_count)
    key_heads = split_heads(keys_all, head_count)
    grad_heads = split_heads(out_grad, head_count)
    probability, score_grad, centre = score_parts(
        query_heads,
        key_heads,
        split_heads(values_all, head_count),
        grad_heads,
        allowed,
        scaling,
        log_total,
        None,
    )
    query_back = (
        jnp.einsum("hqk,khd->qhd", score_grad, key_heads, preferred_element_type=jnp.float32)
        * scaling
    )
    key_back = (
        jnp.einsum("hqk,qhd->khd", score_grad, query_heads, preferred_element_type=jnp.float32)
        * scaling
    )
    value_back = jnp.einsum(
        "hqk,qhd->khd",
        probability.astype(jnp.bfloat16),
        grad_heads,
        preferred_element_type=jnp.float32,
    )
    width = queries.shape[1]
    return (
        query_back.reshape(queries.shape[0], width),
        key_back.reshape(keys_all.shape[0], width),
        value_back.reshape(keys_all.shape[0], width),
    )


def per_device(
    tokens,
    memory,
    expert_slot,
    doc_lengths,
    source_lengths,
    cotangent,
    norm1_gain,
    norm1_shift,
    self_query,
    self_key,
    self_value,
    self_out,
    norm2_gain,
    norm2_shift,
    cross_query,
    cross_key,
    cross_value,
    cross_out,
    norm3_gain,
    norm3_shift,
    up_weight,
    up_bias,
    down_weight,
    down_bias,
):
    micro = tokens.shape[0]
    rows = tokens.shape[1]
    width = tokens.shape[2]
    source_rows = memory.shape[1]
    parts = lax.axis_size("dp")
    place = lax.axis_index("dp")
    experts_here = up_weight.shape[0]
    capacity = CAP
    head_count = HEADS
    local_places = place * rows + jnp.arange(rows, dtype=jnp.int32)
    stream_places = jnp.arange(rows * parts, dtype=jnp.int32)
    source_places = jnp.arange(source_rows * parts, dtype=jnp.int32)
    slot_ids = jnp.arange(experts_here * capacity, dtype=jnp.int32)
    expert_ids = jnp.arange(experts_here, dtype=jnp.int32)
    inputs = tokens.astype(jnp.float32)
    normed_first, first_back = jax.vjp(layer_norm, inputs, norm1_gain, norm1_shift)
    attn_in = normed_first.astype(jnp.bfloat16)
    queries = product(attn_in, self_query).astype(jnp.bfloat16)
    keys_mine = product(attn_in, self_key).astype(jnp.bfloat16)
    values_mine = product(attn_in, self_value).astype(jnp.bfloat16)
    keys_all, values_all = (
        lax.all_gather(keys_mine, "dp", axis=1, tiled=True),
        lax.all_gather(values_mine, "dp", axis=1, tiled=True),
    )
    cross_keys_all, cross_values_all = (
        lax.all_gather(product(memory, cross_key).astype(jnp.bfloat16), "dp", axis=1, tiled=True),
        lax.all_gather(product(memory, cross_value).astype(jnp.bfloat16), "dp", axis=1, tiled=True),
    )
    square_zero = jnp.zeros((width, width), jnp.float32)
    vector_zero = jnp.zeros((width,), jnp.float32)
    grad_self_query, grad_self_key, grad_self_value, grad_self_out = (
        square_zero,
        square_zero,
        square_zero,
        square_zero,
    )
    grad_cross_query, grad_cross_key, grad_cross_value, grad_cross_out = (
        square_zero,
        square_zero,
        square_zero,
        square_zero,
    )
    second_gain_sum, second_shift_sum, third_gain_sum, third_shift_sum = (
        vector_zero,
        vector_zero,
        vector_zero,
        vector_zero,
    )
    grad_up = jnp.zeros(up_weight.shape, jnp.float32)
    grad_up_bias = jnp.zeros(up_bias.shape, jnp.float32)
    grad_down = jnp.zeros(down_weight.shape, jnp.float32)
    grad_down_bias = jnp.zeros(down_bias.shape, jnp.float32)
    outputs = []
    attn_in_grads = []
    resid_grads = []
    for batch_index in range(micro):
        lengths_now = doc_lengths[batch_index, 0]
        query_docs = doc_index(lengths_now, local_places)
        stream_docs = doc_index(lengths_now, stream_places)
        source_docs = doc_index(source_lengths[batch_index, 0], source_places)
        self_allowed = (query_docs[:, None] == stream_docs[None, :]) & (
            stream_places[None, :] <= local_places[:, None]
        )
        cross_allowed = query_docs[:, None] == source_docs[None, :]
        self_result, self_log = attend_forward(
            queries[batch_index],
            keys_all[batch_index],
            values_all[batch_index],
            self_allowed,
            head_count,
        )
        self_mixed = self_result.astype(jnp.bfloat16)
        after_self = inputs[batch_index] + product(self_mixed, self_out)
        normed_second, second_back = jax.vjp(layer_norm, after_self, norm2_gain, norm2_shift)
        cross_in = normed_second.astype(jnp.bfloat16)
        cross_queries = product(cross_in, cross_query).astype(jnp.bfloat16)
        cross_result, cross_log = attend_forward(
            cross_queries,
            cross_keys_all[batch_index],
            cross_values_all[batch_index],
            cross_allowed,
            head_count,
        )
        cross_mixed = cross_result.astype(jnp.bfloat16)
        after_cross = after_self + product(cross_mixed, cross_out)
        normed_third, third_back = jax.vjp(layer_norm, after_cross, norm3_gain, norm3_shift)
        expert_in = normed_third.astype(jnp.bfloat16)
        chosen = expert_slot[batch_index, :, 0]
        one_hot = (chosen[:, None] == expert_ids[None, :]).astype(jnp.int32)
        ranks = jnp.sum((jnp.cumsum(one_hot, axis=0) - 1) * one_hot, axis=1)
        target = chosen * capacity + ranks
        dispatch = (slot_ids[:, None] == target[None, :]).astype(jnp.bfloat16)
        buffer_in = (
            product(dispatch, expert_in).astype(jnp.bfloat16).reshape(experts_here, capacity, width)
        )
        pre_act = (
            jnp.einsum("ecd,edf->ecf", buffer_in, up_weight, preferred_element_type=jnp.float32)
            + up_bias[:, None, :]
        )
        activated, gelu_back = jax.vjp(jax.nn.gelu, pre_act)
        hidden = activated.astype(jnp.bfloat16)
        buffer_out = (
            jnp.einsum("ecf,efd->ecd", hidden, down_weight, preferred_element_type=jnp.float32)
            + down_bias[:, None, :]
        )
        expert_out = jnp.take(buffer_out.reshape(experts_here * capacity, width), target, axis=0)
        outputs.append((after_cross + expert_out).astype(jnp.bfloat16))
        out_grad = cotangent[batch_index].astype(jnp.float32)
        grad_rows = out_grad.astype(jnp.bfloat16)
        buffer_grad = (
            product(dispatch, grad_rows).astype(jnp.bfloat16).reshape(experts_here, capacity, width)
        )
        grad_down = grad_down + jnp.einsum(
            "ecf,ecd->efd", hidden, buffer_grad, preferred_element_type=jnp.float32
        )
        grad_down_bias = grad_down_bias + jnp.sum(buffer_grad.astype(jnp.float32), axis=1)
        hidden_grad = jnp.einsum(
            "ecd,efd->ecf", buffer_grad, down_weight, preferred_element_type=jnp.float32
        )
        pre_grad = gelu_back(hidden_grad)[0].astype(jnp.bfloat16)
        grad_up = grad_up + jnp.einsum(
            "ecd,ecf->edf", buffer_in, pre_grad, preferred_element_type=jnp.float32
        )
        grad_up_bias = grad_up_bias + jnp.sum(pre_grad.astype(jnp.float32), axis=1)
        buffer_back = jnp.einsum(
            "ecf,edf->ecd", pre_grad, up_weight, preferred_element_type=jnp.float32
        )
        expert_in_grad = jnp.take(
            buffer_back.reshape(experts_here * capacity, width), target, axis=0
        )
        third_resid, third_gain, third_shift = third_back(expert_in_grad)
        third_gain_sum = third_gain_sum + third_gain
        third_shift_sum = third_shift_sum + third_shift
        cross_grad = out_grad + third_resid
        cross_rows_grad = cross_grad.astype(jnp.bfloat16)
        grad_cross_out = grad_cross_out + left_product(cross_mixed, cross_rows_grad)
        cross_mixed_grad = right_product(cross_rows_grad, cross_out).astype(jnp.bfloat16)
        cross_query_back, cross_key_back, cross_value_back = attend_backward(
            cross_queries,
            cross_keys_all[batch_index],
            cross_values_all[batch_index],
            cross_allowed,
            head_count,
            cross_log,
            cross_mixed_grad,
        )
        cross_query_low = cross_query_back.astype(jnp.bfloat16)
        grad_cross_query = grad_cross_query + left_product(cross_in, cross_query_low)
        cross_key_mine, cross_value_mine = (
            lax.psum_scatter(
                cross_key_back.astype(jnp.bfloat16), "dp", scatter_dimension=0, tiled=True
            ).astype(jnp.float32),
            lax.psum_scatter(
                cross_value_back.astype(jnp.bfloat16), "dp", scatter_dimension=0, tiled=True
            ).astype(jnp.float32),
        )
        source_exact = memory[batch_index].astype(jnp.float32)
        grad_cross_key = grad_cross_key + exact_left(source_exact, cross_key_mine)
        grad_cross_value = grad_cross_value + exact_left(source_exact, cross_value_mine)
        second_resid, second_gain, second_shift = second_back(
            right_product(cross_query_low, cross_query)
        )
        second_gain_sum = second_gain_sum + second_gain
        second_shift_sum = second_shift_sum + second_shift
        self_grad = cross_grad + second_resid
        self_rows_grad = self_grad.astype(jnp.bfloat16)
        grad_self_out = grad_self_out + left_product(self_mixed, self_rows_grad)
        self_mixed_grad = right_product(self_rows_grad, self_out).astype(jnp.bfloat16)
        self_query_back, self_key_back, self_value_back = attend_backward(
            queries[batch_index],
            keys_all[batch_index],
            values_all[batch_index],
            self_allowed,
            head_count,
            self_log,
            self_mixed_grad,
        )
        self_key_mine, self_value_mine = (
            lax.psum_scatter(
                self_key_back.astype(jnp.bfloat16), "dp", scatter_dimension=0, tiled=True
            ).astype(jnp.float32),
            lax.psum_scatter(
                self_value_back.astype(jnp.bfloat16), "dp", scatter_dimension=0, tiled=True
            ).astype(jnp.float32),
        )
        query_low = self_query_back.astype(jnp.bfloat16)
        key_low = self_key_mine.astype(jnp.bfloat16)
        value_low = self_value_mine.astype(jnp.bfloat16)
        grad_self_query = grad_self_query + left_product(attn_in[batch_index], query_low)
        grad_self_key = grad_self_key + left_product(attn_in[batch_index], key_low)
        grad_self_value = grad_self_value + left_product(attn_in[batch_index], value_low)
        attn_in_grads.append(
            right_product(query_low, self_query)
            + right_product(key_low, self_key)
            + right_product(value_low, self_value)
        )
        resid_grads.append(self_grad)
    first_resid, first_gain, first_shift = first_back(jnp.stack(attn_in_grads))
    token_grad = jnp.stack(resid_grads) + first_resid
    block_out = jnp.stack(outputs)
    up_share, up_bias_share, down_share, down_bias_share = (
        lax.psum_scatter(
            grad_up.astype(jnp.bfloat16), "dp", scatter_dimension=2, tiled=True
        ).astype(jnp.float32),
        lax.psum_scatter(
            grad_up_bias.astype(jnp.bfloat16), "dp", scatter_dimension=1, tiled=True
        ).astype(jnp.float32),
        lax.psum_scatter(
            grad_down.astype(jnp.bfloat16), "dp", scatter_dimension=1, tiled=True
        ).astype(jnp.float32),
        lax.psum_scatter(
            grad_down_bias.astype(jnp.bfloat16), "dp", scatter_dimension=1, tiled=True
        ).astype(jnp.float32),
    )
    up_total, up_bias_total, down_total, down_bias_total = (
        lax.all_gather(up_share.astype(jnp.bfloat16), "dp", axis=2, tiled=True).astype(
            up_share.dtype
        ),
        lax.all_gather(up_bias_share.astype(jnp.bfloat16), "dp", axis=1, tiled=True).astype(
            up_bias_share.dtype
        ),
        lax.all_gather(down_share.astype(jnp.bfloat16), "dp", axis=1, tiled=True).astype(
            down_share.dtype
        ),
        lax.all_gather(down_bias_share.astype(jnp.bfloat16), "dp", axis=1, tiled=True).astype(
            down_bias_share.dtype
        ),
    )
    shared = lax.psum(
        (
            first_gain,
            first_shift,
            grad_self_query,
            grad_self_key,
            grad_self_value,
            grad_self_out,
            second_gain_sum,
            second_shift_sum,
            grad_cross_query,
            grad_cross_key,
            grad_cross_value,
            grad_cross_out,
            third_gain_sum,
            third_shift_sum,
        ),
        ("grp", "dp"),
    )
    return (
        block_out,
        token_grad,
        shared[0],
        shared[1],
        shared[2],
        shared[3],
        shared[4],
        shared[5],
        shared[6],
        shared[7],
        shared[8],
        shared[9],
        shared[10],
        shared[11],
        shared[12],
        shared[13],
        up_total,
        up_bias_total,
        down_total,
        down_bias_total,
    )


MESH = pl.DeviceIdType.MESH
BF = jnp.bfloat16
F32 = jnp.float32
VMEM_BYTES = 56 * 1024 * 1024
HIDE = -1e30


def mm(left, right):
    return lax.dot_general(left, right, (((1,), (0,)), ((), ())), preferred_element_type=F32)


def mm_right(left, right):
    return lax.dot_general(left, right, (((1,), (1,)), ((), ())), preferred_element_type=F32)


def mm_left(left, right):
    return lax.dot_general(left, right, (((0,), (0,)), ((), ())), preferred_element_type=F32)


def norm_parts(inputs):
    mean_row = jnp.mean(inputs, axis=-1, keepdims=True)
    centred = inputs - mean_row
    spread = jnp.mean(centred * centred, axis=-1, keepdims=True)
    inverse = lax.rsqrt(spread + 1e-05)
    return centred * inverse, inverse


def norm_back(unit, inverse, gain, grad):
    scaled = grad * gain
    first = jnp.mean(scaled, axis=-1, keepdims=True)
    second = jnp.mean(scaled * unit, axis=-1, keepdims=True)
    return inverse * (scaled - first - unit * second)


def col_sum(values):
    return jnp.sum(values, axis=0, keepdims=True)


def three_parts(values):
    high = values.astype(BF).astype(F32)
    rest = values - high
    middle = rest.astype(BF).astype(F32)
    return high, middle, rest - middle


def doc_of(lengths_ref, batch, positions):
    total = jnp.int32(0)
    docs = jnp.zeros(positions.shape, jnp.int32)
    for j in range(lengths_ref.shape[2]):
        total = total + lengths_ref[batch, 0, j]
        docs = docs + (positions >= total).astype(jnp.int32)
    return docs


def lanes_of(shape, head):
    lane = lax.broadcasted_iota(jnp.int32, shape, 1)
    half = shape[1] // 2
    own = (lane < half) if head == 0 else (lane >= half)
    return own, (lane - half if head == 0 else lane)


def greet(grp, me, parts):
    barrier = pltpu.get_barrier_semaphore()
    for k in range(1, parts):
        pl.semaphore_signal(
            barrier, inc=1, device_id=(grp, lax.rem(me + k, parts)), device_id_type=MESH
        )
    pl.semaphore_wait(barrier, parts - 1)


def sender(grp, src, dst, ssem, rsem, target):
    return pltpu.make_async_remote_copy(
        src_ref=src,
        dst_ref=dst,
        send_sem=ssem,
        recv_sem=rsem,
        device_id=(grp, target),
        device_id_type=MESH,
    )


def partner_of(grp, me, axis):
    place = lax.div(me, 2)
    if axis == "core":
        return grp + 1 - 2 * lax.rem(grp, 2), me
    if axis == "x":
        return lax.rem(grp + 2, 4), me
    if axis == "y":
        return grp, me + 1 - 2 * lax.rem(me, 2)
    if axis == "near":
        return grp, me + 2 - 4 * lax.rem(place, 2)
    return grp, lax.rem(me + 4, 8)


def push(src, dst, ssem, rsem, device):
    return pltpu.make_async_remote_copy(
        src_ref=src, dst_ref=dst, send_sem=ssem, recv_sem=rsem, device_id=device, device_id_type=MESH
    )


def key_features(values, docs, head):
    own, place = lanes_of(values.shape, head)
    other = jnp.where(place == docs, 0.0, HIDE)
    other = jnp.where((place >= 4) & (place < 7), 1.0, other)
    return jnp.where(own, values.astype(F32), other).astype(BF)


def query_features(values, docs, head, scaling):
    own, place = lanes_of(values.shape, head)
    return jnp.where(
        own, values.astype(F32) * scaling, jnp.where(place == docs, 1.0, 0.0)
    ).astype(BF)


def value_features(values, head):
    own, _ = lanes_of(values.shape, head)
    return jnp.where(own, values.astype(F32), 1.0).astype(BF)


def forward_kernel(
    parts, pairs, rows, scaling,
    doc_len, src_len, tokens, memory, gain1, shift1, gain2, shift2,
    wq, wk, wv, wo, cq, ck, cv, co, cot, marks,
    a_all, m_all, x1_out, c_out, x2_out, o1_own, o2_own,
    qa1, ka1, va1, o1, qa2, ka2, va2, o2, gf_got, marks_got,
    a_own, st_q2, rv_q2,
    s_a, r_a, s_m, r_m, s_o1, r_o1, s_q2, r_q2, s_o2, r_o2, s_y, r_y,
):
    grp = lax.axis_index("grp")
    me = lax.axis_index("dp")
    batch = lax.div(me, pairs)
    pair = lax.rem(me, pairs)
    micro = tokens.shape[0]
    lanes = 128
    low_half = batch == 0
    half = lax.rem(me, 2)
    place = lax.div(me, 2)
    inner = (place == 1) | (place == 2)
    to_y = partner_of(grp, me, "y")
    to_near = partner_of(grp, me, "near")
    entry = jnp.where(low_half, 4, 2) + half
    far_end = jnp.where(low_half, 6, 0) + half

    def a2a(src, dst, ssem, rsem, target):
        return sender(grp, src.at[target], dst.at[me], ssem.at[target], rsem.at[me], target)

    def arrived(dst, ssem, rsem, source):
        sender(grp, dst.at[source], dst.at[source], ssem.at[source], rsem.at[source], source).wait_recv()

    greet(grp, me, parts)

    def first_norm(mb, _):
        unit, _inv = norm_parts(tokens[mb].astype(F32))
        a_own[mb] = (unit * gain1[...] + shift1[...]).astype(BF)
        return 0

    lax.fori_loop(0, micro, first_norm, 0)

    def source_of(i):
        return jnp.where(i == 0, me, jnp.where(i == 1, to_near[1], jnp.where(i == 2, entry, far_end)))

    def spread_first(own, out, ssem, rsem):
        there = (grp, entry)
        return [
            push(own.at[batch], out.at[me], ssem.at[4], rsem.at[me], to_near),
            push(own.at[1 - batch], out.at[me], ssem.at[5], rsem.at[me], there),
        ]

    def spread_y(out, ssem, rsem, i):
        j = source_of(i)
        return push(out.at[j], out.at[j], ssem.at[i], rsem.at[j], to_y)

    def spread_near(out, ssem, rsem, i):
        j = source_of(i)
        return push(out.at[j], out.at[j], ssem.at[4 + i], rsem.at[j], to_near)

    def spread_start(own, out, ssem, rsem):
        for copy in spread_first(own, out, ssem, rsem):
            copy.start()
        out[me] = own[batch]
        spread_y(out, ssem, rsem, 0).start()

    def spread_on(out, ssem, rsem, i):
        arrived(out, ssem, rsem, source_of(i))
        spread_y(out, ssem, rsem, i).start()

        @pl.when(inner & (i >= 2))
        def _():
            spread_near(out, ssem, rsem, i).start()

    def spread_done(own, out, ssem, rsem):
        for copy in spread_first(own, out, ssem, rsem):
            copy.wait_send()
        for i in range(4):
            spread_y(out, ssem, rsem, i).wait_send()

        @pl.when(inner)
        def _():
            for i in (2, 3):
                spread_near(out, ssem, rsem, i).wait_send()

    def y_of(i):
        return source_of(i) + 1 - 2 * half

    def build_self(j):
        r0 = pl.multiple_of(j * rows, rows)
        places = r0 + lax.broadcasted_iota(jnp.int32, (rows, lanes), 0)
        docs = doc_of(doc_len, batch, places)
        a = a_all[j]
        query, key, value = (mm(a, weight[...]).astype(BF) for weight in (wq, wk, wv))
        for h in range(2):
            qa1[h, pl.ds(r0, rows), :] = query_features(query, docs, h, scaling)
            ka1[h, pl.ds(r0, rows), :] = key_features(key, docs, h)
            va1[h, pl.ds(r0, rows), :] = value_features(value, h)

    spread_start(a_own, a_all, s_a, r_a)

    def same_y(i, _):
        @pl.when(i > 0)
        def _():
            spread_on(a_all, s_a, r_a, i)

        build_self(source_of(i))
        return 0

    def other_y(i, _):
        arrived(a_all, s_a, r_a, y_of(i))
        build_self(y_of(i))
        return 0

    lax.fori_loop(0, 4, same_y, 0)
    lax.fori_loop(0, 4, other_y, 0)
    spread_start(memory, m_all, s_m, r_m)

    def finish(qa, r0, h, query, top, acc):
        own, place = lanes_of((rows, lanes), h)
        total = pltpu.roll(acc, lanes // 2, 1)
        high, middle, low = three_parts(top + jnp.log(acc))
        query = query.astype(F32)
        query = jnp.where(~own & (place == 4), -high, query)
        query = jnp.where(~own & (place == 5), -middle, query)
        query = jnp.where(~own & (place == 6), -low, query)
        qa[h, pl.ds(r0, rows), :] = query.astype(BF)
        return acc / total

    def emit(t, heads, out, own_ref, ssem, rsem):
        own, _ = lanes_of((rows, lanes), 0)
        out[t] = jnp.where(own, heads[0], heads[1]).astype(BF)

        @pl.when(t != me)
        def _():
            sender(grp, out.at[t], own_ref.at[me], ssem.at[t], rsem.at[me], t).start()

        @pl.when(t == me)
        def _():
            own_ref[me] = out[t]

    for e in range(parts // 2):
        reach = 2 * rows * (e + 1)
        cut = reach - 2 * rows

        def self_block(i, _, reach=reach, cut=cut, e=e):
            t = 2 * e + i
            r0 = pl.multiple_of(t * rows, rows)
            row = r0 + lax.broadcasted_iota(jnp.int32, (rows, 2 * rows), 0)
            col = cut + lax.broadcasted_iota(jnp.int32, (rows, 2 * rows), 1)
            heads = []
            for h in range(2):
                query = qa1[h, pl.ds(r0, rows), :]
                near = mm_right(query, ka1[h, cut:reach, :])
                near = jnp.where(col <= row, near, HIDE)
                top = jnp.max(near, axis=1, keepdims=True)
                if cut:
                    far = mm_right(query, ka1[h, 0:cut, :])
                    top = jnp.maximum(top, jnp.max(far, axis=1, keepdims=True))
                acc = mm(jnp.exp(near - top).astype(BF), va1[h, cut:reach, :])
                if cut:
                    acc = acc + mm(jnp.exp(far - top).astype(BF), va1[h, 0:cut, :])
                heads.append(finish(qa1, r0, h, query, top, acc))
            emit(t, heads, o1, o1_own, s_o1, r_o1)
            return 0

        lax.fori_loop(0, 2, self_block, 0)
        if e == 2:
            spread_on(m_all, s_m, r_m, 1)

    def own_wait(own_ref, ssem, rsem):
        for k in range(1, parts):
            arrived(own_ref, ssem, rsem, lax.rem(me + k, parts))

    spread_on(m_all, s_m, r_m, 2)
    spread_on(m_all, s_m, r_m, 3)
    own_wait(o1_own, s_o1, r_o1)

    def second_norm(mb, _):
        mixed = jnp.concatenate([o1_own[mb * pairs + p] for p in range(pairs)], axis=1)
        x1 = tokens[mb].astype(F32) + mm(mixed, wo[...])
        x1_out[mb] = x1
        unit, _inv = norm_parts(x1)
        c = (unit * gain2[...] + shift2[...]).astype(BF)
        c_out[mb] = c
        got = mm(c, cq[...]).astype(BF)
        for p in range(pairs):
            st_q2[mb * pairs + p] = got[:, p * lanes : (p + 1) * lanes]

        def send(p, _):
            target = mb * pairs + p

            @pl.when(target != me)
            def _():
                a2a(st_q2, rv_q2, s_q2, r_q2, target).start()

            @pl.when(target == me)
            def _():
                rv_q2[me] = st_q2[me]

            return 0

        lax.fori_loop(0, pairs, send, 0)
        return 0

    lax.fori_loop(0, micro, second_norm, 0)

    def build_cross(i, _):
        j = jnp.where(i < 4, source_of(i), y_of(i - 4))

        @pl.when(i >= 4)
        def _():
            arrived(m_all, s_m, r_m, j)

        r0 = pl.multiple_of(j * rows, rows)
        places = r0 + lax.broadcasted_iota(jnp.int32, (rows, lanes), 0)
        docs = doc_of(src_len, batch, places)
        source = m_all[j]
        key, value = (mm(source, weight[...]).astype(BF) for weight in (ck, cv))
        for h in range(2):
            ka2[h, pl.ds(r0, rows), :] = key_features(key, docs, h)
            va2[h, pl.ds(r0, rows), :] = value_features(value, h)
        return 0

    lax.fori_loop(0, parts, build_cross, 0)

    swaps = [
        push(cot, gf_got, s_y.at[0], r_y.at[0], to_y),
        push(marks, marks_got, s_y.at[1], r_y.at[1], to_y),
    ]
    for swap in swaps:
        swap.start()

    def cross_block(k, _):
        t = lax.rem(me + k, parts)

        @pl.when(k > 0)
        def _():
            arrived(rv_q2, s_q2, r_q2, t)

        r0 = pl.multiple_of(t * rows, rows)
        places = r0 + lax.broadcasted_iota(jnp.int32, (rows, lanes), 0)
        docs = doc_of(doc_len, batch, places)
        heads = []
        for h in range(2):
            query = query_features(rv_q2[t], docs, h, scaling)
            scores = mm_right(query, ka2[h])
            top = jnp.max(scores, axis=1, keepdims=True)
            acc = mm(jnp.exp(scores - top).astype(BF), va2[h])
            heads.append(finish(qa2, r0, h, query, top, acc))
        emit(t, heads, o2, o2_own, s_o2, r_o2)
        return 0

    lax.fori_loop(0, parts, cross_block, 0)
    own_wait(o2_own, s_o2, r_o2)

    def third(mb, _):
        mixed = jnp.concatenate([o2_own[mb * pairs + p] for p in range(pairs)], axis=1)
        x2_out[mb] = x1_out[mb] + mm(mixed, co[...])
        return 0

    lax.fori_loop(0, micro, third, 0)

    for k in range(1, parts):
        target = lax.rem(me + k, parts)
        a2a(st_q2, rv_q2, s_q2, r_q2, target).wait_send()
        a2a(o1, o1_own, s_o1, r_o1, target).wait_send()
        a2a(o2, o2_own, s_o2, r_o2, target).wait_send()
    for swap in swaps:
        swap.wait()
    spread_done(a_own, a_all, s_a, r_a)
    spread_done(memory, m_all, s_m, r_m)


def gelu_both(z):
    root = math.sqrt(2.0 / math.pi)
    square = z * z
    bent = jnp.tanh(root * z * (1.0 + 0.044715 * square))
    half = 0.5 * (1.0 + bent)
    slope = half + 0.5 * z * (1.0 - bent * bent) * (root * (1.0 + 3 * 0.044715 * square))
    return z * half, slope


def expert_kernel(
    pairs, tiles,
    x2, o2_own, marks, marks_got, cot, gf_got, gain3, shift3, up_hbm, up_b, down_hbm, down_b, co,
    block_out, gx2_out, do2, g_co, vec, shares,
    up, down, e_all, act, du_all, de_acc, de_low, de_got, y_low, y_got,
    load_sem, ssem, rsem,
):
    grp = lax.axis_index("grp")
    me = lax.axis_index("dp")
    half = lax.rem(me, 2)
    other = partner_of(grp, me, "y")
    micro, rows, width = x2.shape
    lanes = 128
    count = micro * rows
    depth = up.shape[2] // tiles
    span = up.shape[2]

    barrier = pltpu.get_barrier_semaphore()
    pl.semaphore_signal(barrier, inc=1, device_id=other, device_id_type=MESH)
    first_col = pl.multiple_of(half * span, span)
    loads = [
        pltpu.make_async_copy(up_hbm.at[:, :, pl.ds(first_col, span)], up, load_sem.at[0]),
        pltpu.make_async_copy(down_hbm.at[:, pl.ds(first_col, span), :], down, load_sem.at[1]),
    ]
    for load in loads:
        load.start()
    mark_all = (marks, marks_got)
    gf_all = tuple(
        jnp.concatenate([ref[mb] for mb in range(micro)], axis=0) for ref in (cot, gf_got)
    )
    for mb in range(micro):
        part = slice(mb * rows, (mb + 1) * rows)
        unit, _inv = norm_parts(x2[mb])
        e_all[0, part, :] = (unit * gain3[...] + shift3[...]).astype(BF)
    pl.semaphore_wait(barrier, 1)
    swaps = [
        push(src, dst, ssem.at[n], rsem.at[n], other)
        for n, (src, dst) in enumerate(
            (
                (e_all.at[0], e_all.at[1]),
                (de_low, de_got),
                (y_low, y_got),
            )
        )
    ]
    swaps[0].start()
    for load in loads:
        load.wait()

    def ones_of(rowset, wide):
        return jnp.concatenate([mark_all[rowset][...]] * (wide // lanes), axis=1) > 0.5

    def split(values, is_one):
        zero = jnp.zeros_like(values)
        return jnp.where(is_one, zero, values), jnp.where(is_one, values, zero)

    def through(rowset):
        de_acc[...] = jnp.zeros_like(de_acc)

        def tile(f, _):
            cols = pl.ds(pl.multiple_of(f * depth, depth), depth)
            bias_cols = pl.ds(pl.multiple_of(first_col + f * depth, depth), depth)
            is_one = ones_of(rowset, depth)
            e = e_all[rowset]
            gf = gf_all[rowset]
            u = jnp.where(
                is_one,
                mm(e, up[1, :, cols]) + up_b[1:2, bias_cols],
                mm(e, up[0, :, cols]) + up_b[0:1, bias_cols],
            )
            hidden, slope = gelu_both(u)
            act[rowset, f] = hidden.astype(BF)
            back = jnp.where(is_one, mm_right(gf, down[1, cols, :]), mm_right(gf, down[0, cols, :]))
            du = (back * slope).astype(BF)
            du_all[rowset, f] = du
            none, one = split(du, is_one)
            de_acc[...] += mm_right(none, up[0, :, cols]) + mm_right(one, up[1, :, cols])
            return 0

        lax.fori_loop(0, tiles, tile, 0)

    def branch(rowset):
        is_one = ones_of(rowset, depth)

        def tile(f, total):
            cols = pl.ds(pl.multiple_of(f * depth, depth), depth)
            none, one = split(act[rowset, f], is_one)
            return total + mm(none, down[0, cols, :]) + mm(one, down[1, cols, :])

        return lax.fori_loop(0, tiles, tile, jnp.zeros((count, width), F32))

    vec[...] = jnp.zeros_like(vec)
    through(0)
    de_mine = de_acc[...]
    swaps[0].wait()
    through(1)
    de_low[...] = de_acc[...].astype(BF)
    swaps[1].start()
    de_acc[...] = de_mine
    y_low[...] = branch(1).astype(BF)
    swaps[2].start()

    for n in range(2):
        def weights(f, _, n=n):
            up_sum = jnp.zeros((width, depth), F32)
            down_sum = jnp.zeros((depth, width), F32)
            bias = jnp.zeros((1, depth), F32)
            for rowset in range(2):
                is_one = ones_of(rowset, depth)
                du_n = split(du_all[rowset, f], is_one)[n]
                act_n = split(act[rowset, f], is_one)[n]
                up_sum = up_sum + mm_left(e_all[rowset], du_n)
                down_sum = down_sum + mm_left(act_n, gf_all[rowset])
                bias = bias + col_sum(du_n.astype(F32))
            strip = depth // 2
            for m in range(4):
                part = slice(m * strip, (m + 1) * strip)
                shares[4 * n + m, f] = up_sum[part, :].astype(BF)
                shares[8 + 4 * n + m, f] = down_sum[
                    (m % 2) * strip : (m % 2 + 1) * strip, (m // 2) * depth : (m // 2 + 1) * depth
                ].astype(BF)
            row = 8 + n * 4 + half * 2 + lax.div(f, 2)
            col = pl.ds(pl.multiple_of(lax.rem(f, 2) * depth, depth), depth)
            vec[pl.ds(row, 1), col] = bias
            return 0

        lax.fori_loop(0, tiles, weights, 0)

    all_grad = gf_all[0].astype(F32)
    none, one = split(all_grad, ones_of(0, width))
    vec[6:7, :] = col_sum(none)
    vec[7:8, :] = col_sum(one)

    swaps[1].wait()
    cross = jnp.zeros((width, width), F32)
    for mb in range(micro):
        part = slice(mb * rows, (mb + 1) * rows)
        unit, inverse = norm_parts(x2[mb])
        grad = de_acc[part, :] + de_got[part, :].astype(F32)
        vec[4:5, :] += col_sum(grad * unit)
        vec[5:6, :] += col_sum(grad)
        gx2 = cot[mb].astype(F32) + norm_back(unit, inverse, gain3[...], grad)
        gx2_out[mb] = gx2
        gy2 = gx2.astype(BF)
        back = mm_right(gy2, co[...]).astype(BF)
        for p in range(pairs):
            do2[mb * pairs + p] = back[:, p * lanes : (p + 1) * lanes]
        mixed = jnp.concatenate([o2_own[mb * pairs + p] for p in range(pairs)], axis=1)
        cross = cross + mm_left(mixed, gy2)
    g_co[...] = cross.astype(BF)

    own_branch = branch(0) + jnp.where(ones_of(0, width), down_b[1:2, :], down_b[0:1, :])
    swaps[2].wait()
    for mb in range(micro):
        part = slice(mb * rows, (mb + 1) * rows)
        block_out[mb] = (x2[mb] + own_branch[part, :] + y_got[part, :].astype(F32)).astype(BF)


def backward_kernel(
    parts, pairs, rows, scaling,
    gx2, do2_st, qa1_in, ka1_in, va1_in, o1, qa2_in, ka2_in, va2_in, o2,
    tokens, x1, c_in, a_in, m_in, o1_own, gain1, gain2,
    wq, wk, wv, wo, cq, g_co, vec_in, shares_in,
    token_grad, vec_out, all_shares, all_early, all_cross, all_late,
    rv_do2, st_dq2, rv_dq2, st_do1, rv_do1, doa, dq_acc, dk_acc, dv_acc, gx1_ref, low_grad,
    qa, ka, va, stream, da_keep, st_y, got_y, st_near, got_near, st_far, got_far, da_sum,
    shares, got_one, got_two, early, cross, late, *rest
):
    got_early, got_cross, got_late, rest = rest[:5], rest[5:8], rest[8:11], rest[11:]
    vec, got_vec, g_cq, g_so, g_cross, g_late, rest = *rest[:6], rest[6:]
    hop_s, hop_r, piece_r, local_sem, load_sem, rest = *rest[:5], rest[5:]
    early_s, early_r, cross_s, cross_r, late_s, late_r, vec_s, vec_r, rest = *rest[:8], rest[8:]
    da_s, da_r, s_do2, r_do2, s_dq2, r_dq2, s_do1, r_do1 = rest
    grp = lax.axis_index("grp")
    me = lax.axis_index("dp")
    micro = tokens.shape[0]
    width = tokens.shape[2]
    lanes = 128
    length = parts * rows

    def a2a(src, dst, ssem, rsem, target):
        return sender(grp, src.at[target], dst.at[me], ssem.at[target], rsem.at[me], target)

    def arrived(dst, ssem, rsem, source):
        sender(grp, dst.at[source], dst.at[source], ssem.at[source], rsem.at[source], source).wait_recv()

    half = lax.rem(me, 2)
    near_bit = lax.rem(lax.div(me, 2), 2)
    far_bit = lax.div(me, 4)
    axes = ("core", "x", "y", "near", "far")
    place = lax.div(me, 2)
    batch = far_bit
    pair = lax.rem(me, pairs)
    inner = (place == 1) | (place == 2)
    bits = (lax.rem(grp, 2), lax.div(grp, 2), half, near_bit, far_bit)
    partners = [partner_of(grp, me, axis) for axis in axes]
    barrier = pltpu.get_barrier_semaphore()
    for k in range(1, parts):
        pl.semaphore_signal(
            barrier, inc=1, device_id=(grp, lax.rem(me + k, parts)), device_id_type=MESH
        )
    for d in range(2):
        pl.semaphore_signal(barrier, inc=1, device_id=partners[d], device_id_type=MESH)
    pl.semaphore_wait(barrier, parts + 1)

    pieces = shares_in.shape[0]
    to_y, to_near, to_far = partners[2:]
    to_mid = (grp, (3 - place) * 2 + half)
    at_end = jnp.where(far_bit == 0, 0, 3)
    at_inner = jnp.where(far_bit == 0, 1, 2)
    at_next = 3 - at_inner
    at_last = 3 - at_end
    three = pl.ds(jnp.where(far_bit == 0, 1, 0), 3)
    away = pl.ds(jnp.where(far_bit == 0, 2, 0), 2)
    home = pl.ds(jnp.where(far_bit == 0, 0, 2), 2)

    def hop(s, n):
        rsem = hop_r.at[s, n]
        if n == 0:
            return push(shares.at[s, three], got_one.at[s], hop_s.at[s, 0], rsem, to_near)
        if n == 1:
            return push(shares.at[s, away], got_two.at[s], hop_s.at[s, 0], rsem, to_mid)
        if n == 2:
            return push(shares.at[s, at_end], got_two.at[s, 0], hop_s.at[s, 1], rsem, to_near)
        return push(all_shares.at[half, s], all_shares.at[half, s], hop_s.at[s, 7], rsem, to_y)

    def piece_first(s, n, piece, device):
        return push(
            shares.at[s, piece], all_shares.at[half, s, piece], hop_s.at[s, n], piece_r.at[s, piece], device
        )

    def piece_on(s, n, piece, device):
        ref = all_shares.at[half, s, piece]
        return push(ref, ref, hop_s.at[s, n], piece_r.at[s, piece], device)

    def piece_wait(s, piece):
        piece_on(s, 4, piece, to_near).wait_recv()

    def share_local(s):
        own = jnp.where(inner, at_inner, at_end)
        return pltpu.make_async_copy(shares.at[s, own], all_shares.at[half, s, own], local_sem.at[s])

    def share_load(s):
        return pltpu.make_async_copy(shares_in.at[s], shares.at[s], load_sem.at[s])

    def add_to(ref, s, piece, more):
        ref[s, piece] = (ref[s, piece].astype(F32) + more.astype(F32)).astype(BF)

    def share_step(s, stage):
        if stage == 0:
            share_load(s).wait()

            @pl.when(~inner)
            def _():
                hop(s, 0).start()

        if stage == 1:

            @pl.when(inner)
            def _():
                hop(s, 0).wait_recv()
                for n in range(3):
                    add_to(shares, s, jnp.where(far_bit == 0, 1, 0) + n, got_one[s, n])
                hop(s, 1).start()

        if stage == 2:

            @pl.when(inner)
            def _():
                hop(s, 1).wait_recv()
                for n in range(2):
                    add_to(shares, s, jnp.where(far_bit == 0, 0, 2) + n, got_two[s, n])
                hop(s, 2).start()
                piece_first(s, 3, at_inner, to_mid).start()
                piece_first(s, 2, at_inner, to_near).start()
                share_local(s).start()

        if stage == 3:

            @pl.when(~inner)
            def _():
                hop(s, 2).wait_recv()
                add_to(shares, s, at_end, got_two[s, 0])
                piece_first(s, 1, at_end, to_near).start()
                share_local(s).start()

            @pl.when(inner)
            def _():
                piece_wait(s, at_next)
                piece_on(s, 4, at_next, to_near).start()

        if stage == 4:

            @pl.when(inner)
            def _():
                piece_wait(s, at_end)
                piece_on(s, 5, at_end, to_mid).start()

        if stage == 5:

            @pl.when(inner)
            def _():
                piece_wait(s, at_last)
                piece_on(s, 6, at_last, to_near).start()

        if stage == 6:

            @pl.when(~inner)
            def _():
                piece_wait(s, at_inner)
                piece_wait(s, at_next)
                piece_wait(s, at_last)

            share_local(s).wait()
            hop(s, 3).start()

    def share_sent(s):
        hop(s, 2).wait_send()
        hop(s, 3).wait_send()

        @pl.when(~inner)
        def _():
            hop(s, 0).wait_send()

        @pl.when(inner)
        def _():
            hop(s, 1).wait_send()
            piece_first(s, 3, at_inner, to_mid).wait_send()
            piece_first(s, 2, at_inner, to_near).wait_send()
            piece_on(s, 4, at_next, to_near).wait_send()
            piece_on(s, 5, at_end, to_mid).wait_send()
            piece_on(s, 6, at_last, to_near).wait_send()

    def load_three(refs, n):
        return [
            pltpu.make_async_copy(src, dst, load_sem.at[pieces + 3 * n + m])
            for m, (src, dst) in enumerate(zip(refs, (qa, ka, va)))
        ]

    def tick(i):
        for stage in (0, 6, 1, 2, 3, 4, 5):
            s = i - stage
            if isinstance(s, int):
                if 0 <= s < pieces:
                    share_step(s, stage)
            else:

                @pl.when((s >= 0) & (s < pieces))
                def _(s=s, stage=stage):
                    share_step(s, stage)

    def offset_of(total, upto):
        place = jnp.int32(0)
        for d in range(upto):
            place = place + bits[d] * (total >> (d + 1))
        return place

    def rows_at(total, start, size):
        unit = total >> 5
        return pl.ds(pl.multiple_of(start, unit), size)

    def sum_copy(own, out, got, ssem, rsem, stage):
        total = own.shape[0]
        if stage < 5:
            size = total >> (stage + 1)
            start = offset_of(total, stage) + (1 - bits[stage]) * size
            return push(
                own.at[rows_at(total, start, size)], got[stage], ssem.at[stage], rsem.at[stage],
                partners[stage],
            )
        d = 9 - stage
        size = total >> (d + 1)
        part = rows_at(total, offset_of(total, d + 1), size)
        src = own if stage == 5 else out
        return push(src.at[part], out.at[part], ssem.at[stage], rsem.at[stage], partners[d])

    def sum_local(own, out, sem):
        total = own.shape[0]
        part = rows_at(total, offset_of(total, 5), total >> 5)
        return pltpu.make_async_copy(own.at[part], out.at[part], sem)

    def sum_step(own, out, got, ssem, rsem, sem, stage):
        total = own.shape[0]
        if 1 <= stage <= 5:
            sum_copy(own, out, got, ssem, rsem, stage - 1).wait_recv()
            size = total >> stage
            part = rows_at(total, offset_of(total, stage), size)
            own[part, :] = (own[part, :].astype(F32) + got[stage - 1][...].astype(F32)).astype(BF)
        if stage == 5:
            sum_local(own, out, sem).start()
        if stage == 6:
            sum_local(own, out, sem).wait()
        if stage >= 6:
            sum_copy(own, out, got, ssem, rsem, stage - 1).wait_recv()
        if stage < 10:
            sum_copy(own, out, got, ssem, rsem, stage).start()

    def early_step(stage):
        sum_step(early, all_early, got_early, early_s, early_r, local_sem.at[pieces], stage)

    slice_axes = (0, 1, 4)

    def slice_rows(total, upto):
        start = jnp.int32(0)
        for d in range(upto):
            start = start + bits[slice_axes[d]] * (total >> (d + 1))
        return pl.ds(pl.multiple_of(start, total >> 3), total >> upto)

    def slice_copy(own, out, got, ssem, rsem, stage):
        total = own.shape[0]
        sems = (ssem.at[stage], rsem.at[stage])
        if stage < 3:
            axis = slice_axes[stage]
            size = total >> (stage + 1)
            start = jnp.int32(0)
            for d in range(stage):
                start = start + bits[slice_axes[d]] * (total >> (d + 1))
            start = start + (1 - bits[axis]) * size
            part = pl.ds(pl.multiple_of(start, total >> 3), size)
            return push(own.at[part], got[stage], *sems, partners[axis])
        if stage == 3:
            part = slice_rows(total, 3)
            return push(own.at[part], out.at[pair, part], *sems, to_y)
        if stage == 4:
            ref = out.at[pl.ds(near_bit * 2, 2), slice_rows(total, 3)]
            return push(ref, ref, *sems, to_near)
        ref = out.at[:, slice_rows(total, 8 - stage)]
        return push(ref, ref, *sems, partners[slice_axes[7 - stage]])

    def slice_local(own, out, sem):
        part = slice_rows(own.shape[0], 3)
        return pltpu.make_async_copy(own.at[part], out.at[pair, part], sem)

    def slice_step(own, out, got, ssem, rsem, sem, stage):
        total = own.shape[0]
        if stage >= 1:
            slice_copy(own, out, got, ssem, rsem, stage - 1).wait_recv()
        if 1 <= stage <= 3:
            part = slice_rows(total, stage)
            own[part, :] = (own[part, :].astype(F32) + got[stage - 1][...].astype(F32)).astype(BF)
        if stage == 3:
            slice_local(own, out, sem).start()
        if stage == 4:
            slice_local(own, out, sem).wait()
        if stage < 8:
            slice_copy(own, out, got, ssem, rsem, stage).start()

    def cross_step(stage):
        slice_step(cross, all_cross, got_cross, cross_s, cross_r, local_sem.at[pieces + 1], stage)

    def vec_copy(d):
        return push(vec.at[d], got_vec.at[d], vec_s.at[d], vec_r.at[d], partners[d])

    def vec_step(stage):
        if 1 <= stage <= 5:
            d = stage - 1
            vec_copy(d).wait_recv()
            row = lax.broadcasted_iota(jnp.int32, vec.shape[1:], 0)
            added = got_vec[d] if d >= 2 else jnp.where(row < 6, got_vec[d], 0.0)
            vec[d + 1] = vec[d] + added
        if stage < 5:
            vec_copy(stage).start()

    for k in range(1, parts):
        a2a(do2_st, rv_do2, s_do2, r_do2, lax.rem(me + k, parts)).start()
    rv_do2[me] = do2_st[me]
    loads = load_three((qa2_in, ka2_in, va2_in), 0)
    for load in loads:
        load.start()
    streams = [
        pltpu.make_async_copy(src, stream, load_sem.at[pieces + 6 + n]) for n, src in enumerate((m_in, a_in))
    ]
    streams[0].start()
    columns = pl.ds(pl.multiple_of(pair * lanes, lanes), lanes)
    for s in range(pieces):
        share_load(s).start()
    tick(0)

    def clear(s, _):
        part = pl.ds(pl.multiple_of(s * rows, rows), rows)
        for h in range(2):
            dk_acc[h, part, :] = jnp.zeros((rows, lanes), F32)
            dv_acc[h, part, :] = jnp.zeros((rows, lanes), F32)
            dq_acc[h, part, :] = jnp.zeros((rows, lanes), F32)
        return 0

    def grad_features(grads, mixed, head):
        own, place = lanes_of(grads.shape, head)
        grads = grads.astype(F32)
        delta = jnp.sum(jnp.where(own, grads * mixed.astype(F32), 0.0), axis=1, keepdims=True)
        high, middle, low = three_parts(delta)
        other = jnp.where(place == 0, -high, 0.0)
        other = jnp.where(place == 1, -middle, other)
        other = jnp.where(place == 2, -low, other)
        return jnp.where(own, grads, other).astype(BF)

    def tile(query, grads, keys, values, mask):
        scores = mm_right(keys, query)
        if mask is not None:
            scores = jnp.where(mask, scores, HIDE)
        prob = jnp.exp(scores)
        back = mm_right(values, grads)
        score_grad = (prob * back).astype(BF)
        return (
            mm_left(score_grad, keys),
            mm(score_grad, query),
            mm(prob.astype(BF), grads),
        )

    def join(zero_head, one_head):
        own, _ = lanes_of(zero_head.shape, 0)
        return jnp.where(own, zero_head, one_head)

    lax.fori_loop(0, parts, clear, 0)

    chunk = 2 * rows
    for load in loads:
        load.wait()

    def cross_block(k, _):
        t = lax.rem(me + k, parts)

        @pl.when(k > 0)
        def _():
            arrived(rv_do2, s_do2, r_do2, t)

        part = pl.ds(pl.multiple_of(t * rows, rows), rows)
        grads = [grad_features(rv_do2[t], o2[t], h) for h in range(2)]
        queries = [qa[h, part, :] for h in range(2)]
        sums = [jnp.zeros((rows, lanes), F32)] * 2
        for n in range(length // chunk):
            keys = slice(n * chunk, (n + 1) * chunk)
            for h in range(2):
                dq, dk, dv = tile(queries[h], grads[h], ka[h, keys, :], va[h, keys, :], None)
                sums[h] = sums[h] + dq
                dk_acc[h, keys, :] += dk
                dv_acc[h, keys, :] += dv
        st_dq2[t] = (join(sums[0], sums[1]) * scaling).astype(BF)

        @pl.when(k > 0)
        def _():
            a2a(st_dq2, rv_dq2, s_dq2, r_dq2, t).start()

        @pl.when(k == 0)
        def _():
            rv_dq2[me] = st_dq2[me]

        tick(k + 1)
        return 0

    lax.fori_loop(0, parts, cross_block, 0)

    loads = load_three((qa1_in, ka1_in, va1_in), 1)
    for load in loads:
        load.start()

    def cross_source(s, total):
        part = pl.ds(pl.multiple_of(s * rows, rows), rows)
        grads = jnp.concatenate(
            [join(dk_acc[0, part, :], dk_acc[1, part, :]), join(dv_acc[0, part, :], dv_acc[1, part, :])], axis=1
        )
        return total + mm_left(stream[s], grads.astype(BF))

    for k in range(1, parts):
        arrived(rv_dq2, s_dq2, r_dq2, lax.rem(me + k, parts))

    def gathered(ref, mb, first):
        return jnp.concatenate(
            [ref[mb * pairs + p, first * rows : (first + 1) * rows, :] for p in range(pairs)], axis=1
        )

    vec[0] = vec_in[...]

    def second_back(mb, _):
        dq2 = gathered(rv_dq2, mb, 0)
        dc = mm_right(dq2, cq[...])
        unit, inverse = norm_parts(x1[mb])
        vec[0, 2:3, :] += col_sum(dc * unit)
        vec[0, 3:4, :] += col_sum(dc)
        gx1 = gx2[mb] + norm_back(unit, inverse, gain2[...], dc)
        gx1_ref[mb] = gx1
        low_grad[mb] = gx1.astype(BF)
        back = mm_right(low_grad[mb], wo[...]).astype(BF)
        for p in range(pairs):
            st_do1[mb * pairs + p] = back[:, p * lanes : (p + 1) * lanes]

        def send(p, _):
            target = mb * pairs + p

            @pl.when(target != me)
            def _():
                a2a(st_do1, rv_do1, s_do1, r_do1, target).start()

            @pl.when(target == me)
            def _():
                rv_do1[me] = st_do1[me]

            return 0

        lax.fori_loop(0, pairs, send, 0)
        return 0

    lax.fori_loop(0, micro, second_back, 0)
    tick(9)
    streams[0].wait()
    g_cross[...] = lax.fori_loop(0, parts, cross_source, jnp.zeros(g_cross.shape, F32))
    streams[1].start()
    for n in range(2):
        cross[n * width : (n + 1) * width, :] = g_cross[:, n * lanes : (n + 1) * lanes].astype(BF)

    g_cq[...] = jnp.zeros_like(g_cq)
    g_so[...] = jnp.zeros_like(g_so)

    def cross_weights(mb, _):
        g_cq[...] += mm_left(c_in[mb], gathered(rv_dq2, mb, 0))
        mixed = jnp.concatenate([o1_own[mb * pairs + p] for p in range(pairs)], axis=1)
        g_so[...] += mm_left(mixed, low_grad[mb])
        return 0

    lax.fori_loop(0, micro, cross_weights, 0)
    early[0:width, :] = g_co[...]
    early[width : 2 * width, :] = g_cq[...].astype(BF)
    early[2 * width : 3 * width, :] = g_so[...].astype(BF)
    early_step(0)
    cross_step(0)
    tick(10)
    for load in loads:
        load.wait()

    tick(11)
    for k in range(1, parts):
        arrived(rv_do1, s_do1, r_do1, lax.rem(me + k, parts))

    lax.fori_loop(0, parts, clear, 0)

    def build(s, _):
        part = pl.ds(pl.multiple_of(s * rows, rows), rows)
        for h in range(2):
            doa[h, part, :] = grad_features(rv_do1[s], o1[s], h)
        return 0

    lax.fori_loop(0, parts, build, 0)

    def self_tile(i, j, mask):
        q_part = pl.ds(pl.multiple_of(i * chunk, chunk), chunk)
        k_part = pl.ds(pl.multiple_of(j * chunk, chunk), chunk)
        for h in range(2):
            dq, dk, dv = tile(
                qa[h, q_part, :], doa[h, q_part, :], ka[h, k_part, :], va[h, k_part, :], mask
            )
            dq_acc[h, q_part, :] += dq
            dk_acc[h, k_part, :] += dk
            dv_acc[h, k_part, :] += dv

    g_late[...] = jnp.zeros_like(g_late)
    streams[1].wait()

    def y_copy(j):
        return push(st_y.at[j], got_y.at[j], da_s.at[j], da_r.at[j], to_y)

    def near_copy(n):
        return push(st_near.at[n], got_near.at[n], da_s.at[4 + n], da_r.at[4 + n], to_near)

    def far_copy():
        return push(st_far, got_far, da_s.at[6], da_r.at[6], to_far)

    def near_step(j):
        y_copy(j).wait_recv()
        da_keep[j] = da_keep[j] + got_y[j].astype(F32)

        @pl.when(lax.rem(j, 2) != near_bit)
        def _():
            st_near[lax.div(j, 2)] = da_keep[j].astype(BF)
            near_copy(lax.div(j, 2)).start()

    def far_step(j):
        @pl.when(lax.rem(j, 2) == near_bit)
        def _():
            near_copy(lax.div(j, 2)).wait_recv()
            total = da_keep[j] + got_near[lax.div(j, 2)].astype(F32)

            @pl.when(j == place)
            def _():
                da_sum[batch] = total

            @pl.when(j != place)
            def _():
                st_far[...] = total.astype(BF)
                far_copy().start()

    def self_column(j, _):
        key_place = lax.broadcasted_iota(jnp.int32, (chunk, chunk), 0)
        query_place = lax.broadcasted_iota(jnp.int32, (chunk, chunk), 1)
        self_tile(j, j, key_place <= query_place)

        def below(i, _):
            self_tile(i, j, None)
            return 0

        lax.fori_loop(j + 1, length // chunk, below, 0)

        part = pl.ds(pl.multiple_of(j * chunk, chunk), chunk)
        grads = jnp.concatenate(
            [
                (join(acc[0, part, :], acc[1, part, :]) * factor).astype(BF)
                for acc, factor in ((dq_acc, scaling), (dk_acc, 1.0), (dv_acc, 1.0))
            ],
            axis=1,
        )
        da = (
            mm_right(grads[:, 0:lanes], wq[...])
            + mm_right(grads[:, lanes : 2 * lanes], wk[...])
            + mm_right(grads[:, 2 * lanes : 3 * lanes], wv[...])
        )
        odd = half == 1
        st_y[j] = jnp.where(odd, da[0:rows], da[rows : 2 * rows]).astype(BF)
        da_keep[j] = jnp.where(odd, da[rows : 2 * rows], da[0:rows])
        y_copy(j).start()
        for n in range(chunk // rows):
            g_late[...] += mm_left(stream[j * (chunk // rows) + n], grads[n * rows : (n + 1) * rows])
        tick(12 + j)

        @pl.when(j >= 1)
        def _():
            near_step(j - 1)

        @pl.when(j >= 2)
        def _():
            far_step(j - 2)

        @pl.when(j == 1)
        def _():
            early_step(1)
            cross_step(1)

        @pl.when(j == 2)
        def _():
            early_step(2)
            cross_step(2)

        @pl.when(j == 3)
        def _():
            early_step(3)
            cross_step(3)

        return 0

    lax.fori_loop(0, length // chunk, self_column, 0)
    for n in range(3):
        late[n * width : (n + 1) * width, :] = g_late[:, n * lanes : (n + 1) * lanes].astype(BF)
    near_step(3)
    late_slice = functools.partial(
        slice_step, late, all_late, got_late, late_s, late_r, local_sem.at[pieces + 2]
    )
    late_slice(0)
    tick(16)
    early_step(4)
    cross_step(4)
    far_step(2)
    late_slice(1)
    tick(17)
    far_step(3)
    late_slice(2)
    early_step(5)
    cross_step(5)
    tick(18)
    late_slice(3)
    far_copy().wait_recv()
    da_sum[1 - batch] = got_far[...].astype(F32)

    def first_back(mb, _):
        da = da_sum[mb]
        unit, inverse = norm_parts(tokens[mb].astype(F32))
        vec[0, 0:1, :] += col_sum(da * unit)
        vec[0, 1:2, :] += col_sum(da)
        token_grad[mb] = gx1_ref[mb] + norm_back(unit, inverse, gain1[...], da)
        return 0

    lax.fori_loop(0, micro, first_back, 0)
    vec_step(0)
    early_step(6)
    cross_step(6)
    tick(19)
    late_slice(4)
    vec_step(1)
    early_step(7)
    cross_step(7)
    tick(20)
    late_slice(5)
    vec_step(2)
    early_step(8)
    cross_step(8)
    tick(21)
    late_slice(6)
    vec_step(3)
    early_step(9)
    late_slice(7)
    vec_step(4)
    early_step(10)
    vec_step(5)
    late_slice(8)
    for s in range(pieces):
        hop(s, 3).wait_recv()
    vec_out[...] = vec[5]
    for s in range(pieces):
        share_sent(s)
    for stage in range(10):
        sum_copy(early, all_early, got_early, early_s, early_r, stage).wait_send()
    for stage in range(8):
        slice_copy(cross, all_cross, got_cross, cross_s, cross_r, stage).wait_send()
        slice_copy(late, all_late, got_late, late_s, late_r, stage).wait_send()
    for d in range(5):
        vec_copy(d).wait_send()
    for j in range(4):
        y_copy(j).wait_send()
    for n in range(2):
        near_copy(n).wait_send()
    far_copy().wait_send()
    for k in range(1, parts):
        target = lax.rem(me + k, parts)
        a2a(do2_st, rv_do2, s_do2, r_do2, target).wait_send()
        a2a(st_dq2, rv_dq2, s_dq2, r_dq2, target).wait_send()
        a2a(st_do1, rv_do1, s_do1, r_do1, target).wait_send()


def finish_kernel(shares, early, cross, late, up, down, *grads):
    strip = shares.shape[3]
    depth = shares.shape[4]
    for n in range(2):
        for m in range(4):
            up[n, m * strip : (m + 1) * strip, :] = shares[0, 4 * n + m, 0].astype(F32)
            down[
                n, (m % 2) * strip : (m % 2 + 1) * strip, (m // 2) * depth : (m // 2 + 1) * depth
            ] = shares[0, 8 + 4 * n + m, 0].astype(F32)
    for n in range(3):
        grads[n][...] = early[n].astype(F32)
    lanes = late.shape[3]
    for source, refs in ((cross, grads[3:5]), (late, grads[5:8])):
        for n, ref in enumerate(refs):
            for p in range(source.shape[0]):
                ref[:, p * lanes : (p + 1) * lanes] = source[p, n].astype(F32)


def vmem_spec():
    return pl.BlockSpec(memory_space=pltpu.VMEM)


def fast_device(
    tokens, memory, expert_slot, doc_lengths, source_lengths, cotangent,
    norm1_gain, norm1_shift, self_query, self_key, self_value, self_out,
    norm2_gain, norm2_shift, cross_query, cross_key, cross_value, cross_out,
    norm3_gain, norm3_shift, up_weight, up_bias, down_weight, down_bias,
):
    micro, rows, width = tokens.shape
    parts = lax.axis_size("dp")
    pairs = HEADS // 2
    lanes = width // pairs
    length = parts * rows
    scaling = 1.0 / math.sqrt(width // HEADS)
    experts, _, hidden = up_weight.shape
    shape = jax.ShapeDtypeStruct
    dma = pltpu.SemaphoreType.DMA((parts,))
    line = lambda v: v.reshape(1, width)

    aug = shape((2, length, lanes), BF)
    blocks = shape((parts, rows, lanes), BF)
    full = shape((micro, rows, width), F32)
    low = shape((micro, rows, width), BF)
    vec = shape((1, width), F32)
    square = shape((width, width), F32)
    buf = lambda n: pltpu.VMEM((parts, n * rows, lanes), BF)

    count = micro * rows
    marks = jnp.broadcast_to(expert_slot.reshape(count, 1).astype(BF), (count, lanes))
    wide_all = shape((parts, rows, width), BF)
    pair = lax.rem(lax.axis_index("dp"), pairs)
    columns = lambda v: lax.dynamic_slice_in_dim(v, pair * lanes, lanes, 1)
    mine_q, mine_k, mine_v, mine_ck, mine_cv = (
        columns(v) for v in (self_query, self_key, self_value, cross_key, cross_value)
    )
    outs1 = [wide_all, wide_all, full, low, full, blocks, blocks, aug, aug, aug, blocks, aug, aug, aug, blocks,
             low, shape((count, lanes), BF)]
    (a_all, m_all, x1, c, x2, o1_own, o2_own, qa1, ka1, va1, o1, qa2, ka2, va2, o2, gf_got, marks_got) = pl.pallas_call(
        functools.partial(forward_kernel, parts, pairs, rows, scaling),
        out_shape=outs1,
        in_specs=[pl.BlockSpec(memory_space=pltpu.SMEM)] * 2 + [vmem_spec()] * 16,
        out_specs=[vmem_spec()] * len(outs1),
        scratch_shapes=[pltpu.VMEM((micro, rows, width), BF), buf(1), buf(1)]
        + [dma] * 10 + [pltpu.SemaphoreType.DMA((2,))] * 2,
        compiler_params=pltpu.CompilerParams(
            collective_id=1, has_side_effects=True, vmem_limit_bytes=VMEM_BYTES
        ),
        name="attend_forward",
    )(
        doc_lengths, source_lengths, tokens, memory, line(norm1_gain), line(norm1_shift),
        line(norm2_gain), line(norm2_shift), mine_q, mine_k, mine_v, self_out,
        cross_query, mine_ck, mine_cv, cross_out, cotangent, marks,
    )

    tiles = 4
    span = hidden // 2
    depth = span // tiles
    any_spec = pl.BlockSpec(memory_space=pl.ANY)
    pieces = 16
    shares_shape = shape((pieces, tiles, depth // 2, depth), BF)
    vec_pack = shape((16, width), F32)
    outs2 = [low, full, blocks, shape((width, width), BF), vec_pack, shares_shape]
    wide = lambda dtype, *dims: pltpu.VMEM(dims, dtype)
    block_out, gx2, do2, g_co, vec, shares = pl.pallas_call(
        functools.partial(expert_kernel, pairs, tiles),
        out_shape=outs2,
        in_specs=[vmem_spec()] * 8 + [any_spec, vmem_spec(), any_spec, vmem_spec(), vmem_spec()],
        out_specs=[vmem_spec()] * len(outs2),
        scratch_shapes=[
            wide(BF, experts, width, span), wide(BF, experts, span, width),
            wide(BF, 2, count, width),
            wide(BF, 2, tiles, count, depth), wide(BF, 2, tiles, count, depth),
            wide(F32, count, width), wide(BF, count, width), wide(BF, count, width),
            wide(BF, count, width), wide(BF, count, width),
            pltpu.SemaphoreType.DMA((2,)), pltpu.SemaphoreType.DMA((3,)), pltpu.SemaphoreType.DMA((3,)),
        ],
        compiler_params=pltpu.CompilerParams(
            collective_id=2, has_side_effects=True, vmem_limit_bytes=VMEM_BYTES
        ),
        name="experts",
    )(
        x2, o2_own, marks, marks_got, cotangent, gf_got, line(norm3_gain), line(norm3_shift),
        up_weight, up_bias, down_weight, down_bias, cross_out,
    )

    strip = depth // 2
    early_shape = shape((3 * width, width), BF)
    cross_shape, late_shape = shape((pairs, 2 * width, lanes), BF), shape((pairs, 3 * width, lanes), BF)
    all_shape = shape((2, pieces, tiles, strip, depth), BF)
    outs3 = [full, vec_pack, all_shape, early_shape, cross_shape, late_shape]
    acc = pltpu.VMEM((2, length, lanes), F32)
    aug_buf = pltpu.VMEM((2, length, lanes), BF)
    block_low = lambda *n: wide(BF, *n, rows, width)
    block_full = lambda *n: wide(F32, *n, rows, width)
    dmas = lambda *dims: pltpu.SemaphoreType.DMA(dims)
    token_grad, vec, all_shares, all_early, all_cross, all_late = pl.pallas_call(
        functools.partial(backward_kernel, parts, pairs, rows, scaling),
        out_shape=outs3,
        in_specs=[vmem_spec()] * 2 + [any_spec] * 3 + [vmem_spec()] + [any_spec] * 3
        + [vmem_spec()] * 4 + [any_spec] * 2 + [vmem_spec()] * 10 + [any_spec],
        out_specs=[vmem_spec()] * 2 + [any_spec] * 4,
        scratch_shapes=[buf(1), buf(1), buf(1), buf(1), buf(1), aug_buf, acc, acc, acc,
                        block_full(micro), block_low(micro), aug_buf, aug_buf, aug_buf,
                        block_low(parts), block_full(4), block_low(4), block_low(4),
                        block_low(2), block_low(2), block_low(), block_low(), block_full(micro),
                        wide(BF, pieces, tiles, strip, depth), wide(BF, pieces, 3, strip, depth),
                        wide(BF, pieces, 2, strip, depth), wide(BF, 3 * width, width),
                        wide(BF, 2 * width, lanes), wide(BF, 3 * width, lanes)]
        + [wide(BF, (3 * width) >> (d + 1), width) for d in range(5)]
        + [wide(BF, (2 * width) >> (d + 1), lanes) for d in range(3)]
        + [wide(BF, (3 * width) >> (d + 1), lanes) for d in range(3)]
        + [wide(F32, 6, 16, width), wide(F32, 5, 16, width), wide(F32, width, width),
           wide(F32, width, width), wide(F32, width, 2 * lanes), wide(F32, width, 3 * lanes)]
        + [dmas(pieces, 8), dmas(pieces, 4), dmas(pieces, tiles), dmas(pieces + 3), dmas(pieces + 8)]
        + [dmas(10), dmas(10), dmas(8), dmas(8), dmas(8), dmas(8), dmas(5), dmas(5), dmas(7), dmas(7)]
        + [dma] * 6,
        compiler_params=pltpu.CompilerParams(
            collective_id=3, has_side_effects=True, vmem_limit_bytes=VMEM_BYTES
        ),
        name="attend_backward",
    )(
        gx2, do2, qa1, ka1, va1, o1, qa2, ka2, va2, o2, tokens, x1, c, a_all, m_all, o1_own,
        line(norm1_gain), line(norm2_gain), mine_q, mine_k, mine_v, self_out, cross_query,
        g_co, vec, shares,
    )

    steps = 2 * tiles
    height = width // steps
    outs4 = [shape(up_weight.shape, F32), shape(down_weight.shape, F32)] + [square] * 8
    up_total, down_total, g_co, g_cq, g_so, g_ck, g_cv, g_sq, g_sk, g_sv = pl.pallas_call(
        finish_kernel,
        grid=(steps,),
        out_shape=outs4,
        in_specs=[
            pl.BlockSpec((1, pieces, 1, strip, depth),
                         lambda i: (lax.div(i, tiles), 0, lax.rem(i, tiles), 0, 0)),
            pl.BlockSpec((3, height, width), lambda i: (0, i, 0)),
            pl.BlockSpec((pairs, 2, height, lanes), lambda i: (0, 0, i, 0)),
            pl.BlockSpec((pairs, 3, height, lanes), lambda i: (0, 0, i, 0)),
        ],
        out_specs=[
            pl.BlockSpec((experts, width, depth), lambda i: (0, 0, i)),
            pl.BlockSpec((experts, depth, width), lambda i: (0, i, 0)),
        ] + [pl.BlockSpec((height, width), lambda i: (i, 0))] * 8,
        compiler_params=pltpu.CompilerParams(vmem_limit_bytes=VMEM_BYTES),
        name="finish",
    )(
        all_shares, all_early.reshape(3, width, width),
        all_cross.reshape(pairs, 2, width, lanes), all_late.reshape(pairs, 3, width, lanes),
    )

    return (
        block_out, token_grad, vec[0], vec[1], g_sq, g_sk, g_sv, g_so, vec[2], vec[3],
        g_cq, g_ck, g_cv, g_co, vec[4], vec[5],
        up_total, vec[8:16].reshape(experts, hidden), down_total, vec[6:8],
    )


def solution(mesh):
    fits = dict(mesh.shape) == {"grp": 4, "dp": 8}
    return jax.shard_map(
        fast_device if fits else per_device,
        mesh=mesh,
        in_specs=(
            P(None, ("grp", "dp"), None),
            P(None, ("grp", "dp"), None),
            P(None, ("grp", "dp"), None),
            P(None, "grp", None),
            P(None, "grp", None),
            P(None, ("grp", "dp"), None),
            P(),
            P(),
            P(),
            P(),
            P(),
            P(),
            P(),
            P(),
            P(),
            P(),
            P(),
            P(),
            P(),
            P(),
            P("grp", None, None),
            P("grp", None),
            P("grp", None, None),
            P("grp", None),
        ),
        out_specs=(
            P(None, ("grp", "dp"), None),
            P(None, ("grp", "dp"), None),
            P(),
            P(),
            P(),
            P(),
            P(),
            P(),
            P(),
            P(),
            P(),
            P(),
            P(),
            P(),
            P(),
            P(),
            P("grp", None, None),
            P("grp", None),
            P("grp", None, None),
            P("grp", None),
        ),
        check_vma=False,
    )
```

```python
import functools
import math

import jax
import jax.numpy as jnp
from jax import lax
from jax.experimental import pallas as pl
from jax.experimental.pallas import tpu as pltpu
from jax.sharding import PartitionSpec as P

HEADS = 8
CAP = 160


masked_score = -1e30


def layer_norm(inputs, norm_gain, norm_shift):
    mean_row = jnp.mean(inputs, axis=-1, keepdims=True)
    centred = inputs - mean_row
    spread = jnp.mean(centred * centred, axis=-1, keepdims=True)
    return centred * lax.rsqrt(spread + 1e-05) * norm_gain + norm_shift


def doc_index(lengths, places):
    doc_ends = jnp.cumsum(lengths)
    return jnp.sum((places[:, None] >= doc_ends[None, :]).astype(jnp.int32), axis=1)


def product(left, right):
    return jnp.dot(left, right, preferred_element_type=jnp.float32)


def left_product(left, right):
    return jnp.einsum("nd,ne->de", left, right, preferred_element_type=jnp.float32)


def right_product(left, right):
    return jnp.einsum("nd,ed->ne", left, right, preferred_element_type=jnp.float32)


def exact_left(left, right):
    return jnp.einsum("nd,ne->de", left, right, precision=lax.Precision.HIGHEST)


def split_heads(matrix, head_count):
    return matrix.reshape(matrix.shape[0], head_count, matrix.shape[1] // head_count)


def attend_forward(queries, keys_all, values_all, allowed, head_count):
    scaling = 1.0 / math.sqrt(queries.shape[1] // head_count)
    scores = (
        jnp.einsum(
            "qhd,khd->hqk",
            split_heads(queries, head_count),
            split_heads(keys_all, head_count),
            preferred_element_type=jnp.float32,
        )
        * scaling
    )
    scores = jnp.where(allowed[None], scores, masked_score)
    maximum = jnp.max(scores, axis=-1, keepdims=True)
    exponent = jnp.exp(scores - maximum)
    totals = jnp.sum(exponent, axis=-1, keepdims=True)
    probability = (exponent / totals).astype(jnp.bfloat16)
    mixed = jnp.einsum(
        "hqk,khd->qhd",
        probability,
        split_heads(values_all, head_count),
        preferred_element_type=jnp.float32,
    )
    return (mixed.reshape(queries.shape[0], queries.shape[1]), maximum + jnp.log(totals))


def score_parts(
    query_heads, key_heads, value_heads, grad_heads, allowed, scaling, log_total, centre
):
    scores = (
        jnp.einsum("qhd,khd->hqk", query_heads, key_heads, preferred_element_type=jnp.float32)
        * scaling
    )
    scores = jnp.where(allowed[None], scores, masked_score)
    probability = jnp.exp(scores - log_total)
    prob_grad = jnp.einsum(
        "qhd,khd->hqk", grad_heads, value_heads, preferred_element_type=jnp.float32
    )
    centre = jnp.sum(probability * prob_grad, axis=-1, keepdims=True)
    score_grad = (probability * (prob_grad - centre)).astype(jnp.bfloat16)
    return (probability, score_grad, centre)


def attend_backward(queries, keys_all, values_all, allowed, head_count, log_total, out_grad):
    scaling = 1.0 / math.sqrt(queries.shape[1] // head_count)
    query_heads = split_heads(queries, head_count)
    key_heads = split_heads(keys_all, head_count)
    grad_heads = split_heads(out_grad, head_count)
    probability, score_grad, centre = score_parts(
        query_heads,
        key_heads,
        split_heads(values_all, head_count),
        grad_heads,
        allowed,
        scaling,
        log_total,
        None,
    )
    query_back = (
        jnp.einsum("hqk,khd->qhd", score_grad, key_heads, preferred_element_type=jnp.float32)
        * scaling
    )
    key_back = (
        jnp.einsum("hqk,qhd->khd", score_grad, query_heads, preferred_element_type=jnp.float32)
        * scaling
    )
    value_back = jnp.einsum(
        "hqk,qhd->khd",
        probability.astype(jnp.bfloat16),
        grad_heads,
        preferred_element_type=jnp.float32,
    )
    width = queries.shape[1]
    return (
        query_back.reshape(queries.shape[0], width),
        key_back.reshape(keys_all.shape[0], width),
        value_back.reshape(keys_all.shape[0], width),
    )


def per_device(
    tokens,
    memory,
    expert_slot,
    doc_lengths,
    source_lengths,
    cotangent,
    norm1_gain,
    norm1_shift,
    self_query,
    self_key,
    self_value,
    self_out,
    norm2_gain,
    norm2_shift,
    cross_query,
    cross_key,
    cross_value,
    cross_out,
    norm3_gain,
    norm3_shift,
    up_weight,
    up_bias,
    down_weight,
    down_bias,
):
    micro = tokens.shape[0]
    rows = tokens.shape[1]
    width = tokens.shape[2]
    source_rows = memory.shape[1]
    parts = lax.axis_size("dp")
    place = lax.axis_index("dp")
    experts_here = up_weight.shape[0]
    capacity = CAP
    head_count = HEADS
    local_places = place * rows + jnp.arange(rows, dtype=jnp.int32)
    stream_places = jnp.arange(rows * parts, dtype=jnp.int32)
    source_places = jnp.arange(source_rows * parts, dtype=jnp.int32)
    slot_ids = jnp.arange(experts_here * capacity, dtype=jnp.int32)
    expert_ids = jnp.arange(experts_here, dtype=jnp.int32)
    inputs = tokens.astype(jnp.float32)
    normed_first, first_back = jax.vjp(layer_norm, inputs, norm1_gain, norm1_shift)
    attn_in = normed_first.astype(jnp.bfloat16)
    queries = product(attn_in, self_query).astype(jnp.bfloat16)
    keys_mine = product(attn_in, self_key).astype(jnp.bfloat16)
    values_mine = product(attn_in, self_value).astype(jnp.bfloat16)
    keys_all, values_all = (
        lax.all_gather(keys_mine, "dp", axis=1, tiled=True),
        lax.all_gather(values_mine, "dp", axis=1, tiled=True),
    )
    cross_keys_all, cross_values_all = (
        lax.all_gather(product(memory, cross_key).astype(jnp.bfloat16), "dp", axis=1, tiled=True),
        lax.all_gather(product(memory, cross_value).astype(jnp.bfloat16), "dp", axis=1, tiled=True),
    )
    square_zero = jnp.zeros((width, width), jnp.float32)
    vector_zero = jnp.zeros((width,), jnp.float32)
    grad_self_query, grad_self_key, grad_self_value, grad_self_out = (
        square_zero,
        square_zero,
        square_zero,
        square_zero,
    )
    grad_cross_query, grad_cross_key, grad_cross_value, grad_cross_out = (
        square_zero,
        square_zero,
        square_zero,
        square_zero,
    )
    second_gain_sum, second_shift_sum, third_gain_sum, third_shift_sum = (
        vector_zero,
        vector_zero,
        vector_zero,
        vector_zero,
    )
    grad_up = jnp.zeros(up_weight.shape, jnp.float32)
    grad_up_bias = jnp.zeros(up_bias.shape, jnp.float32)
    grad_down = jnp.zeros(down_weight.shape, jnp.float32)
    grad_down_bias = jnp.zeros(down_bias.shape, jnp.float32)
    outputs = []
    attn_in_grads = []
    resid_grads = []
    for batch_index in range(micro):
        lengths_now = doc_lengths[batch_index, 0]
        query_docs = doc_index(lengths_now, local_places)
        stream_docs = doc_index(lengths_now, stream_places)
        source_docs = doc_index(source_lengths[batch_index, 0], source_places)
        self_allowed = (query_docs[:, None] == stream_docs[None, :]) & (
            stream_places[None, :] <= local_places[:, None]
        )
        cross_allowed = query_docs[:, None] == source_docs[None, :]
        self_result, self_log = attend_forward(
            queries[batch_index],
            keys_all[batch_index],
            values_all[batch_index],
            self_allowed,
            head_count,
        )
        self_mixed = self_result.astype(jnp.bfloat16)
        after_self = inputs[batch_index] + product(self_mixed, self_out)
        normed_second, second_back = jax.vjp(layer_norm, after_self, norm2_gain, norm2_shift)
        cross_in = normed_second.astype(jnp.bfloat16)
        cross_queries = product(cross_in, cross_query).astype(jnp.bfloat16)
        cross_result, cross_log = attend_forward(
            cross_queries,
            cross_keys_all[batch_index],
            cross_values_all[batch_index],
            cross_allowed,
            head_count,
        )
        cross_mixed = cross_result.astype(jnp.bfloat16)
        after_cross = after_self + product(cross_mixed, cross_out)
        normed_third, third_back = jax.vjp(layer_norm, after_cross, norm3_gain, norm3_shift)
        expert_in = normed_third.astype(jnp.bfloat16)
        chosen = expert_slot[batch_index, :, 0]
        one_hot = (chosen[:, None] == expert_ids[None, :]).astype(jnp.int32)
        ranks = jnp.sum((jnp.cumsum(one_hot, axis=0) - 1) * one_hot, axis=1)
        target = chosen * capacity + ranks
        dispatch = (slot_ids[:, None] == target[None, :]).astype(jnp.bfloat16)
        buffer_in = (
            product(dispatch, expert_in).astype(jnp.bfloat16).reshape(experts_here, capacity, width)
        )
        pre_act = (
            jnp.einsum("ecd,edf->ecf", buffer_in, up_weight, preferred_element_type=jnp.float32)
            + up_bias[:, None, :]
        )
        activated, gelu_back = jax.vjp(jax.nn.gelu, pre_act)
        hidden = activated.astype(jnp.bfloat16)
        buffer_out = (
            jnp.einsum("ecf,efd->ecd", hidden, down_weight, preferred_element_type=jnp.float32)
            + down_bias[:, None, :]
        )
        expert_out = jnp.take(buffer_out.reshape(experts_here * capacity, width), target, axis=0)
        outputs.append((after_cross + expert_out).astype(jnp.bfloat16))
        out_grad = cotangent[batch_index].astype(jnp.float32)
        grad_rows = out_grad.astype(jnp.bfloat16)
        buffer_grad = (
            product(dispatch, grad_rows).astype(jnp.bfloat16).reshape(experts_here, capacity, width)
        )
        grad_down = grad_down + jnp.einsum(
            "ecf,ecd->efd", hidden, buffer_grad, preferred_element_type=jnp.float32
        )
        grad_down_bias = grad_down_bias + jnp.sum(buffer_grad.astype(jnp.float32), axis=1)
        hidden_grad = jnp.einsum(
            "ecd,efd->ecf", buffer_grad, down_weight, preferred_element_type=jnp.float32
        )
        pre_grad = gelu_back(hidden_grad)[0].astype(jnp.bfloat16)
        grad_up = grad_up + jnp.einsum(
            "ecd,ecf->edf", buffer_in, pre_grad, preferred_element_type=jnp.float32
        )
        grad_up_bias = grad_up_bias + jnp.sum(pre_grad.astype(jnp.float32), axis=1)
        buffer_back = jnp.einsum(
            "ecf,edf->ecd", pre_grad, up_weight, preferred_element_type=jnp.float32
        )
        expert_in_grad = jnp.take(
            buffer_back.reshape(experts_here * capacity, width), target, axis=0
        )
        third_resid, third_gain, third_shift = third_back(expert_in_grad)
        third_gain_sum = third_gain_sum + third_gain
        third_shift_sum = third_shift_sum + third_shift
        cross_grad = out_grad + third_resid
        cross_rows_grad = cross_grad.astype(jnp.bfloat16)
        grad_cross_out = grad_cross_out + left_product(cross_mixed, cross_rows_grad)
        cross_mixed_grad = right_product(cross_rows_grad, cross_out).astype(jnp.bfloat16)
        cross_query_back, cross_key_back, cross_value_back = attend_backward(
            cross_queries,
            cross_keys_all[batch_index],
            cross_values_all[batch_index],
            cross_allowed,
            head_count,
            cross_log,
            cross_mixed_grad,
        )
        cross_query_low = cross_query_back.astype(jnp.bfloat16)
        grad_cross_query = grad_cross_query + left_product(cross_in, cross_query_low)
        cross_key_mine, cross_value_mine = (
            lax.psum_scatter(
                cross_key_back.astype(jnp.bfloat16), "dp", scatter_dimension=0, tiled=True
            ).astype(jnp.float32),
            lax.psum_scatter(
                cross_value_back.astype(jnp.bfloat16), "dp", scatter_dimension=0, tiled=True
            ).astype(jnp.float32),
        )
        source_exact = memory[batch_index].astype(jnp.float32)
        grad_cross_key = grad_cross_key + exact_left(source_exact, cross_key_mine)
        grad_cross_value = grad_cross_value + exact_left(source_exact, cross_value_mine)
        second_resid, second_gain, second_shift = second_back(
            right_product(cross_query_low, cross_query)
        )
        second_gain_sum = second_gain_sum + second_gain
        second_shift_sum = second_shift_sum + second_shift
        self_grad = cross_grad + second_resid
        self_rows_grad = self_grad.astype(jnp.bfloat16)
        grad_self_out = grad_self_out + left_product(self_mixed, self_rows_grad)
        self_mixed_grad = right_product(self_rows_grad, self_out).astype(jnp.bfloat16)
        self_query_back, self_key_back, self_value_back = attend_backward(
            queries[batch_index],
            keys_all[batch_index],
            values_all[batch_index],
            self_allowed,
            head_count,
            self_log,
            self_mixed_grad,
        )
        self_key_mine, self_value_mine = (
            lax.psum_scatter(
                self_key_back.astype(jnp.bfloat16), "dp", scatter_dimension=0, tiled=True
            ).astype(jnp.float32),
            lax.psum_scatter(
                self_value_back.astype(jnp.bfloat16), "dp", scatter_dimension=0, tiled=True
            ).astype(jnp.float32),
        )
        query_low = self_query_back.astype(jnp.bfloat16)
        key_low = self_key_mine.astype(jnp.bfloat16)
        value_low = self_value_mine.astype(jnp.bfloat16)
        grad_self_query = grad_self_query + left_product(attn_in[batch_index], query_low)
        grad_self_key = grad_self_key + left_product(attn_in[batch_index], key_low)
        grad_self_value = grad_self_value + left_product(attn_in[batch_index], value_low)
        attn_in_grads.append(
            right_product(query_low, self_query)
            + right_product(key_low, self_key)
            + right_product(value_low, self_value)
        )
        resid_grads.append(self_grad)
    first_resid, first_gain, first_shift = first_back(jnp.stack(attn_in_grads))
    token_grad = jnp.stack(resid_grads) + first_resid
    block_out = jnp.stack(outputs)
    up_share, up_bias_share, down_share, down_bias_share = (
        lax.psum_scatter(
            grad_up.astype(jnp.bfloat16), "dp", scatter_dimension=2, tiled=True
        ).astype(jnp.float32),
        lax.psum_scatter(
            grad_up_bias.astype(jnp.bfloat16), "dp", scatter_dimension=1, tiled=True
        ).astype(jnp.float32),
        lax.psum_scatter(
            grad_down.astype(jnp.bfloat16), "dp", scatter_dimension=1, tiled=True
        ).astype(jnp.float32),
        lax.psum_scatter(
            grad_down_bias.astype(jnp.bfloat16), "dp", scatter_dimension=1, tiled=True
        ).astype(jnp.float32),
    )
    up_total, up_bias_total, down_total, down_bias_total = (
        lax.all_gather(up_share.astype(jnp.bfloat16), "dp", axis=2, tiled=True).astype(
            up_share.dtype
        ),
        lax.all_gather(up_bias_share.astype(jnp.bfloat16), "dp", axis=1, tiled=True).astype(
            up_bias_share.dtype
        ),
        lax.all_gather(down_share.astype(jnp.bfloat16), "dp", axis=1, tiled=True).astype(
            down_share.dtype
        ),
        lax.all_gather(down_bias_share.astype(jnp.bfloat16), "dp", axis=1, tiled=True).astype(
            down_bias_share.dtype
        ),
    )
    shared = lax.psum(
        (
            first_gain,
            first_shift,
            grad_self_query,
            grad_self_key,
            grad_self_value,
            grad_self_out,
            second_gain_sum,
            second_shift_sum,
            grad_cross_query,
            grad_cross_key,
            grad_cross_value,
            grad_cross_out,
            third_gain_sum,
            third_shift_sum,
        ),
        ("grp", "dp"),
    )
    return (
        block_out,
        token_grad,
        shared[0],
        shared[1],
        shared[2],
        shared[3],
        shared[4],
        shared[5],
        shared[6],
        shared[7],
        shared[8],
        shared[9],
        shared[10],
        shared[11],
        shared[12],
        shared[13],
        up_total,
        up_bias_total,
        down_total,
        down_bias_total,
    )


MESH = pl.DeviceIdType.MESH
BF = jnp.bfloat16
F32 = jnp.float32
VMEM_BYTES = 56 * 1024 * 1024
HIDE = -1e30


def mm(left, right):
    return lax.dot_general(left, right, (((1,), (0,)), ((), ())), preferred_element_type=F32)


def mm_right(left, right):
    return lax.dot_general(left, right, (((1,), (1,)), ((), ())), preferred_element_type=F32)


def mm_left(left, right):
    return lax.dot_general(left, right, (((0,), (0,)), ((), ())), preferred_element_type=F32)


def norm_parts(inputs):
    mean_row = jnp.mean(inputs, axis=-1, keepdims=True)
    centred = inputs - mean_row
    spread = jnp.mean(centred * centred, axis=-1, keepdims=True)
    inverse = lax.rsqrt(spread + 1e-05)
    return centred * inverse, inverse


def norm_back(unit, inverse, gain, grad):
    scaled = grad * gain
    first = jnp.mean(scaled, axis=-1, keepdims=True)
    second = jnp.mean(scaled * unit, axis=-1, keepdims=True)
    return inverse * (scaled - first - unit * second)


def col_sum(values):
    return jnp.sum(values, axis=0, keepdims=True)


def three_parts(values):
    high = values.astype(BF).astype(F32)
    rest = values - high
    middle = rest.astype(BF).astype(F32)
    return high, middle, rest - middle


def doc_of(lengths_ref, batch, positions):
    total = jnp.int32(0)
    docs = jnp.zeros(positions.shape, jnp.int32)
    for j in range(lengths_ref.shape[2]):
        total = total + lengths_ref[batch, 0, j]
        docs = docs + (positions >= total).astype(jnp.int32)
    return docs


def lanes_of(shape, head):
    lane = lax.broadcasted_iota(jnp.int32, shape, 1)
    half = shape[1] // 2
    own = (lane < half) if head == 0 else (lane >= half)
    return own, (lane - half if head == 0 else lane)


def greet(grp, me, parts):
    barrier = pltpu.get_barrier_semaphore()
    for k in range(1, parts):
        pl.semaphore_signal(
            barrier, inc=1, device_id=(grp, lax.rem(me + k, parts)), device_id_type=MESH
        )
    pl.semaphore_wait(barrier, parts - 1)


def sender(grp, src, dst, ssem, rsem, target):
    return pltpu.make_async_remote_copy(
        src_ref=src,
        dst_ref=dst,
        send_sem=ssem,
        recv_sem=rsem,
        device_id=(grp, target),
        device_id_type=MESH,
    )


def partner_of(grp, me, axis):
    place = lax.div(me, 2)
    if axis == "core":
        return grp + 1 - 2 * lax.rem(grp, 2), me
    if axis == "x":
        return lax.rem(grp + 2, 4), me
    if axis == "y":
        return grp, me + 1 - 2 * lax.rem(me, 2)
    if axis == "near":
        return grp, me + 2 - 4 * lax.rem(place, 2)
    return grp, lax.rem(me + 4, 8)


def push(src, dst, ssem, rsem, device):
    return pltpu.make_async_remote_copy(
        src_ref=src, dst_ref=dst, send_sem=ssem, recv_sem=rsem, device_id=device, device_id_type=MESH
    )


def wait_in(ref, sem, device):
    push(ref, ref, sem, sem, device).wait_recv()


def wait_out(ref, sem, device):
    push(ref, ref, sem, sem, device).wait_send()


def key_features(values, docs, head):
    own, place = lanes_of(values.shape, head)
    other = jnp.where(place == docs, 0.0, HIDE)
    other = jnp.where((place >= 4) & (place < 7), 1.0, other)
    return jnp.where(own, values.astype(F32), other).astype(BF)


def query_features(values, docs, head, scaling):
    own, place = lanes_of(values.shape, head)
    return jnp.where(
        own, values.astype(F32) * scaling, jnp.where(place == docs, 1.0, 0.0)
    ).astype(BF)


def value_features(values, head):
    own, _ = lanes_of(values.shape, head)
    return jnp.where(own, values.astype(F32), 1.0).astype(BF)


def forward_kernel(
    parts, pairs, rows, scaling,
    doc_len, src_len, tokens, memory, gain1, shift1, gain2, shift2,
    wq, wk, wv, wo, cq, ck, cv, co, cot, marks,
    a_all, m_all, x1_out, c_out, x2_out, o1_own, o2_own,
    qa1, ka1, va1, o1, qa2, ka2, va2, o2, gf_got, marks_got,
    a_own, st_q2, rv_q2,
    s_a, r_a, s_m, r_m, s_o1, r_o1, s_q2, r_q2, s_o2, r_o2, s_y, r_y,
):
    grp = lax.axis_index("grp")
    me = lax.axis_index("dp")
    batch = lax.div(me, pairs)
    pair = lax.rem(me, pairs)
    micro = tokens.shape[0]
    lanes = 128
    low_half = batch == 0
    half = lax.rem(me, 2)
    place = lax.div(me, 2)
    inner = (place == 1) | (place == 2)
    to_y = partner_of(grp, me, "y")
    to_near = partner_of(grp, me, "near")
    entry = jnp.where(low_half, 4, 2) + half
    far_end = jnp.where(low_half, 6, 0) + half

    def a2a(src, dst, ssem, rsem, target):
        return sender(grp, src.at[target], dst.at[me], ssem, rsem.at[me], target)

    def arrived(dst, ssem, rsem, source):
        wait_in(dst.at[source], rsem.at[source], to_y)

    greet(grp, me, parts)

    def first_norm(mb, _):
        unit, _inv = norm_parts(tokens[mb].astype(F32))
        a_own[mb] = (unit * gain1[...] + shift1[...]).astype(BF)
        return 0

    lax.fori_loop(0, micro, first_norm, 0)

    def source_of(i):
        return jnp.where(i == 0, me, jnp.where(i == 1, to_near[1], jnp.where(i == 2, entry, far_end)))

    def spread_first(own, out, ssem, rsem):
        there = (grp, entry)
        return [
            push(own.at[batch], out.at[me], ssem.at[4], rsem.at[me], to_near),
            push(own.at[1 - batch], out.at[me], ssem.at[5], rsem.at[me], there),
        ]

    def spread_y(out, ssem, rsem, i):
        j = source_of(i)
        return push(out.at[j], out.at[j], ssem.at[i], rsem.at[j], to_y)

    def spread_near(out, ssem, rsem, i):
        j = source_of(i)
        return push(out.at[j], out.at[j], ssem.at[4 + i], rsem.at[j], to_near)

    def spread_start(own, out, ssem, rsem):
        for copy in spread_first(own, out, ssem, rsem):
            copy.start()
        out[me] = own[batch]
        spread_y(out, ssem, rsem, 0).start()

    def spread_on(out, ssem, rsem, i):
        arrived(out, ssem, rsem, source_of(i))
        spread_y(out, ssem, rsem, i).start()

        @pl.when(inner & (i >= 2))
        def _():
            spread_near(out, ssem, rsem, i).start()

    def spread_done(own, out, ssem, rsem):
        for copy in spread_first(own, out, ssem, rsem):
            copy.wait_send()
        for i in range(4):
            spread_y(out, ssem, rsem, i).wait_send()

        @pl.when(inner)
        def _():
            for i in (2, 3):
                spread_near(out, ssem, rsem, i).wait_send()

    def y_of(i):
        return source_of(i) + 1 - 2 * half

    def build_self(j):
        r0 = pl.multiple_of(j * rows, rows)
        places = r0 + lax.broadcasted_iota(jnp.int32, (rows, lanes), 0)
        docs = doc_of(doc_len, batch, places)
        a = a_all[j]
        query, key, value = (mm(a, weight[...]).astype(BF) for weight in (wq, wk, wv))
        for h in range(2):
            qa1[h, pl.ds(r0, rows), :] = query_features(query, docs, h, scaling)
            ka1[h, pl.ds(r0, rows), :] = key_features(key, docs, h)
            va1[h, pl.ds(r0, rows), :] = value_features(value, h)

    spread_start(a_own, a_all, s_a, r_a)

    def same_y(i, _):
        @pl.when(i > 0)
        def _():
            spread_on(a_all, s_a, r_a, i)

        build_self(source_of(i))
        return 0

    def other_y(i, _):
        arrived(a_all, s_a, r_a, y_of(i))
        build_self(y_of(i))
        return 0

    lax.fori_loop(0, 4, same_y, 0)
    lax.fori_loop(0, 4, other_y, 0)
    spread_start(memory, m_all, s_m, r_m)

    def finish(qa, r0, h, query, top, acc):
        own, place = lanes_of((rows, lanes), h)
        total = pltpu.roll(acc, lanes // 2, 1)
        high, middle, low = three_parts(top + jnp.log(acc))
        query = query.astype(F32)
        query = jnp.where(~own & (place == 4), -high, query)
        query = jnp.where(~own & (place == 5), -middle, query)
        query = jnp.where(~own & (place == 6), -low, query)
        qa[h, pl.ds(r0, rows), :] = query.astype(BF)
        return acc / total

    def emit(t, heads, out, own_ref, ssem, rsem):
        own, _ = lanes_of((rows, lanes), 0)
        out[t] = jnp.where(own, heads[0], heads[1]).astype(BF)

        @pl.when(t != me)
        def _():
            sender(grp, out.at[t], own_ref.at[me], ssem, rsem, t).start()

        @pl.when(t == me)
        def _():
            own_ref[me] = out[t]

    for e in range(parts // 2):
        reach = 2 * rows * (e + 1)
        cut = reach - 2 * rows

        def self_block(i, _, reach=reach, cut=cut, e=e):
            t = 2 * e + i
            r0 = pl.multiple_of(t * rows, rows)
            row = r0 + lax.broadcasted_iota(jnp.int32, (rows, 2 * rows), 0)
            col = cut + lax.broadcasted_iota(jnp.int32, (rows, 2 * rows), 1)
            heads = []
            for h in range(2):
                query = qa1[h, pl.ds(r0, rows), :]
                near = mm_right(query, ka1[h, cut:reach, :])
                near = jnp.where(col <= row, near, HIDE)
                top = jnp.max(near, axis=1, keepdims=True)
                if cut:
                    far = mm_right(query, ka1[h, 0:cut, :])
                    top = jnp.maximum(top, jnp.max(far, axis=1, keepdims=True))
                acc = mm(jnp.exp(near - top).astype(BF), va1[h, cut:reach, :])
                if cut:
                    acc = acc + mm(jnp.exp(far - top).astype(BF), va1[h, 0:cut, :])
                heads.append(finish(qa1, r0, h, query, top, acc))
            emit(t, heads, o1, o1_own, s_o1, r_o1)
            return 0

        lax.fori_loop(0, 2, self_block, 0)
        if e == 2:
            spread_on(m_all, s_m, r_m, 1)

    def own_wait(own_ref, ssem, rsem):
        wait_in(own_ref.at[pl.ds(0, parts - 1)], rsem, to_y)

    spread_on(m_all, s_m, r_m, 2)
    spread_on(m_all, s_m, r_m, 3)
    own_wait(o1_own, s_o1, r_o1)

    def second_norm(mb, _):
        mixed = jnp.concatenate([o1_own[mb * pairs + p] for p in range(pairs)], axis=1)
        x1 = tokens[mb].astype(F32) + mm(mixed, wo[...])
        x1_out[mb] = x1
        unit, _inv = norm_parts(x1)
        c = (unit * gain2[...] + shift2[...]).astype(BF)
        c_out[mb] = c
        got = mm(c, cq[...]).astype(BF)
        for p in range(pairs):
            st_q2[mb * pairs + p] = got[:, p * lanes : (p + 1) * lanes]

        def send(p, _):
            target = mb * pairs + p

            @pl.when(target != me)
            def _():
                a2a(st_q2, rv_q2, s_q2, r_q2, target).start()

            @pl.when(target == me)
            def _():
                rv_q2[me] = st_q2[me]

            return 0

        lax.fori_loop(0, pairs, send, 0)
        return 0

    lax.fori_loop(0, micro, second_norm, 0)

    def build_cross(i, _):
        j = jnp.where(i < 4, source_of(i), y_of(i - 4))

        @pl.when(i >= 4)
        def _():
            arrived(m_all, s_m, r_m, j)

        r0 = pl.multiple_of(j * rows, rows)
        places = r0 + lax.broadcasted_iota(jnp.int32, (rows, lanes), 0)
        docs = doc_of(src_len, batch, places)
        source = m_all[j]
        key, value = (mm(source, weight[...]).astype(BF) for weight in (ck, cv))
        for h in range(2):
            ka2[h, pl.ds(r0, rows), :] = key_features(key, docs, h)
            va2[h, pl.ds(r0, rows), :] = value_features(value, h)
        return 0

    lax.fori_loop(0, parts, build_cross, 0)

    swaps = [
        push(cot, gf_got, s_y.at[0], r_y.at[0], to_y),
        push(marks, marks_got, s_y.at[1], r_y.at[1], to_y),
    ]
    for swap in swaps:
        swap.start()

    def cross_block(k, _):
        t = lax.rem(me + k, parts)

        @pl.when(k > 0)
        def _():
            arrived(rv_q2, s_q2, r_q2, t)

        r0 = pl.multiple_of(t * rows, rows)
        places = r0 + lax.broadcasted_iota(jnp.int32, (rows, lanes), 0)
        docs = doc_of(doc_len, batch, places)
        heads = []
        for h in range(2):
            query = query_features(rv_q2[t], docs, h, scaling)
            scores = mm_right(query, ka2[h])
            top = jnp.max(scores, axis=1, keepdims=True)
            acc = mm(jnp.exp(scores - top).astype(BF), va2[h])
            heads.append(finish(qa2, r0, h, query, top, acc))
        emit(t, heads, o2, o2_own, s_o2, r_o2)
        return 0

    lax.fori_loop(0, parts, cross_block, 0)
    own_wait(o2_own, s_o2, r_o2)

    def third(mb, _):
        mixed = jnp.concatenate([o2_own[mb * pairs + p] for p in range(pairs)], axis=1)
        x2_out[mb] = x1_out[mb] + mm(mixed, co[...])
        return 0

    lax.fori_loop(0, micro, third, 0)

    for ref, sem in ((st_q2, s_q2), (o1, s_o1), (o2, s_o2)):
        wait_out(ref.at[pl.ds(0, parts - 1)], sem, to_y)
    for swap in swaps:
        swap.wait()
    spread_done(a_own, a_all, s_a, r_a)
    spread_done(memory, m_all, s_m, r_m)


def gelu_both(z):
    root = math.sqrt(2.0 / math.pi)
    square = z * z
    bent = jnp.tanh(root * z * (1.0 + 0.044715 * square))
    half = 0.5 * (1.0 + bent)
    slope = half + 0.5 * z * (1.0 - bent * bent) * (root * (1.0 + 3 * 0.044715 * square))
    return z * half, slope


LAG = 1
TICKS = (3, 3, 1, 1, 1, 1)


def backward_kernel(
    parts, pairs, rows, scaling,
    x2_in, o2_own, marks, marks_got, cot_in, gf_in, gain3, shift3, up_hbm, up_b, down_hbm, down_b, co,
    qa1_in, ka1_in, va1_in, o1, qa2_in, ka2_in, va2_in, o2,
    tokens_in, x1_in, c_in, a_in, m_in, o1_own, gain1, gain2,
    wq, wk, wv, wo, cq,
    block_out, token_grad, vec_out, all_shares, all_early, all_cross, all_late,
    x_buf, c_buf, t_buf, o_buf, e_all, gx2_ref, st_do, rv_do, rv_dq2, doa, dq_acc, dk_acc, dv_acc, gx1_ref, low_grad,
    qa, ka, va, stream, da_keep, st_y, got_y, st_near, got_near, st_far, got_far, da_sum,
    shares, final, got_one, got_two, early, cross, late, *rest
):
    got_early, got_cross, got_late, rest = rest[:5], rest[5:8], rest[8:11], rest[11:]
    vec, got_vec, g_late, rest = *rest[:3], rest[3:]
    hop_s, hop_r, piece_r, local_sem, load_sem, rest = *rest[:5], rest[5:]
    early_s, early_r, cross_s, cross_r, late_s, late_r, vec_s, vec_r, rest = *rest[:8], rest[8:]
    swap_s, swap_r, da_s, da_r, s_do2, r_do2, s_dq2, r_dq2, s_do1, r_do1 = rest
    grp = lax.axis_index("grp")
    me = lax.axis_index("dp")
    micro, rows, width = x_buf.shape
    count = micro * rows
    span = up_b.shape[1] // 2
    lanes = 128
    length = parts * rows

    def a2a(src, dst, ssem, rsem, target):
        return sender(grp, src.at[target], dst.at[me], ssem, rsem, target)

    def all_arrived(dst, rsem):
        wait_in(dst.at[pl.ds(0, parts - 1)], rsem, partners[2])

    half = lax.rem(me, 2)
    near_bit = lax.rem(lax.div(me, 2), 2)
    far_bit = lax.div(me, 4)
    axes = ("core", "x", "y", "near", "far")
    place = lax.div(me, 2)
    batch = far_bit
    pair = lax.rem(me, pairs)
    inner = (place == 1) | (place == 2)
    bits = (lax.rem(grp, 2), lax.div(grp, 2), half, near_bit, far_bit)
    partners = [partner_of(grp, me, axis) for axis in axes]
    barrier = pltpu.get_barrier_semaphore()
    for k in range(1, parts):
        pl.semaphore_signal(
            barrier, inc=1, device_id=(grp, lax.rem(me + k, parts)), device_id_type=MESH
        )
    for k in range(1, 4):
        for f in range(2):
            there = (lax.rem(grp + k, 4), f * 4 + pair)
            pl.semaphore_signal(barrier, inc=1, device_id=there, device_id_type=MESH)

    pieces, tiles, strip, depth = shares.shape
    to_y, to_near, to_far = partners[2:]
    to_mid = (grp, (3 - place) * 2 + half)
    at_end = jnp.where(far_bit == 0, 0, 3)
    at_inner = jnp.where(far_bit == 0, 1, 2)
    at_next = 3 - at_inner
    at_last = 3 - at_end
    three = pl.ds(jnp.where(far_bit == 0, 1, 0), 3)
    away = pl.ds(jnp.where(far_bit == 0, 2, 0), 2)
    home = pl.ds(jnp.where(far_bit == 0, 0, 2), 2)

    def hop(s, n):
        rsem = hop_r.at[s, n]
        if n == 0:
            return push(shares.at[s, three], got_one.at[s], hop_s.at[0], rsem, to_near)
        if n == 1:
            return push(shares.at[s, away], got_two.at[s], hop_s.at[0], rsem, to_mid)
        return push(shares.at[s, at_end], got_two.at[s, 0], hop_s.at[0], rsem, to_near)

    def piece_on(s, n, piece, device):
        ref = final.at[s, piece]
        return push(ref, ref, hop_s.at[1], piece_r.at[s, n], device)

    def y_copy_of(s):
        return push(final.at[s], all_shares.at[half, s], hop_s.at[2], hop_s.at[3], to_y)

    def summed(s, piece, more):
        return (shares[s, piece].astype(F32) + more.astype(F32)).astype(BF)

    first_three = jnp.where(far_bit == 0, 1, 0)
    first_home = jnp.where(far_bit == 0, 0, 2)

    def share_step(s, stage):
        if stage == 0:

            @pl.when(~inner)
            def _():
                hop(s, 0).start()

        if stage == 1:

            @pl.when(inner)
            def _():
                hop(s, 0).wait_recv()
                for n in range(3):
                    shares[s, first_three + n] = summed(s, first_three + n, got_one[s, n])
                hop(s, 1).start()

        if stage == 2:

            @pl.when(inner)
            def _():
                hop(s, 1).wait_recv()
                shares[s, at_end] = summed(s, at_end, got_two[s, at_end - first_home])
                hop(s, 2).start()
                final[s, at_inner] = summed(s, at_inner, got_two[s, at_inner - first_home])
                piece_on(s, 0, at_inner, to_mid).start()
                piece_on(s, 1, at_inner, to_near).start()

        if stage == 3:

            @pl.when(~inner)
            def _():
                hop(s, 2).wait_recv()
                final[s, at_end] = summed(s, at_end, got_two[s, 0])
                piece_on(s, 2, at_end, to_near).start()

        if stage == 4:

            @pl.when(inner)
            def _():
                piece_on(s, 2, at_end, to_near).wait_recv()
                piece_on(s, 3, at_end, to_mid).start()

        if stage == 5:

            @pl.when(inner)
            def _():
                piece_on(s, 0, at_next, to_mid).wait_recv()
                piece_on(s, 3, at_last, to_mid).wait_recv()
                ref = final.at[s, away]
                push(ref, ref, hop_s.at[1], piece_r.at[s, 4], to_near).start()
                y_copy_of(s).start()

        if stage == 6:

            @pl.when(~inner)
            def _():
                piece_on(s, 1, at_inner, to_near).wait_recv()
                ref = final.at[s, away]
                push(ref, ref, hop_s.at[1], piece_r.at[s, 4], to_near).wait_recv()
                y_copy_of(s).start()

    def shares_done():
        out = pltpu.make_async_copy(final, all_shares.at[half], local_sem.at[3])
        out.start()
        wait_in(all_shares.at[1 - half], hop_s.at[3], to_y)
        wait_out(final, hop_s.at[2], to_y)

        @pl.when(inner)
        def _():
            wait_out(got_one, hop_s.at[0], to_y)
            wait_out(final, hop_s.at[1], to_y)
            wait_out(final.at[:, 0], hop_s.at[1], to_y)

        @pl.when(~inner)
        def _():
            wait_out(got_one, hop_s.at[0], to_y)
            wait_out(final.at[:, 0], hop_s.at[1], to_y)

        out.wait()

    def load_three(refs, n):
        return [
            pltpu.make_async_copy(src, dst, load_sem.at[5 + 3 * n + m])
            for m, (src, dst) in enumerate(zip(refs, (qa, ka, va)))
        ]

    def tick(i):
        for stage in range(7):
            s = i - LAG * stage
            if isinstance(s, int):
                if 0 <= s < pieces:
                    share_step(s, stage)
            else:

                @pl.when((s >= 0) & (s < pieces))
                def _(s=s, stage=stage):
                    share_step(s, stage)

    def ticks(start, count):
        def one(i, _):
            tick(start + i)
            return 0

        lax.fori_loop(0, count, one, 0)

    def seven(one):
        def body(k, _):
            one(k)
            return 0

        lax.fori_loop(1, 8, body, 0)

    slice_axes = (0, 1, 4)

    def slice_start(total, upto):
        start = jnp.int32(0)
        for d in range(upto):
            start = start + bits[slice_axes[d]] * (total >> (d + 1))
        return start

    def slice_rows(total, upto):
        return pl.ds(pl.multiple_of(slice_start(total, upto), total >> 3), total >> upto)

    def slice_copy(own, out, got, ssem, rsem, stage):
        total = own.shape[0]
        sems = (ssem.at[stage], rsem.at[stage])
        if stage < 3:
            axis = slice_axes[stage]
            size = total >> (stage + 1)
            start = slice_start(total, stage) + (1 - bits[axis]) * size
            part = pl.ds(pl.multiple_of(start, total >> 3), size)
            return push(own.at[part], got[stage], *sems, partners[axis])
        if stage == 3:
            part = slice_rows(total, 3)
            return push(own.at[part], out.at[pair, part], *sems, to_far)
        if stage == 4:
            ref = out.at[pair, slice_rows(total, 2)]
            return push(ref, ref, *sems, to_y)
        if stage == 5:
            ref = out.at[pl.ds(near_bit * 2, 2), slice_rows(total, 2)]
            return push(ref, ref, *sems, to_near)
        ref = out.at[:, slice_rows(total, 8 - stage)]
        return push(ref, ref, *sems, partners[7 - stage])

    def slice_local(own, out, sem):
        part = slice_rows(own.shape[0], 3)
        return pltpu.make_async_copy(own.at[part], out.at[pair, part], sem)

    def slice_step(own, out, got, ssem, rsem, sem, stage):
        total = own.shape[0]
        if stage >= 1:
            slice_copy(own, out, got, ssem, rsem, stage - 1).wait_recv()
        if 1 <= stage <= 3:
            part = slice_rows(total, stage)
            own[part, :] = (own[part, :].astype(F32) + got[stage - 1][...].astype(F32)).astype(BF)
        if stage == 3:
            slice_local(own, out, sem).start()
        if stage == 4:
            slice_local(own, out, sem).wait()
        if stage < 8:
            slice_copy(own, out, got, ssem, rsem, stage).start()
        if stage == 8:
            for n in range(8):
                slice_copy(own, out, got, ssem, rsem, n).wait_send()

    def cross_step(stage):
        slice_step(cross, all_cross, got_cross, cross_s, cross_r, local_sem.at[0], stage)

    def late_step(stage):
        slice_step(late, all_late, got_late, late_s, late_r, local_sem.at[1], stage)

    def offset_of(total, upto):
        start = jnp.int32(0)
        for d in range(upto):
            start = start + bits[d] * (total >> (d + 1))
        return start

    def rows_at(total, start, size):
        return pl.ds(pl.multiple_of(start, total >> 5), size)

    def early_copy(stage):
        total = early.shape[0]
        sems = (early_s.at[stage], early_r.at[stage])
        if stage < 5:
            size = total >> (stage + 1)
            start = offset_of(total, stage) + (1 - bits[stage]) * size
            return push(early.at[rows_at(total, start, size)], got_early[stage], *sems, partners[stage])
        d = 9 - stage
        part = rows_at(total, offset_of(total, d + 1), total >> (d + 1))
        src = early if stage == 5 else all_early
        return push(src.at[part], all_early.at[part], *sems, partners[d])

    def early_local():
        total = early.shape[0]
        part = rows_at(total, offset_of(total, 5), total >> 5)
        return pltpu.make_async_copy(early.at[part], all_early.at[part], local_sem.at[2])

    def early_step(stage):
        total = early.shape[0]
        if stage >= 1:
            early_copy(stage - 1).wait_recv()
        if 1 <= stage <= 5:
            part = rows_at(total, offset_of(total, stage), total >> stage)
            early[part, :] = (early[part, :].astype(F32) + got_early[stage - 1][...].astype(F32)).astype(BF)
        if stage == 5:
            early_local().start()
        if stage == 6:
            early_local().wait()
        if stage < 10:
            early_copy(stage).start()
        if stage == 10:
            for n in range(10):
                early_copy(n).wait_send()

    def vec_first(k):
        j = lax.rem(me + k, parts)
        return push(vec.at[0], got_vec.at[me], vec_s.at[0], vec_r.at[0], (grp, j))

    def vec_cross(k):
        other = lax.rem(grp + k, 4)
        return push(
            vec.at[1, 0:8], got_vec.at[8 + grp, 0:8], vec_s.at[1], vec_r.at[1], (other, me)
        )

    def vec_step(stage):
        if stage == 0:
            seven(lambda k: vec_first(k).start())
        if stage == 1:

            wait_in(got_vec.at[pl.ds(0, 7)], vec_r.at[0], to_y)

            def more(k, total):
                return total + got_vec[lax.rem(me + k, parts)]

            vec[1] = lax.fori_loop(1, 8, more, vec[0])
            for k in range(1, 4):
                vec_cross(k).start()
        if stage == 2:
            total = jnp.zeros((8, width), F32)
            wait_in(got_vec.at[pl.ds(0, 3), 0:8], vec_r.at[1], to_y)
            for k in range(1, 4):
                total = total + got_vec[8 + lax.rem(grp + k, 4), 0:8]
            row = lax.broadcasted_iota(jnp.int32, (8, width), 0)
            vec[2, 0:8] = vec[1, 0:8] + jnp.where(row < 6, total, 0.0)
            vec[2, 8:16] = vec[1, 8:16]
            wait_out(got_vec.at[pl.ds(0, 7)], vec_s.at[0], to_y)
            wait_out(got_vec.at[pl.ds(0, 3), 0:8], vec_s.at[1], to_y)

    first_col = pl.multiple_of(half * span, span)

    def load(src, dst, n):
        return pltpu.make_async_copy(src, dst, load_sem.at[n])

    in_loads = [
        load(src, dst, 13 + n)
        for n, (src, dst) in enumerate(((x2_in, x_buf), (cot_in, c_buf), (gf_in, t_buf), (o2_own, o_buf)))
    ]
    for one in in_loads:
        one.start()

    def weight_load(k, _):
        n, f = lax.div(k, tiles), lax.rem(k, tiles)
        cols = pl.ds(pl.multiple_of(first_col + f * depth, depth), depth)
        load(up_hbm.at[n, :, :, cols], final.at[k], 17).start()
        load(down_hbm.at[n, cols, :], stream.at[k], 18).start()
        return 0

    lax.fori_loop(0, 2 * tiles, weight_load, 0)
    vec[0] = jnp.zeros(vec.shape[1:], F32)
    in_loads[0].wait()
    for mb in range(micro):
        part = slice(mb * rows, (mb + 1) * rows)
        unit, _inv = norm_parts(x_buf[mb])
        e_all[0, part, :] = (unit * gain3[...] + shift3[...]).astype(BF)
    pl.semaphore_wait(barrier, parts + 5)
    swaps = [
        push(src, dst, swap_s.at[n], swap_r.at[n], to_y)
        for n, (src, dst) in enumerate(
            (
                (e_all.at[0], e_all.at[1]),
                (st_y.at[pl.ds(0, 2)], got_y.at[pl.ds(0, 2)]),
                (low_grad, got_y.at[pl.ds(2, 2)]),
            )
        )
    ]
    swaps[0].start()
    for one in in_loads[1:]:
        one.wait()
    load(final.at[pl.ds(0, 2 * tiles)], final.at[pl.ds(0, 2 * tiles)], 17).wait()
    load(stream, stream, 18).wait()
    mark_all = (marks, marks_got)
    gf_refs = (c_buf, t_buf)

    def up_tile(n, f):
        return final[n * tiles + f].reshape(width, depth)

    def down_tile(n, f):
        return stream[n * tiles + f]

    def gf_of(rowset):
        return jnp.concatenate([gf_refs[rowset][mb] for mb in range(micro)], axis=0)

    def folded(values):
        return values.reshape(micro, rows, width)

    def ones_of(rowset, wide):
        return jnp.concatenate([mark_all[rowset][...]] * (wide // lanes), axis=1) > 0.5

    def split(values, is_one):
        zero = jnp.zeros_like(values)
        return jnp.where(is_one, zero, values), jnp.where(is_one, values, zero)

    def kept_tile(low, high, rowset, f):
        part = pl.ds(pl.multiple_of(f * count, count), count)
        return jnp.concatenate([low[rowset, part, :], high[rowset, part, :]], axis=1)

    def through(rowset, acc):
        acc[...] = jnp.zeros_like(acc)

        def tile(f, _):
            bias_cols = pl.ds(pl.multiple_of(first_col + f * depth, depth), depth)
            is_one = ones_of(rowset, depth)
            e = e_all[rowset]
            gf = gf_of(rowset)
            u = jnp.where(
                is_one,
                mm(e, up_tile(1, f)) + up_b[1:2, bias_cols],
                mm(e, up_tile(0, f)) + up_b[0:1, bias_cols],
            )
            hidden, slope = gelu_both(u)
            part = pl.ds(pl.multiple_of(f * count, count), count)
            hidden = hidden.astype(BF)
            qa[rowset, part, :] = hidden[:, 0:lanes]
            ka[rowset, part, :] = hidden[:, lanes : 2 * lanes]
            back = jnp.where(is_one, mm_right(gf, down_tile(1, f)), mm_right(gf, down_tile(0, f)))
            du = (back * slope).astype(BF)
            va[rowset, part, :] = du[:, 0:lanes]
            doa[rowset, part, :] = du[:, lanes : 2 * lanes]
            none, one = split(du, is_one)
            acc[...] += folded(mm_right(none, up_tile(0, f)) + mm_right(one, up_tile(1, f)))
            return 0

        lax.fori_loop(0, tiles, tile, 0)

    def branch(rowset):
        is_one = ones_of(rowset, depth)

        def tile(f, total):
            none, one = split(kept_tile(qa, ka, rowset, f), is_one)
            return total + mm(none, down_tile(0, f)) + mm(one, down_tile(1, f))

        return lax.fori_loop(0, tiles, tile, jnp.zeros((count, width), F32))

    through(0, gx1_ref)
    swaps[0].wait()
    through(1, gx2_ref)
    st_y[0:2] = gx2_ref[...].astype(BF)
    swaps[1].start()

    def expert_weights(n):
        def weights(f, _):
            up_sum = jnp.zeros((width, depth), F32)
            down_sum = jnp.zeros((depth, width), F32)
            bias = jnp.zeros((1, depth), F32)
            for rowset in range(2):
                is_one = ones_of(rowset, depth)
                du_n = split(kept_tile(va, doa, rowset, f), is_one)[n]
                act_n = split(kept_tile(qa, ka, rowset, f), is_one)[n]
                up_sum = up_sum + mm_left(e_all[rowset], du_n)
                down_sum = down_sum + mm_left(act_n, gf_of(rowset))
                bias = bias + col_sum(du_n.astype(F32))
            per = pieces // 4
            down_rows = depth // strip
            for m in range(per):
                row, col = m % down_rows, m // down_rows
                shares[2 * n * per + m, f] = up_sum[m * strip : (m + 1) * strip, :].astype(BF)
                shares[(2 * n + 1) * per + m, f] = down_sum[
                    row * strip : (row + 1) * strip, col * depth : (col + 1) * depth
                ].astype(BF)
            row = 8 + n * 4 + half * 2 + lax.div(f, 2)
            col = pl.ds(pl.multiple_of(lax.rem(f, 2) * depth, depth), depth)
            vec[0, pl.ds(row, 1), col] = bias
            return 0

        lax.fori_loop(0, tiles, weights, 0)

    expert_weights(0)
    ticks(0, TICKS[0])
    low_grad[...] = folded(branch(1)).astype(BF)
    swaps[2].start()
    none, one = split(gf_of(0).astype(F32), ones_of(0, width))
    vec[0, 6:7, :] = col_sum(none)
    vec[0, 7:8, :] = col_sum(one)
    swaps[1].wait()

    def do2_copy(target):
        return push(st_do.at[target], rv_do.at[me], s_do2, r_do2, (grp, target))

    cross_out = jnp.zeros((width, width), F32)
    for mb in range(micro):
        unit, inverse = norm_parts(x_buf[mb])
        grad = gx1_ref[mb] + got_y[mb].astype(F32)
        vec[0, 4:5, :] += col_sum(grad * unit)
        vec[0, 5:6, :] += col_sum(grad)
        gx2 = c_buf[mb].astype(F32) + norm_back(unit, inverse, gain3[...], grad)
        gx2_ref[mb] = gx2
        gy2 = gx2.astype(BF)
        back = mm_right(gy2, co[...]).astype(BF)
        for p in range(pairs):
            st_do[mb * pairs + p] = back[:, p * lanes : (p + 1) * lanes]

        def send(p, _, mb=mb):
            target = mb * pairs + p

            @pl.when(target != me)
            def _():
                do2_copy(target).start()

            @pl.when(target == me)
            def _():
                rv_do[me] = st_do[me]

            return 0

        lax.fori_loop(0, pairs, send, 0)
        mixed = jnp.concatenate([o_buf[mb * pairs + p] for p in range(pairs)], axis=1)
        cross_out = cross_out + mm_left(mixed, gy2)
    early[0:width, :] = cross_out.astype(BF)
    expert_weights(1)
    ticks(TICKS[0], TICKS[1])
    gx1_ref[...] = folded(
        branch(0) + jnp.where(ones_of(0, width), down_b[1:2, :], down_b[0:1, :])
    )
    streams = [load(src, stream, 11 + n) for n, src in enumerate((m_in, a_in))]
    streams[0].start()
    loads = load_three((qa2_in, ka2_in, va2_in), 0)
    for one in loads:
        one.start()
    swaps[2].wait()
    for mb in range(micro):
        block_out[mb] = (x_buf[mb] + gx1_ref[mb] + got_y[2 + mb].astype(F32)).astype(BF)
    in_loads = [
        load(src, dst, 13 + n)
        for n, (src, dst) in enumerate(((x1_in, x_buf), (c_in, c_buf), (tokens_in, t_buf), (o1_own, o_buf)))
    ]
    for one in in_loads:
        one.start()
    wait_in(rv_do.at[pl.ds(0, parts - 1)], r_do2, to_y)
    wait_out(st_do.at[pl.ds(0, parts - 1)], s_do2, to_y)
    for one in loads:
        one.wait()

    def clear(s, _):
        part = pl.ds(pl.multiple_of(s * rows, rows), rows)
        for h in range(2):
            dk_acc[h, part, :] = jnp.zeros((rows, lanes), F32)
            dv_acc[h, part, :] = jnp.zeros((rows, lanes), F32)
            dq_acc[h, part, :] = jnp.zeros((rows, lanes), F32)
        return 0

    def grad_features(grads, mixed, head):
        own, place = lanes_of(grads.shape, head)
        grads = grads.astype(F32)
        delta = jnp.sum(jnp.where(own, grads * mixed.astype(F32), 0.0), axis=1, keepdims=True)
        high, middle, low = three_parts(delta)
        other = jnp.where(place == 0, -high, 0.0)
        other = jnp.where(place == 1, -middle, other)
        other = jnp.where(place == 2, -low, other)
        return jnp.where(own, grads, other).astype(BF)

    def tile(query, grads, keys, values, mask):
        scores = mm_right(keys, query)
        if mask is not None:
            scores = jnp.where(mask, scores, HIDE)
        prob = jnp.exp(scores)
        back = mm_right(values, grads)
        score_grad = (prob * back).astype(BF)
        return (
            mm_left(score_grad, keys),
            mm(score_grad, query),
            mm(prob.astype(BF), grads),
        )

    def join(zero_head, one_head):
        own, _ = lanes_of(zero_head.shape, 0)
        return jnp.where(own, zero_head, one_head)

    lax.fori_loop(0, parts, clear, 0)

    chunk = 2 * rows
    def cross_block(k, _):
        t = lax.rem(me + 1 + k, parts)
        part = pl.ds(pl.multiple_of(t * rows, rows), rows)
        grads = [grad_features(rv_do[t], o2[t], h) for h in range(2)]
        queries = [qa[h, part, :] for h in range(2)]
        sums = [jnp.zeros((rows, lanes), F32)] * 2
        for n in range(length // chunk):
            keys = slice(n * chunk, (n + 1) * chunk)
            for h in range(2):
                dq, dk, dv = tile(queries[h], grads[h], ka[h, keys, :], va[h, keys, :], None)
                sums[h] = sums[h] + dq
                dk_acc[h, keys, :] += dk
                dv_acc[h, keys, :] += dv
        st_do[t] = (join(sums[0], sums[1]) * scaling).astype(BF)

        @pl.when(k < parts - 1)
        def _():
            a2a(st_do, rv_dq2, s_dq2, r_dq2, t).start()

        @pl.when(k == parts - 1)
        def _():
            rv_dq2[me] = st_do[me]

        @pl.when(lax.rem(k, 2) == 0)
        def _():
            ticks(TICKS[0] + TICKS[1] + lax.div(k, 2) * TICKS[2], TICKS[2])

        return 0

    lax.fori_loop(0, parts, cross_block, 0)

    loads = load_three((qa1_in, ka1_in, va1_in), 1)
    for load in loads:
        load.start()

    def cross_source(s, total):
        part = pl.ds(pl.multiple_of(s * rows, rows), rows)
        grads = jnp.concatenate(
            [join(dk_acc[0, part, :], dk_acc[1, part, :]), join(dv_acc[0, part, :], dv_acc[1, part, :])], axis=1
        )
        return total + mm_left(stream[s], grads.astype(BF))

    all_arrived(rv_dq2, r_dq2)
    wait_out(st_do.at[pl.ds(0, parts - 1)], s_dq2, to_y)
    for one in in_loads:
        one.wait()

    def gathered(ref, mb, first):
        return jnp.concatenate(
            [ref[mb * pairs + p, first * rows : (first + 1) * rows, :] for p in range(pairs)], axis=1
        )

    def second_back(mb, _):
        dq2 = gathered(rv_dq2, mb, 0)
        dc = mm_right(dq2, cq[...])
        unit, inverse = norm_parts(x_buf[mb])
        vec[0, 2:3, :] += col_sum(dc * unit)
        vec[0, 3:4, :] += col_sum(dc)
        gx1 = gx2_ref[mb] + norm_back(unit, inverse, gain2[...], dc)
        gx1_ref[mb] = gx1
        low_grad[mb] = gx1.astype(BF)
        back = mm_right(low_grad[mb], wo[...]).astype(BF)
        for p in range(pairs):
            st_do[mb * pairs + p] = back[:, p * lanes : (p + 1) * lanes]

        def send(p, _):
            target = mb * pairs + p

            @pl.when(target != me)
            def _():
                a2a(st_do, rv_do, s_do1, r_do1, target).start()

            @pl.when(target == me)
            def _():
                rv_do[me] = st_do[me]

            return 0

        lax.fori_loop(0, pairs, send, 0)
        return 0

    lax.fori_loop(0, micro, second_back, 0)
    ticks(TICKS[0] + TICKS[1] + 4 * TICKS[2], TICKS[3])
    streams[0].wait()
    sums = lax.fori_loop(0, parts, cross_source, jnp.zeros((width, 2 * lanes), F32))
    streams[1].start()
    for n in range(2):
        cross[n * width : (n + 1) * width, :] = sums[:, n * lanes : (n + 1) * lanes].astype(BF)

    total = jnp.zeros((width, width), F32)
    for mb in range(micro):
        total = total + mm_left(c_buf[mb], gathered(rv_dq2, mb, 0))
    early[width : 2 * width, :] = total.astype(BF)
    total = jnp.zeros((width, width), F32)
    for mb in range(micro):
        mixed = jnp.concatenate([o_buf[mb * pairs + p] for p in range(pairs)], axis=1)
        total = total + mm_left(mixed, low_grad[mb])
    early[2 * width : 3 * width, :] = total.astype(BF)
    early_step(0)
    cross_step(0)
    ticks(TICKS[0] + TICKS[1] + 4 * TICKS[2] + TICKS[3], TICKS[4])
    for load in loads:
        load.wait()

    early_step(1)
    cross_step(1)
    all_arrived(rv_do, r_do1)

    lax.fori_loop(0, parts, clear, 0)

    def build(s, _):
        part = pl.ds(pl.multiple_of(s * rows, rows), rows)
        for h in range(2):
            doa[h, part, :] = grad_features(rv_do[s], o1[s], h)
        return 0

    lax.fori_loop(0, parts, build, 0)

    def self_tile(i, j, mask):
        q_part = pl.ds(pl.multiple_of(i * chunk, chunk), chunk)
        k_part = pl.ds(pl.multiple_of(j * chunk, chunk), chunk)
        for h in range(2):
            dq, dk, dv = tile(
                qa[h, q_part, :], doa[h, q_part, :], ka[h, k_part, :], va[h, k_part, :], mask
            )
            dq_acc[h, q_part, :] += dq
            dk_acc[h, k_part, :] += dk
            dv_acc[h, k_part, :] += dv

    g_late[...] = jnp.zeros_like(g_late)
    streams[1].wait()

    def y_copy(j):
        return push(st_y.at[j], got_y.at[j], da_s.at[j], da_r.at[j], to_y)

    def near_copy(n):
        return push(st_near.at[n], got_near.at[n], da_s.at[4 + n], da_r.at[4 + n], to_near)

    def far_copy():
        return push(st_far, got_far, da_s.at[6], da_r.at[6], to_far)

    def near_step(j):
        y_copy(j).wait_recv()
        da_keep[j] = (da_keep[j].astype(F32) + got_y[j].astype(F32)).astype(BF)

        @pl.when(lax.rem(j, 2) != near_bit)
        def _():
            st_near[lax.div(j, 2)] = da_keep[j]
            near_copy(lax.div(j, 2)).start()

    def far_step(j):
        @pl.when(lax.rem(j, 2) == near_bit)
        def _():
            near_copy(lax.div(j, 2)).wait_recv()
            total = da_keep[j].astype(F32) + got_near[lax.div(j, 2)].astype(F32)

            @pl.when(j == place)
            def _():
                da_sum[batch] = total

            @pl.when(j != place)
            def _():
                st_far[...] = total.astype(BF)
                far_copy().start()

    def self_column(j, _):
        key_place = lax.broadcasted_iota(jnp.int32, (chunk, chunk), 0)
        query_place = lax.broadcasted_iota(jnp.int32, (chunk, chunk), 1)
        self_tile(j, j, key_place <= query_place)

        def below(i, _):
            self_tile(i, j, None)
            return 0

        lax.fori_loop(j + 1, length // chunk, below, 0)

        part = pl.ds(pl.multiple_of(j * chunk, chunk), chunk)
        grads = jnp.concatenate(
            [
                (join(acc[0, part, :], acc[1, part, :]) * factor).astype(BF)
                for acc, factor in ((dq_acc, scaling), (dk_acc, 1.0), (dv_acc, 1.0))
            ],
            axis=1,
        )
        da = (
            mm_right(grads[:, 0:lanes], wq[...])
            + mm_right(grads[:, lanes : 2 * lanes], wk[...])
            + mm_right(grads[:, 2 * lanes : 3 * lanes], wv[...])
        )
        odd = half == 1
        st_y[j] = jnp.where(odd, da[0:rows], da[rows : 2 * rows]).astype(BF)
        da_keep[j] = jnp.where(odd, da[rows : 2 * rows], da[0:rows]).astype(BF)
        y_copy(j).start()
        for n in range(chunk // rows):
            g_late[...] += mm_left(stream[j * (chunk // rows) + n], grads[n * rows : (n + 1) * rows])
        ticks(TICKS[0] + TICKS[1] + 4 * TICKS[2] + TICKS[3] + TICKS[4] + j * TICKS[5], TICKS[5])

        @pl.when(j >= 1)
        def _():
            near_step(j - 1)

        @pl.when(j >= 2)
        def _():
            far_step(j - 2)

        @pl.when(j == 0)
        def _():
            early_step(2)
            cross_step(2)

        @pl.when(j == 1)
        def _():
            early_step(3)
            cross_step(3)

        @pl.when(j == 2)
        def _():
            early_step(4)
            cross_step(4)

        @pl.when(j == 3)
        def _():
            early_step(5)
            cross_step(5)

        return 0

    lax.fori_loop(0, length // chunk, self_column, 0)
    after = TICKS[0] + TICKS[1] + 4 * TICKS[2] + TICKS[3] + TICKS[4] + 4 * TICKS[5]
    left = pieces + 6 * LAG - after
    share = [(n + 1) * left // 5 - n * left // 5 for n in range(5)]
    starts = [after + n * left // 5 for n in range(6)]
    for n in range(3):
        late[n * width : (n + 1) * width, :] = g_late[:, n * lanes : (n + 1) * lanes].astype(BF)
    late_step(0)
    near_step(3)
    late_step(1)
    early_step(6)
    cross_step(6)
    ticks(starts[0], share[0])
    far_step(2)
    late_step(2)
    far_step(3)
    early_step(7)
    cross_step(7)
    ticks(starts[1], share[1])
    late_step(3)
    early_step(8)

    def first_back(mb, _):
        da = da_sum[mb]
        unit, inverse = norm_parts(t_buf[mb].astype(F32))
        vec[0, 0:1, :] += col_sum(da * unit)
        vec[0, 1:2, :] += col_sum(da)
        token_grad[mb] = gx1_ref[mb] + norm_back(unit, inverse, gain1[...], da)
        return 0

    first_back(batch, 0)
    late_step(4)
    ticks(starts[2], share[2])
    far_copy().wait_recv()
    da_sum[1 - batch] = got_far[...].astype(F32)
    first_back(1 - batch, 0)
    vec_step(0)
    late_step(5)
    early_step(9)
    ticks(starts[3], share[3])
    late_step(6)
    vec_step(1)
    ticks(starts[4], share[4])
    late_step(7)
    vec_step(2)
    cross_step(8)
    early_step(10)
    late_step(8)
    vec_out[...] = vec[2]
    shares_done()
    for j in range(4):
        y_copy(j).wait_send()
    for n in range(2):
        near_copy(n).wait_send()
    far_copy().wait_send()
    wait_out(st_do.at[pl.ds(0, parts - 1)], s_do1, to_y)


def finish_kernel(shares, early, cross, late, up, down, *grads):
    strip = shares.shape[3]
    depth = shares.shape[4]
    for n in range(2):
        per = shares.shape[1] // 4
        for m in range(per):
            row, col = m % (depth // strip), m // (depth // strip)
            up[n, m * strip : (m + 1) * strip, :] = shares[0, 2 * n * per + m, 0].astype(F32)
            down[n, row * strip : (row + 1) * strip, col * depth : (col + 1) * depth] = shares[
                0, (2 * n + 1) * per + m, 0
            ].astype(F32)
    for n in range(3):
        grads[n][...] = early[n].astype(F32)
    lanes = late.shape[3]
    for source, refs in ((cross, grads[3:5]), (late, grads[5:8])):
        for n, ref in enumerate(refs):
            for p in range(source.shape[0]):
                ref[:, p * lanes : (p + 1) * lanes] = source[p, n].astype(F32)


def vmem_spec():
    return pl.BlockSpec(memory_space=pltpu.VMEM)


def fast_device(
    tokens, memory, expert_slot, doc_lengths, source_lengths, cotangent,
    norm1_gain, norm1_shift, self_query, self_key, self_value, self_out,
    norm2_gain, norm2_shift, cross_query, cross_key, cross_value, cross_out,
    norm3_gain, norm3_shift, up_weight, up_bias, down_weight, down_bias,
):
    micro, rows, width = tokens.shape
    parts = lax.axis_size("dp")
    pairs = HEADS // 2
    lanes = width // pairs
    length = parts * rows
    scaling = 1.0 / math.sqrt(width // HEADS)
    experts, _, hidden = up_weight.shape
    shape = jax.ShapeDtypeStruct
    dma, one = pltpu.SemaphoreType.DMA((parts,)), pltpu.SemaphoreType.DMA
    line = lambda v: v.reshape(1, width)

    aug = shape((2, length, lanes), BF)
    blocks = shape((parts, rows, lanes), BF)
    full = shape((micro, rows, width), F32)
    low = shape((micro, rows, width), BF)
    vec = shape((1, width), F32)
    square = shape((width, width), F32)
    buf = lambda n: pltpu.VMEM((parts, n * rows, lanes), BF)

    count = micro * rows
    marks = jnp.broadcast_to(expert_slot.reshape(count, 1).astype(BF), (count, lanes))
    wide_all = shape((parts, rows, width), BF)
    pair = lax.rem(lax.axis_index("dp"), pairs)
    columns = lambda v: lax.dynamic_slice_in_dim(v, pair * lanes, lanes, 1)
    mine_q, mine_k, mine_v, mine_ck, mine_cv = (
        columns(v) for v in (self_query, self_key, self_value, cross_key, cross_value)
    )
    outs1 = [wide_all, wide_all, full, low, full, blocks, blocks, aug, aug, aug, blocks, aug, aug, aug, blocks,
             low, shape((count, lanes), BF)]
    (a_all, m_all, x1, c, x2, o1_own, o2_own, qa1, ka1, va1, o1, qa2, ka2, va2, o2, gf_got, marks_got) = pl.pallas_call(
        functools.partial(forward_kernel, parts, pairs, rows, scaling),
        out_shape=outs1,
        in_specs=[pl.BlockSpec(memory_space=pltpu.SMEM)] * 2 + [vmem_spec()] * 16,
        out_specs=[vmem_spec()] * len(outs1),
        scratch_shapes=[pltpu.VMEM((micro, rows, width), BF), buf(1), buf(1)]
        + [dma] * 4 + [one, one, one, dma, one, one] + [pltpu.SemaphoreType.DMA((2,))] * 2,
        compiler_params=pltpu.CompilerParams(
            collective_id=1, has_side_effects=True, vmem_limit_bytes=VMEM_BYTES
        ),
        name="attend_forward",
    )(
        doc_lengths, source_lengths, tokens, memory, line(norm1_gain), line(norm1_shift),
        line(norm2_gain), line(norm2_shift), mine_q, mine_k, mine_v, self_out,
        cross_query, mine_ck, mine_cv, cross_out, cotangent, marks,
    )

    tiles = 4
    span = hidden // 2
    depth = span // tiles
    any_spec = pl.BlockSpec(memory_space=pl.ANY)
    pieces = 16
    strip = 4 * width // pieces
    vec_pack = shape((16, width), F32)
    wide = lambda dtype, *dims: pltpu.VMEM(dims, dtype)
    early_shape = shape((3 * width, width), BF)
    cross_shape, late_shape = shape((pairs, 2 * width, lanes), BF), shape((pairs, 3 * width, lanes), BF)
    all_shape = shape((2, pieces, tiles, strip, depth), BF)
    outs3 = [low, full, vec_pack, all_shape, early_shape, cross_shape, late_shape]
    acc = pltpu.VMEM((2, length, lanes), F32)
    aug_buf = pltpu.VMEM((2, length, lanes), BF)
    block_low = lambda *n: wide(BF, *n, rows, width)
    block_full = lambda *n: wide(F32, *n, rows, width)
    dmas = lambda *dims: pltpu.SemaphoreType.DMA(dims)
    block_out, token_grad, vec, all_shares, all_early, all_cross, all_late = pl.pallas_call(
        functools.partial(backward_kernel, parts, pairs, rows, scaling),
        out_shape=outs3,
        in_specs=[any_spec] * 2 + [vmem_spec()] * 2 + [any_spec] * 2 + [vmem_spec()] * 2
        + [any_spec, vmem_spec(), any_spec, vmem_spec(), vmem_spec()]
        + [any_spec] * 3 + [vmem_spec()] + [any_spec] * 3 + [vmem_spec()]
        + [any_spec] * 6 + [vmem_spec()] * 7,
        out_specs=[vmem_spec()] * 3 + [any_spec] * 4,
        scratch_shapes=[block_full(micro), block_low(micro), block_low(micro), buf(1),
                        wide(BF, 2, count, width), block_full(micro), buf(1), buf(1), buf(1), aug_buf, acc, acc, acc,
                        block_full(micro), block_low(micro), aug_buf, aug_buf, aug_buf,
                        block_low(parts), block_low(4), block_low(4), block_low(4),
                        block_low(2), block_low(2), block_low(), block_low(), block_full(micro),
                        wide(BF, pieces, tiles, strip, depth), wide(BF, pieces, tiles, strip, depth),
                        wide(BF, pieces, 3, strip, depth),
                        wide(BF, pieces, 2, strip, depth), wide(BF, 3 * width, width),
                        wide(BF, 2 * width, lanes), wide(BF, 3 * width, lanes)]
        + [wide(BF, (3 * width) >> (d + 1), width) for d in range(5)]
        + [wide(BF, (2 * width) >> (d + 1), lanes) for d in range(3)]
        + [wide(BF, (3 * width) >> (d + 1), lanes) for d in range(3)]
        + [wide(F32, 3, 16, width), wide(F32, 12, 16, width), wide(F32, width, 3 * lanes)]
        + [dmas(4), dmas(pieces, 3), dmas(pieces, 5), dmas(4), dmas(19)]
        + [dmas(10), dmas(10), dmas(8), dmas(8), dmas(8), dmas(8), dmas(2), dmas(2), dmas(3), dmas(3), dmas(7), dmas(7)]
        + [one] * 6,
        compiler_params=pltpu.CompilerParams(
            collective_id=3, has_side_effects=True, vmem_limit_bytes=VMEM_BYTES
        ),
        name="attend_backward",
    )(
        x2, o2_own, marks, marks_got, cotangent, gf_got, line(norm3_gain), line(norm3_shift),
        up_weight.reshape(experts, 4, width // 4, hidden), up_bias, down_weight, down_bias, cross_out,
        qa1, ka1, va1, o1, qa2, ka2, va2, o2, tokens, x1, c, a_all, m_all, o1_own,
        line(norm1_gain), line(norm2_gain), mine_q, mine_k, mine_v, self_out, cross_query,
    )

    steps = 2 * tiles
    height = width // steps
    outs4 = [shape(up_weight.shape, F32), shape(down_weight.shape, F32)] + [square] * 8
    up_total, down_total, g_co, g_cq, g_so, g_ck, g_cv, g_sq, g_sk, g_sv = pl.pallas_call(
        finish_kernel,
        grid=(steps,),
        out_shape=outs4,
        in_specs=[
            pl.BlockSpec((1, pieces, 1, strip, depth),
                         lambda i: (lax.div(i, tiles), 0, lax.rem(i, tiles), 0, 0)),
            pl.BlockSpec((3, height, width), lambda i: (0, i, 0)),
            pl.BlockSpec((pairs, 2, height, lanes), lambda i: (0, 0, i, 0)),
            pl.BlockSpec((pairs, 3, height, lanes), lambda i: (0, 0, i, 0)),
        ],
        out_specs=[
            pl.BlockSpec((experts, width, depth), lambda i: (0, 0, i)),
            pl.BlockSpec((experts, depth, width), lambda i: (0, i, 0)),
        ] + [pl.BlockSpec((height, width), lambda i: (i, 0))] * 8,
        compiler_params=pltpu.CompilerParams(vmem_limit_bytes=VMEM_BYTES),
        name="finish",
    )(
        all_shares, all_early.reshape(3, width, width),
        all_cross.reshape(pairs, 2, width, lanes), all_late.reshape(pairs, 3, width, lanes),
    )

    return (
        block_out, token_grad, vec[0], vec[1], g_sq, g_sk, g_sv, g_so, vec[2], vec[3],
        g_cq, g_ck, g_cv, g_co, vec[4], vec[5],
        up_total, vec[8:16].reshape(experts, hidden), down_total, vec[6:8],
    )


def solution(mesh):
    fits = dict(mesh.shape) == {"grp": 4, "dp": 8}
    return jax.shard_map(
        fast_device if fits else per_device,
        mesh=mesh,
        in_specs=(
            P(None, ("grp", "dp"), None),
            P(None, ("grp", "dp"), None),
            P(None, ("grp", "dp"), None),
            P(None, "grp", None),
            P(None, "grp", None),
            P(None, ("grp", "dp"), None),
            P(),
            P(),
            P(),
            P(),
            P(),
            P(),
            P(),
            P(),
            P(),
            P(),
            P(),
            P(),
            P(),
            P(),
            P("grp", None, None),
            P("grp", None),
            P("grp", None, None),
            P("grp", None),
        ),
        out_specs=(
            P(None, ("grp", "dp"), None),
            P(None, ("grp", "dp"), None),
            P(),
            P(),
            P(),
            P(),
            P(),
            P(),
            P(),
            P(),
            P(),
            P(),
            P(),
            P(),
            P(),
            P(),
            P("grp", None, None),
            P("grp", None),
            P("grp", None, None),
            P("grp", None),
        ),
        check_vma=False,
    )
```

```python
import functools
import math

import jax
import jax.numpy as jnp
from jax import lax
from jax.experimental import pallas as pl
from jax.experimental.pallas import tpu as pltpu
from jax.sharding import PartitionSpec as P

HEADS = 8
CAP = 160


masked_score = -1e30


def layer_norm(inputs, norm_gain, norm_shift):
    mean_row = jnp.mean(inputs, axis=-1, keepdims=True)
    centred = inputs - mean_row
    spread = jnp.mean(centred * centred, axis=-1, keepdims=True)
    return centred * lax.rsqrt(spread + 1e-05) * norm_gain + norm_shift


def doc_index(lengths, places):
    doc_ends = jnp.cumsum(lengths)
    return jnp.sum((places[:, None] >= doc_ends[None, :]).astype(jnp.int32), axis=1)


def product(left, right):
    return jnp.dot(left, right, preferred_element_type=jnp.float32)


def left_product(left, right):
    return jnp.einsum("nd,ne->de", left, right, preferred_element_type=jnp.float32)


def right_product(left, right):
    return jnp.einsum("nd,ed->ne", left, right, preferred_element_type=jnp.float32)


def exact_left(left, right):
    return jnp.einsum("nd,ne->de", left, right, precision=lax.Precision.HIGHEST)


def split_heads(matrix, head_count):
    return matrix.reshape(matrix.shape[0], head_count, matrix.shape[1] // head_count)


def attend_forward(queries, keys_all, values_all, allowed, head_count):
    scaling = 1.0 / math.sqrt(queries.shape[1] // head_count)
    scores = (
        jnp.einsum(
            "qhd,khd->hqk",
            split_heads(queries, head_count),
            split_heads(keys_all, head_count),
            preferred_element_type=jnp.float32,
        )
        * scaling
    )
    scores = jnp.where(allowed[None], scores, masked_score)
    maximum = jnp.max(scores, axis=-1, keepdims=True)
    exponent = jnp.exp(scores - maximum)
    totals = jnp.sum(exponent, axis=-1, keepdims=True)
    probability = (exponent / totals).astype(jnp.bfloat16)
    mixed = jnp.einsum(
        "hqk,khd->qhd",
        probability,
        split_heads(values_all, head_count),
        preferred_element_type=jnp.float32,
    )
    return (mixed.reshape(queries.shape[0], queries.shape[1]), maximum + jnp.log(totals))


def score_parts(
    query_heads, key_heads, value_heads, grad_heads, allowed, scaling, log_total, centre
):
    scores = (
        jnp.einsum("qhd,khd->hqk", query_heads, key_heads, preferred_element_type=jnp.float32)
        * scaling
    )
    scores = jnp.where(allowed[None], scores, masked_score)
    probability = jnp.exp(scores - log_total)
    prob_grad = jnp.einsum(
        "qhd,khd->hqk", grad_heads, value_heads, preferred_element_type=jnp.float32
    )
    centre = jnp.sum(probability * prob_grad, axis=-1, keepdims=True)
    score_grad = (probability * (prob_grad - centre)).astype(jnp.bfloat16)
    return (probability, score_grad, centre)


def attend_backward(queries, keys_all, values_all, allowed, head_count, log_total, out_grad):
    scaling = 1.0 / math.sqrt(queries.shape[1] // head_count)
    query_heads = split_heads(queries, head_count)
    key_heads = split_heads(keys_all, head_count)
    grad_heads = split_heads(out_grad, head_count)
    probability, score_grad, centre = score_parts(
        query_heads,
        key_heads,
        split_heads(values_all, head_count),
        grad_heads,
        allowed,
        scaling,
        log_total,
        None,
    )
    query_back = (
        jnp.einsum("hqk,khd->qhd", score_grad, key_heads, preferred_element_type=jnp.float32)
        * scaling
    )
    key_back = (
        jnp.einsum("hqk,qhd->khd", score_grad, query_heads, preferred_element_type=jnp.float32)
        * scaling
    )
    value_back = jnp.einsum(
        "hqk,qhd->khd",
        probability.astype(jnp.bfloat16),
        grad_heads,
        preferred_element_type=jnp.float32,
    )
    width = queries.shape[1]
    return (
        query_back.reshape(queries.shape[0], width),
        key_back.reshape(keys_all.shape[0], width),
        value_back.reshape(keys_all.shape[0], width),
    )


def per_device(
    tokens,
    memory,
    expert_slot,
    doc_lengths,
    source_lengths,
    cotangent,
    norm1_gain,
    norm1_shift,
    self_query,
    self_key,
    self_value,
    self_out,
    norm2_gain,
    norm2_shift,
    cross_query,
    cross_key,
    cross_value,
    cross_out,
    norm3_gain,
    norm3_shift,
    up_weight,
    up_bias,
    down_weight,
    down_bias,
):
    micro = tokens.shape[0]
    rows = tokens.shape[1]
    width = tokens.shape[2]
    source_rows = memory.shape[1]
    parts = lax.axis_size("dp")
    place = lax.axis_index("dp")
    experts_here = up_weight.shape[0]
    capacity = CAP
    head_count = HEADS
    local_places = place * rows + jnp.arange(rows, dtype=jnp.int32)
    stream_places = jnp.arange(rows * parts, dtype=jnp.int32)
    source_places = jnp.arange(source_rows * parts, dtype=jnp.int32)
    slot_ids = jnp.arange(experts_here * capacity, dtype=jnp.int32)
    expert_ids = jnp.arange(experts_here, dtype=jnp.int32)
    inputs = tokens.astype(jnp.float32)
    normed_first, first_back = jax.vjp(layer_norm, inputs, norm1_gain, norm1_shift)
    attn_in = normed_first.astype(jnp.bfloat16)
    queries = product(attn_in, self_query).astype(jnp.bfloat16)
    keys_mine = product(attn_in, self_key).astype(jnp.bfloat16)
    values_mine = product(attn_in, self_value).astype(jnp.bfloat16)
    keys_all, values_all = (
        lax.all_gather(keys_mine, "dp", axis=1, tiled=True),
        lax.all_gather(values_mine, "dp", axis=1, tiled=True),
    )
    cross_keys_all, cross_values_all = (
        lax.all_gather(product(memory, cross_key).astype(jnp.bfloat16), "dp", axis=1, tiled=True),
        lax.all_gather(product(memory, cross_value).astype(jnp.bfloat16), "dp", axis=1, tiled=True),
    )
    square_zero = jnp.zeros((width, width), jnp.float32)
    vector_zero = jnp.zeros((width,), jnp.float32)
    grad_self_query, grad_self_key, grad_self_value, grad_self_out = (
        square_zero,
        square_zero,
        square_zero,
        square_zero,
    )
    grad_cross_query, grad_cross_key, grad_cross_value, grad_cross_out = (
        square_zero,
        square_zero,
        square_zero,
        square_zero,
    )
    second_gain_sum, second_shift_sum, third_gain_sum, third_shift_sum = (
        vector_zero,
        vector_zero,
        vector_zero,
        vector_zero,
    )
    grad_up = jnp.zeros(up_weight.shape, jnp.float32)
    grad_up_bias = jnp.zeros(up_bias.shape, jnp.float32)
    grad_down = jnp.zeros(down_weight.shape, jnp.float32)
    grad_down_bias = jnp.zeros(down_bias.shape, jnp.float32)
    outputs = []
    attn_in_grads = []
    resid_grads = []
    for batch_index in range(micro):
        lengths_now = doc_lengths[batch_index, 0]
        query_docs = doc_index(lengths_now, local_places)
        stream_docs = doc_index(lengths_now, stream_places)
        source_docs = doc_index(source_lengths[batch_index, 0], source_places)
        self_allowed = (query_docs[:, None] == stream_docs[None, :]) & (
            stream_places[None, :] <= local_places[:, None]
        )
        cross_allowed = query_docs[:, None] == source_docs[None, :]
        self_result, self_log = attend_forward(
            queries[batch_index],
            keys_all[batch_index],
            values_all[batch_index],
            self_allowed,
            head_count,
        )
        self_mixed = self_result.astype(jnp.bfloat16)
        after_self = inputs[batch_index] + product(self_mixed, self_out)
        normed_second, second_back = jax.vjp(layer_norm, after_self, norm2_gain, norm2_shift)
        cross_in = normed_second.astype(jnp.bfloat16)
        cross_queries = product(cross_in, cross_query).astype(jnp.bfloat16)
        cross_result, cross_log = attend_forward(
            cross_queries,
            cross_keys_all[batch_index],
            cross_values_all[batch_index],
            cross_allowed,
            head_count,
        )
        cross_mixed = cross_result.astype(jnp.bfloat16)
        after_cross = after_self + product(cross_mixed, cross_out)
        normed_third, third_back = jax.vjp(layer_norm, after_cross, norm3_gain, norm3_shift)
        expert_in = normed_third.astype(jnp.bfloat16)
        chosen = expert_slot[batch_index, :, 0]
        one_hot = (chosen[:, None] == expert_ids[None, :]).astype(jnp.int32)
        ranks = jnp.sum((jnp.cumsum(one_hot, axis=0) - 1) * one_hot, axis=1)
        target = chosen * capacity + ranks
        dispatch = (slot_ids[:, None] == target[None, :]).astype(jnp.bfloat16)
        buffer_in = (
            product(dispatch, expert_in).astype(jnp.bfloat16).reshape(experts_here, capacity, width)
        )
        pre_act = (
            jnp.einsum("ecd,edf->ecf", buffer_in, up_weight, preferred_element_type=jnp.float32)
            + up_bias[:, None, :]
        )
        activated, gelu_back = jax.vjp(jax.nn.gelu, pre_act)
        hidden = activated.astype(jnp.bfloat16)
        buffer_out = (
            jnp.einsum("ecf,efd->ecd", hidden, down_weight, preferred_element_type=jnp.float32)
            + down_bias[:, None, :]
        )
        expert_out = jnp.take(buffer_out.reshape(experts_here * capacity, width), target, axis=0)
        outputs.append((after_cross + expert_out).astype(jnp.bfloat16))
        out_grad = cotangent[batch_index].astype(jnp.float32)
        grad_rows = out_grad.astype(jnp.bfloat16)
        buffer_grad = (
            product(dispatch, grad_rows).astype(jnp.bfloat16).reshape(experts_here, capacity, width)
        )
        grad_down = grad_down + jnp.einsum(
            "ecf,ecd->efd", hidden, buffer_grad, preferred_element_type=jnp.float32
        )
        grad_down_bias = grad_down_bias + jnp.sum(buffer_grad.astype(jnp.float32), axis=1)
        hidden_grad = jnp.einsum(
            "ecd,efd->ecf", buffer_grad, down_weight, preferred_element_type=jnp.float32
        )
        pre_grad = gelu_back(hidden_grad)[0].astype(jnp.bfloat16)
        grad_up = grad_up + jnp.einsum(
            "ecd,ecf->edf", buffer_in, pre_grad, preferred_element_type=jnp.float32
        )
        grad_up_bias = grad_up_bias + jnp.sum(pre_grad.astype(jnp.float32), axis=1)
        buffer_back = jnp.einsum(
            "ecf,edf->ecd", pre_grad, up_weight, preferred_element_type=jnp.float32
        )
        expert_in_grad = jnp.take(
            buffer_back.reshape(experts_here * capacity, width), target, axis=0
        )
        third_resid, third_gain, third_shift = third_back(expert_in_grad)
        third_gain_sum = third_gain_sum + third_gain
        third_shift_sum = third_shift_sum + third_shift
        cross_grad = out_grad + third_resid
        cross_rows_grad = cross_grad.astype(jnp.bfloat16)
        grad_cross_out = grad_cross_out + left_product(cross_mixed, cross_rows_grad)
        cross_mixed_grad = right_product(cross_rows_grad, cross_out).astype(jnp.bfloat16)
        cross_query_back, cross_key_back, cross_value_back = attend_backward(
            cross_queries,
            cross_keys_all[batch_index],
            cross_values_all[batch_index],
            cross_allowed,
            head_count,
            cross_log,
            cross_mixed_grad,
        )
        cross_query_low = cross_query_back.astype(jnp.bfloat16)
        grad_cross_query = grad_cross_query + left_product(cross_in, cross_query_low)
        cross_key_mine, cross_value_mine = (
            lax.psum_scatter(
                cross_key_back.astype(jnp.bfloat16), "dp", scatter_dimension=0, tiled=True
            ).astype(jnp.float32),
            lax.psum_scatter(
                cross_value_back.astype(jnp.bfloat16), "dp", scatter_dimension=0, tiled=True
            ).astype(jnp.float32),
        )
        source_exact = memory[batch_index].astype(jnp.float32)
        grad_cross_key = grad_cross_key + exact_left(source_exact, cross_key_mine)
        grad_cross_value = grad_cross_value + exact_left(source_exact, cross_value_mine)
        second_resid, second_gain, second_shift = second_back(
            right_product(cross_query_low, cross_query)
        )
        second_gain_sum = second_gain_sum + second_gain
        second_shift_sum = second_shift_sum + second_shift
        self_grad = cross_grad + second_resid
        self_rows_grad = self_grad.astype(jnp.bfloat16)
        grad_self_out = grad_self_out + left_product(self_mixed, self_rows_grad)
        self_mixed_grad = right_product(self_rows_grad, self_out).astype(jnp.bfloat16)
        self_query_back, self_key_back, self_value_back = attend_backward(
            queries[batch_index],
            keys_all[batch_index],
            values_all[batch_index],
            self_allowed,
            head_count,
            self_log,
            self_mixed_grad,
        )
        self_key_mine, self_value_mine = (
            lax.psum_scatter(
                self_key_back.astype(jnp.bfloat16), "dp", scatter_dimension=0, tiled=True
            ).astype(jnp.float32),
            lax.psum_scatter(
                self_value_back.astype(jnp.bfloat16), "dp", scatter_dimension=0, tiled=True
            ).astype(jnp.float32),
        )
        query_low = self_query_back.astype(jnp.bfloat16)
        key_low = self_key_mine.astype(jnp.bfloat16)
        value_low = self_value_mine.astype(jnp.bfloat16)
        grad_self_query = grad_self_query + left_product(attn_in[batch_index], query_low)
        grad_self_key = grad_self_key + left_product(attn_in[batch_index], key_low)
        grad_self_value = grad_self_value + left_product(attn_in[batch_index], value_low)
        attn_in_grads.append(
            right_product(query_low, self_query)
            + right_product(key_low, self_key)
            + right_product(value_low, self_value)
        )
        resid_grads.append(self_grad)
    first_resid, first_gain, first_shift = first_back(jnp.stack(attn_in_grads))
    token_grad = jnp.stack(resid_grads) + first_resid
    block_out = jnp.stack(outputs)
    up_share, up_bias_share, down_share, down_bias_share = (
        lax.psum_scatter(
            grad_up.astype(jnp.bfloat16), "dp", scatter_dimension=2, tiled=True
        ).astype(jnp.float32),
        lax.psum_scatter(
            grad_up_bias.astype(jnp.bfloat16), "dp", scatter_dimension=1, tiled=True
        ).astype(jnp.float32),
        lax.psum_scatter(
            grad_down.astype(jnp.bfloat16), "dp", scatter_dimension=1, tiled=True
        ).astype(jnp.float32),
        lax.psum_scatter(
            grad_down_bias.astype(jnp.bfloat16), "dp", scatter_dimension=1, tiled=True
        ).astype(jnp.float32),
    )
    up_total, up_bias_total, down_total, down_bias_total = (
        lax.all_gather(up_share.astype(jnp.bfloat16), "dp", axis=2, tiled=True).astype(
            up_share.dtype
        ),
        lax.all_gather(up_bias_share.astype(jnp.bfloat16), "dp", axis=1, tiled=True).astype(
            up_bias_share.dtype
        ),
        lax.all_gather(down_share.astype(jnp.bfloat16), "dp", axis=1, tiled=True).astype(
            down_share.dtype
        ),
        lax.all_gather(down_bias_share.astype(jnp.bfloat16), "dp", axis=1, tiled=True).astype(
            down_bias_share.dtype
        ),
    )
    shared = lax.psum(
        (
            first_gain,
            first_shift,
            grad_self_query,
            grad_self_key,
            grad_self_value,
            grad_self_out,
            second_gain_sum,
            second_shift_sum,
            grad_cross_query,
            grad_cross_key,
            grad_cross_value,
            grad_cross_out,
            third_gain_sum,
            third_shift_sum,
        ),
        ("grp", "dp"),
    )
    return (
        block_out,
        token_grad,
        shared[0],
        shared[1],
        shared[2],
        shared[3],
        shared[4],
        shared[5],
        shared[6],
        shared[7],
        shared[8],
        shared[9],
        shared[10],
        shared[11],
        shared[12],
        shared[13],
        up_total,
        up_bias_total,
        down_total,
        down_bias_total,
    )


MESH = pl.DeviceIdType.MESH
BF = jnp.bfloat16
F32 = jnp.float32
VMEM_BYTES = 56 * 1024 * 1024
HIDE = -1e30


def mm(left, right):
    return lax.dot_general(left, right, (((1,), (0,)), ((), ())), preferred_element_type=F32)


def mm_right(left, right):
    return lax.dot_general(left, right, (((1,), (1,)), ((), ())), preferred_element_type=F32)


def mm_left(left, right):
    return lax.dot_general(left, right, (((0,), (0,)), ((), ())), preferred_element_type=F32)


def norm_parts(inputs):
    mean_row = jnp.mean(inputs, axis=-1, keepdims=True)
    centred = inputs - mean_row
    spread = jnp.mean(centred * centred, axis=-1, keepdims=True)
    inverse = lax.rsqrt(spread + 1e-05)
    return centred * inverse, inverse


def norm_back(unit, inverse, gain, grad):
    scaled = grad * gain
    first = jnp.mean(scaled, axis=-1, keepdims=True)
    second = jnp.mean(scaled * unit, axis=-1, keepdims=True)
    return inverse * (scaled - first - unit * second)


def col_sum(values):
    return jnp.sum(values, axis=0, keepdims=True)


def three_parts(values):
    high = values.astype(BF).astype(F32)
    rest = values - high
    middle = rest.astype(BF).astype(F32)
    return high, middle, rest - middle


def doc_of(lengths_ref, batch, positions):
    total = jnp.int32(0)
    docs = jnp.zeros(positions.shape, jnp.int32)
    for j in range(lengths_ref.shape[2]):
        total = total + lengths_ref[batch, 0, j]
        docs = docs + (positions >= total).astype(jnp.int32)
    return docs


def lanes_of(shape, head):
    lane = lax.broadcasted_iota(jnp.int32, shape, 1)
    half = shape[1] // 2
    own = (lane < half) if head == 0 else (lane >= half)
    return own, (lane - half if head == 0 else lane)


def greet(grp, me, parts):
    barrier = pltpu.get_barrier_semaphore()
    for k in range(1, parts):
        pl.semaphore_signal(
            barrier, inc=1, device_id=(grp, lax.rem(me + k, parts)), device_id_type=MESH
        )
    pl.semaphore_wait(barrier, parts - 1)


def sender(grp, src, dst, ssem, rsem, target):
    return pltpu.make_async_remote_copy(
        src_ref=src,
        dst_ref=dst,
        send_sem=ssem,
        recv_sem=rsem,
        device_id=(grp, target),
        device_id_type=MESH,
    )


def partner_of(grp, me, axis):
    place = lax.div(me, 2)
    if axis == "core":
        return grp + 1 - 2 * lax.rem(grp, 2), me
    if axis == "x":
        return lax.rem(grp + 2, 4), me
    if axis == "y":
        return grp, me + 1 - 2 * lax.rem(me, 2)
    if axis == "near":
        return grp, me + 2 - 4 * lax.rem(place, 2)
    return grp, lax.rem(me + 4, 8)


def push(src, dst, ssem, rsem, device):
    return pltpu.make_async_remote_copy(
        src_ref=src, dst_ref=dst, send_sem=ssem, recv_sem=rsem, device_id=device, device_id_type=MESH
    )


def wait_in(ref, sem, device):
    push(ref, ref, sem, sem, device).wait_recv()


def wait_out(ref, sem, device):
    push(ref, ref, sem, sem, device).wait_send()


def key_features(values, docs, head):
    own, place = lanes_of(values.shape, head)
    other = jnp.where(place == docs, 0.0, HIDE)
    other = jnp.where((place >= 4) & (place < 7), 1.0, other)
    return jnp.where(own, values.astype(F32), other).astype(BF)


def query_features(values, docs, head, scaling):
    own, place = lanes_of(values.shape, head)
    return jnp.where(
        own, values.astype(F32) * scaling, jnp.where(place == docs, 1.0, 0.0)
    ).astype(BF)


def value_features(values, head):
    own, _ = lanes_of(values.shape, head)
    return jnp.where(own, values.astype(F32), 1.0).astype(BF)


def forward_kernel(
    parts, pairs, rows, scaling,
    doc_len, src_len, tokens, memory, gain1, shift1, gain2, shift2,
    wq_in, wk_in, wv_in, wo, cq, ck_in, cv_in, co, cot, marks,
    a_out, m_out, x1_out, c_out, x2_out, o1_own, o2_own,
    qa1_out, ka1_out, va1_out, o1, qa2_out, ka2_out, va2_out, o2, gf_got, marks_got,
    a_all, m_all, qa1, ka1, va1, qa2, ka2, va2, wq, wk, wv, ck, cv, load_sem, out_sem,
    a_own, st_q2, rv_q2,
    s_a, r_a, s_m, r_m, s_o1, r_o1, s_q2, r_q2, s_o2, r_o2, s_y, r_y,
):
    grp = lax.axis_index("grp")
    me = lax.axis_index("dp")
    batch = lax.div(me, pairs)
    pair = lax.rem(me, pairs)
    micro = tokens.shape[0]
    lanes = 128
    low_half = batch == 0
    half = lax.rem(me, 2)
    place = lax.div(me, 2)
    inner = (place == 1) | (place == 2)
    to_y = partner_of(grp, me, "y")
    to_near = partner_of(grp, me, "near")
    entry = jnp.where(low_half, 4, 2) + half
    far_end = jnp.where(low_half, 6, 0) + half

    def a2a(src, dst, ssem, rsem, target):
        return sender(grp, src.at[target], dst.at[me], ssem, rsem.at[me], target)

    def arrived(dst, ssem, rsem, source):
        wait_in(dst.at[source], rsem.at[source], to_y)

    columns = pl.ds(pl.multiple_of(pair * lanes, lanes), lanes)
    loads = [
        pltpu.make_async_copy(src.at[:, columns], dst, load_sem.at[n])
        for n, (src, dst) in enumerate(
            ((wq_in, wq), (wk_in, wk), (wv_in, wv), (ck_in, ck), (cv_in, cv))
        )
    ]
    for load in loads:
        load.start()
    outs = [
        pltpu.make_async_copy(src, dst, out_sem.at[n])
        for n, (src, dst) in enumerate(
            (
                (a_all, a_out), (ka1, ka1_out), (va1, va1_out), (qa1, qa1_out),
                (m_all, m_out), (ka2, ka2_out), (va2, va2_out), (qa2, qa2_out),
            )
        )
    ]
    greet(grp, me, parts)

    def first_norm(mb, _):
        unit, _inv = norm_parts(tokens[mb].astype(F32))
        a_own[mb] = (unit * gain1[...] + shift1[...]).astype(BF)
        return 0

    lax.fori_loop(0, micro, first_norm, 0)

    def source_of(i):
        return jnp.where(i == 0, me, jnp.where(i == 1, to_near[1], jnp.where(i == 2, entry, far_end)))

    def spread_first(own, out, ssem, rsem):
        there = (grp, entry)
        return [
            push(own.at[batch], out.at[me], ssem.at[4], rsem.at[me], to_near),
            push(own.at[1 - batch], out.at[me], ssem.at[5], rsem.at[me], there),
        ]

    def spread_y(out, ssem, rsem, i):
        j = source_of(i)
        return push(out.at[j], out.at[j], ssem.at[i], rsem.at[j], to_y)

    def spread_near(out, ssem, rsem, i):
        j = source_of(i)
        return push(out.at[j], out.at[j], ssem.at[4 + i], rsem.at[j], to_near)

    def spread_start(own, out, ssem, rsem):
        for copy in spread_first(own, out, ssem, rsem):
            copy.start()
        out[me] = own[batch]
        spread_y(out, ssem, rsem, 0).start()

    def spread_on(out, ssem, rsem, i):
        arrived(out, ssem, rsem, source_of(i))
        spread_y(out, ssem, rsem, i).start()

        @pl.when(inner & (i >= 2))
        def _():
            spread_near(out, ssem, rsem, i).start()

    def spread_done(own, out, ssem, rsem):
        for copy in spread_first(own, out, ssem, rsem):
            copy.wait_send()
        for i in range(4):
            spread_y(out, ssem, rsem, i).wait_send()

        @pl.when(inner)
        def _():
            for i in (2, 3):
                spread_near(out, ssem, rsem, i).wait_send()

    def y_of(i):
        return source_of(i) + 1 - 2 * half

    def build_self(j):
        r0 = pl.multiple_of(j * rows, rows)
        places = r0 + lax.broadcasted_iota(jnp.int32, (rows, lanes), 0)
        docs = doc_of(doc_len, batch, places)
        a = a_all[j]
        query, key, value = (mm(a, weight[...]).astype(BF) for weight in (wq, wk, wv))
        for h in range(2):
            qa1[h, pl.ds(r0, rows), :] = query_features(query, docs, h, scaling)
            ka1[h, pl.ds(r0, rows), :] = key_features(key, docs, h)
            va1[h, pl.ds(r0, rows), :] = value_features(value, h)

    spread_start(a_own, a_all, s_a, r_a)
    for load in loads:
        load.wait()

    def same_y(i, _):
        @pl.when(i > 0)
        def _():
            spread_on(a_all, s_a, r_a, i)

        build_self(source_of(i))
        return 0

    def other_y(i, _):
        arrived(a_all, s_a, r_a, y_of(i))
        build_self(y_of(i))
        return 0

    lax.fori_loop(0, 4, same_y, 0)
    lax.fori_loop(0, 4, other_y, 0)
    spread_start(memory, m_all, s_m, r_m)
    for out in outs[0:3]:
        out.start()

    def finish(qa, r0, h, query, top, acc):
        own, place = lanes_of((rows, lanes), h)
        total = pltpu.roll(acc, lanes // 2, 1)
        high, middle, low = three_parts(top + jnp.log(acc))
        query = query.astype(F32)
        query = jnp.where(~own & (place == 4), -high, query)
        query = jnp.where(~own & (place == 5), -middle, query)
        query = jnp.where(~own & (place == 6), -low, query)
        qa[h, pl.ds(r0, rows), :] = query.astype(BF)
        return acc / total

    def emit(t, heads, out, own_ref, ssem, rsem):
        own, _ = lanes_of((rows, lanes), 0)
        out[t] = jnp.where(own, heads[0], heads[1]).astype(BF)

        @pl.when(t != me)
        def _():
            sender(grp, out.at[t], own_ref.at[me], ssem, rsem, t).start()

        @pl.when(t == me)
        def _():
            own_ref[me] = out[t]

    for e in range(parts // 2):
        reach = 2 * rows * (e + 1)
        cut = reach - 2 * rows

        def self_block(i, _, reach=reach, cut=cut, e=e):
            t = 2 * e + i
            r0 = pl.multiple_of(t * rows, rows)
            row = r0 + lax.broadcasted_iota(jnp.int32, (rows, 2 * rows), 0)
            col = cut + lax.broadcasted_iota(jnp.int32, (rows, 2 * rows), 1)
            heads = []
            for h in range(2):
                query = qa1[h, pl.ds(r0, rows), :]
                near = mm_right(query, ka1[h, cut:reach, :])
                near = jnp.where(col <= row, near, HIDE)
                top = jnp.max(near, axis=1, keepdims=True)
                if cut:
                    far = mm_right(query, ka1[h, 0:cut, :])
                    top = jnp.maximum(top, jnp.max(far, axis=1, keepdims=True))
                acc = mm(jnp.exp(near - top).astype(BF), va1[h, cut:reach, :])
                if cut:
                    acc = acc + mm(jnp.exp(far - top).astype(BF), va1[h, 0:cut, :])
                heads.append(finish(qa1, r0, h, query, top, acc))
            emit(t, heads, o1, o1_own, s_o1, r_o1)
            return 0

        lax.fori_loop(0, 2, self_block, 0)
        if e == 2:
            spread_on(m_all, s_m, r_m, 1)

    def own_wait(own_ref, ssem, rsem):
        wait_in(own_ref.at[pl.ds(0, parts - 1)], rsem, to_y)

    spread_on(m_all, s_m, r_m, 2)
    spread_on(m_all, s_m, r_m, 3)
    outs[3].start()
    own_wait(o1_own, s_o1, r_o1)

    def second_norm(mb, _):
        mixed = jnp.concatenate([o1_own[mb * pairs + p] for p in range(pairs)], axis=1)
        x1 = tokens[mb].astype(F32) + mm(mixed, wo[...])
        x1_out[mb] = x1
        unit, _inv = norm_parts(x1)
        c = (unit * gain2[...] + shift2[...]).astype(BF)
        c_out[mb] = c
        got = mm(c, cq[...]).astype(BF)
        for p in range(pairs):
            st_q2[mb * pairs + p] = got[:, p * lanes : (p + 1) * lanes]

        def send(p, _):
            target = mb * pairs + p

            @pl.when(target != me)
            def _():
                a2a(st_q2, rv_q2, s_q2, r_q2, target).start()

            @pl.when(target == me)
            def _():
                rv_q2[me] = st_q2[me]

            return 0

        lax.fori_loop(0, pairs, send, 0)
        return 0

    lax.fori_loop(0, micro, second_norm, 0)

    def build_cross(i, _):
        j = jnp.where(i < 4, source_of(i), y_of(i - 4))

        @pl.when(i >= 4)
        def _():
            arrived(m_all, s_m, r_m, j)

        r0 = pl.multiple_of(j * rows, rows)
        places = r0 + lax.broadcasted_iota(jnp.int32, (rows, lanes), 0)
        docs = doc_of(src_len, batch, places)
        source = m_all[j]
        key, value = (mm(source, weight[...]).astype(BF) for weight in (ck, cv))
        for h in range(2):
            ka2[h, pl.ds(r0, rows), :] = key_features(key, docs, h)
            va2[h, pl.ds(r0, rows), :] = value_features(value, h)
        return 0

    lax.fori_loop(0, parts, build_cross, 0)
    for out in outs[4:7]:
        out.start()

    swaps = [
        push(cot, gf_got, s_y.at[0], r_y.at[0], to_y),
        push(marks, marks_got, s_y.at[1], r_y.at[1], to_y),
    ]
    for swap in swaps:
        swap.start()

    def cross_block(k, _):
        t = lax.rem(me + k, parts)

        @pl.when(k > 0)
        def _():
            arrived(rv_q2, s_q2, r_q2, t)

        r0 = pl.multiple_of(t * rows, rows)
        places = r0 + lax.broadcasted_iota(jnp.int32, (rows, lanes), 0)
        docs = doc_of(doc_len, batch, places)
        heads = []
        for h in range(2):
            query = query_features(rv_q2[t], docs, h, scaling)
            scores = mm_right(query, ka2[h])
            top = jnp.max(scores, axis=1, keepdims=True)
            acc = mm(jnp.exp(scores - top).astype(BF), va2[h])
            heads.append(finish(qa2, r0, h, query, top, acc))
        emit(t, heads, o2, o2_own, s_o2, r_o2)
        return 0

    lax.fori_loop(0, parts, cross_block, 0)
    outs[7].start()
    own_wait(o2_own, s_o2, r_o2)

    def third(mb, _):
        mixed = jnp.concatenate([o2_own[mb * pairs + p] for p in range(pairs)], axis=1)
        x2_out[mb] = x1_out[mb] + mm(mixed, co[...])
        return 0

    lax.fori_loop(0, micro, third, 0)

    for ref, sem in ((st_q2, s_q2), (o1, s_o1), (o2, s_o2)):
        wait_out(ref.at[pl.ds(0, parts - 1)], sem, to_y)
    for swap in swaps:
        swap.wait()
    spread_done(a_own, a_all, s_a, r_a)
    spread_done(memory, m_all, s_m, r_m)
    for out in outs:
        out.wait()


def gelu_both(z):
    root = math.sqrt(2.0 / math.pi)
    square = z * z
    bent = jnp.tanh(root * z * (1.0 + 0.044715 * square))
    half = 0.5 * (1.0 + bent)
    slope = half + 0.5 * z * (1.0 - bent * bent) * (root * (1.0 + 3 * 0.044715 * square))
    return z * half, slope


LAG = 1
TICKS = (3, 3, 1, 1, 1, 1)


def backward_kernel(
    parts, pairs, rows, scaling,
    x2_in, o2_own, marks, marks_got, cot_in, gf_in, gain3, shift3, up_hbm, up_b, down_hbm, down_b, co,
    qa1_in, ka1_in, va1_in, o1, qa2_in, ka2_in, va2_in, o2,
    tokens_in, x1_in, c_in, a_in, m_in, o1_own, gain1, gain2,
    wq_in, wk_in, wv_in, wo, cq,
    block_out, token_grad, vec_out, all_shares, all_early, all_cross, all_late,
    wq, wk, wv, x_buf, c_buf, t_buf, o_buf, e_all, gx2_ref, st_do, rv_do, rv_dq2, doa, dq_acc, dk_acc, dv_acc, gx1_ref, low_grad,
    qa, ka, va, stream, da_keep, st_y, got_y, st_near, got_near, st_far, got_far, da_sum,
    shares, final, got_one, got_two, early, cross, late, *rest
):
    got_early, got_cross, got_late, rest = rest[:5], rest[5:8], rest[8:11], rest[11:]
    vec, got_vec, g_late, rest = *rest[:3], rest[3:]
    hop_s, hop_r, piece_r, local_sem, load_sem, rest = *rest[:5], rest[5:]
    early_s, early_r, cross_s, cross_r, late_s, late_r, vec_s, vec_r, rest = *rest[:8], rest[8:]
    swap_s, swap_r, da_s, da_r, s_do2, r_do2, s_dq2, r_dq2, s_do1, r_do1 = rest
    grp = lax.axis_index("grp")
    me = lax.axis_index("dp")
    micro, rows, width = x_buf.shape
    count = micro * rows
    span = up_b.shape[1] // 2
    lanes = 128
    length = parts * rows

    def a2a(src, dst, ssem, rsem, target):
        return sender(grp, src.at[target], dst.at[me], ssem, rsem, target)

    def all_arrived(dst, rsem):
        wait_in(dst.at[pl.ds(0, parts - 1)], rsem, partners[2])

    half = lax.rem(me, 2)
    near_bit = lax.rem(lax.div(me, 2), 2)
    far_bit = lax.div(me, 4)
    axes = ("core", "x", "y", "near", "far")
    place = lax.div(me, 2)
    batch = far_bit
    pair = lax.rem(me, pairs)
    inner = (place == 1) | (place == 2)
    bits = (lax.rem(grp, 2), lax.div(grp, 2), half, near_bit, far_bit)
    partners = [partner_of(grp, me, axis) for axis in axes]
    barrier = pltpu.get_barrier_semaphore()
    for k in range(1, parts):
        pl.semaphore_signal(
            barrier, inc=1, device_id=(grp, lax.rem(me + k, parts)), device_id_type=MESH
        )
    for k in range(1, 4):
        for f in range(2):
            there = (lax.rem(grp + k, 4), f * 4 + pair)
            pl.semaphore_signal(barrier, inc=1, device_id=there, device_id_type=MESH)

    pieces, tiles, strip, depth = shares.shape
    to_y, to_near, to_far = partners[2:]
    to_mid = (grp, (3 - place) * 2 + half)
    at_end = jnp.where(far_bit == 0, 0, 3)
    at_inner = jnp.where(far_bit == 0, 1, 2)
    at_next = 3 - at_inner
    at_last = 3 - at_end
    three = pl.ds(jnp.where(far_bit == 0, 1, 0), 3)
    away = pl.ds(jnp.where(far_bit == 0, 2, 0), 2)
    home = pl.ds(jnp.where(far_bit == 0, 0, 2), 2)

    def hop(s, n):
        rsem = hop_r.at[s, n]
        if n == 0:
            return push(shares.at[s, three], got_one.at[s], hop_s.at[0], rsem, to_near)
        if n == 1:
            return push(shares.at[s, away], got_two.at[s], hop_s.at[0], rsem, to_mid)
        return push(shares.at[s, at_end], got_two.at[s, 0], hop_s.at[0], rsem, to_near)

    def piece_on(s, n, piece, device):
        ref = final.at[s, piece]
        return push(ref, ref, hop_s.at[1], piece_r.at[s, n], device)

    def y_copy_of(s):
        return push(final.at[s], all_shares.at[half, s], hop_s.at[2], hop_s.at[3], to_y)

    def summed(s, piece, more):
        return (shares[s, piece].astype(F32) + more.astype(F32)).astype(BF)

    first_three = jnp.where(far_bit == 0, 1, 0)
    first_home = jnp.where(far_bit == 0, 0, 2)

    def share_step(s, stage):
        if stage == 0:

            @pl.when(~inner)
            def _():
                hop(s, 0).start()

        if stage == 1:

            @pl.when(inner)
            def _():
                hop(s, 0).wait_recv()
                for n in range(3):
                    shares[s, first_three + n] = summed(s, first_three + n, got_one[s, n])
                hop(s, 1).start()

        if stage == 2:

            @pl.when(inner)
            def _():
                hop(s, 1).wait_recv()
                shares[s, at_end] = summed(s, at_end, got_two[s, at_end - first_home])
                hop(s, 2).start()
                final[s, at_inner] = summed(s, at_inner, got_two[s, at_inner - first_home])
                piece_on(s, 0, at_inner, to_mid).start()
                piece_on(s, 1, at_inner, to_near).start()

        if stage == 3:

            @pl.when(~inner)
            def _():
                hop(s, 2).wait_recv()
                final[s, at_end] = summed(s, at_end, got_two[s, 0])
                piece_on(s, 2, at_end, to_near).start()

        if stage == 4:

            @pl.when(inner)
            def _():
                piece_on(s, 2, at_end, to_near).wait_recv()
                piece_on(s, 3, at_end, to_mid).start()

        if stage == 5:

            @pl.when(inner)
            def _():
                piece_on(s, 0, at_next, to_mid).wait_recv()
                piece_on(s, 3, at_last, to_mid).wait_recv()
                ref = final.at[s, away]
                push(ref, ref, hop_s.at[1], piece_r.at[s, 4], to_near).start()
                y_copy_of(s).start()

        if stage == 6:

            @pl.when(~inner)
            def _():
                piece_on(s, 1, at_inner, to_near).wait_recv()
                ref = final.at[s, away]
                push(ref, ref, hop_s.at[1], piece_r.at[s, 4], to_near).wait_recv()
                y_copy_of(s).start()

    def shares_done():
        out = pltpu.make_async_copy(final, all_shares.at[half], local_sem.at[3])
        out.start()
        wait_in(all_shares.at[1 - half], hop_s.at[3], to_y)
        wait_out(final, hop_s.at[2], to_y)

        @pl.when(inner)
        def _():
            wait_out(got_one, hop_s.at[0], to_y)
            wait_out(final, hop_s.at[1], to_y)
            wait_out(final.at[:, 0], hop_s.at[1], to_y)

        @pl.when(~inner)
        def _():
            wait_out(got_one, hop_s.at[0], to_y)
            wait_out(final.at[:, 0], hop_s.at[1], to_y)

        out.wait()

    def load_three(refs, n):
        return [
            pltpu.make_async_copy(src, dst, load_sem.at[5 + 3 * n + m])
            for m, (src, dst) in enumerate(zip(refs, (qa, ka, va)))
        ]

    def tick(i):
        for stage in range(7):
            s = i - LAG * stage
            if isinstance(s, int):
                if 0 <= s < pieces:
                    share_step(s, stage)
            else:

                @pl.when((s >= 0) & (s < pieces))
                def _(s=s, stage=stage):
                    share_step(s, stage)

    def ticks(start, count):
        def one(i, _):
            tick(start + i)
            return 0

        lax.fori_loop(0, count, one, 0)

    def seven(one):
        def body(k, _):
            one(k)
            return 0

        lax.fori_loop(1, 8, body, 0)

    slice_axes = (0, 1, 4)

    def slice_start(total, upto):
        start = jnp.int32(0)
        for d in range(upto):
            start = start + bits[slice_axes[d]] * (total >> (d + 1))
        return start

    def slice_rows(total, upto):
        return pl.ds(pl.multiple_of(slice_start(total, upto), total >> 3), total >> upto)

    def slice_copy(own, out, got, ssem, rsem, stage):
        total = own.shape[0]
        sems = (ssem.at[stage], rsem.at[stage])
        if stage < 3:
            axis = slice_axes[stage]
            size = total >> (stage + 1)
            start = slice_start(total, stage) + (1 - bits[axis]) * size
            part = pl.ds(pl.multiple_of(start, total >> 3), size)
            return push(own.at[part], got[stage], *sems, partners[axis])
        if stage == 3:
            part = slice_rows(total, 3)
            return push(own.at[part], out.at[pair, part], *sems, to_far)
        if stage == 4:
            ref = out.at[pair, slice_rows(total, 2)]
            return push(ref, ref, *sems, to_y)
        if stage == 5:
            ref = out.at[pl.ds(near_bit * 2, 2), slice_rows(total, 2)]
            return push(ref, ref, *sems, to_near)
        ref = out.at[:, slice_rows(total, 8 - stage)]
        return push(ref, ref, *sems, partners[7 - stage])

    def slice_local(own, out, sem):
        part = slice_rows(own.shape[0], 3)
        return pltpu.make_async_copy(own.at[part], out.at[pair, part], sem)

    def slice_step(own, out, got, ssem, rsem, sem, stage):
        total = own.shape[0]
        if stage >= 1:
            slice_copy(own, out, got, ssem, rsem, stage - 1).wait_recv()
        if 1 <= stage <= 3:
            part = slice_rows(total, stage)
            own[part, :] = (own[part, :].astype(F32) + got[stage - 1][...].astype(F32)).astype(BF)
        if stage == 3:
            slice_local(own, out, sem).start()
        if stage == 4:
            slice_local(own, out, sem).wait()
        if stage < 8:
            slice_copy(own, out, got, ssem, rsem, stage).start()
        if stage == 8:
            for n in range(8):
                slice_copy(own, out, got, ssem, rsem, n).wait_send()

    def cross_step(stage):
        slice_step(cross, all_cross, got_cross, cross_s, cross_r, local_sem.at[0], stage)

    def late_step(stage):
        slice_step(late, all_late, got_late, late_s, late_r, local_sem.at[1], stage)

    def offset_of(total, upto):
        start = jnp.int32(0)
        for d in range(upto):
            start = start + bits[d] * (total >> (d + 1))
        return start

    def rows_at(total, start, size):
        return pl.ds(pl.multiple_of(start, total >> 5), size)

    def early_copy(stage):
        total = early.shape[0]
        sems = (early_s.at[stage], early_r.at[stage])
        if stage < 5:
            size = total >> (stage + 1)
            start = offset_of(total, stage) + (1 - bits[stage]) * size
            return push(early.at[rows_at(total, start, size)], got_early[stage], *sems, partners[stage])
        d = 9 - stage
        part = rows_at(total, offset_of(total, d + 1), total >> (d + 1))
        src = early if stage == 5 else all_early
        return push(src.at[part], all_early.at[part], *sems, partners[d])

    def early_local():
        total = early.shape[0]
        part = rows_at(total, offset_of(total, 5), total >> 5)
        return pltpu.make_async_copy(early.at[part], all_early.at[part], local_sem.at[2])

    def early_step(stage):
        total = early.shape[0]
        if stage >= 1:
            early_copy(stage - 1).wait_recv()
        if 1 <= stage <= 5:
            part = rows_at(total, offset_of(total, stage), total >> stage)
            early[part, :] = (early[part, :].astype(F32) + got_early[stage - 1][...].astype(F32)).astype(BF)
        if stage == 5:
            early_local().start()
        if stage == 6:
            early_local().wait()
        if stage < 10:
            early_copy(stage).start()
        if stage == 10:
            for n in range(10):
                early_copy(n).wait_send()

    def vec_first(k):
        j = lax.rem(me + k, parts)
        return push(vec.at[0], got_vec.at[me], vec_s.at[0], vec_r.at[0], (grp, j))

    def vec_cross(k):
        other = lax.rem(grp + k, 4)
        return push(
            vec.at[1, 0:8], got_vec.at[8 + grp, 0:8], vec_s.at[1], vec_r.at[1], (other, me)
        )

    def vec_step(stage):
        if stage == 0:
            seven(lambda k: vec_first(k).start())
        if stage == 1:

            wait_in(got_vec.at[pl.ds(0, 7)], vec_r.at[0], to_y)

            def more(k, total):
                return total + got_vec[lax.rem(me + k, parts)]

            vec[1] = lax.fori_loop(1, 8, more, vec[0])
            for k in range(1, 4):
                vec_cross(k).start()
        if stage == 2:
            total = jnp.zeros((8, width), F32)
            wait_in(got_vec.at[pl.ds(0, 3), 0:8], vec_r.at[1], to_y)
            for k in range(1, 4):
                total = total + got_vec[8 + lax.rem(grp + k, 4), 0:8]
            row = lax.broadcasted_iota(jnp.int32, (8, width), 0)
            vec[2, 0:8] = vec[1, 0:8] + jnp.where(row < 6, total, 0.0)
            vec[2, 8:16] = vec[1, 8:16]
            wait_out(got_vec.at[pl.ds(0, 7)], vec_s.at[0], to_y)
            wait_out(got_vec.at[pl.ds(0, 3), 0:8], vec_s.at[1], to_y)

    first_col = pl.multiple_of(half * span, span)

    def load(src, dst, n):
        return pltpu.make_async_copy(src, dst, load_sem.at[n])

    in_loads = [
        load(src, dst, 13 + n)
        for n, (src, dst) in enumerate(((x2_in, x_buf), (cot_in, c_buf), (gf_in, t_buf), (o2_own, o_buf)))
    ]
    for one in in_loads:
        one.start()

    columns = pl.ds(pl.multiple_of(pair * lanes, lanes), lanes)
    pair_loads = [
        load(src.at[:, columns], dst, 19 + n)
        for n, (src, dst) in enumerate(((wq_in, wq), (wk_in, wk), (wv_in, wv)))
    ]
    for one in pair_loads:
        one.start()

    def weight_load(k, _):
        n, f = lax.div(k, tiles), lax.rem(k, tiles)
        cols = pl.ds(pl.multiple_of(first_col + f * depth, depth), depth)
        load(up_hbm.at[n, :, :, cols], final.at[k], 17).start()
        load(down_hbm.at[n, cols, :], stream.at[k], 18).start()
        return 0

    lax.fori_loop(0, 2 * tiles, weight_load, 0)
    vec[0] = jnp.zeros(vec.shape[1:], F32)
    in_loads[0].wait()
    for mb in range(micro):
        part = slice(mb * rows, (mb + 1) * rows)
        unit, _inv = norm_parts(x_buf[mb])
        e_all[0, part, :] = (unit * gain3[...] + shift3[...]).astype(BF)
    pl.semaphore_wait(barrier, parts + 5)
    swaps = [
        push(src, dst, swap_s.at[n], swap_r.at[n], to_y)
        for n, (src, dst) in enumerate(
            (
                (e_all.at[0], e_all.at[1]),
                (st_y.at[pl.ds(0, 2)], got_y.at[pl.ds(0, 2)]),
                (low_grad, got_y.at[pl.ds(2, 2)]),
            )
        )
    ]
    swaps[0].start()
    for one in in_loads[1:] + pair_loads:
        one.wait()
    load(final.at[pl.ds(0, 2 * tiles)], final.at[pl.ds(0, 2 * tiles)], 17).wait()
    load(stream, stream, 18).wait()
    mark_all = (marks, marks_got)
    gf_refs = (c_buf, t_buf)

    def up_tile(n, f):
        return final[n * tiles + f].reshape(width, depth)

    def down_tile(n, f):
        return stream[n * tiles + f]

    def gf_of(rowset):
        return jnp.concatenate([gf_refs[rowset][mb] for mb in range(micro)], axis=0)

    def folded(values):
        return values.reshape(micro, rows, width)

    def ones_of(rowset, wide):
        return jnp.concatenate([mark_all[rowset][...]] * (wide // lanes), axis=1) > 0.5

    def split(values, is_one):
        zero = jnp.zeros_like(values)
        return jnp.where(is_one, zero, values), jnp.where(is_one, values, zero)

    def kept_tile(low, high, rowset, f):
        part = pl.ds(pl.multiple_of(f * count, count), count)
        return jnp.concatenate([low[rowset, part, :], high[rowset, part, :]], axis=1)

    def through(rowset, acc):
        acc[...] = jnp.zeros_like(acc)

        def tile(f, _):
            bias_cols = pl.ds(pl.multiple_of(first_col + f * depth, depth), depth)
            is_one = ones_of(rowset, depth)
            e = e_all[rowset]
            gf = gf_of(rowset)
            u = jnp.where(
                is_one,
                mm(e, up_tile(1, f)) + up_b[1:2, bias_cols],
                mm(e, up_tile(0, f)) + up_b[0:1, bias_cols],
            )
            hidden, slope = gelu_both(u)
            part = pl.ds(pl.multiple_of(f * count, count), count)
            hidden = hidden.astype(BF)
            qa[rowset, part, :] = hidden[:, 0:lanes]
            ka[rowset, part, :] = hidden[:, lanes : 2 * lanes]
            back = jnp.where(is_one, mm_right(gf, down_tile(1, f)), mm_right(gf, down_tile(0, f)))
            du = (back * slope).astype(BF)
            va[rowset, part, :] = du[:, 0:lanes]
            doa[rowset, part, :] = du[:, lanes : 2 * lanes]
            none, one = split(du, is_one)
            acc[...] += folded(mm_right(none, up_tile(0, f)) + mm_right(one, up_tile(1, f)))
            return 0

        lax.fori_loop(0, tiles, tile, 0)

    def branch(rowset):
        is_one = ones_of(rowset, depth)

        def tile(f, total):
            none, one = split(kept_tile(qa, ka, rowset, f), is_one)
            return total + mm(none, down_tile(0, f)) + mm(one, down_tile(1, f))

        return lax.fori_loop(0, tiles, tile, jnp.zeros((count, width), F32))

    through(0, gx1_ref)
    swaps[0].wait()
    through(1, gx2_ref)
    st_y[0:2] = gx2_ref[...].astype(BF)
    swaps[1].start()

    def expert_weights(n):
        def weights(f, _):
            up_sum = jnp.zeros((width, depth), F32)
            down_sum = jnp.zeros((depth, width), F32)
            bias = jnp.zeros((1, depth), F32)
            for rowset in range(2):
                is_one = ones_of(rowset, depth)
                du_n = split(kept_tile(va, doa, rowset, f), is_one)[n]
                act_n = split(kept_tile(qa, ka, rowset, f), is_one)[n]
                up_sum = up_sum + mm_left(e_all[rowset], du_n)
                down_sum = down_sum + mm_left(act_n, gf_of(rowset))
                bias = bias + col_sum(du_n.astype(F32))
            per = pieces // 4
            down_rows = depth // strip
            for m in range(per):
                row, col = m % down_rows, m // down_rows
                shares[2 * n * per + m, f] = up_sum[m * strip : (m + 1) * strip, :].astype(BF)
                shares[(2 * n + 1) * per + m, f] = down_sum[
                    row * strip : (row + 1) * strip, col * depth : (col + 1) * depth
                ].astype(BF)
            row = 8 + n * 4 + half * 2 + lax.div(f, 2)
            col = pl.ds(pl.multiple_of(lax.rem(f, 2) * depth, depth), depth)
            vec[0, pl.ds(row, 1), col] = bias
            return 0

        lax.fori_loop(0, tiles, weights, 0)

    expert_weights(0)
    ticks(0, TICKS[0])
    low_grad[...] = folded(branch(1)).astype(BF)
    swaps[2].start()
    none, one = split(gf_of(0).astype(F32), ones_of(0, width))
    vec[0, 6:7, :] = col_sum(none)
    vec[0, 7:8, :] = col_sum(one)
    swaps[1].wait()

    def do2_copy(target):
        return push(st_do.at[target], rv_do.at[me], s_do2, r_do2, (grp, target))

    cross_out = jnp.zeros((width, width), F32)
    for mb in range(micro):
        unit, inverse = norm_parts(x_buf[mb])
        grad = gx1_ref[mb] + got_y[mb].astype(F32)
        vec[0, 4:5, :] += col_sum(grad * unit)
        vec[0, 5:6, :] += col_sum(grad)
        gx2 = c_buf[mb].astype(F32) + norm_back(unit, inverse, gain3[...], grad)
        gx2_ref[mb] = gx2
        gy2 = gx2.astype(BF)
        back = mm_right(gy2, co[...]).astype(BF)
        for p in range(pairs):
            st_do[mb * pairs + p] = back[:, p * lanes : (p + 1) * lanes]

        def send(p, _, mb=mb):
            target = mb * pairs + p

            @pl.when(target != me)
            def _():
                do2_copy(target).start()

            @pl.when(target == me)
            def _():
                rv_do[me] = st_do[me]

            return 0

        lax.fori_loop(0, pairs, send, 0)
        mixed = jnp.concatenate([o_buf[mb * pairs + p] for p in range(pairs)], axis=1)
        cross_out = cross_out + mm_left(mixed, gy2)
    early[0:width, :] = cross_out.astype(BF)
    expert_weights(1)
    ticks(TICKS[0], TICKS[1])
    gx1_ref[...] = folded(
        branch(0) + jnp.where(ones_of(0, width), down_b[1:2, :], down_b[0:1, :])
    )
    streams = [load(src, stream, 11 + n) for n, src in enumerate((m_in, a_in))]
    streams[0].start()
    loads = load_three((qa2_in, ka2_in, va2_in), 0)
    for one in loads:
        one.start()
    swaps[2].wait()
    for mb in range(micro):
        block_out[mb] = (x_buf[mb] + gx1_ref[mb] + got_y[2 + mb].astype(F32)).astype(BF)
    in_loads = [
        load(src, dst, 13 + n)
        for n, (src, dst) in enumerate(((x1_in, x_buf), (c_in, c_buf), (tokens_in, t_buf), (o1_own, o_buf)))
    ]
    for one in in_loads:
        one.start()
    wait_in(rv_do.at[pl.ds(0, parts - 1)], r_do2, to_y)
    wait_out(st_do.at[pl.ds(0, parts - 1)], s_do2, to_y)
    for one in loads:
        one.wait()

    def clear(s, _):
        part = pl.ds(pl.multiple_of(s * rows, rows), rows)
        for h in range(2):
            dk_acc[h, part, :] = jnp.zeros((rows, lanes), F32)
            dv_acc[h, part, :] = jnp.zeros((rows, lanes), F32)
            dq_acc[h, part, :] = jnp.zeros((rows, lanes), F32)
        return 0

    def grad_features(grads, mixed, head):
        own, place = lanes_of(grads.shape, head)
        grads = grads.astype(F32)
        delta = jnp.sum(jnp.where(own, grads * mixed.astype(F32), 0.0), axis=1, keepdims=True)
        high, middle, low = three_parts(delta)
        other = jnp.where(place == 0, -high, 0.0)
        other = jnp.where(place == 1, -middle, other)
        other = jnp.where(place == 2, -low, other)
        return jnp.where(own, grads, other).astype(BF)

    def tile(query, grads, keys, values, mask):
        scores = mm_right(keys, query)
        if mask is not None:
            scores = jnp.where(mask, scores, HIDE)
        prob = jnp.exp(scores)
        back = mm_right(values, grads)
        score_grad = (prob * back).astype(BF)
        return (
            mm_left(score_grad, keys),
            mm(score_grad, query),
            mm(prob.astype(BF), grads),
        )

    def join(zero_head, one_head):
        own, _ = lanes_of(zero_head.shape, 0)
        return jnp.where(own, zero_head, one_head)

    lax.fori_loop(0, parts, clear, 0)

    chunk = 2 * rows
    def cross_block(k, _):
        t = lax.rem(me + 1 + k, parts)
        part = pl.ds(pl.multiple_of(t * rows, rows), rows)
        grads = [grad_features(rv_do[t], o2[t], h) for h in range(2)]
        queries = [qa[h, part, :] for h in range(2)]
        sums = [jnp.zeros((rows, lanes), F32)] * 2
        for n in range(length // chunk):
            keys = slice(n * chunk, (n + 1) * chunk)
            for h in range(2):
                dq, dk, dv = tile(queries[h], grads[h], ka[h, keys, :], va[h, keys, :], None)
                sums[h] = sums[h] + dq
                dk_acc[h, keys, :] += dk
                dv_acc[h, keys, :] += dv
        st_do[t] = (join(sums[0], sums[1]) * scaling).astype(BF)

        @pl.when(k < parts - 1)
        def _():
            a2a(st_do, rv_dq2, s_dq2, r_dq2, t).start()

        @pl.when(k == parts - 1)
        def _():
            rv_dq2[me] = st_do[me]

        @pl.when(lax.rem(k, 2) == 0)
        def _():
            ticks(TICKS[0] + TICKS[1] + lax.div(k, 2) * TICKS[2], TICKS[2])

        return 0

    lax.fori_loop(0, parts, cross_block, 0)

    loads = load_three((qa1_in, ka1_in, va1_in), 1)
    for load in loads:
        load.start()

    def cross_source(s, total):
        part = pl.ds(pl.multiple_of(s * rows, rows), rows)
        grads = jnp.concatenate(
            [join(dk_acc[0, part, :], dk_acc[1, part, :]), join(dv_acc[0, part, :], dv_acc[1, part, :])], axis=1
        )
        return total + mm_left(stream[s], grads.astype(BF))

    all_arrived(rv_dq2, r_dq2)
    wait_out(st_do.at[pl.ds(0, parts - 1)], s_dq2, to_y)
    for one in in_loads:
        one.wait()

    def gathered(ref, mb, first):
        return jnp.concatenate(
            [ref[mb * pairs + p, first * rows : (first + 1) * rows, :] for p in range(pairs)], axis=1
        )

    def second_back(mb, _):
        dq2 = gathered(rv_dq2, mb, 0)
        dc = mm_right(dq2, cq[...])
        unit, inverse = norm_parts(x_buf[mb])
        vec[0, 2:3, :] += col_sum(dc * unit)
        vec[0, 3:4, :] += col_sum(dc)
        gx1 = gx2_ref[mb] + norm_back(unit, inverse, gain2[...], dc)
        gx1_ref[mb] = gx1
        low_grad[mb] = gx1.astype(BF)
        back = mm_right(low_grad[mb], wo[...]).astype(BF)
        for p in range(pairs):
            st_do[mb * pairs + p] = back[:, p * lanes : (p + 1) * lanes]

        def send(p, _):
            target = mb * pairs + p

            @pl.when(target != me)
            def _():
                a2a(st_do, rv_do, s_do1, r_do1, target).start()

            @pl.when(target == me)
            def _():
                rv_do[me] = st_do[me]

            return 0

        lax.fori_loop(0, pairs, send, 0)
        return 0

    lax.fori_loop(0, micro, second_back, 0)
    ticks(TICKS[0] + TICKS[1] + 4 * TICKS[2], TICKS[3])
    streams[0].wait()
    sums = lax.fori_loop(0, parts, cross_source, jnp.zeros((width, 2 * lanes), F32))
    streams[1].start()
    for n in range(2):
        cross[n * width : (n + 1) * width, :] = sums[:, n * lanes : (n + 1) * lanes].astype(BF)

    total = jnp.zeros((width, width), F32)
    for mb in range(micro):
        total = total + mm_left(c_buf[mb], gathered(rv_dq2, mb, 0))
    early[width : 2 * width, :] = total.astype(BF)
    total = jnp.zeros((width, width), F32)
    for mb in range(micro):
        mixed = jnp.concatenate([o_buf[mb * pairs + p] for p in range(pairs)], axis=1)
        total = total + mm_left(mixed, low_grad[mb])
    early[2 * width : 3 * width, :] = total.astype(BF)
    early_step(0)
    cross_step(0)
    ticks(TICKS[0] + TICKS[1] + 4 * TICKS[2] + TICKS[3], TICKS[4])
    for load in loads:
        load.wait()

    early_step(1)
    cross_step(1)
    all_arrived(rv_do, r_do1)

    lax.fori_loop(0, parts, clear, 0)

    def build(s, _):
        part = pl.ds(pl.multiple_of(s * rows, rows), rows)
        for h in range(2):
            doa[h, part, :] = grad_features(rv_do[s], o1[s], h)
        return 0

    lax.fori_loop(0, parts, build, 0)

    def self_tile(i, j, mask):
        q_part = pl.ds(pl.multiple_of(i * chunk, chunk), chunk)
        k_part = pl.ds(pl.multiple_of(j * chunk, chunk), chunk)
        for h in range(2):
            dq, dk, dv = tile(
                qa[h, q_part, :], doa[h, q_part, :], ka[h, k_part, :], va[h, k_part, :], mask
            )
            dq_acc[h, q_part, :] += dq
            dk_acc[h, k_part, :] += dk
            dv_acc[h, k_part, :] += dv

    g_late[...] = jnp.zeros_like(g_late)
    streams[1].wait()

    def y_copy(j):
        return push(st_y.at[j], got_y.at[j], da_s.at[j], da_r.at[j], to_y)

    def near_copy(n):
        return push(st_near.at[n], got_near.at[n], da_s.at[4 + n], da_r.at[4 + n], to_near)

    def far_copy():
        return push(st_far, got_far, da_s.at[6], da_r.at[6], to_far)

    def near_step(j):
        y_copy(j).wait_recv()
        da_keep[j] = (da_keep[j].astype(F32) + got_y[j].astype(F32)).astype(BF)

        @pl.when(lax.rem(j, 2) != near_bit)
        def _():
            st_near[lax.div(j, 2)] = da_keep[j]
            near_copy(lax.div(j, 2)).start()

    def far_step(j):
        @pl.when(lax.rem(j, 2) == near_bit)
        def _():
            near_copy(lax.div(j, 2)).wait_recv()
            total = da_keep[j].astype(F32) + got_near[lax.div(j, 2)].astype(F32)

            @pl.when(j == place)
            def _():
                da_sum[batch] = total

            @pl.when(j != place)
            def _():
                st_far[...] = total.astype(BF)
                far_copy().start()

    def self_column(j, _):
        key_place = lax.broadcasted_iota(jnp.int32, (chunk, chunk), 0)
        query_place = lax.broadcasted_iota(jnp.int32, (chunk, chunk), 1)
        self_tile(j, j, key_place <= query_place)

        def below(i, _):
            self_tile(i, j, None)
            return 0

        lax.fori_loop(j + 1, length // chunk, below, 0)

        part = pl.ds(pl.multiple_of(j * chunk, chunk), chunk)
        grads = jnp.concatenate(
            [
                (join(acc[0, part, :], acc[1, part, :]) * factor).astype(BF)
                for acc, factor in ((dq_acc, scaling), (dk_acc, 1.0), (dv_acc, 1.0))
            ],
            axis=1,
        )
        da = (
            mm_right(grads[:, 0:lanes], wq[...])
            + mm_right(grads[:, lanes : 2 * lanes], wk[...])
            + mm_right(grads[:, 2 * lanes : 3 * lanes], wv[...])
        )
        odd = half == 1
        st_y[j] = jnp.where(odd, da[0:rows], da[rows : 2 * rows]).astype(BF)
        da_keep[j] = jnp.where(odd, da[rows : 2 * rows], da[0:rows]).astype(BF)
        y_copy(j).start()
        for n in range(chunk // rows):
            g_late[...] += mm_left(stream[j * (chunk // rows) + n], grads[n * rows : (n + 1) * rows])
        ticks(TICKS[0] + TICKS[1] + 4 * TICKS[2] + TICKS[3] + TICKS[4] + j * TICKS[5], TICKS[5])

        @pl.when(j >= 1)
        def _():
            near_step(j - 1)

        @pl.when(j >= 2)
        def _():
            far_step(j - 2)

        @pl.when(j == 0)
        def _():
            early_step(2)
            cross_step(2)

        @pl.when(j == 1)
        def _():
            early_step(3)
            cross_step(3)

        @pl.when(j == 2)
        def _():
            early_step(4)
            cross_step(4)

        @pl.when(j == 3)
        def _():
            early_step(5)
            cross_step(5)

        return 0

    lax.fori_loop(0, length // chunk, self_column, 0)
    after = TICKS[0] + TICKS[1] + 4 * TICKS[2] + TICKS[3] + TICKS[4] + 4 * TICKS[5]
    left = pieces + 6 * LAG - after
    share = [(n + 1) * left // 5 - n * left // 5 for n in range(5)]
    starts = [after + n * left // 5 for n in range(6)]
    for n in range(3):
        late[n * width : (n + 1) * width, :] = g_late[:, n * lanes : (n + 1) * lanes].astype(BF)
    late_step(0)
    near_step(3)
    late_step(1)
    early_step(6)
    cross_step(6)
    ticks(starts[0], share[0])
    far_step(2)
    late_step(2)
    far_step(3)
    early_step(7)
    cross_step(7)
    ticks(starts[1], share[1])
    late_step(3)
    early_step(8)

    def first_back(mb, _):
        da = da_sum[mb]
        unit, inverse = norm_parts(t_buf[mb].astype(F32))
        vec[0, 0:1, :] += col_sum(da * unit)
        vec[0, 1:2, :] += col_sum(da)
        token_grad[mb] = gx1_ref[mb] + norm_back(unit, inverse, gain1[...], da)
        return 0

    first_back(batch, 0)
    late_step(4)
    ticks(starts[2], share[2])
    far_copy().wait_recv()
    da_sum[1 - batch] = got_far[...].astype(F32)
    first_back(1 - batch, 0)
    vec_step(0)
    late_step(5)
    early_step(9)
    ticks(starts[3], share[3])
    late_step(6)
    vec_step(1)
    ticks(starts[4], share[4])
    late_step(7)
    vec_step(2)
    cross_step(8)
    early_step(10)
    late_step(8)
    vec_out[...] = vec[2]
    shares_done()
    for j in range(4):
        y_copy(j).wait_send()
    for n in range(2):
        near_copy(n).wait_send()
    far_copy().wait_send()
    wait_out(st_do.at[pl.ds(0, parts - 1)], s_do1, to_y)


def finish_kernel(shares, early, cross, late, vec, up, down, up_bias, down_bias, *grads):
    per, strip, depth = shares.shape[1] // 4, shares.shape[3], shares.shape[4]
    for n in range(2):
        for m in range(per):
            row, col = m % (depth // strip), m // (depth // strip)
            up[n, m * strip : (m + 1) * strip, :] = shares[0, 2 * n * per + m, 0].astype(F32)
            down[n, row * strip : (row + 1) * strip, col * depth : (col + 1) * depth] = shares[
                0, (2 * n + 1) * per + m, 0
            ].astype(F32)
    width = vec.shape[1]
    for n in range(2):
        down_bias[n : n + 1, :] = vec[6 + n : 7 + n, :]
        for k in range(4):
            row = 8 + n * 4 + k
            up_bias[n : n + 1, k * width : (k + 1) * width] = vec[row : row + 1, :]
    for n in range(3):
        grads[n][...] = early[n].astype(F32)
    lanes = late.shape[3]
    for source, refs in ((cross, grads[3:5]), (late, grads[5:8])):
        for n, ref in enumerate(refs):
            for p in range(source.shape[0]):
                ref[:, p * lanes : (p + 1) * lanes] = source[p, n].astype(F32)


def vmem_spec():
    return pl.BlockSpec(memory_space=pltpu.VMEM)


def fast_device(
    tokens, memory, expert_slot, doc_lengths, source_lengths, cotangent,
    norm1_gain, norm1_shift, self_query, self_key, self_value, self_out,
    norm2_gain, norm2_shift, cross_query, cross_key, cross_value, cross_out,
    norm3_gain, norm3_shift, up_weight, up_bias, down_weight, down_bias,
):
    micro, rows, width = tokens.shape
    parts = lax.axis_size("dp")
    pairs = HEADS // 2
    lanes = width // pairs
    length = parts * rows
    scaling = 1.0 / math.sqrt(width // HEADS)
    experts, _, hidden = up_weight.shape
    shape = jax.ShapeDtypeStruct
    dma, one = pltpu.SemaphoreType.DMA((parts,)), pltpu.SemaphoreType.DMA
    line = lambda v: v.reshape(1, width)

    any_spec = pl.BlockSpec(memory_space=pl.ANY)
    aug = shape((2, length, lanes), BF)
    blocks = shape((parts, rows, lanes), BF)
    full = shape((micro, rows, width), F32)
    low = shape((micro, rows, width), BF)
    vec = shape((1, width), F32)
    square = shape((width, width), F32)
    buf = lambda n: pltpu.VMEM((parts, n * rows, lanes), BF)

    count = micro * rows
    marks = jnp.broadcast_to(expert_slot.reshape(count, 1).astype(BF), (count, lanes))
    wide_all = shape((parts, rows, width), BF)
    outs1 = [wide_all, wide_all, full, low, full, blocks, blocks, aug, aug, aug, blocks, aug, aug, aug, blocks,
             low, shape((count, lanes), BF)]
    (a_all, m_all, x1, c, x2, o1_own, o2_own, qa1, ka1, va1, o1, qa2, ka2, va2, o2, gf_got, marks_got) = pl.pallas_call(
        functools.partial(forward_kernel, parts, pairs, rows, scaling),
        out_shape=outs1,
        in_specs=[pl.BlockSpec(memory_space=pltpu.SMEM)] * 2 + [vmem_spec()] * 6 + [any_spec] * 3
        + [vmem_spec()] * 2 + [any_spec] * 2 + [vmem_spec()] * 3,
        out_specs=[any_spec] * 2 + [vmem_spec()] * 5
        + ([any_spec] * 3 + [vmem_spec()]) * 2 + [vmem_spec()] * 2,
        scratch_shapes=[pltpu.VMEM((parts, rows, width), BF)] * 2
        + [pltpu.VMEM((2, length, lanes), BF)] * 6 + [pltpu.VMEM((width, lanes), BF)] * 5
        + [pltpu.SemaphoreType.DMA((5,)), pltpu.SemaphoreType.DMA((8,))]
        + [pltpu.VMEM((micro, rows, width), BF), buf(1), buf(1)]
        + [dma] * 4 + [one, one, one, dma, one, one] + [pltpu.SemaphoreType.DMA((2,))] * 2,
        compiler_params=pltpu.CompilerParams(
            collective_id=1, has_side_effects=True, vmem_limit_bytes=VMEM_BYTES
        ),
        name="attend_forward",
    )(
        doc_lengths, source_lengths, tokens, memory, line(norm1_gain), line(norm1_shift),
        line(norm2_gain), line(norm2_shift), self_query, self_key, self_value, self_out,
        cross_query, cross_key, cross_value, cross_out, cotangent, marks,
    )

    tiles = 4
    span = hidden // 2
    depth = span // tiles
    pieces = 16
    strip = 4 * width // pieces
    vec_pack = shape((16, width), F32)
    wide = lambda dtype, *dims: pltpu.VMEM(dims, dtype)
    early_shape = shape((3 * width, width), BF)
    cross_shape, late_shape = shape((pairs, 2 * width, lanes), BF), shape((pairs, 3 * width, lanes), BF)
    all_shape = shape((2, pieces, tiles, strip, depth), BF)
    outs3 = [low, full, vec_pack, all_shape, early_shape, cross_shape, late_shape]
    acc = pltpu.VMEM((2, length, lanes), F32)
    aug_buf = pltpu.VMEM((2, length, lanes), BF)
    block_low = lambda *n: wide(BF, *n, rows, width)
    block_full = lambda *n: wide(F32, *n, rows, width)
    dmas = lambda *dims: pltpu.SemaphoreType.DMA(dims)
    block_out, token_grad, vec, all_shares, all_early, all_cross, all_late = pl.pallas_call(
        functools.partial(backward_kernel, parts, pairs, rows, scaling),
        out_shape=outs3,
        in_specs=[any_spec] * 2 + [vmem_spec()] * 2 + [any_spec] * 2 + [vmem_spec()] * 2
        + [any_spec, vmem_spec(), any_spec, vmem_spec(), vmem_spec()]
        + [any_spec] * 3 + [vmem_spec()] + [any_spec] * 3 + [vmem_spec()]
        + [any_spec] * 6 + [vmem_spec()] * 2 + [any_spec] * 3 + [vmem_spec()] * 2,
        out_specs=[vmem_spec()] * 3 + [any_spec] * 4,
        scratch_shapes=[wide(BF, width, lanes)] * 3
        + [block_full(micro), block_low(micro), block_low(micro), buf(1),
                        wide(BF, 2, count, width), block_full(micro), buf(1), buf(1), buf(1), aug_buf, acc, acc, acc,
                        block_full(micro), block_low(micro), aug_buf, aug_buf, aug_buf,
                        block_low(parts), block_low(4), block_low(4), block_low(4),
                        block_low(2), block_low(2), block_low(), block_low(), block_full(micro),
                        wide(BF, pieces, tiles, strip, depth), wide(BF, pieces, tiles, strip, depth),
                        wide(BF, pieces, 3, strip, depth),
                        wide(BF, pieces, 2, strip, depth), wide(BF, 3 * width, width),
                        wide(BF, 2 * width, lanes), wide(BF, 3 * width, lanes)]
        + [wide(BF, (3 * width) >> (d + 1), width) for d in range(5)]
        + [wide(BF, (2 * width) >> (d + 1), lanes) for d in range(3)]
        + [wide(BF, (3 * width) >> (d + 1), lanes) for d in range(3)]
        + [wide(F32, 3, 16, width), wide(F32, 12, 16, width), wide(F32, width, 3 * lanes)]
        + [dmas(4), dmas(pieces, 3), dmas(pieces, 5), dmas(4), dmas(22)]
        + [dmas(10), dmas(10), dmas(8), dmas(8), dmas(8), dmas(8), dmas(2), dmas(2), dmas(3), dmas(3), dmas(7), dmas(7)]
        + [one] * 6,
        compiler_params=pltpu.CompilerParams(
            collective_id=3, has_side_effects=True, vmem_limit_bytes=VMEM_BYTES
        ),
        name="attend_backward",
    )(
        x2, o2_own, marks, marks_got, cotangent, gf_got, line(norm3_gain), line(norm3_shift),
        up_weight.reshape(experts, 4, width // 4, hidden), up_bias, down_weight, down_bias, cross_out,
        qa1, ka1, va1, o1, qa2, ka2, va2, o2, tokens, x1, c, a_all, m_all, o1_own,
        line(norm1_gain), line(norm2_gain), self_query, self_key, self_value, self_out, cross_query,
    )

    steps = 2 * tiles
    height = width // steps
    outs4 = [shape(up_weight.shape, F32), shape(down_weight.shape, F32), shape(up_bias.shape, F32),
             shape(down_bias.shape, F32)] + [square] * 8
    whole = lambda v: pl.BlockSpec(v, lambda i: (0,) * len(v))
    (up_total, down_total, up_bias_total, down_bias_total,
     g_co, g_cq, g_so, g_ck, g_cv, g_sq, g_sk, g_sv) = pl.pallas_call(
        finish_kernel,
        grid=(steps,),
        out_shape=outs4,
        in_specs=[
            pl.BlockSpec((1, pieces, 1, strip, depth),
                         lambda i: (lax.div(i, tiles), 0, lax.rem(i, tiles), 0, 0)),
            pl.BlockSpec((3, height, width), lambda i: (0, i, 0)),
            pl.BlockSpec((pairs, 2, height, lanes), lambda i: (0, 0, i, 0)),
            pl.BlockSpec((pairs, 3, height, lanes), lambda i: (0, 0, i, 0)),
            whole((16, width)),
        ],
        out_specs=[
            pl.BlockSpec((experts, width, depth), lambda i: (0, 0, i)),
            pl.BlockSpec((experts, depth, width), lambda i: (0, i, 0)),
            whole(up_bias.shape),
            whole(down_bias.shape),
        ] + [pl.BlockSpec((height, width), lambda i: (i, 0))] * 8,
        compiler_params=pltpu.CompilerParams(vmem_limit_bytes=VMEM_BYTES),
        name="finish",
    )(
        all_shares, all_early.reshape(3, width, width),
        all_cross.reshape(pairs, 2, width, lanes), all_late.reshape(pairs, 3, width, lanes), vec,
    )

    return (
        block_out, token_grad, vec[0], vec[1], g_sq, g_sk, g_sv, g_so, vec[2], vec[3],
        g_cq, g_ck, g_cv, g_co, vec[4], vec[5],
        up_total, up_bias_total, down_total, down_bias_total,
    )


def solution(mesh):
    fits = dict(mesh.shape) == {"grp": 4, "dp": 8}
    return jax.shard_map(
        fast_device if fits else per_device,
        mesh=mesh,
        in_specs=(
            P(None, ("grp", "dp"), None),
            P(None, ("grp", "dp"), None),
            P(None, ("grp", "dp"), None),
            P(None, "grp", None),
            P(None, "grp", None),
            P(None, ("grp", "dp"), None),
            P(),
            P(),
            P(),
            P(),
            P(),
            P(),
            P(),
            P(),
            P(),
            P(),
            P(),
            P(),
            P(),
            P(),
            P("grp", None, None),
            P("grp", None),
            P("grp", None, None),
            P("grp", None),
        ),
        out_specs=(
            P(None, ("grp", "dp"), None),
            P(None, ("grp", "dp"), None),
            P(),
            P(),
            P(),
            P(),
            P(),
            P(),
            P(),
            P(),
            P(),
            P(),
            P(),
            P(),
            P(),
            P(),
            P("grp", None, None),
            P("grp", None),
            P("grp", None, None),
            P("grp", None),
        ),
        check_vma=False,
    )
```

```python
import functools
import math

import jax
import jax.numpy as jnp
from jax import lax
from jax.experimental import pallas as pl
from jax.experimental.pallas import tpu as pltpu
from jax.sharding import PartitionSpec as P

HEADS = 8
CAP = 160


masked_score = -1e30


def layer_norm(inputs, norm_gain, norm_shift):
    mean_row = jnp.mean(inputs, axis=-1, keepdims=True)
    centred = inputs - mean_row
    spread = jnp.mean(centred * centred, axis=-1, keepdims=True)
    return centred * lax.rsqrt(spread + 1e-05) * norm_gain + norm_shift


def doc_index(lengths, places):
    doc_ends = jnp.cumsum(lengths)
    return jnp.sum((places[:, None] >= doc_ends[None, :]).astype(jnp.int32), axis=1)


def product(left, right):
    return jnp.dot(left, right, preferred_element_type=jnp.float32)


def left_product(left, right):
    return jnp.einsum("nd,ne->de", left, right, preferred_element_type=jnp.float32)


def right_product(left, right):
    return jnp.einsum("nd,ed->ne", left, right, preferred_element_type=jnp.float32)


def exact_left(left, right):
    return jnp.einsum("nd,ne->de", left, right, precision=lax.Precision.HIGHEST)


def split_heads(matrix, head_count):
    return matrix.reshape(matrix.shape[0], head_count, matrix.shape[1] // head_count)


def attend_forward(queries, keys_all, values_all, allowed, head_count):
    scaling = 1.0 / math.sqrt(queries.shape[1] // head_count)
    scores = (
        jnp.einsum(
            "qhd,khd->hqk",
            split_heads(queries, head_count),
            split_heads(keys_all, head_count),
            preferred_element_type=jnp.float32,
        )
        * scaling
    )
    scores = jnp.where(allowed[None], scores, masked_score)
    maximum = jnp.max(scores, axis=-1, keepdims=True)
    exponent = jnp.exp(scores - maximum)
    totals = jnp.sum(exponent, axis=-1, keepdims=True)
    probability = (exponent / totals).astype(jnp.bfloat16)
    mixed = jnp.einsum(
        "hqk,khd->qhd",
        probability,
        split_heads(values_all, head_count),
        preferred_element_type=jnp.float32,
    )
    return (mixed.reshape(queries.shape[0], queries.shape[1]), maximum + jnp.log(totals))


def score_parts(
    query_heads, key_heads, value_heads, grad_heads, allowed, scaling, log_total, centre
):
    scores = (
        jnp.einsum("qhd,khd->hqk", query_heads, key_heads, preferred_element_type=jnp.float32)
        * scaling
    )
    scores = jnp.where(allowed[None], scores, masked_score)
    probability = jnp.exp(scores - log_total)
    prob_grad = jnp.einsum(
        "qhd,khd->hqk", grad_heads, value_heads, preferred_element_type=jnp.float32
    )
    centre = jnp.sum(probability * prob_grad, axis=-1, keepdims=True)
    score_grad = (probability * (prob_grad - centre)).astype(jnp.bfloat16)
    return (probability, score_grad, centre)


def attend_backward(queries, keys_all, values_all, allowed, head_count, log_total, out_grad):
    scaling = 1.0 / math.sqrt(queries.shape[1] // head_count)
    query_heads = split_heads(queries, head_count)
    key_heads = split_heads(keys_all, head_count)
    grad_heads = split_heads(out_grad, head_count)
    probability, score_grad, centre = score_parts(
        query_heads,
        key_heads,
        split_heads(values_all, head_count),
        grad_heads,
        allowed,
        scaling,
        log_total,
        None,
    )
    query_back = (
        jnp.einsum("hqk,khd->qhd", score_grad, key_heads, preferred_element_type=jnp.float32)
        * scaling
    )
    key_back = (
        jnp.einsum("hqk,qhd->khd", score_grad, query_heads, preferred_element_type=jnp.float32)
        * scaling
    )
    value_back = jnp.einsum(
        "hqk,qhd->khd",
        probability.astype(jnp.bfloat16),
        grad_heads,
        preferred_element_type=jnp.float32,
    )
    width = queries.shape[1]
    return (
        query_back.reshape(queries.shape[0], width),
        key_back.reshape(keys_all.shape[0], width),
        value_back.reshape(keys_all.shape[0], width),
    )


def per_device(
    tokens,
    memory,
    expert_slot,
    doc_lengths,
    source_lengths,
    cotangent,
    norm1_gain,
    norm1_shift,
    self_query,
    self_key,
    self_value,
    self_out,
    norm2_gain,
    norm2_shift,
    cross_query,
    cross_key,
    cross_value,
    cross_out,
    norm3_gain,
    norm3_shift,
    up_weight,
    up_bias,
    down_weight,
    down_bias,
):
    micro = tokens.shape[0]
    rows = tokens.shape[1]
    width = tokens.shape[2]
    source_rows = memory.shape[1]
    parts = lax.axis_size("dp")
    place = lax.axis_index("dp")
    experts_here = up_weight.shape[0]
    capacity = CAP
    head_count = HEADS
    local_places = place * rows + jnp.arange(rows, dtype=jnp.int32)
    stream_places = jnp.arange(rows * parts, dtype=jnp.int32)
    source_places = jnp.arange(source_rows * parts, dtype=jnp.int32)
    slot_ids = jnp.arange(experts_here * capacity, dtype=jnp.int32)
    expert_ids = jnp.arange(experts_here, dtype=jnp.int32)
    inputs = tokens.astype(jnp.float32)
    normed_first, first_back = jax.vjp(layer_norm, inputs, norm1_gain, norm1_shift)
    attn_in = normed_first.astype(jnp.bfloat16)
    queries = product(attn_in, self_query).astype(jnp.bfloat16)
    keys_mine = product(attn_in, self_key).astype(jnp.bfloat16)
    values_mine = product(attn_in, self_value).astype(jnp.bfloat16)
    keys_all, values_all = (
        lax.all_gather(keys_mine, "dp", axis=1, tiled=True),
        lax.all_gather(values_mine, "dp", axis=1, tiled=True),
    )
    cross_keys_all, cross_values_all = (
        lax.all_gather(product(memory, cross_key).astype(jnp.bfloat16), "dp", axis=1, tiled=True),
        lax.all_gather(product(memory, cross_value).astype(jnp.bfloat16), "dp", axis=1, tiled=True),
    )
    square_zero = jnp.zeros((width, width), jnp.float32)
    vector_zero = jnp.zeros((width,), jnp.float32)
    grad_self_query, grad_self_key, grad_self_value, grad_self_out = (
        square_zero,
        square_zero,
        square_zero,
        square_zero,
    )
    grad_cross_query, grad_cross_key, grad_cross_value, grad_cross_out = (
        square_zero,
        square_zero,
        square_zero,
        square_zero,
    )
    second_gain_sum, second_shift_sum, third_gain_sum, third_shift_sum = (
        vector_zero,
        vector_zero,
        vector_zero,
        vector_zero,
    )
    grad_up = jnp.zeros(up_weight.shape, jnp.float32)
    grad_up_bias = jnp.zeros(up_bias.shape, jnp.float32)
    grad_down = jnp.zeros(down_weight.shape, jnp.float32)
    grad_down_bias = jnp.zeros(down_bias.shape, jnp.float32)
    outputs = []
    attn_in_grads = []
    resid_grads = []
    for batch_index in range(micro):
        lengths_now = doc_lengths[batch_index, 0]
        query_docs = doc_index(lengths_now, local_places)
        stream_docs = doc_index(lengths_now, stream_places)
        source_docs = doc_index(source_lengths[batch_index, 0], source_places)
        self_allowed = (query_docs[:, None] == stream_docs[None, :]) & (
            stream_places[None, :] <= local_places[:, None]
        )
        cross_allowed = query_docs[:, None] == source_docs[None, :]
        self_result, self_log = attend_forward(
            queries[batch_index],
            keys_all[batch_index],
            values_all[batch_index],
            self_allowed,
            head_count,
        )
        self_mixed = self_result.astype(jnp.bfloat16)
        after_self = inputs[batch_index] + product(self_mixed, self_out)
        normed_second, second_back = jax.vjp(layer_norm, after_self, norm2_gain, norm2_shift)
        cross_in = normed_second.astype(jnp.bfloat16)
        cross_queries = product(cross_in, cross_query).astype(jnp.bfloat16)
        cross_result, cross_log = attend_forward(
            cross_queries,
            cross_keys_all[batch_index],
            cross_values_all[batch_index],
            cross_allowed,
            head_count,
        )
        cross_mixed = cross_result.astype(jnp.bfloat16)
        after_cross = after_self + product(cross_mixed, cross_out)
        normed_third, third_back = jax.vjp(layer_norm, after_cross, norm3_gain, norm3_shift)
        expert_in = normed_third.astype(jnp.bfloat16)
        chosen = expert_slot[batch_index, :, 0]
        one_hot = (chosen[:, None] == expert_ids[None, :]).astype(jnp.int32)
        ranks = jnp.sum((jnp.cumsum(one_hot, axis=0) - 1) * one_hot, axis=1)
        target = chosen * capacity + ranks
        dispatch = (slot_ids[:, None] == target[None, :]).astype(jnp.bfloat16)
        buffer_in = (
            product(dispatch, expert_in).astype(jnp.bfloat16).reshape(experts_here, capacity, width)
        )
        pre_act = (
            jnp.einsum("ecd,edf->ecf", buffer_in, up_weight, preferred_element_type=jnp.float32)
            + up_bias[:, None, :]
        )
        activated, gelu_back = jax.vjp(jax.nn.gelu, pre_act)
        hidden = activated.astype(jnp.bfloat16)
        buffer_out = (
            jnp.einsum("ecf,efd->ecd", hidden, down_weight, preferred_element_type=jnp.float32)
            + down_bias[:, None, :]
        )
        expert_out = jnp.take(buffer_out.reshape(experts_here * capacity, width), target, axis=0)
        outputs.append((after_cross + expert_out).astype(jnp.bfloat16))
        out_grad = cotangent[batch_index].astype(jnp.float32)
        grad_rows = out_grad.astype(jnp.bfloat16)
        buffer_grad = (
            product(dispatch, grad_rows).astype(jnp.bfloat16).reshape(experts_here, capacity, width)
        )
        grad_down = grad_down + jnp.einsum(
            "ecf,ecd->efd", hidden, buffer_grad, preferred_element_type=jnp.float32
        )
        grad_down_bias = grad_down_bias + jnp.sum(buffer_grad.astype(jnp.float32), axis=1)
        hidden_grad = jnp.einsum(
            "ecd,efd->ecf", buffer_grad, down_weight, preferred_element_type=jnp.float32
        )
        pre_grad = gelu_back(hidden_grad)[0].astype(jnp.bfloat16)
        grad_up = grad_up + jnp.einsum(
            "ecd,ecf->edf", buffer_in, pre_grad, preferred_element_type=jnp.float32
        )
        grad_up_bias = grad_up_bias + jnp.sum(pre_grad.astype(jnp.float32), axis=1)
        buffer_back = jnp.einsum(
            "ecf,edf->ecd", pre_grad, up_weight, preferred_element_type=jnp.float32
        )
        expert_in_grad = jnp.take(
            buffer_back.reshape(experts_here * capacity, width), target, axis=0
        )
        third_resid, third_gain, third_shift = third_back(expert_in_grad)
        third_gain_sum = third_gain_sum + third_gain
        third_shift_sum = third_shift_sum + third_shift
        cross_grad = out_grad + third_resid
        cross_rows_grad = cross_grad.astype(jnp.bfloat16)
        grad_cross_out = grad_cross_out + left_product(cross_mixed, cross_rows_grad)
        cross_mixed_grad = right_product(cross_rows_grad, cross_out).astype(jnp.bfloat16)
        cross_query_back, cross_key_back, cross_value_back = attend_backward(
            cross_queries,
            cross_keys_all[batch_index],
            cross_values_all[batch_index],
            cross_allowed,
            head_count,
            cross_log,
            cross_mixed_grad,
        )
        cross_query_low = cross_query_back.astype(jnp.bfloat16)
        grad_cross_query = grad_cross_query + left_product(cross_in, cross_query_low)
        cross_key_mine, cross_value_mine = (
            lax.psum_scatter(
                cross_key_back.astype(jnp.bfloat16), "dp", scatter_dimension=0, tiled=True
            ).astype(jnp.float32),
            lax.psum_scatter(
                cross_value_back.astype(jnp.bfloat16), "dp", scatter_dimension=0, tiled=True
            ).astype(jnp.float32),
        )
        source_exact = memory[batch_index].astype(jnp.float32)
        grad_cross_key = grad_cross_key + exact_left(source_exact, cross_key_mine)
        grad_cross_value = grad_cross_value + exact_left(source_exact, cross_value_mine)
        second_resid, second_gain, second_shift = second_back(
            right_product(cross_query_low, cross_query)
        )
        second_gain_sum = second_gain_sum + second_gain
        second_shift_sum = second_shift_sum + second_shift
        self_grad = cross_grad + second_resid
        self_rows_grad = self_grad.astype(jnp.bfloat16)
        grad_self_out = grad_self_out + left_product(self_mixed, self_rows_grad)
        self_mixed_grad = right_product(self_rows_grad, self_out).astype(jnp.bfloat16)
        self_query_back, self_key_back, self_value_back = attend_backward(
            queries[batch_index],
            keys_all[batch_index],
            values_all[batch_index],
            self_allowed,
            head_count,
            self_log,
            self_mixed_grad,
        )
        self_key_mine, self_value_mine = (
            lax.psum_scatter(
                self_key_back.astype(jnp.bfloat16), "dp", scatter_dimension=0, tiled=True
            ).astype(jnp.float32),
            lax.psum_scatter(
                self_value_back.astype(jnp.bfloat16), "dp", scatter_dimension=0, tiled=True
            ).astype(jnp.float32),
        )
        query_low = self_query_back.astype(jnp.bfloat16)
        key_low = self_key_mine.astype(jnp.bfloat16)
        value_low = self_value_mine.astype(jnp.bfloat16)
        grad_self_query = grad_self_query + left_product(attn_in[batch_index], query_low)
        grad_self_key = grad_self_key + left_product(attn_in[batch_index], key_low)
        grad_self_value = grad_self_value + left_product(attn_in[batch_index], value_low)
        attn_in_grads.append(
            right_product(query_low, self_query)
            + right_product(key_low, self_key)
            + right_product(value_low, self_value)
        )
        resid_grads.append(self_grad)
    first_resid, first_gain, first_shift = first_back(jnp.stack(attn_in_grads))
    token_grad = jnp.stack(resid_grads) + first_resid
    block_out = jnp.stack(outputs)
    up_share, up_bias_share, down_share, down_bias_share = (
        lax.psum_scatter(
            grad_up.astype(jnp.bfloat16), "dp", scatter_dimension=2, tiled=True
        ).astype(jnp.float32),
        lax.psum_scatter(
            grad_up_bias.astype(jnp.bfloat16), "dp", scatter_dimension=1, tiled=True
        ).astype(jnp.float32),
        lax.psum_scatter(
            grad_down.astype(jnp.bfloat16), "dp", scatter_dimension=1, tiled=True
        ).astype(jnp.float32),
        lax.psum_scatter(
            grad_down_bias.astype(jnp.bfloat16), "dp", scatter_dimension=1, tiled=True
        ).astype(jnp.float32),
    )
    up_total, up_bias_total, down_total, down_bias_total = (
        lax.all_gather(up_share.astype(jnp.bfloat16), "dp", axis=2, tiled=True).astype(
            up_share.dtype
        ),
        lax.all_gather(up_bias_share.astype(jnp.bfloat16), "dp", axis=1, tiled=True).astype(
            up_bias_share.dtype
        ),
        lax.all_gather(down_share.astype(jnp.bfloat16), "dp", axis=1, tiled=True).astype(
            down_share.dtype
        ),
        lax.all_gather(down_bias_share.astype(jnp.bfloat16), "dp", axis=1, tiled=True).astype(
            down_bias_share.dtype
        ),
    )
    shared = lax.psum(
        (
            first_gain,
            first_shift,
            grad_self_query,
            grad_self_key,
            grad_self_value,
            grad_self_out,
            second_gain_sum,
            second_shift_sum,
            grad_cross_query,
            grad_cross_key,
            grad_cross_value,
            grad_cross_out,
            third_gain_sum,
            third_shift_sum,
        ),
        ("grp", "dp"),
    )
    return (
        block_out,
        token_grad,
        shared[0],
        shared[1],
        shared[2],
        shared[3],
        shared[4],
        shared[5],
        shared[6],
        shared[7],
        shared[8],
        shared[9],
        shared[10],
        shared[11],
        shared[12],
        shared[13],
        up_total,
        up_bias_total,
        down_total,
        down_bias_total,
    )


MESH = pl.DeviceIdType.MESH
BF = jnp.bfloat16
F32 = jnp.float32
VMEM_BYTES = 56 * 1024 * 1024
HIDE = -1e30


def mm(left, right):
    return lax.dot_general(left, right, (((1,), (0,)), ((), ())), preferred_element_type=F32)


def mm_right(left, right):
    return lax.dot_general(left, right, (((1,), (1,)), ((), ())), preferred_element_type=F32)


def mm_left(left, right):
    return lax.dot_general(left, right, (((0,), (0,)), ((), ())), preferred_element_type=F32)


def norm_parts(inputs):
    mean_row = jnp.mean(inputs, axis=-1, keepdims=True)
    centred = inputs - mean_row
    spread = jnp.mean(centred * centred, axis=-1, keepdims=True)
    inverse = lax.rsqrt(spread + 1e-05)
    return centred * inverse, inverse


def norm_back(unit, inverse, gain, grad):
    scaled = grad * gain
    first = jnp.mean(scaled, axis=-1, keepdims=True)
    second = jnp.mean(scaled * unit, axis=-1, keepdims=True)
    return inverse * (scaled - first - unit * second)


def col_sum(values):
    return jnp.sum(values, axis=0, keepdims=True)


def three_parts(values):
    high = values.astype(BF).astype(F32)
    rest = values - high
    middle = rest.astype(BF).astype(F32)
    return high, middle, rest - middle


def doc_of(lengths_ref, batch, positions):
    total = jnp.int32(0)
    docs = jnp.zeros(positions.shape, jnp.int32)
    for j in range(lengths_ref.shape[2]):
        total = total + lengths_ref[batch, 0, j]
        docs = docs + (positions >= total).astype(jnp.int32)
    return docs


def lanes_of(shape, head):
    lane = lax.broadcasted_iota(jnp.int32, shape, 1)
    half = shape[1] // 2
    own = (lane < half) if head == 0 else (lane >= half)
    return own, (lane - half if head == 0 else lane)


def greet(grp, me, parts):
    barrier = pltpu.get_barrier_semaphore()
    for k in range(1, parts):
        pl.semaphore_signal(
            barrier, inc=1, device_id=(grp, lax.rem(me + k, parts)), device_id_type=MESH
        )
    pl.semaphore_wait(barrier, parts - 1)


def sender(grp, src, dst, ssem, rsem, target):
    return pltpu.make_async_remote_copy(
        src_ref=src,
        dst_ref=dst,
        send_sem=ssem,
        recv_sem=rsem,
        device_id=(grp, target),
        device_id_type=MESH,
    )


def partner_of(grp, me, axis):
    place = lax.div(me, 2)
    if axis == "core":
        return grp + 1 - 2 * lax.rem(grp, 2), me
    if axis == "x":
        return lax.rem(grp + 2, 4), me
    if axis == "y":
        return grp, me + 1 - 2 * lax.rem(me, 2)
    if axis == "near":
        return grp, me + 2 - 4 * lax.rem(place, 2)
    return grp, lax.rem(me + 4, 8)


def push(src, dst, ssem, rsem, device):
    return pltpu.make_async_remote_copy(
        src_ref=src, dst_ref=dst, send_sem=ssem, recv_sem=rsem, device_id=device, device_id_type=MESH
    )


def wait_in(ref, sem, device):
    push(ref, ref, sem, sem, device).wait_recv()


def wait_out(ref, sem, device):
    push(ref, ref, sem, sem, device).wait_send()


def key_features(values, docs, head):
    own, place = lanes_of(values.shape, head)
    other = jnp.where(place == docs, 0.0, HIDE)
    other = jnp.where((place >= 4) & (place < 7), 1.0, other)
    return jnp.where(own, values.astype(F32), other).astype(BF)


def query_features(values, docs, head, scaling):
    own, place = lanes_of(values.shape, head)
    return jnp.where(
        own, values.astype(F32) * scaling, jnp.where(place == docs, 1.0, 0.0)
    ).astype(BF)


def value_features(values, head):
    own, _ = lanes_of(values.shape, head)
    return jnp.where(own, values.astype(F32), 1.0).astype(BF)


def forward_kernel(
    parts, pairs, rows, scaling,
    doc_len, src_len, tokens, memory, gain1, shift1, gain2, shift2,
    wq_in, wk_in, wv_in, wo, cq, ck_in, cv_in, co, cot, marks,
    a_out, m_out, x1_out, c_out, x2_out, o1_own, o2_own,
    qa1_out, ka1_out, va1_out, o1, qa2_out, ka2_out, va2_out, o2, gf_got, marks_got,
    a_all, m_all, qa1, ka1, va1, qa2, ka2, va2, wq, wk, wv, ck, cv, load_sem, out_sem,
    a_own, st_q2, rv_q2,
    s_a, r_a, s_m, r_m, s_o1, r_o1, s_q2, r_q2, s_o2, r_o2, s_y, r_y,
):
    grp = lax.axis_index("grp")
    me = lax.axis_index("dp")
    batch = lax.div(me, pairs)
    pair = lax.rem(me, pairs)
    micro = tokens.shape[0]
    lanes = 128
    low_half = batch == 0
    half = lax.rem(me, 2)
    place = lax.div(me, 2)
    inner = (place == 1) | (place == 2)
    to_y = partner_of(grp, me, "y")
    to_near = partner_of(grp, me, "near")
    entry = jnp.where(low_half, 4, 2) + half
    far_end = jnp.where(low_half, 6, 0) + half

    def a2a(src, dst, ssem, rsem, target):
        return sender(grp, src.at[target], dst.at[me], ssem, rsem.at[me], target)

    def arrived(dst, ssem, rsem, source):
        wait_in(dst.at[source], rsem.at[source], to_y)

    columns = pl.ds(pl.multiple_of(pair * lanes, lanes), lanes)
    loads = [
        pltpu.make_async_copy(src.at[:, columns], dst, load_sem.at[n])
        for n, (src, dst) in enumerate(
            ((wq_in, wq), (wk_in, wk), (wv_in, wv), (ck_in, ck), (cv_in, cv))
        )
    ]
    for load in loads:
        load.start()
    outs = [
        pltpu.make_async_copy(src, dst, out_sem.at[n])
        for n, (src, dst) in enumerate(
            (
                (a_all, a_out), (ka1, ka1_out), (va1, va1_out), (qa1, qa1_out),
                (m_all, m_out), (ka2, ka2_out), (va2, va2_out), (qa2, qa2_out),
            )
        )
    ]
    greet(grp, me, parts)

    def first_norm(mb, _):
        unit, _inv = norm_parts(tokens[mb].astype(F32))
        a_own[mb] = (unit * gain1[...] + shift1[...]).astype(BF)
        return 0

    lax.fori_loop(0, micro, first_norm, 0)

    def source_of(i):
        return jnp.where(i == 0, me, jnp.where(i == 1, to_near[1], jnp.where(i == 2, entry, far_end)))

    def spread_first(own, out, ssem, rsem):
        there = (grp, entry)
        return [
            push(own.at[batch], out.at[me], ssem.at[4], rsem.at[me], to_near),
            push(own.at[1 - batch], out.at[me], ssem.at[5], rsem.at[me], there),
        ]

    def spread_y(out, ssem, rsem, i):
        j = source_of(i)
        return push(out.at[j], out.at[j], ssem.at[i], rsem.at[j], to_y)

    def spread_near(out, ssem, rsem, i):
        j = source_of(i)
        return push(out.at[j], out.at[j], ssem.at[4 + i], rsem.at[j], to_near)

    def spread_start(own, out, ssem, rsem):
        for copy in spread_first(own, out, ssem, rsem):
            copy.start()
        out[me] = own[batch]
        spread_y(out, ssem, rsem, 0).start()

    def spread_on(out, ssem, rsem, i):
        arrived(out, ssem, rsem, source_of(i))
        spread_y(out, ssem, rsem, i).start()

        @pl.when(inner & (i >= 2))
        def _():
            spread_near(out, ssem, rsem, i).start()

    def spread_done(own, out, ssem, rsem):
        for copy in spread_first(own, out, ssem, rsem):
            copy.wait_send()
        for i in range(4):
            spread_y(out, ssem, rsem, i).wait_send()

        @pl.when(inner)
        def _():
            for i in (2, 3):
                spread_near(out, ssem, rsem, i).wait_send()

    def y_of(i):
        return source_of(i) + 1 - 2 * half

    def build_self(j):
        r0 = pl.multiple_of(j * rows, rows)
        places = r0 + lax.broadcasted_iota(jnp.int32, (rows, lanes), 0)
        docs = doc_of(doc_len, batch, places)
        a = a_all[j]
        query, key, value = (mm(a, weight[...]).astype(BF) for weight in (wq, wk, wv))
        for h in range(2):
            qa1[h, pl.ds(r0, rows), :] = query_features(query, docs, h, scaling)
            ka1[h, pl.ds(r0, rows), :] = key_features(key, docs, h)
            va1[h, pl.ds(r0, rows), :] = value_features(value, h)

    spread_start(a_own, a_all, s_a, r_a)
    for load in loads:
        load.wait()

    def same_y(i, _):
        @pl.when(i > 0)
        def _():
            spread_on(a_all, s_a, r_a, i)

        build_self(source_of(i))
        return 0

    def other_y(i, _):
        arrived(a_all, s_a, r_a, y_of(i))
        build_self(y_of(i))
        return 0

    lax.fori_loop(0, 4, same_y, 0)
    lax.fori_loop(0, 4, other_y, 0)
    spread_start(memory, m_all, s_m, r_m)
    for out in outs[0:3]:
        out.start()

    def finish(qa, r0, h, query, top, acc):
        own, place = lanes_of((rows, lanes), h)
        total = pltpu.roll(acc, lanes // 2, 1)
        high, middle, low = three_parts(top + jnp.log(acc))
        query = query.astype(F32)
        query = jnp.where(~own & (place == 4), -high, query)
        query = jnp.where(~own & (place == 5), -middle, query)
        query = jnp.where(~own & (place == 6), -low, query)
        qa[h, pl.ds(r0, rows), :] = query.astype(BF)
        return acc / total

    def emit(t, heads, out, own_ref, ssem, rsem):
        own, _ = lanes_of((rows, lanes), 0)
        out[t] = jnp.where(own, heads[0], heads[1]).astype(BF)

        @pl.when(t != me)
        def _():
            sender(grp, out.at[t], own_ref.at[me], ssem, rsem, t).start()

        @pl.when(t == me)
        def _():
            own_ref[me] = out[t]

    for e in range(parts // 2):
        reach = 2 * rows * (e + 1)
        cut = reach - 2 * rows

        def self_block(i, _, reach=reach, cut=cut, e=e):
            t = 2 * e + i
            r0 = pl.multiple_of(t * rows, rows)
            row = r0 + lax.broadcasted_iota(jnp.int32, (rows, 2 * rows), 0)
            col = cut + lax.broadcasted_iota(jnp.int32, (rows, 2 * rows), 1)
            heads = []
            for h in range(2):
                query = qa1[h, pl.ds(r0, rows), :]
                near = mm_right(query, ka1[h, cut:reach, :])
                near = jnp.where(col <= row, near, HIDE)
                top = jnp.max(near, axis=1, keepdims=True)
                if cut:
                    far = mm_right(query, ka1[h, 0:cut, :])
                    top = jnp.maximum(top, jnp.max(far, axis=1, keepdims=True))
                acc = mm(jnp.exp(near - top).astype(BF), va1[h, cut:reach, :])
                if cut:
                    acc = acc + mm(jnp.exp(far - top).astype(BF), va1[h, 0:cut, :])
                heads.append(finish(qa1, r0, h, query, top, acc))
            emit(t, heads, o1, o1_own, s_o1, r_o1)
            return 0

        lax.fori_loop(0, 2, self_block, 0)
        if e == 2:
            spread_on(m_all, s_m, r_m, 1)

    def own_wait(own_ref, ssem, rsem):
        wait_in(own_ref.at[pl.ds(0, parts - 1)], rsem, to_y)

    spread_on(m_all, s_m, r_m, 2)
    spread_on(m_all, s_m, r_m, 3)
    outs[3].start()
    own_wait(o1_own, s_o1, r_o1)

    def second_norm(mb, _):
        mixed = jnp.concatenate([o1_own[mb * pairs + p] for p in range(pairs)], axis=1)
        x1 = tokens[mb].astype(F32) + mm(mixed, wo[...])
        x1_out[mb] = x1
        unit, _inv = norm_parts(x1)
        c = (unit * gain2[...] + shift2[...]).astype(BF)
        c_out[mb] = c
        got = mm(c, cq[...]).astype(BF)
        for p in range(pairs):
            st_q2[mb * pairs + p] = got[:, p * lanes : (p + 1) * lanes]

        def send(p, _):
            target = mb * pairs + p

            @pl.when(target != me)
            def _():
                a2a(st_q2, rv_q2, s_q2, r_q2, target).start()

            @pl.when(target == me)
            def _():
                rv_q2[me] = st_q2[me]

            return 0

        lax.fori_loop(0, pairs, send, 0)
        return 0

    lax.fori_loop(0, micro, second_norm, 0)

    def build_cross(i, _):
        j = jnp.where(i < 4, source_of(i), y_of(i - 4))

        @pl.when(i >= 4)
        def _():
            arrived(m_all, s_m, r_m, j)

        r0 = pl.multiple_of(j * rows, rows)
        places = r0 + lax.broadcasted_iota(jnp.int32, (rows, lanes), 0)
        docs = doc_of(src_len, batch, places)
        source = m_all[j]
        key, value = (mm(source, weight[...]).astype(BF) for weight in (ck, cv))
        for h in range(2):
            ka2[h, pl.ds(r0, rows), :] = key_features(key, docs, h)
            va2[h, pl.ds(r0, rows), :] = value_features(value, h)
        return 0

    lax.fori_loop(0, parts, build_cross, 0)
    for out in outs[4:7]:
        out.start()

    swaps = [
        push(cot, gf_got, s_y.at[0], r_y.at[0], to_y),
        push(marks, marks_got, s_y.at[1], r_y.at[1], to_y),
    ]
    def cross_block(k, _):
        t = lax.rem(me + k, parts)

        @pl.when(k == 2)
        def _():
            swaps[0].start()
            swaps[1].start()

        @pl.when(k > 0)
        def _():
            arrived(rv_q2, s_q2, r_q2, t)

        r0 = pl.multiple_of(t * rows, rows)
        places = r0 + lax.broadcasted_iota(jnp.int32, (rows, lanes), 0)
        docs = doc_of(doc_len, batch, places)
        heads = []
        for h in range(2):
            query = query_features(rv_q2[t], docs, h, scaling)
            scores = mm_right(query, ka2[h])
            top = jnp.max(scores, axis=1, keepdims=True)
            acc = mm(jnp.exp(scores - top).astype(BF), va2[h])
            heads.append(finish(qa2, r0, h, query, top, acc))
        emit(t, heads, o2, o2_own, s_o2, r_o2)
        return 0

    lax.fori_loop(0, parts, cross_block, 0)
    outs[7].start()
    own_wait(o2_own, s_o2, r_o2)

    def third(mb, _):
        mixed = jnp.concatenate([o2_own[mb * pairs + p] for p in range(pairs)], axis=1)
        x2_out[mb] = x1_out[mb] + mm(mixed, co[...])
        return 0

    lax.fori_loop(0, micro, third, 0)

    for ref, sem in ((st_q2, s_q2), (o1, s_o1), (o2, s_o2)):
        wait_out(ref.at[pl.ds(0, parts - 1)], sem, to_y)
    for swap in swaps:
        swap.wait()
    spread_done(a_own, a_all, s_a, r_a)
    spread_done(memory, m_all, s_m, r_m)
    for out in outs:
        out.wait()


def gelu_both(z):
    root = math.sqrt(2.0 / math.pi)
    square = z * z
    bent = jnp.tanh(root * z * (1.0 + 0.044715 * square))
    half = 0.5 * (1.0 + bent)
    slope = half + 0.5 * z * (1.0 - bent * bent) * (root * (1.0 + 3 * 0.044715 * square))
    return z * half, slope


LAG = 1
TICKS = (3, 3, 1, 1, 1, 1)
TAIL = (1, 1, 1, 1, 2)


def backward_kernel(
    parts, pairs, rows, scaling,
    x2_in, o2_own, marks, marks_got, cot_in, gf_in, gain3, shift3, up_hbm, up_b, down_hbm, down_b, co,
    qa1_in, ka1_in, va1_in, o1, qa2_in, ka2_in, va2_in, o2,
    tokens_in, x1_in, c_in, a_in, m_in, o1_own, gain1, gain2,
    wq_in, wk_in, wv_in, wo, cq,
    block_out, token_grad, vec_out, all_shares, all_early, all_cross, all_late,
    wq, wk, wv, x_buf, c_buf, t_buf, o_buf, e_all, gx2_ref, st_do, rv_do, rv_dq2, doa, dq_acc, dk_acc, dv_acc, gx1_ref, low_grad,
    qa, ka, va, stream, da_keep, st_y, got_y, st_near, got_near, st_far, got_far, da_sum,
    shares, final, got_one, got_two, early, cross, late, *rest
):
    got_early, got_cross, got_late, rest = rest[:5], rest[5:8], rest[8:11], rest[11:]
    vec, got_vec, g_late, rest = *rest[:3], rest[3:]
    hop_s, hop_r, piece_r, local_sem, load_sem, rest = *rest[:5], rest[5:]
    early_s, early_r, cross_s, cross_r, late_s, late_r, vec_s, vec_r, rest = *rest[:8], rest[8:]
    swap_s, swap_r, da_s, da_r, s_do2, r_do2, s_dq2, r_dq2, s_do1, r_do1 = rest
    grp = lax.axis_index("grp")
    me = lax.axis_index("dp")
    micro, rows, width = x_buf.shape
    count = micro * rows
    span = up_b.shape[1] // 2
    lanes = 128
    length = parts * rows

    def a2a(src, dst, ssem, rsem, target):
        return sender(grp, src.at[target], dst.at[me], ssem, rsem, target)

    def all_arrived(dst, rsem):
        wait_in(dst.at[pl.ds(0, parts - 1)], rsem, partners[2])

    half = lax.rem(me, 2)
    near_bit = lax.rem(lax.div(me, 2), 2)
    far_bit = lax.div(me, 4)
    axes = ("core", "x", "y", "near", "far")
    place = lax.div(me, 2)
    batch = far_bit
    pair = lax.rem(me, pairs)
    inner = (place == 1) | (place == 2)
    bits = (lax.rem(grp, 2), lax.div(grp, 2), half, near_bit, far_bit)
    partners = [partner_of(grp, me, axis) for axis in axes]
    barrier = pltpu.get_barrier_semaphore()
    for k in range(1, parts):
        pl.semaphore_signal(
            barrier, inc=1, device_id=(grp, lax.rem(me + k, parts)), device_id_type=MESH
        )
    for k in range(1, 4):
        for f in range(2):
            there = (lax.rem(grp + k, 4), f * 4 + pair)
            pl.semaphore_signal(barrier, inc=1, device_id=there, device_id_type=MESH)

    pieces, tiles, strip, depth = shares.shape
    to_y, to_near, to_far = partners[2:]
    to_mid = (grp, (3 - place) * 2 + half)
    at_end = jnp.where(far_bit == 0, 0, 3)
    at_inner = jnp.where(far_bit == 0, 1, 2)
    at_next = 3 - at_inner
    at_last = 3 - at_end
    three = pl.ds(jnp.where(far_bit == 0, 1, 0), 3)
    away = pl.ds(jnp.where(far_bit == 0, 2, 0), 2)
    home = pl.ds(jnp.where(far_bit == 0, 0, 2), 2)

    def hop(s, n):
        rsem = hop_r.at[s, n]
        if n == 0:
            return push(shares.at[s, three], got_one.at[s], hop_s.at[0], rsem, to_near)
        if n == 1:
            return push(shares.at[s, away], got_two.at[s], hop_s.at[0], rsem, to_mid)
        return push(shares.at[s, at_end], got_two.at[s, 0], hop_s.at[0], rsem, to_near)

    def piece_on(s, n, piece, device):
        ref = final.at[s, piece]
        return push(ref, ref, hop_s.at[1], piece_r.at[s, n], device)

    def y_copy_of(s):
        return push(final.at[s], all_shares.at[half, s], hop_s.at[2], hop_s.at[3], to_y)

    def summed(s, piece, more):
        return (shares[s, piece].astype(F32) + more.astype(F32)).astype(BF)

    first_three = jnp.where(far_bit == 0, 1, 0)
    first_home = jnp.where(far_bit == 0, 0, 2)

    def share_step(s, stage):
        if stage == 0:

            @pl.when(~inner)
            def _():
                hop(s, 0).start()

        if stage == 1:

            @pl.when(inner)
            def _():
                hop(s, 0).wait_recv()
                for n in range(3):
                    shares[s, first_three + n] = summed(s, first_three + n, got_one[s, n])
                hop(s, 1).start()

        if stage == 2:

            @pl.when(inner)
            def _():
                hop(s, 1).wait_recv()
                shares[s, at_end] = summed(s, at_end, got_two[s, at_end - first_home])
                hop(s, 2).start()
                final[s, at_inner] = summed(s, at_inner, got_two[s, at_inner - first_home])
                piece_on(s, 0, at_inner, to_mid).start()
                piece_on(s, 1, at_inner, to_near).start()

        if stage == 3:

            @pl.when(~inner)
            def _():
                hop(s, 2).wait_recv()
                final[s, at_end] = summed(s, at_end, got_two[s, 0])
                piece_on(s, 2, at_end, to_near).start()

        if stage == 4:

            @pl.when(inner)
            def _():
                piece_on(s, 2, at_end, to_near).wait_recv()
                piece_on(s, 3, at_end, to_mid).start()

        if stage == 5:

            @pl.when(inner)
            def _():
                piece_on(s, 0, at_next, to_mid).wait_recv()
                piece_on(s, 3, at_last, to_mid).wait_recv()
                ref = final.at[s, away]
                push(ref, ref, hop_s.at[1], piece_r.at[s, 4], to_near).start()
                y_copy_of(s).start()

        if stage == 6:

            @pl.when(~inner)
            def _():
                piece_on(s, 1, at_inner, to_near).wait_recv()
                ref = final.at[s, away]
                push(ref, ref, hop_s.at[1], piece_r.at[s, 4], to_near).wait_recv()
                y_copy_of(s).start()

    def shares_done():
        out = pltpu.make_async_copy(final, all_shares.at[half], local_sem.at[3])
        out.start()
        wait_in(all_shares.at[1 - half], hop_s.at[3], to_y)
        wait_out(final, hop_s.at[2], to_y)

        @pl.when(inner)
        def _():
            wait_out(got_one, hop_s.at[0], to_y)
            wait_out(final, hop_s.at[1], to_y)
            wait_out(final.at[:, 0], hop_s.at[1], to_y)

        @pl.when(~inner)
        def _():
            wait_out(got_one, hop_s.at[0], to_y)
            wait_out(final.at[:, 0], hop_s.at[1], to_y)

        out.wait()

    def load_three(refs, n):
        return [
            pltpu.make_async_copy(src, dst, load_sem.at[5 + 3 * n + m])
            for m, (src, dst) in enumerate(zip(refs, (qa, ka, va)))
        ]

    def tick(i):
        for stage in (6, 5, 4, 3, 2, 1, 0):
            s = i - LAG * stage
            if isinstance(s, int):
                if 0 <= s < pieces:
                    share_step(s, stage)
            else:

                @pl.when((s >= 0) & (s < pieces))
                def _(s=s, stage=stage):
                    share_step(s, stage)

    def ticks(start, count):
        def one(i, _):
            tick(start + i)
            return 0

        lax.fori_loop(0, count, one, 0)

    def seven(one):
        def body(k, _):
            one(k)
            return 0

        lax.fori_loop(1, 8, body, 0)

    slice_axes = (0, 1, 4)

    def slice_start(total, upto):
        start = jnp.int32(0)
        for d in range(upto):
            start = start + bits[slice_axes[d]] * (total >> (d + 1))
        return start

    def slice_rows(total, upto):
        return pl.ds(pl.multiple_of(slice_start(total, upto), total >> 3), total >> upto)

    def slice_copy(own, out, got, ssem, rsem, stage):
        total = own.shape[0]
        sems = (ssem.at[stage], rsem.at[stage])
        if stage < 3:
            axis = slice_axes[stage]
            size = total >> (stage + 1)
            start = slice_start(total, stage) + (1 - bits[axis]) * size
            part = pl.ds(pl.multiple_of(start, total >> 3), size)
            return push(own.at[part], got[stage], *sems, partners[axis])
        if stage == 3:
            part = slice_rows(total, 3)
            return push(own.at[part], out.at[pair, part], *sems, to_far)
        if stage == 4:
            ref = out.at[pair, slice_rows(total, 2)]
            return push(ref, ref, *sems, to_y)
        if stage == 5:
            ref = out.at[pl.ds(near_bit * 2, 2), slice_rows(total, 2)]
            return push(ref, ref, *sems, to_near)
        ref = out.at[:, slice_rows(total, 8 - stage)]
        return push(ref, ref, *sems, partners[7 - stage])

    def slice_local(own, out, sem):
        part = slice_rows(own.shape[0], 3)
        return pltpu.make_async_copy(own.at[part], out.at[pair, part], sem)

    def slice_step(own, out, got, ssem, rsem, sem, stage):
        total = own.shape[0]
        if stage >= 1:
            slice_copy(own, out, got, ssem, rsem, stage - 1).wait_recv()
        if 1 <= stage <= 3:
            part = slice_rows(total, stage)
            own[part, :] = (own[part, :].astype(F32) + got[stage - 1][...].astype(F32)).astype(BF)
        if stage == 3:
            slice_local(own, out, sem).start()
        if stage == 4:
            slice_local(own, out, sem).wait()
        if stage < 8:
            slice_copy(own, out, got, ssem, rsem, stage).start()
        if stage == 8:
            for n in range(8):
                slice_copy(own, out, got, ssem, rsem, n).wait_send()

    def cross_step(stage):
        slice_step(cross, all_cross, got_cross, cross_s, cross_r, local_sem.at[0], stage)

    def late_step(stage):
        slice_step(late, all_late, got_late, late_s, late_r, local_sem.at[1], stage)

    def offset_of(total, upto):
        start = jnp.int32(0)
        for d in range(upto):
            start = start + bits[d] * (total >> (d + 1))
        return start

    def rows_at(total, start, size):
        return pl.ds(pl.multiple_of(start, total >> 5), size)

    def early_copy(stage):
        total = early.shape[0]
        sems = (early_s.at[stage], early_r.at[stage])
        if stage < 5:
            size = total >> (stage + 1)
            start = offset_of(total, stage) + (1 - bits[stage]) * size
            return push(early.at[rows_at(total, start, size)], got_early[stage], *sems, partners[stage])
        d = 9 - stage
        part = rows_at(total, offset_of(total, d + 1), total >> (d + 1))
        src = early if stage == 5 else all_early
        return push(src.at[part], all_early.at[part], *sems, partners[d])

    def early_local():
        total = early.shape[0]
        part = rows_at(total, offset_of(total, 5), total >> 5)
        return pltpu.make_async_copy(early.at[part], all_early.at[part], local_sem.at[2])

    def early_step(stage):
        total = early.shape[0]
        if stage >= 1:
            early_copy(stage - 1).wait_recv()
        if 1 <= stage <= 5:
            part = rows_at(total, offset_of(total, stage), total >> stage)
            early[part, :] = (early[part, :].astype(F32) + got_early[stage - 1][...].astype(F32)).astype(BF)
        if stage == 5:
            early_local().start()
        if stage == 6:
            early_local().wait()
        if stage < 10:
            early_copy(stage).start()
        if stage == 10:
            for n in range(10):
                early_copy(n).wait_send()

    def vec_first(k):
        j = lax.rem(me + k, parts)
        return push(vec.at[0], got_vec.at[me], vec_s.at[0], vec_r.at[0], (grp, j))

    def vec_cross(k):
        other = lax.rem(grp + k, 4)
        return push(
            vec.at[1, 0:8], got_vec.at[8 + grp, 0:8], vec_s.at[1], vec_r.at[1], (other, me)
        )

    def vec_step(stage):
        if stage == 0:
            seven(lambda k: vec_first(k).start())
        if stage == 1:

            wait_in(got_vec.at[pl.ds(0, 7)], vec_r.at[0], to_y)

            def more(k, total):
                return total + got_vec[lax.rem(me + k, parts)]

            vec[1] = lax.fori_loop(1, 8, more, vec[0])
            for k in range(1, 4):
                vec_cross(k).start()
        if stage == 2:
            total = jnp.zeros((8, width), F32)
            wait_in(got_vec.at[pl.ds(0, 3), 0:8], vec_r.at[1], to_y)
            for k in range(1, 4):
                total = total + got_vec[8 + lax.rem(grp + k, 4), 0:8]
            row = lax.broadcasted_iota(jnp.int32, (8, width), 0)
            vec[2, 0:8] = vec[1, 0:8] + jnp.where(row < 6, total, 0.0)
            vec[2, 8:16] = vec[1, 8:16]
            wait_out(got_vec.at[pl.ds(0, 7)], vec_s.at[0], to_y)
            wait_out(got_vec.at[pl.ds(0, 3), 0:8], vec_s.at[1], to_y)

    first_col = pl.multiple_of(half * span, span)

    def load(src, dst, n):
        return pltpu.make_async_copy(src, dst, load_sem.at[n])

    in_loads = [
        load(src, dst, 13 + n)
        for n, (src, dst) in enumerate(((x2_in, x_buf), (cot_in, c_buf), (gf_in, t_buf), (o2_own, o_buf)))
    ]
    for one in in_loads:
        one.start()

    columns = pl.ds(pl.multiple_of(pair * lanes, lanes), lanes)
    pair_loads = [
        load(src.at[:, columns], dst, 19 + n)
        for n, (src, dst) in enumerate(((wq_in, wq), (wk_in, wk), (wv_in, wv)))
    ]
    for one in pair_loads:
        one.start()

    def weight_load(k, _):
        n, f = lax.div(k, tiles), lax.rem(k, tiles)
        cols = pl.ds(pl.multiple_of(first_col + f * depth, depth), depth)
        load(up_hbm.at[n, :, :, cols], final.at[k], 17).start()
        load(down_hbm.at[n, cols, :], stream.at[k], 18).start()
        return 0

    lax.fori_loop(0, 2 * tiles, weight_load, 0)
    vec[0] = jnp.zeros(vec.shape[1:], F32)
    in_loads[0].wait()
    for mb in range(micro):
        part = slice(mb * rows, (mb + 1) * rows)
        unit, _inv = norm_parts(x_buf[mb])
        e_all[0, part, :] = (unit * gain3[...] + shift3[...]).astype(BF)
    pl.semaphore_wait(barrier, parts + 5)
    swaps = [
        push(src, dst, swap_s.at[n], swap_r.at[n], to_y)
        for n, (src, dst) in enumerate(
            (
                (e_all.at[0], e_all.at[1]),
                (st_y.at[pl.ds(0, 2)], got_y.at[pl.ds(0, 2)]),
                (low_grad, got_y.at[pl.ds(2, 2)]),
            )
        )
    ]
    swaps[0].start()
    for one in in_loads[1:] + pair_loads:
        one.wait()
    load(final.at[pl.ds(0, 2 * tiles)], final.at[pl.ds(0, 2 * tiles)], 17).wait()
    load(stream, stream, 18).wait()
    mark_all = (marks, marks_got)
    gf_refs = (c_buf, t_buf)

    def up_tile(n, f):
        return final[n * tiles + f].reshape(width, depth)

    def down_tile(n, f):
        return stream[n * tiles + f]

    def gf_of(rowset):
        return jnp.concatenate([gf_refs[rowset][mb] for mb in range(micro)], axis=0)

    def folded(values):
        return values.reshape(micro, rows, width)

    def ones_of(rowset, wide):
        return jnp.concatenate([mark_all[rowset][...]] * (wide // lanes), axis=1) > 0.5

    def split(values, is_one):
        zero = jnp.zeros_like(values)
        return jnp.where(is_one, zero, values), jnp.where(is_one, values, zero)

    def kept_tile(low, high, rowset, f):
        part = pl.ds(pl.multiple_of(f * count, count), count)
        return jnp.concatenate([low[rowset, part, :], high[rowset, part, :]], axis=1)

    def through(rowset, acc):
        acc[...] = jnp.zeros_like(acc)

        def tile(f, _):
            bias_cols = pl.ds(pl.multiple_of(first_col + f * depth, depth), depth)
            is_one = ones_of(rowset, depth)
            e = e_all[rowset]
            gf = gf_of(rowset)
            u = jnp.where(
                is_one,
                mm(e, up_tile(1, f)) + up_b[1:2, bias_cols],
                mm(e, up_tile(0, f)) + up_b[0:1, bias_cols],
            )
            hidden, slope = gelu_both(u)
            part = pl.ds(pl.multiple_of(f * count, count), count)
            hidden = hidden.astype(BF)
            qa[rowset, part, :] = hidden[:, 0:lanes]
            ka[rowset, part, :] = hidden[:, lanes : 2 * lanes]
            back = jnp.where(is_one, mm_right(gf, down_tile(1, f)), mm_right(gf, down_tile(0, f)))
            du = (back * slope).astype(BF)
            va[rowset, part, :] = du[:, 0:lanes]
            doa[rowset, part, :] = du[:, lanes : 2 * lanes]
            none, one = split(du, is_one)
            acc[...] += folded(mm_right(none, up_tile(0, f)) + mm_right(one, up_tile(1, f)))
            return 0

        lax.fori_loop(0, tiles, tile, 0)

    def branch(rowset):
        is_one = ones_of(rowset, depth)

        def tile(f, total):
            none, one = split(kept_tile(qa, ka, rowset, f), is_one)
            return total + mm(none, down_tile(0, f)) + mm(one, down_tile(1, f))

        return lax.fori_loop(0, tiles, tile, jnp.zeros((count, width), F32))

    through(0, gx1_ref)
    swaps[0].wait()
    through(1, gx2_ref)
    st_y[0:2] = gx2_ref[...].astype(BF)
    swaps[1].start()

    def expert_weights(n):
        def weights(f, _):
            up_sum = jnp.zeros((width, depth), F32)
            down_sum = jnp.zeros((depth, width), F32)
            bias = jnp.zeros((1, depth), F32)
            for rowset in range(2):
                is_one = ones_of(rowset, depth)
                du_n = split(kept_tile(va, doa, rowset, f), is_one)[n]
                act_n = split(kept_tile(qa, ka, rowset, f), is_one)[n]
                up_sum = up_sum + mm_left(e_all[rowset], du_n)
                down_sum = down_sum + mm_left(act_n, gf_of(rowset))
                bias = bias + col_sum(du_n.astype(F32))
            per = pieces // 4
            down_rows = depth // strip
            for m in range(per):
                row, col = m % down_rows, m // down_rows
                shares[2 * n * per + m, f] = up_sum[m * strip : (m + 1) * strip, :].astype(BF)
                shares[(2 * n + 1) * per + m, f] = down_sum[
                    row * strip : (row + 1) * strip, col * depth : (col + 1) * depth
                ].astype(BF)
            row = 8 + n * 4 + half * 2 + lax.div(f, 2)
            col = pl.ds(pl.multiple_of(lax.rem(f, 2) * depth, depth), depth)
            vec[0, pl.ds(row, 1), col] = bias
            return 0

        lax.fori_loop(0, tiles, weights, 0)

    expert_weights(0)
    ticks(0, TICKS[0])
    low_grad[...] = folded(branch(1)).astype(BF)
    swaps[2].start()
    none, one = split(gf_of(0).astype(F32), ones_of(0, width))
    vec[0, 6:7, :] = col_sum(none)
    vec[0, 7:8, :] = col_sum(one)
    swaps[1].wait()

    def do2_copy(target):
        return push(st_do.at[target], rv_do.at[me], s_do2, r_do2, (grp, target))

    cross_out = jnp.zeros((width, width), F32)
    for mb in range(micro):
        unit, inverse = norm_parts(x_buf[mb])
        grad = gx1_ref[mb] + got_y[mb].astype(F32)
        vec[0, 4:5, :] += col_sum(grad * unit)
        vec[0, 5:6, :] += col_sum(grad)
        gx2 = c_buf[mb].astype(F32) + norm_back(unit, inverse, gain3[...], grad)
        gx2_ref[mb] = gx2
        gy2 = gx2.astype(BF)
        back = mm_right(gy2, co[...]).astype(BF)
        for p in range(pairs):
            st_do[mb * pairs + p] = back[:, p * lanes : (p + 1) * lanes]

        def send(p, _, mb=mb):
            target = mb * pairs + p

            @pl.when(target != me)
            def _():
                do2_copy(target).start()

            @pl.when(target == me)
            def _():
                rv_do[me] = st_do[me]

            return 0

        lax.fori_loop(0, pairs, send, 0)
        mixed = jnp.concatenate([o_buf[mb * pairs + p] for p in range(pairs)], axis=1)
        cross_out = cross_out + mm_left(mixed, gy2)
    early[0:width, :] = cross_out.astype(BF)
    expert_weights(1)
    ticks(TICKS[0], TICKS[1])
    gx1_ref[...] = folded(
        branch(0) + jnp.where(ones_of(0, width), down_b[1:2, :], down_b[0:1, :])
    )
    streams = [load(src, stream, 11 + n) for n, src in enumerate((m_in, a_in))]
    streams[0].start()
    loads = load_three((qa2_in, ka2_in, va2_in), 0)
    for one in loads:
        one.start()
    swaps[2].wait()
    for mb in range(micro):
        block_out[mb] = (x_buf[mb] + gx1_ref[mb] + got_y[2 + mb].astype(F32)).astype(BF)
    in_loads = [
        load(src, dst, 13 + n)
        for n, (src, dst) in enumerate(((x1_in, x_buf), (c_in, c_buf), (tokens_in, t_buf), (o1_own, o_buf)))
    ]
    for one in in_loads:
        one.start()
    wait_in(rv_do.at[pl.ds(0, parts - 1)], r_do2, to_y)
    wait_out(st_do.at[pl.ds(0, parts - 1)], s_do2, to_y)
    for one in loads:
        one.wait()

    def clear(s, _):
        part = pl.ds(pl.multiple_of(s * rows, rows), rows)
        for h in range(2):
            dk_acc[h, part, :] = jnp.zeros((rows, lanes), F32)
            dv_acc[h, part, :] = jnp.zeros((rows, lanes), F32)
            dq_acc[h, part, :] = jnp.zeros((rows, lanes), F32)
        return 0

    def grad_features(grads, mixed, head):
        own, place = lanes_of(grads.shape, head)
        grads = grads.astype(F32)
        delta = jnp.sum(jnp.where(own, grads * mixed.astype(F32), 0.0), axis=1, keepdims=True)
        high, middle, low = three_parts(delta)
        other = jnp.where(place == 0, -high, 0.0)
        other = jnp.where(place == 1, -middle, other)
        other = jnp.where(place == 2, -low, other)
        return jnp.where(own, grads, other).astype(BF)

    def tile(query, grads, keys, values, mask):
        scores = mm_right(keys, query)
        if mask is not None:
            scores = jnp.where(mask, scores, HIDE)
        prob = jnp.exp(scores)
        back = mm_right(values, grads)
        score_grad = (prob * back).astype(BF)
        return (
            mm_left(score_grad, keys),
            mm(score_grad, query),
            mm(prob.astype(BF), grads),
        )

    def join(zero_head, one_head):
        own, _ = lanes_of(zero_head.shape, 0)
        return jnp.where(own, zero_head, one_head)

    lax.fori_loop(0, parts, clear, 0)

    chunk = 2 * rows
    def cross_block(k, _):
        t = lax.rem(me + 1 + k, parts)
        part = pl.ds(pl.multiple_of(t * rows, rows), rows)
        grads = [grad_features(rv_do[t], o2[t], h) for h in range(2)]
        queries = [qa[h, part, :] for h in range(2)]
        sums = [jnp.zeros((rows, lanes), F32)] * 2
        for n in range(length // chunk):
            keys = slice(n * chunk, (n + 1) * chunk)
            for h in range(2):
                dq, dk, dv = tile(queries[h], grads[h], ka[h, keys, :], va[h, keys, :], None)
                sums[h] = sums[h] + dq
                dk_acc[h, keys, :] += dk
                dv_acc[h, keys, :] += dv
        st_do[t] = (join(sums[0], sums[1]) * scaling).astype(BF)

        @pl.when(k < parts - 1)
        def _():
            a2a(st_do, rv_dq2, s_dq2, r_dq2, t).start()

        @pl.when(k == parts - 1)
        def _():
            rv_dq2[me] = st_do[me]

        @pl.when(lax.rem(k, 2) == 0)
        def _():
            ticks(TICKS[0] + TICKS[1] + lax.div(k, 2) * TICKS[2], TICKS[2])

        return 0

    lax.fori_loop(0, parts, cross_block, 0)

    loads = load_three((qa1_in, ka1_in, va1_in), 1)
    for load in loads:
        load.start()

    def cross_source(s, total):
        part = pl.ds(pl.multiple_of(s * rows, rows), rows)
        grads = jnp.concatenate(
            [join(dk_acc[0, part, :], dk_acc[1, part, :]), join(dv_acc[0, part, :], dv_acc[1, part, :])], axis=1
        )
        return total + mm_left(stream[s], grads.astype(BF))

    all_arrived(rv_dq2, r_dq2)
    wait_out(st_do.at[pl.ds(0, parts - 1)], s_dq2, to_y)
    for one in in_loads:
        one.wait()

    def gathered(ref, mb, first):
        return jnp.concatenate(
            [ref[mb * pairs + p, first * rows : (first + 1) * rows, :] for p in range(pairs)], axis=1
        )

    def second_back(mb, _):
        dq2 = gathered(rv_dq2, mb, 0)
        dc = mm_right(dq2, cq[...])
        unit, inverse = norm_parts(x_buf[mb])
        vec[0, 2:3, :] += col_sum(dc * unit)
        vec[0, 3:4, :] += col_sum(dc)
        gx1 = gx2_ref[mb] + norm_back(unit, inverse, gain2[...], dc)
        gx1_ref[mb] = gx1
        low_grad[mb] = gx1.astype(BF)
        back = mm_right(low_grad[mb], wo[...]).astype(BF)
        for p in range(pairs):
            st_do[mb * pairs + p] = back[:, p * lanes : (p + 1) * lanes]

        def send(p, _):
            target = mb * pairs + p

            @pl.when(target != me)
            def _():
                a2a(st_do, rv_do, s_do1, r_do1, target).start()

            @pl.when(target == me)
            def _():
                rv_do[me] = st_do[me]

            return 0

        lax.fori_loop(0, pairs, send, 0)
        return 0

    lax.fori_loop(0, micro, second_back, 0)
    ticks(TICKS[0] + TICKS[1] + 4 * TICKS[2], TICKS[3])
    streams[0].wait()
    sums = lax.fori_loop(0, parts, cross_source, jnp.zeros((width, 2 * lanes), F32))
    streams[1].start()
    for n in range(2):
        cross[n * width : (n + 1) * width, :] = sums[:, n * lanes : (n + 1) * lanes].astype(BF)

    total = jnp.zeros((width, width), F32)
    for mb in range(micro):
        total = total + mm_left(c_buf[mb], gathered(rv_dq2, mb, 0))
    early[width : 2 * width, :] = total.astype(BF)
    total = jnp.zeros((width, width), F32)
    for mb in range(micro):
        mixed = jnp.concatenate([o_buf[mb * pairs + p] for p in range(pairs)], axis=1)
        total = total + mm_left(mixed, low_grad[mb])
    early[2 * width : 3 * width, :] = total.astype(BF)
    early_step(0)
    cross_step(0)
    ticks(TICKS[0] + TICKS[1] + 4 * TICKS[2] + TICKS[3], TICKS[4])
    for load in loads:
        load.wait()

    early_step(1)
    cross_step(1)
    all_arrived(rv_do, r_do1)

    lax.fori_loop(0, parts, clear, 0)

    def build(s, _):
        part = pl.ds(pl.multiple_of(s * rows, rows), rows)
        for h in range(2):
            doa[h, part, :] = grad_features(rv_do[s], o1[s], h)
        return 0

    lax.fori_loop(0, parts, build, 0)

    def self_tile(i, j, mask):
        q_part = pl.ds(pl.multiple_of(i * chunk, chunk), chunk)
        k_part = pl.ds(pl.multiple_of(j * chunk, chunk), chunk)
        for h in range(2):
            dq, dk, dv = tile(
                qa[h, q_part, :], doa[h, q_part, :], ka[h, k_part, :], va[h, k_part, :], mask
            )
            dq_acc[h, q_part, :] += dq
            dk_acc[h, k_part, :] += dk
            dv_acc[h, k_part, :] += dv

    g_late[...] = jnp.zeros_like(g_late)
    streams[1].wait()

    def y_copy(j):
        return push(st_y.at[j], got_y.at[j], da_s.at[j], da_r.at[j], to_y)

    def near_copy(n):
        return push(st_near.at[n], got_near.at[n], da_s.at[4 + n], da_r.at[4 + n], to_near)

    def far_copy():
        return push(st_far, got_far, da_s.at[6], da_r.at[6], to_far)

    def near_step(j):
        y_copy(j).wait_recv()
        da_keep[j] = (da_keep[j].astype(F32) + got_y[j].astype(F32)).astype(BF)

        @pl.when(lax.rem(j, 2) != near_bit)
        def _():
            st_near[lax.div(j, 2)] = da_keep[j]
            near_copy(lax.div(j, 2)).start()

    def far_step(j):
        @pl.when(lax.rem(j, 2) == near_bit)
        def _():
            near_copy(lax.div(j, 2)).wait_recv()
            total = da_keep[j].astype(F32) + got_near[lax.div(j, 2)].astype(F32)

            @pl.when(j == place)
            def _():
                da_sum[batch] = total

            @pl.when(j != place)
            def _():
                st_far[...] = total.astype(BF)
                far_copy().start()

    def self_column(j, _):
        key_place = lax.broadcasted_iota(jnp.int32, (chunk, chunk), 0)
        query_place = lax.broadcasted_iota(jnp.int32, (chunk, chunk), 1)
        self_tile(j, j, key_place <= query_place)

        def below(i, _):
            self_tile(i, j, None)
            return 0

        lax.fori_loop(j + 1, length // chunk, below, 0)

        part = pl.ds(pl.multiple_of(j * chunk, chunk), chunk)
        grads = jnp.concatenate(
            [
                (join(acc[0, part, :], acc[1, part, :]) * factor).astype(BF)
                for acc, factor in ((dq_acc, scaling), (dk_acc, 1.0), (dv_acc, 1.0))
            ],
            axis=1,
        )
        da = (
            mm_right(grads[:, 0:lanes], wq[...])
            + mm_right(grads[:, lanes : 2 * lanes], wk[...])
            + mm_right(grads[:, 2 * lanes : 3 * lanes], wv[...])
        )
        odd = half == 1
        st_y[j] = jnp.where(odd, da[0:rows], da[rows : 2 * rows]).astype(BF)
        da_keep[j] = jnp.where(odd, da[rows : 2 * rows], da[0:rows]).astype(BF)
        y_copy(j).start()
        for n in range(chunk // rows):
            g_late[...] += mm_left(stream[j * (chunk // rows) + n], grads[n * rows : (n + 1) * rows])
        ticks(TICKS[0] + TICKS[1] + 4 * TICKS[2] + TICKS[3] + TICKS[4] + j * TICKS[5], TICKS[5])

        @pl.when(j >= 1)
        def _():
            near_step(j - 1)

        @pl.when(j >= 2)
        def _():
            far_step(j - 2)

        @pl.when(j == 0)
        def _():
            early_step(2)
            cross_step(2)

        @pl.when(j == 1)
        def _():
            early_step(3)
            cross_step(3)

        @pl.when(j == 2)
        def _():
            early_step(4)
            cross_step(4)

        @pl.when(j == 3)
        def _():
            early_step(5)
            cross_step(5)

        return 0

    lax.fori_loop(0, length // chunk, self_column, 0)
    after = TICKS[0] + TICKS[1] + 4 * TICKS[2] + TICKS[3] + TICKS[4] + 4 * TICKS[5]
    share = TAIL
    starts = [after + sum(TAIL[:n]) for n in range(5)]
    assert after + sum(TAIL) == pieces + 6 * LAG
    for n in range(3):
        late[n * width : (n + 1) * width, :] = g_late[:, n * lanes : (n + 1) * lanes].astype(BF)
    late_step(0)
    near_step(3)
    late_step(1)
    early_step(6)
    cross_step(6)
    ticks(starts[0], share[0])
    far_step(2)
    late_step(2)
    far_step(3)
    early_step(7)
    cross_step(7)
    ticks(starts[1], share[1])
    late_step(3)
    early_step(8)

    def first_back(mb, _):
        da = da_sum[mb]
        unit, inverse = norm_parts(t_buf[mb].astype(F32))
        vec[0, 0:1, :] += col_sum(da * unit)
        vec[0, 1:2, :] += col_sum(da)
        token_grad[mb] = gx1_ref[mb] + norm_back(unit, inverse, gain1[...], da)
        return 0

    first_back(batch, 0)
    late_step(4)
    ticks(starts[2], share[2])
    far_copy().wait_recv()
    da_sum[1 - batch] = got_far[...].astype(F32)
    first_back(1 - batch, 0)
    vec_step(0)
    late_step(5)
    early_step(9)
    ticks(starts[3], share[3])
    late_step(6)
    vec_step(1)
    ticks(starts[4], share[4])
    late_step(7)
    vec_step(2)
    cross_step(8)
    early_step(10)
    late_step(8)
    vec_out[...] = vec[2]
    shares_done()
    for j in range(4):
        y_copy(j).wait_send()
    for n in range(2):
        near_copy(n).wait_send()
    far_copy().wait_send()
    wait_out(st_do.at[pl.ds(0, parts - 1)], s_do1, to_y)


def finish_kernel(shares, early, cross, late, vec, up, down, up_bias, down_bias, *grads):
    per, strip, depth = shares.shape[1] // 4, shares.shape[3], shares.shape[4]
    for n in range(2):
        for m in range(per):
            row, col = m % (depth // strip), m // (depth // strip)
            up[n, m * strip : (m + 1) * strip, :] = shares[0, 2 * n * per + m, 0].astype(F32)
            down[n, row * strip : (row + 1) * strip, col * depth : (col + 1) * depth] = shares[
                0, (2 * n + 1) * per + m, 0
            ].astype(F32)
    width = vec.shape[1]
    for n in range(2):
        down_bias[n : n + 1, :] = vec[6 + n : 7 + n, :]
        for k in range(4):
            row = 8 + n * 4 + k
            up_bias[n : n + 1, k * width : (k + 1) * width] = vec[row : row + 1, :]
    for n in range(3):
        grads[n][...] = early[n].astype(F32)
    lanes = late.shape[3]
    for source, refs in ((cross, grads[3:5]), (late, grads[5:8])):
        for n, ref in enumerate(refs):
            for p in range(source.shape[0]):
                ref[:, p * lanes : (p + 1) * lanes] = source[p, n].astype(F32)


def vmem_spec():
    return pl.BlockSpec(memory_space=pltpu.VMEM)


def fast_device(
    tokens, memory, expert_slot, doc_lengths, source_lengths, cotangent,
    norm1_gain, norm1_shift, self_query, self_key, self_value, self_out,
    norm2_gain, norm2_shift, cross_query, cross_key, cross_value, cross_out,
    norm3_gain, norm3_shift, up_weight, up_bias, down_weight, down_bias,
):
    micro, rows, width = tokens.shape
    parts = lax.axis_size("dp")
    pairs = HEADS // 2
    lanes = width // pairs
    length = parts * rows
    scaling = 1.0 / math.sqrt(width // HEADS)
    experts, _, hidden = up_weight.shape
    shape = jax.ShapeDtypeStruct
    dma, one = pltpu.SemaphoreType.DMA((parts,)), pltpu.SemaphoreType.DMA
    line = lambda v: v.reshape(1, width)

    any_spec = pl.BlockSpec(memory_space=pl.ANY)
    aug = shape((2, length, lanes), BF)
    blocks = shape((parts, rows, lanes), BF)
    full = shape((micro, rows, width), F32)
    low = shape((micro, rows, width), BF)
    vec = shape((1, width), F32)
    square = shape((width, width), F32)
    buf = lambda n: pltpu.VMEM((parts, n * rows, lanes), BF)

    count = micro * rows
    marks = jnp.broadcast_to(expert_slot.reshape(count, 1).astype(BF), (count, lanes))
    wide_all = shape((parts, rows, width), BF)
    outs1 = [wide_all, wide_all, full, low, full, blocks, blocks, aug, aug, aug, blocks, aug, aug, aug, blocks,
             low, shape((count, lanes), BF)]
    (a_all, m_all, x1, c, x2, o1_own, o2_own, qa1, ka1, va1, o1, qa2, ka2, va2, o2, gf_got, marks_got) = pl.pallas_call(
        functools.partial(forward_kernel, parts, pairs, rows, scaling),
        out_shape=outs1,
        in_specs=[pl.BlockSpec(memory_space=pltpu.SMEM)] * 2 + [vmem_spec()] * 6 + [any_spec] * 3
        + [vmem_spec()] * 2 + [any_spec] * 2 + [vmem_spec()] * 3,
        out_specs=[any_spec] * 2 + [vmem_spec()] * 5
        + ([any_spec] * 3 + [vmem_spec()]) * 2 + [vmem_spec()] * 2,
        scratch_shapes=[pltpu.VMEM((parts, rows, width), BF)] * 2
        + [pltpu.VMEM((2, length, lanes), BF)] * 6 + [pltpu.VMEM((width, lanes), BF)] * 5
        + [pltpu.SemaphoreType.DMA((5,)), pltpu.SemaphoreType.DMA((8,))]
        + [pltpu.VMEM((micro, rows, width), BF), buf(1), buf(1)]
        + [dma] * 4 + [one, one, one, dma, one, one] + [pltpu.SemaphoreType.DMA((2,))] * 2,
        compiler_params=pltpu.CompilerParams(
            collective_id=1, has_side_effects=True, vmem_limit_bytes=VMEM_BYTES
        ),
        name="attend_forward",
    )(
        doc_lengths, source_lengths, tokens, memory, line(norm1_gain), line(norm1_shift),
        line(norm2_gain), line(norm2_shift), self_query, self_key, self_value, self_out,
        cross_query, cross_key, cross_value, cross_out, cotangent, marks,
    )

    tiles = 4
    span = hidden // 2
    depth = span // tiles
    pieces = 16
    strip = 4 * width // pieces
    vec_pack = shape((16, width), F32)
    wide = lambda dtype, *dims: pltpu.VMEM(dims, dtype)
    early_shape = shape((3 * width, width), BF)
    cross_shape, late_shape = shape((pairs, 2 * width, lanes), BF), shape((pairs, 3 * width, lanes), BF)
    all_shape = shape((2, pieces, tiles, strip, depth), BF)
    outs3 = [low, full, vec_pack, all_shape, early_shape, cross_shape, late_shape]
    acc = pltpu.VMEM((2, length, lanes), F32)
    aug_buf = pltpu.VMEM((2, length, lanes), BF)
    block_low = lambda *n: wide(BF, *n, rows, width)
    block_full = lambda *n: wide(F32, *n, rows, width)
    dmas = lambda *dims: pltpu.SemaphoreType.DMA(dims)
    block_out, token_grad, vec, all_shares, all_early, all_cross, all_late = pl.pallas_call(
        functools.partial(backward_kernel, parts, pairs, rows, scaling),
        out_shape=outs3,
        in_specs=[any_spec] * 2 + [vmem_spec()] * 2 + [any_spec] * 2 + [vmem_spec()] * 2
        + [any_spec, vmem_spec(), any_spec, vmem_spec(), vmem_spec()]
        + [any_spec] * 3 + [vmem_spec()] + [any_spec] * 3 + [vmem_spec()]
        + [any_spec] * 6 + [vmem_spec()] * 2 + [any_spec] * 3 + [vmem_spec()] * 2,
        out_specs=[vmem_spec()] * 3 + [any_spec] * 4,
        scratch_shapes=[wide(BF, width, lanes)] * 3
        + [block_full(micro), block_low(micro), block_low(micro), buf(1),
                        wide(BF, 2, count, width), block_full(micro), buf(1), buf(1), buf(1), aug_buf, acc, acc, acc,
                        block_full(micro), block_low(micro), aug_buf, aug_buf, aug_buf,
                        block_low(parts), block_low(4), block_low(4), block_low(4),
                        block_low(2), block_low(2), block_low(), block_low(), block_full(micro),
                        wide(BF, pieces, tiles, strip, depth), wide(BF, pieces, tiles, strip, depth),
                        wide(BF, pieces, 3, strip, depth),
                        wide(BF, pieces, 2, strip, depth), wide(BF, 3 * width, width),
                        wide(BF, 2 * width, lanes), wide(BF, 3 * width, lanes)]
        + [wide(BF, (3 * width) >> (d + 1), width) for d in range(5)]
        + [wide(BF, (2 * width) >> (d + 1), lanes) for d in range(3)]
        + [wide(BF, (3 * width) >> (d + 1), lanes) for d in range(3)]
        + [wide(F32, 3, 16, width), wide(F32, 12, 16, width), wide(F32, width, 3 * lanes)]
        + [dmas(4), dmas(pieces, 3), dmas(pieces, 5), dmas(4), dmas(22)]
        + [dmas(10), dmas(10), dmas(8), dmas(8), dmas(8), dmas(8), dmas(2), dmas(2), dmas(3), dmas(3), dmas(7), dmas(7)]
        + [one] * 6,
        compiler_params=pltpu.CompilerParams(
            collective_id=3, has_side_effects=True, vmem_limit_bytes=VMEM_BYTES
        ),
        name="attend_backward",
    )(
        x2, o2_own, marks, marks_got, cotangent, gf_got, line(norm3_gain), line(norm3_shift),
        up_weight.reshape(experts, 4, width // 4, hidden), up_bias, down_weight, down_bias, cross_out,
        qa1, ka1, va1, o1, qa2, ka2, va2, o2, tokens, x1, c, a_all, m_all, o1_own,
        line(norm1_gain), line(norm2_gain), self_query, self_key, self_value, self_out, cross_query,
    )

    steps = 2 * tiles
    height = width // steps
    outs4 = [shape(up_weight.shape, F32), shape(down_weight.shape, F32), shape(up_bias.shape, F32),
             shape(down_bias.shape, F32)] + [square] * 8
    whole = lambda v: pl.BlockSpec(v, lambda i: (0,) * len(v))
    (up_total, down_total, up_bias_total, down_bias_total,
     g_co, g_cq, g_so, g_ck, g_cv, g_sq, g_sk, g_sv) = pl.pallas_call(
        finish_kernel,
        grid=(steps,),
        out_shape=outs4,
        in_specs=[
            pl.BlockSpec((1, pieces, 1, strip, depth),
                         lambda i: (lax.div(i, tiles), 0, lax.rem(i, tiles), 0, 0)),
            pl.BlockSpec((3, height, width), lambda i: (0, i, 0)),
            pl.BlockSpec((pairs, 2, height, lanes), lambda i: (0, 0, i, 0)),
            pl.BlockSpec((pairs, 3, height, lanes), lambda i: (0, 0, i, 0)),
            whole((16, width)),
        ],
        out_specs=[
            pl.BlockSpec((experts, width, depth), lambda i: (0, 0, i)),
            pl.BlockSpec((experts, depth, width), lambda i: (0, i, 0)),
            whole(up_bias.shape),
            whole(down_bias.shape),
        ] + [pl.BlockSpec((height, width), lambda i: (i, 0))] * 8,
        compiler_params=pltpu.CompilerParams(vmem_limit_bytes=VMEM_BYTES),
        name="finish",
    )(
        all_shares, all_early.reshape(3, width, width),
        all_cross.reshape(pairs, 2, width, lanes), all_late.reshape(pairs, 3, width, lanes), vec,
    )

    return (
        block_out, token_grad, vec[0], vec[1], g_sq, g_sk, g_sv, g_so, vec[2], vec[3],
        g_cq, g_ck, g_cv, g_co, vec[4], vec[5],
        up_total, up_bias_total, down_total, down_bias_total,
    )


def solution(mesh):
    fits = dict(mesh.shape) == {"grp": 4, "dp": 8}
    return jax.shard_map(
        fast_device if fits else per_device,
        mesh=mesh,
        in_specs=(
            P(None, ("grp", "dp"), None),
            P(None, ("grp", "dp"), None),
            P(None, ("grp", "dp"), None),
            P(None, "grp", None),
            P(None, "grp", None),
            P(None, ("grp", "dp"), None),
            P(),
            P(),
            P(),
            P(),
            P(),
            P(),
            P(),
            P(),
            P(),
            P(),
            P(),
            P(),
            P(),
            P(),
            P("grp", None, None),
            P("grp", None),
            P("grp", None, None),
            P("grp", None),
        ),
        out_specs=(
            P(None, ("grp", "dp"), None),
            P(None, ("grp", "dp"), None),
            P(),
            P(),
            P(),
            P(),
            P(),
            P(),
            P(),
            P(),
            P(),
            P(),
            P(),
            P(),
            P(),
            P(),
            P("grp", None, None),
            P("grp", None),
            P("grp", None, None),
            P("grp", None),
        ),
        check_vma=False,
    )
```
